128 devices in a mesh: fsdp: 64 (over x, y_hi, z, core), rep: 2 (over y_lo).
Axes of the slice: x: 4, y: 4 (y_hi: 2, y_lo: 2; y = y_hi * 2 + y_lo), z: 4, core: 2. Of those that a mesh axis runs over, the one named last changes fastest.
Arguments:
- tokens: bfloat16 [2, 16384, 1152], P(None, ('fsdp', 'rep')), may hold values from -6 to 6
- picture: int32 [2, 16384], replicated, may hold values from -16384 to 319, as said below
- cotangent: bfloat16 [2, 16384, 1152], P(None, ('fsdp', 'rep')), may hold values from -6 to 6
- ln1_gain: float32 [1152], replicated, may hold values from 0.1 to 1.9
- ln1_bias: float32 [1152], replicated, may hold values from -1.75 to 1.75
- w_query: bfloat16 [1152, 1152], P('fsdp'), may hold values from -0.1875 to 0.1875
- b_query: float32 [1152], replicated, may hold values from -1.75 to 1.75
- w_key: bfloat16 [1152, 1152], P('fsdp'), may hold values from -0.1875 to 0.1875
- w_value: bfloat16 [1152, 1152], P('fsdp'), may hold values from -0.1875 to 0.1875
- b_value: float32 [1152], replicated, may hold values from -1.75 to 1.75
- w_out: bfloat16 [1152, 1152], P('fsdp'), may hold values from -0.875 to 0.875
- b_out: float32 [1152], replicated, may hold values from -1.75 to 1.75
- ln2_gain: float32 [1152], replicated, may hold values from 0.1 to 1.9
- ln2_bias: float32 [1152], replicated, may hold values from -1.75 to 1.75
- w_fc1: bfloat16 [1152, 4304], P('fsdp'), may hold values from -0.1875 to 0.1875
- b_fc1: float32 [4304], replicated, may hold values from -1.75 to 1.75
- w_fc2: bfloat16 [4304, 1152], P(None, 'fsdp'), may hold values from -0.09375 to 0.09375
- b_fc2: float32 [1152], replicated, may hold values from -1.75 to 1.75
Outputs:
- mixed: bfloat16 [2, 16384, 1152], P(None, ('fsdp', 'rep'))
- grad_tokens: bfloat16 [2, 16384, 1152], P(None, ('fsdp', 'rep'))
- grad_ln1_gain: float32 [1152], replicated
- grad_ln1_bias: float32 [1152], replicated
- grad_w_query: float32 [1152, 1152], P('fsdp')
- grad_b_query: float32 [1152], replicated
- grad_w_key: float32 [1152, 1152], P('fsdp')
- grad_w_value: float32 [1152, 1152], P('fsdp')
- grad_b_value: float32 [1152], replicated
- grad_w_out: float32 [1152, 1152], P('fsdp')
- grad_b_out: float32 [1152], replicated
- grad_ln2_gain: float32 [1152], replicated
- grad_ln2_bias: float32 [1152], replicated
- grad_w_fc1: float32 [1152, 4304], P('fsdp')
- grad_b_fc1: float32 [4304], replicated
- grad_w_fc2: float32 [4304, 1152], P(None, 'fsdp')
- grad_b_fc2: float32 [1152], replicated
The draws below stay inside these ranges and needn't reach their ends.
Inputs may be any that keep to these rules, and one draw needn't show every extreme that they name: Tokens with one nonnegative id form one picture of 100 to 1024 consecutive tokens inside one packed row of 2048 tokens (rows are consecutive runs of 2048 tokens); each row begins with a picture of odd length followed by a picture of exactly 1024 tokens; every negative id marks a padding token and occurs once in its micro-batch.
All inputs are finite; a program needn't handle non-finite values.
Results may differ from the reference program's by a relative error of at most 0.014.
Values may be sent and summed in bfloat16 or wider, within the bound.
A program may use at most 320 MiB of HBM per device.

```python
import jax
import jax.numpy as jnp
from jax import lax

D = 1152
HEADS = 16
HEAD_DIM = 72
FF = 4304
MICRO = 2
ROW = 2048
PIC_MIN = 100
PIC_MAX = 1024
TOKENS_MB = 16384


def draw_picture(key, part):
    key = jax.random.fold_in(key, 7)
    row_count = MICRO * (TOKENS_MB // ROW)
    slots = ROW // PIC_MIN
    key_first, key_rest = jax.random.split(key)
    first = 2 * jax.random.randint(key_first, (row_count, 1), PIC_MIN // 2, PIC_MAX // 2) + 1
    second = jnp.full((row_count, 1), PIC_MAX, jnp.int32)
    others = jax.random.randint(key_rest, (row_count, slots - 2), PIC_MIN, PIC_MAX + 1)
    lengths = jnp.concatenate([first.astype(jnp.int32), second, others.astype(jnp.int32)], axis=1)
    ends = jnp.cumsum(lengths, axis=1)
    starts = ends - lengths
    used = ends <= ROW
    place = jnp.arange(ROW, dtype=jnp.int32)
    inside = (place[None, :, None] >= starts[:, None, :]) & (place[None, :, None] < ends[:, None, :]) & used[:, None, :]
    which = jnp.sum(inside.astype(jnp.int32) * jnp.arange(slots, dtype=jnp.int32)[None, None, :], axis=2)
    valid = jnp.any(inside, axis=2)
    row_index = jnp.arange(row_count, dtype=jnp.int32)[:, None]
    ident = row_index * slots + which
    flat = row_index % (TOKENS_MB // ROW) * ROW + place[None, :]
    ids = jnp.where(valid, ident, -(flat + 1))
    return ids.reshape(MICRO, TOKENS_MB).astype(jnp.int32)


def block_scale(stream_key, extent, cuts, least, largest):
    factor_of = 1.0
    for position, shards_of in cuts:
        heights = jax.random.uniform(jax.random.fold_in(jax.random.fold_in(stream_key, 6), position), (shards_of,), jnp.float32, least / len(cuts), largest / len(cuts))
        factor_of = factor_of * jnp.repeat(jnp.exp(heights), extent[position] // shards_of).reshape((-1,) + (1,) * (len(extent) - 1 - position))
    return factor_of


def noise(key, shape, width, reach, cuts=(), held_as=jnp.bfloat16):
    loudness = block_scale(key, shape, cuts, -0.22, 0.18) if cuts else 1.0
    values = jax.random.normal(key, shape, jnp.float32) * width * loudness
    return jnp.minimum(jnp.maximum(values, -reach), reach).astype(held_as)


def setup_inputs(seed: int = 0) -> dict:
    splits = jax.random.split(jax.random.key(seed), 19)
    tokens = noise(splits[0], (MICRO, TOKENS_MB, D), 1.0, 6.0, ((1, 128),))
    picture = draw_picture(jax.random.fold_in(splits[18], 71), 0)
    cotangent = noise(splits[2], (MICRO, TOKENS_MB, D), 1.0, 6.0, ((1, 128),))
    ln1_gain = jnp.clip(1.0 + 0.18 * jax.random.normal(splits[3], (D,), jnp.float32), 0.1, 1.9)
    ln1_bias = noise(splits[4], (D,), 0.3, 1.75, (), jnp.float32)
    w_query = noise(splits[5], (D, D), D ** -0.5, 0.1875, ((0, 64),))
    b_query = noise(splits[6], (D,), 0.3, 1.75, (), jnp.float32)
    w_key = noise(splits[7], (D, D), D ** -0.5, 0.1875, ((0, 64),))
    w_value = noise(splits[8], (D, D), D ** -0.5, 0.1875, ((0, 64),))
    b_value = noise(splits[9], (D,), 0.3, 1.75, (), jnp.float32)
    w_out = noise(splits[10], (D, D), (D // 24) ** -0.5, 0.875, ((0, 64),))
    b_out = noise(splits[11], (D,), 0.3, 1.75, (), jnp.float32)
    ln2_gain = jnp.clip(1.0 + 0.18 * jax.random.normal(splits[12], (D,), jnp.float32), 0.1, 1.9)
    ln2_bias = noise(splits[13], (D,), 0.3, 1.75, (), jnp.float32)
    w_fc1 = noise(splits[14], (D, FF), D ** -0.5, 0.1875, ((0, 64),))
    b_fc1 = noise(splits[15], (FF,), 0.3, 1.75, (), jnp.float32)
    w_fc2 = noise(splits[16], (FF, D), FF ** -0.5, 0.09375, ((1, 64),))
    b_fc2 = noise(splits[17], (D,), 0.3, 1.75, (), jnp.float32)
    return dict(tokens=tokens, picture=picture, cotangent=cotangent, ln1_gain=ln1_gain, ln1_bias=ln1_bias, w_query=w_query, b_query=b_query, w_key=w_key, w_value=w_value, b_value=b_value, w_out=w_out, b_out=b_out, ln2_gain=ln2_gain, ln2_bias=ln2_bias, w_fc1=w_fc1, b_fc1=b_fc1, w_fc2=w_fc2, b_fc2=b_fc2)


@jax.custom_vjp
def low(v):
    return lax.optimization_barrier(v.astype(jnp.bfloat16)).astype(jnp.float32)

@jax.custom_vjp
def low_back(v):
    return v

def low_keep(v):
    return (low(v), None)

def low_pass(kept, grad):
    return (grad,)

def back_keep(v):
    return (v, None)

def back_low(kept, grad):
    return (low(grad),)
low.defvjp(low_keep, low_pass)
low_back.defvjp(back_keep, back_low)
EPS = 1e-06
NEG = -1e+30

def normalize(values, gain, bias):
    center = values - lax.optimization_barrier(jnp.mean(values, axis=-1, keepdims=True))
    spread = lax.optimization_barrier(jnp.mean(center * center, axis=-1, keepdims=True))
    return center * lax.rsqrt(spread + EPS) * gain + bias

def matmul(left, right):
    return jnp.dot(left, right, precision=lax.Precision.HIGHEST, preferred_element_type=jnp.float32)

def layer(inputs, ids, params):
    gain_one, bias_one, w_query, b_query, w_key, w_value, b_value, w_out, b_out, gain_two, bias_two, w_fc1, b_fc1, w_fc2, b_fc2 = params
    length = inputs.shape[0]
    normed1 = low(normalize(inputs, gain_one, bias_one))
    query = low(low_back(matmul(normed1, w_query) + b_query)).reshape(length, HEADS, HEAD_DIM)
    keys = low(low_back(matmul(normed1, w_key))).reshape(length, HEADS, HEAD_DIM)
    values = low(low_back(matmul(normed1, w_value) + b_value)).reshape(length, HEADS, HEAD_DIM)
    scores = jnp.einsum('qhd,khd->hqk', query, keys, precision=lax.Precision.HIGHEST) * HEAD_DIM ** (-0.5)
    scores = low_back(scores)
    allowed = (ids[:, None] == ids[None, :])[None]
    scores = jnp.where(allowed, scores, NEG)
    probs = low(jax.nn.softmax(scores, axis=-1))
    attended = jnp.einsum('hqk,khd->qhd', probs, values, precision=lax.Precision.HIGHEST).reshape(length, HEADS * HEAD_DIM)
    attended = low(low_back(attended))
    mid = inputs + low_back(matmul(attended, w_out) + b_out)
    normed2 = low(normalize(mid, gain_two, bias_two))
    hidden = low_back(matmul(normed2, w_fc1) + b_fc1)
    active = low(jax.nn.gelu(hidden, approximate=True))
    return mid + low_back(matmul(active, w_fc2) + b_fc2)

def reference(tokens, picture, cotangent, ln1_gain, ln1_bias, w_query, b_query, w_key, w_value, b_value, w_out, b_out, ln2_gain, ln2_bias, w_fc1, b_fc1, w_fc2, b_fc2):
    params = tuple((item.astype(jnp.float32) for item in (ln1_gain, ln1_bias, w_query, b_query, w_key, w_value, b_value, w_out, b_out, ln2_gain, ln2_bias, w_fc1, b_fc1, w_fc2, b_fc2)))
    rows_in = tokens.astype(jnp.float32).reshape(-1, ROW, D)
    rows_ids = picture.reshape(-1, ROW)
    rows_cot = cotangent.astype(jnp.float32).reshape(-1, ROW, D)

    def step(carry, item):
        row_in, row_ids, row_cot = item
        result, back = jax.vjp(lambda inputs, weights: layer(inputs, row_ids, weights), row_in, params)
        grad_in, grad_params = back(row_cot)
        carry = jax.tree.map(lambda left, right: left + right, carry, grad_params)
        return (carry, (result.astype(jnp.bfloat16), grad_in.astype(jnp.bfloat16)))
    zeros = tuple((jnp.zeros_like(item) for item in params))
    grads, (results, grad_rows) = lax.scan(step, zeros, (rows_in, rows_ids, rows_cot))
    mixed = results.reshape(tokens.shape)
    grad_tokens = grad_rows.reshape(tokens.shape)
    return (mixed, grad_tokens, grads[0], grads[1], grads[2], grads[3], grads[4], grads[5], grads[6], grads[7], grads[8], grads[9], grads[10], grads[11], grads[12], grads[13], grads[14])
```

```python
import functools

import jax
import jax.numpy as jnp
import numpy as np
from jax import lax
from jax.experimental import pallas as pl
from jax.experimental.pallas import tpu as pltpu
from jax.sharding import PartitionSpec as P

MESH = pl.DeviceIdType.MESH
BF = jnp.bfloat16
F32 = jnp.float32
LANES = 128
ORDERS = (("x", "y", "z"), ("y", "z", "x"), ("z", "x", "y"))
AXES = ("x", "y", "z")


def here():
    shard = lax.axis_index("fsdp")
    low = lax.axis_index("rep")
    place = {
        "x": lax.div(shard, 16),
        "y": lax.rem(lax.div(shard, 8), 2) * 2 + low,
        "z": lax.rem(lax.div(shard, 2), 4),
    }
    return place, lax.rem(shard, 2)


def moved(place, axis, steps):
    steps = steps % 4
    if steps == 0:
        return place
    other = dict(place)
    other[axis] = lax.rem(place[axis] + steps, 4)
    return other


def device_at(place, core):
    high = lax.div(place["y"], 2)
    return (((place["x"] * 2 + high) * 4 + place["z"]) * 2 + core, lax.rem(place["y"], 2))


def greet(peers):
    barrier = pltpu.get_barrier_semaphore()
    for peer in peers:
        pl.semaphore_signal(barrier, inc=1, device_id=peer, device_id_type=MESH)
    pl.semaphore_wait(barrier, len(peers))


def torus_peers(place, core):
    peers = [device_at(place, 1 - core)]
    for axis in AXES:
        for steps in (1, 2, 3):
            peers.append(device_at(moved(place, axis, steps), core))
    return peers


def part_columns(part, half, width):
    return pl.ds(pl.multiple_of(part * 2 * width + half * width, LANES), width)


def piece_of(ref, part, width, place, core):
    return ref.at[
        place["x"],
        lax.div(place["y"], 2),
        place["z"],
        core,
        :,
        part_columns(part, lax.rem(place["y"], 2), width),
    ]


def block_of(ref, part, width, place, core, axis, half=None):
    where = {"x": place["x"], "y": lax.div(place["y"], 2), "z": place["z"]}
    if axis == "y":
        where["y"] = pl.ds(0, 2) if half is None else pl.ds(half, 1)
        columns = pl.ds(part * 2 * width, 2 * width)
    else:
        where[axis] = pl.ds(0, 4) if half is None else pl.ds(2 * half, 2)
        columns = part_columns(part, lax.rem(place["y"], 2), width)
    return ref.at[where["x"], where["y"], where["z"], core, :, columns]


GATHER_SEMS = 3 + 3 + 8 + 8 + 16


def gather_kernel(width, own, full, send, recv, local):
    place, core = here()
    greet(torus_peers(place, core))
    twin = device_at(place, 1 - core)
    started = []

    def sem_index(part, kind, index):
        return part * GATHER_SEMS + {"a": 0, "b": 3, "c": 6, "d": 14, "s": 22}[kind] + index

    def push(source, target, slot, device):
        copy = pltpu.make_async_remote_copy(
            src_ref=source,
            dst_ref=target,
            send_sem=send.at[slot],
            recv_sem=recv.at[slot],
            device_id=device,
            device_id_type=MESH,
        )
        copy.start()
        started.append(copy)

    def arrived(region, slot):
        pltpu.make_async_remote_copy(
            src_ref=region,
            dst_ref=region,
            send_sem=send.at[slot],
            recv_sem=recv.at[slot],
            device_id=twin,
            device_id_type=MESH,
        ).wait_recv()

    low = lax.rem(place["y"], 2)
    locals_ = []
    for part, (one, two, three) in enumerate(ORDERS):
        source = own.at[:, part_columns(part, low, width)]
        target = piece_of(full, part, width, place, core)
        copy = pltpu.make_async_copy(source, target, local.at[part])
        copy.start()
        locals_.append(copy)
        for steps in (1, 3, 2):
            push(
                source,
                target,
                sem_index(part, "a", steps - 1),
                device_at(moved(place, one, steps), core),
            )
    for part, (one, two, three) in enumerate(ORDERS):
        locals_[part].wait()
        for steps in (1, 3, 2):
            arrived(
                piece_of(full, part, width, moved(place, one, -steps), core),
                sem_index(part, "a", steps - 1),
            )
        block = block_of(full, part, width, place, core, one)
        for steps in (1, 3, 2):
            push(block, block, sem_index(part, "b", steps - 1), device_at(moved(place, two, steps), core))
        for way in (1, 3):
            push(block, block, sem_index(part, "c", (way // 2) * 4), device_at(moved(place, three, way), core))
        push(block, block, sem_index(part, "s", 0), twin)
    for steps in (1, 3, 2):
        for part, (one, two, three) in enumerate(ORDERS):
            block = block_of(full, part, width, moved(place, two, -steps), core, one)
            arrived(block, sem_index(part, "b", steps - 1))
            for way in (1, 3):
                push(
                    block,
                    block,
                    sem_index(part, "c", (way // 2) * 4 + steps),
                    device_at(moved(place, three, way), core),
                )
            push(block, block, sem_index(part, "s", steps), twin)
    for steps in (0, 1, 3, 2):
        for part, (one, two, three) in enumerate(ORDERS):
            for way in (1, 3):
                origin = moved(moved(place, two, -steps), three, -way)
                block = block_of(full, part, width, origin, core, one)
                arrived(block, sem_index(part, "c", (way // 2) * 4 + steps))
                piece = block_of(full, part, width, origin, core, one, way // 2)
                push(
                    piece,
                    piece,
                    sem_index(part, "d", (way // 2) * 4 + steps),
                    device_at(moved(place, three, way), core),
                )
                push(block, block, sem_index(part, "s", way * 4 + steps), twin)
    for steps in (0, 1, 3, 2):
        for part, (one, two, three) in enumerate(ORDERS):
            origin = moved(moved(place, two, -steps), three, 2)
            for way in (1, 3):
                arrived(
                    block_of(full, part, width, origin, core, one, way // 2),
                    sem_index(part, "d", (way // 2) * 4 + steps),
                )
            block = block_of(full, part, width, origin, core, one)
            push(block, block, sem_index(part, "s", 8 + steps), twin)
    for part, (one, two, three) in enumerate(ORDERS):
        for way in range(4):
            for steps in range(4):
                origin = moved(moved(place, two, -steps), three, -way)
                arrived(
                    block_of(full, part, width, origin, 1 - core, one),
                    sem_index(part, "s", way * 4 + steps),
                )
    for copy in started:
        copy.wait_send()


def gather_slab(slab, tag):
    total = slab.shape[1]
    width = total // 6
    full = pl.pallas_call(
        functools.partial(gather_kernel, width),
        out_shape=jax.ShapeDtypeStruct((4, 2, 4, 2, 16, total), slab.dtype),
        in_specs=[pl.BlockSpec(memory_space=pl.ANY)],
        out_specs=pl.BlockSpec(memory_space=pl.ANY),
        scratch_shapes=[
            pltpu.SemaphoreType.DMA((3 * GATHER_SEMS,)),
            pltpu.SemaphoreType.DMA((3 * GATHER_SEMS,)),
            pltpu.SemaphoreType.DMA((3,)),
        ],
        compiler_params=pltpu.CompilerParams(collective_id=tag, has_side_effects=True),
        name="gather_slab",
    )(slab)
    return full.reshape(1024, total)


def reduce_kernel(width, grads, out, *scratch):
    acc, sib, mid, far, side, line, done = [scratch[3 * i : 3 * i + 3] for i in range(7)]
    send, recv, local = scratch[21:]
    place, core = here()
    greet(torus_peers(place, core))
    twin = device_at(place, 1 - core)
    started = []
    count = 16 + 8 + 8 + 3 + 3 + 1

    def slot_of(part, kind, index):
        return part * count + {"s": 0, "m": 16, "f": 24, "d": 32, "l": 35, "o": 38}[kind] + index

    def push(source, target, slot, device):
        copy = pltpu.make_async_remote_copy(
            src_ref=source,
            dst_ref=target,
            send_sem=send.at[slot],
            recv_sem=recv.at[slot],
            device_id=device,
            device_id_type=MESH,
        )
        copy.start()
        started.append(copy)

    def arrived(region, slot):
        pltpu.make_async_remote_copy(
            src_ref=region,
            dst_ref=region,
            send_sem=send.at[slot],
            recv_sem=recv.at[slot],
            device_id=twin,
            device_id_type=MESH,
        ).wait_recv()

    def add(target, *terms):
        def row(index, carry):
            total = target[index].astype(F32)
            for term in terms:
                total = total + term[index].astype(F32)
            target[index] = total.astype(BF)
            return carry

        lax.fori_loop(0, target.shape[0], row, 0)

    def half_of(ref, half):
        size = ref.shape[0] // 2
        return ref.at[pl.ds(half * size, size)]

    loads = {}
    for ahead in (2, 1, 3, 0):
        for part, (one, two, three) in enumerate(ORDERS):
            for over in range(4):
                spot = moved(moved(place, two, over), three, ahead)
                push(
                    block_of(grads, part, width, spot, 1 - core, one),
                    sib[part].at[ahead, over],
                    slot_of(part, "s", ahead * 4 + over),
                    twin,
                )
                copy = pltpu.make_async_copy(
                    block_of(grads, part, width, spot, core, one),
                    acc[part].at[ahead, over],
                    local.at[part * 16 + ahead * 4 + over],
                )
                copy.start()
                loads[part, ahead, over] = copy

    def ready(part, ahead, over):
        loads[part, ahead, over].wait()
        arrived(sib[part].at[ahead, over], slot_of(part, "s", ahead * 4 + over))

    for over in range(4):
        for part, (one, two, three) in enumerate(ORDERS):
            ready(part, 2, over)
            add(acc[part].at[2, over], sib[part].at[2, over])
            for half, way in ((0, 3), (1, 1)):
                push(
                    half_of(acc[part].at[2, over], half),
                    mid[part].at[half, over],
                    slot_of(part, "m", half * 4 + over),
                    device_at(moved(place, three, way), core),
                )
    for over in range(4):
        for part, (one, two, three) in enumerate(ORDERS):
            for half, way in ((0, 3), (1, 1)):
                ready(part, way, over)
                add(acc[part].at[way, over], sib[part].at[way, over])
                arrived(mid[part].at[half, over], slot_of(part, "m", half * 4 + over))
                add(half_of(acc[part].at[way, over], half), mid[part].at[half, over])
                push(
                    acc[part].at[way, over],
                    far[part].at[half, over],
                    slot_of(part, "f", half * 4 + over),
                    device_at(moved(place, three, way), core),
                )
    for over in (2, 1, 3, 0):
        for part, (one, two, three) in enumerate(ORDERS):
            ready(part, 0, over)
            for half in range(2):
                arrived(far[part].at[half, over], slot_of(part, "f", half * 4 + over))
            add(
                acc[part].at[0, over],
                sib[part].at[0, over],
                far[part].at[0, over],
                far[part].at[1, over],
            )
            if over:
                push(
                    acc[part].at[0, over],
                    side[part].at[over - 1],
                    slot_of(part, "d", over - 1),
                    device_at(moved(place, two, over), core),
                )

    def piece(part, axis, spot):
        if axis == "y":
            return acc[part].at[
                0,
                0,
                lax.div(spot["y"], 2),
                :,
                pl.ds(pl.multiple_of(lax.rem(spot["y"], 2) * width, LANES), width),
            ]
        return acc[part].at[0, 0, spot[axis]]

    for part, (one, two, three) in enumerate(ORDERS):
        for over in (1, 2, 3):
            arrived(side[part].at[over - 1], slot_of(part, "d", over - 1))
        add(acc[part].at[0, 0], side[part].at[0], side[part].at[1], side[part].at[2])
        for over in (2, 1, 3):
            spot = moved(place, one, over)
            push(
                piece(part, one, spot),
                line[part].at[over - 1],
                slot_of(part, "l", over - 1),
                device_at(spot, core),
            )
    low = lax.rem(place["y"], 2)
    partner = (lax.axis_index("fsdp"), 1 - low)
    for part, (one, two, three) in enumerate(ORDERS):
        for over in (1, 2, 3):
            arrived(line[part].at[over - 1], slot_of(part, "l", over - 1))
        total = piece(part, one, place)[...].astype(F32)
        for over in range(3):
            total = total + line[part][over].astype(F32)
        done[part][...] = total.astype(BF)
        columns = part_columns(part, low, width)
        push(done[part], out.at[:, columns], slot_of(part, "o", 0), partner)
        out[:, columns] = done[part][...]
    for part in range(3):
        arrived(out.at[:, part_columns(part, 1 - low, width)], slot_of(part, "o", 0))
    for copy in started:
        copy.wait_send()


def reduce_slab(grads, tag):
    total = grads.shape[1]
    width = total // 6

    def shapes(lead, half=False):
        found = []
        for one, two, three in ORDERS:
            if one == "y":
                found.append(pltpu.VMEM(lead + (1 if half else 2, 16, 2 * width), BF))
            else:
                found.append(pltpu.VMEM(lead + (2 if half else 4, 16, width), BF))
        return found

    count = 16 + 8 + 8 + 3 + 3 + 1
    return pl.pallas_call(
        functools.partial(reduce_kernel, width),
        out_shape=jax.ShapeDtypeStruct((16, total), BF),
        in_specs=[pl.BlockSpec(memory_space=pl.ANY)],
        out_specs=pl.BlockSpec(memory_space=pltpu.VMEM),
        scratch_shapes=(
            shapes((4, 4))
            + shapes((4, 4))
            + shapes((2, 4), True)
            + shapes((2, 4))
            + shapes((3,))
            + [pltpu.VMEM((3, 16, width), BF)] * 3
            + [pltpu.VMEM((16, width), BF)] * 3
            + [
                pltpu.SemaphoreType.DMA((3 * count,)),
                pltpu.SemaphoreType.DMA((3 * count,)),
                pltpu.SemaphoreType.DMA((48,)),
            ]
        ),
        compiler_params=pltpu.CompilerParams(
            collective_id=tag, has_side_effects=True, vmem_limit_bytes=60 << 20
        ),
        name="reduce_slab",
    )(grads.reshape(4, 2, 4, 2, 16, total))


def swap_kernel(own, full, send, recv, local):
    place, core = here()
    low = lax.rem(place["y"], 2)
    mine = (place["z"] * 2 + core) * 2 + low
    base = lax.div(lax.axis_index("fsdp"), 8) * 8

    def peer(index):
        return (base + lax.div(index, 2), lax.rem(index, 2))

    def partner(k):
        zz = lax.rem(place["z"] + k // 4, 4)
        cc = lax.rem(core + (k // 2) % 2, 2)
        ll = lax.rem(low + k % 2, 2)
        return (zz * 2 + cc) * 2 + ll

    def source(k):
        zz = lax.rem(place["z"] + 4 - k // 4, 4)
        cc = lax.rem(core + (k // 2) % 2, 2)
        ll = lax.rem(low + k % 2, 2)
        return (zz * 2 + cc) * 2 + ll

    greet([peer(partner(k)) for k in range(1, 16)])
    keep = pltpu.make_async_copy(own.at[mine], full.at[mine], local.at[0])
    keep.start()
    copies = []
    for k in (9, 11, 5, 13, 7, 15, 1, 3, 8, 10, 4, 12, 6, 14, 2):
        target = partner(k)
        copy = pltpu.make_async_remote_copy(
            src_ref=own.at[target],
            dst_ref=full.at[mine],
            send_sem=send.at[k],
            recv_sem=recv.at[k],
            device_id=peer(target),
            device_id_type=MESH,
        )
        copy.start()
        copies.append(copy)
    for k in range(1, 16):
        region = full.at[source(k)]
        pltpu.make_async_remote_copy(
            src_ref=region,
            dst_ref=region,
            send_sem=send.at[k],
            recv_sem=recv.at[k],
            device_id=peer(partner(k)),
            device_id_type=MESH,
        ).wait_recv()
    keep.wait()
    for copy in copies:
        copy.wait_send()


def swap_heads(blocks, tag):
    return pl.pallas_call(
        swap_kernel,
        out_shape=jax.ShapeDtypeStruct(blocks.shape, blocks.dtype),
        in_specs=[pl.BlockSpec(memory_space=pl.ANY)],
        out_specs=pl.BlockSpec(memory_space=pl.ANY),
        scratch_shapes=[
            pltpu.SemaphoreType.DMA((16,)),
            pltpu.SemaphoreType.DMA((16,)),
            pltpu.SemaphoreType.DMA((1,)),
        ],
        compiler_params=pltpu.CompilerParams(collective_id=tag, has_side_effects=True),
        name="swap_heads",
    )(blocks)


D = 1152
HEADS = 16
HEAD_DIM = 72
FF = 4304
ROW = 2048
EPS = 1e-06
NEG = -1e30
SCALE = HEAD_DIM**-0.5
LEAD = 1024
TAIL = 128
PACK = 3 * HEAD_DIM
WIDE = 256
VALUE_LANE = 16
FF_PAD = 4352
STEP = 256
STEPS = FF_PAD // STEP
QKV = HEADS * PACK
ATTN_MAIN = QKV + D
ATTN_CHUNK = 640
ATTN_TOTAL = 5376
MLP_MAIN = 2 * FF_PAD
MLP_CHUNK = 1152
MLP_TOTAL = 9984
TANH_A = 0.7978845608028654
TANH_B = 0.044715


def dot(left, right):
    return jnp.dot(left, right, preferred_element_type=F32)


def dot_nt(left, right):
    return lax.dot_general(left, right, (((1,), (1,)), ((), ())), preferred_element_type=F32)


def dot_tn(left, right):
    return lax.dot_general(left, right, (((0,), (0,)), ((), ())), preferred_element_type=F32)


def origin(index):
    lead = (index >> 4) * 18 + (index & 15)
    rest = index - LEAD
    tail = (rest >> 1) * 18 + 16 + (rest & 1)
    return jnp.where(index < LEAD, lead, tail)


def iota(shape, axis):
    return lax.broadcasted_iota(jnp.int32, shape, axis)


def onehot(mask):
    return mask.astype(F32).astype(BF)


def pick_rows(chunk, count):
    return onehot(iota((TAIL, count), 1) == 8 * iota((TAIL, count), 0) + chunk)


def normal(values):
    center = values - jnp.mean(values, axis=-1, keepdims=True)
    rate = lax.rsqrt(jnp.mean(center * center, axis=-1, keepdims=True) + EPS)
    return center * rate, rate


def normal_back(unit, rate, gain, grad):
    inner = grad * gain
    first = jnp.mean(inner, axis=-1, keepdims=True)
    second = jnp.mean(inner * unit, axis=-1, keepdims=True)
    return rate * (inner - first - unit * second)


def column_total(values):
    return jnp.sum(values, axis=0, keepdims=True)


def lanes(start, size):
    return pl.ds(pl.multiple_of(start, LANES), size)


def params(limit=60):
    return pltpu.CompilerParams(vmem_limit_bytes=limit << 20)


def project_kernel(x_ref, weight_ref, vec_ref, bias_ref, heads_ref, h_ref, tail_ref, flat):
    unit, _ = normal(x_ref[...].astype(F32))
    h_ref[...] = (unit * vec_ref[0:1] + vec_ref[1:2]).astype(BF)

    def spread(chunk, carry):
        picked = dot(pick_rows(chunk, LEAD), weight_ref[:, ATTN_MAIN : ATTN_MAIN + ATTN_CHUNK])
        tail_ref[:, lanes(chunk * ATTN_CHUNK, ATTN_CHUNK)] = picked.astype(BF)
        return carry

    lax.fori_loop(0, 8, spread, 0)

    def columns(index, carry):
        place = lanes(index * 384, 384)
        value = dot(h_ref[:, :LEAD], weight_ref[:, place]) + dot(h_ref[:, LEAD:], tail_ref[:, place])
        flat[:, place] = (value + bias_ref[:, place]).astype(BF)
        return carry

    lax.fori_loop(0, QKV // 384, columns, 0)
    for head in range(HEADS):
        block = flat[:, PACK * head : PACK * head + PACK]
        heads_ref[head] = jnp.concatenate([block, jnp.zeros((256, WIDE - PACK), BF)], axis=1)


def project_heads(x, weight, vec, bias):
    return pl.pallas_call(
        project_kernel,
        out_shape=(
            jax.ShapeDtypeStruct((HEADS, 256, WIDE), BF),
            jax.ShapeDtypeStruct((256, D), BF),
            jax.ShapeDtypeStruct((TAIL, 8 * ATTN_CHUNK), BF),
        ),
        scratch_shapes=[pltpu.VMEM((256, QKV), BF)],
        compiler_params=params(),
        name="project_heads",
    )(x, weight, vec, bias)


def attend_kernel(spans, packed_ref, row_ref, col_ref, o_ref, keep_ref, keys, queries, scores):
    row = pl.program_id(0)
    packed = packed_ref[...].reshape(ROW, WIDE)
    lane = iota((ROW, LANES), 1)
    zero = jnp.zeros((ROW, LANES), BF)
    keys[...] = jnp.where(lane < HEAD_DIM, packed[:, :LANES], zero)
    turned = jnp.concatenate(
        [packed[:, HEAD_DIM : 2 * HEAD_DIM], jnp.zeros((ROW, LANES - HEAD_DIM), BF)], axis=1
    )
    queries[...] = turned

    def block(index, carry):
        rows = pl.ds(index * 256, 256)
        query = queries[rows, :]
        mine = col_ref[0, rows, :]
        low = spans[row * 16 + index]
        high = spans[row * 16 + 8 + index]

        def score(step, top):
            part = pl.ds(step * 256, 256)
            value = dot_nt(query, keys[part, :]) * SCALE
            value = jnp.where(mine == row_ref[0, :, lanes(step * 256, 256)], value, NEG)
            scores[:, lanes(step * 256, 256)] = value
            return jnp.maximum(top, jnp.maximum(value[:, :LANES], value[:, LANES:]))

        top = lax.fori_loop(low, high, score, jnp.full((256, LANES), NEG, F32))
        top = jnp.max(top, axis=1, keepdims=True)

        def weigh(step, carry):
            mass, total = carry
            expo = jnp.exp(scores[:, lanes(step * 256, 256)] - top)
            mass = mass + expo[:, :LANES] + expo[:, LANES:]
            value = packed_ref[pl.ds(step * 2, 2), :, LANES:].reshape(256, LANES)
            return mass, total + dot(expo.astype(BF), value)

        zeros = jnp.zeros((256, LANES), F32)
        mass, total = lax.fori_loop(low, high, weigh, (zeros, zeros))
        mass = jnp.sum(mass, axis=1, keepdims=True)
        total = total / mass
        o_ref[pl.ds(index * 2, 2)] = total.astype(BF).reshape(2, 128, LANES)
        lane = iota((256, LANES), 1)
        keep_ref[0, rows, :] = jnp.where(lane == 0, top + jnp.log(mass), total)
        return carry

    lax.fori_loop(0, 8, block, 0)


def attend(spans, packed, row_ids, col_ids):
    return pl.pallas_call(
        attend_kernel,
        out_shape=(
            jax.ShapeDtypeStruct((16, 256, LANES), BF),
            jax.ShapeDtypeStruct((2, ROW, LANES), F32),
        ),
        grid_spec=pltpu.PrefetchScalarGridSpec(
            num_scalar_prefetch=1,
            grid=(2,),
            in_specs=[
                pl.BlockSpec((16, 128, WIDE), lambda m, s: (0, m, 0)),
                pl.BlockSpec((1, 1, ROW), lambda m, s: (m, 0, 0)),
                pl.BlockSpec((1, ROW, 1), lambda m, s: (m, 0, 0)),
            ],
            out_specs=(
                pl.BlockSpec((16, 128, LANES), lambda m, s: (0, m, 0)),
                pl.BlockSpec((1, ROW, LANES), lambda m, s: (m, 0, 0)),
            ),
            scratch_shapes=[
                pltpu.VMEM((ROW, LANES), BF),
                pltpu.VMEM((ROW, LANES), BF),
                pltpu.VMEM((256, ROW), F32),
            ],
        ),
        compiler_params=params(),
        name="attend",
    )(spans, packed, row_ids, col_ids)


def attend_back_kernel(
    spans, packed_ref, go_ref, keep_ref, row_ref, col_ref, out_ref, keys, queries, dkeys, dvalues
):
    row = pl.program_id(0)
    packed = packed_ref[...].reshape(ROW, WIDE)
    lane = iota((ROW, LANES), 1)
    zero = jnp.zeros((ROW, LANES), BF)
    keys[...] = jnp.where(lane < HEAD_DIM, packed[:, :LANES], zero)
    turned = jnp.concatenate(
        [packed[:, HEAD_DIM : 2 * HEAD_DIM], jnp.zeros((ROW, LANES - HEAD_DIM), BF)], axis=1
    )
    queries[...] = turned
    dkeys[...] = jnp.zeros_like(dkeys)
    dvalues[...] = jnp.zeros_like(dvalues)

    def block(index, carry):
        rows = pl.ds(index * 256, 256)
        query = queries[rows, :]
        back = go_ref[pl.ds(index * 2, 2)].reshape(256, LANES)
        mine = row_ref[0, :, lanes(index * 256, 256)]
        low = spans[row * 16 + index]
        high = spans[row * 16 + 8 + index]
        kept = keep_ref[0, rows, :]
        inner = jnp.sum(back.astype(F32) * kept, axis=1, keepdims=True)
        lane = iota((256, LANES), 1)
        stats = jnp.transpose(jnp.where(lane == 0, kept, inner))
        logsum = stats[0:1]
        inner = stats[1:2]

        def step(part, total):
            span = pl.ds(part * 256, 256)
            key = keys[span, :]
            value = packed_ref[pl.ds(part * 2, 2), :, LANES:].reshape(256, LANES)
            score = dot_nt(key, query) * SCALE
            prob = jnp.exp(jnp.where(col_ref[0, span, :] == mine, score - logsum, NEG))
            grad = prob * (dot_nt(value, back) - inner)
            grad = grad.astype(BF)
            dvalues[span, :] += dot(prob.astype(BF), back)
            dkeys[span, :] += dot(grad, query)
            return total + dot_tn(grad, key)

        total = lax.fori_loop(low, high, step, jnp.zeros((256, LANES), F32)) * SCALE
        moved_q = jnp.concatenate(
            [
                jnp.zeros((256, HEAD_DIM), F32),
                total[:, :HEAD_DIM],
                jnp.zeros((256, WIDE - 2 * HEAD_DIM), F32),
            ],
            axis=1,
        )
        out_ref[pl.ds(index * 2, 2)] = moved_q.astype(BF).reshape(2, 128, WIDE)
        return carry

    lax.fori_loop(0, 8, block, 0)
    wide = jnp.concatenate([dkeys[...] * SCALE, dvalues[...]], axis=1)
    lane = iota((ROW, WIDE), 1)
    old = out_ref[...].reshape(ROW, WIDE)
    inside = (lane >= HEAD_DIM) & (lane < 2 * HEAD_DIM)
    out_ref[...] = jnp.where(inside, old, wide.astype(BF)).reshape(16, 128, WIDE)


def attend_back(spans, packed, go, keep, row_ids, col_ids):
    return pl.pallas_call(
        attend_back_kernel,
        out_shape=jax.ShapeDtypeStruct((16, 256, WIDE), BF),
        grid_spec=pltpu.PrefetchScalarGridSpec(
            num_scalar_prefetch=1,
            grid=(2,),
            in_specs=[
                pl.BlockSpec((16, 128, WIDE), lambda m, s: (0, m, 0)),
                pl.BlockSpec((16, 128, LANES), lambda m, s: (0, m, 0)),
                pl.BlockSpec((1, ROW, LANES), lambda m, s: (m, 0, 0)),
                pl.BlockSpec((1, 1, ROW), lambda m, s: (m, 0, 0)),
                pl.BlockSpec((1, ROW, 1), lambda m, s: (m, 0, 0)),
            ],
            out_specs=pl.BlockSpec((16, 128, WIDE), lambda m, s: (0, m, 0)),
            scratch_shapes=[
                pltpu.VMEM((ROW, LANES), BF),
                pltpu.VMEM((ROW, LANES), BF),
                pltpu.VMEM((ROW, LANES), F32),
                pltpu.VMEM((ROW, LANES), F32),
            ],
        ),
        compiler_params=params(),
        name="attend_back",
    )(spans, packed, go, keep, row_ids, col_ids)


def head_place(head):
    spot = iota((LANES, D), 0) - VALUE_LANE
    inside = (spot >= 0) & (spot < HEAD_DIM)
    return onehot(inside & (origin(iota((LANES, D), 1)) == HEAD_DIM * head + spot))


def unmix(value):
    return onehot(origin(iota((D, LANES), 0)) == value * LANES + iota((D, LANES), 1))


def middle_kernel(
    o_ref,
    x_ref,
    g_ref,
    out_a_ref,
    out_b_ref,
    vec_ref,
    bias_ref,
    up_ref,
    down_ref,
    whole_ref,
    mixed_ref,
    do_ref,
    dmid_ref,
    gout_ref,
    gvec_ref,
    gbias_ref,
    gw_ref,
    o_perm,
    mid,
    h2,
    h2_t,
    g_t,
    result,
    dh2,
    packed,
    tail,
    gtail,
    gup,
    gdown,
    gpack,
    sems,
):
    step = pl.program_id(0)

    @pl.when(step == 0)
    def _():
        fetch = pltpu.make_async_copy(
            whole_ref.at[:, pl.ds(MLP_MAIN, MLP_CHUNK)], packed, sems.at[4]
        )
        fetch.start()
        mid[...] = jnp.zeros_like(mid)

        def gather_head(head, carry):
            mid[...] += dot(o_ref[head], head_place(head))
            return carry

        lax.fori_loop(0, HEADS, gather_head, 0)
        o_perm[...] = mid[...].astype(BF)
        for part in range(3):
            place = slice(384 * part, 384 * part + 384)
            value = dot(o_perm[:, :LEAD], out_a_ref[:, place])
            value = value + dot(o_perm[:, LEAD:], out_b_ref[:, place])
            mid[:, place] = x_ref[:, place].astype(F32) + value + vec_ref[2:3, place]
        unit, _ = normal(mid[...])
        h2[...] = (unit * vec_ref[0:1] + vec_ref[1:2]).astype(BF)
        h2_t[...] = jnp.transpose(h2[...])
        g_t[...] = jnp.transpose(g_ref[...])
        result[...] = jnp.zeros_like(result)
        dh2[...] = jnp.zeros_like(dh2)
        gtail[:, MLP_MAIN:] = jnp.zeros((TAIL, 8 * MLP_CHUNK - MLP_MAIN), BF)
        fetch.wait()

        def spread(chunk, carry):
            picked = dot(pick_rows(chunk, LEAD), packed[...])
            tail[:, lanes(chunk * MLP_CHUNK, MLP_CHUNK)] = picked.astype(BF)
            return carry

        lax.fori_loop(0, 8, spread, 0)

    up_place = lanes(step * STEP, STEP)
    down_place = lanes(FF_PAD + step * STEP, STEP)
    up = up_ref[...]
    down = down_ref[...]
    up_tail = tail[:, up_place]
    down_tail = tail[:, down_place]
    pre = dot(h2[:, :LEAD], up) + dot(h2[:, LEAD:], up_tail) + bias_ref[...]
    square = pre * pre
    bend = jnp.tanh(TANH_A * pre * (1.0 + TANH_B * square))
    half = 0.5 * (1.0 + bend)
    active = (pre * half).astype(BF)
    slope = half + 0.5 * pre * (1.0 - bend * bend) * (TANH_A * (1.0 + 3.0 * TANH_B * square))
    back = dot(g_ref[:, :LEAD], down) + dot(g_ref[:, LEAD:], down_tail)
    dpre32 = back * slope
    dpre = dpre32.astype(BF)
    result[:, :LEAD] += dot_nt(active, down)
    result[:, LEAD:] += dot_nt(active, down_tail)
    dh2[:, :LEAD] += dot_nt(dpre, up)
    dh2[:, LEAD:] += dot_nt(dpre, up_tail)
    gbias_ref[...] = column_total(dpre.astype(F32))
    slot = lax.rem(step, 2)

    def leave(index, buffer, place):
        return pltpu.make_async_copy(
            buffer.at[slot], gw_ref.at[:, place], sems.at[index * 2 + slot]
        )

    @pl.when(step >= 2)
    def _():
        leave(0, gup, up_place).wait()
        leave(1, gdown, down_place).wait()

    gup[slot] = dot(h2_t[:LEAD], dpre).astype(BF)
    gdown[slot] = dot(g_t[:LEAD], active).astype(BF)
    leave(0, gup, up_place).start()
    leave(1, gdown, down_place).start()
    gtail[:, up_place] = dot(h2_t[LEAD:], dpre).astype(BF)
    gtail[:, down_place] = dot(g_t[LEAD:], active).astype(BF)

    @pl.when(step == STEPS - 1)
    def _():
        other = 1 - slot
        for index, buffer in ((0, gup), (1, gdown)):
            for which in (slot, other):
                pltpu.make_async_copy(
                    buffer.at[which], gw_ref.at[:, up_place], sems.at[index * 2 + which]
                ).wait()
        gpack[:, MLP_CHUNK:] = jnp.zeros((LEAD, LANES), BF)

        def collect(part, carry):
            total = jnp.zeros((LEAD, 384), F32)
            for chunk in range(8):
                place = lanes(chunk * MLP_CHUNK + part * 384, 384)
                total = total + dot_tn(pick_rows(chunk, LEAD), gtail[:, place])
            gpack[:, lanes(part * 384, 384)] = total.astype(BF)
            return carry

        lax.fori_loop(0, 3, collect, 0)
        leave_pack = pltpu.make_async_copy(
            gpack, gw_ref.at[:, pl.ds(MLP_MAIN, MLP_TOTAL - MLP_MAIN)], sems.at[4]
        )
        leave_pack.start()
        gain = vec_ref[0:1]
        unit, rate = normal(mid[...])
        grad = dh2[...]
        gvec_ref[...] = jnp.zeros_like(gvec_ref)
        gvec_ref[0:1] = column_total(grad * unit)
        gvec_ref[1:2] = column_total(grad)
        gvec_ref[3:4] = column_total(g_ref[...].astype(F32))
        dmid = g_ref[...].astype(F32) + normal_back(unit, rate, gain, grad)
        dmid_ref[...] = dmid
        dlow = dmid.astype(BF)
        gvec_ref[2:3] = column_total(dlow.astype(F32))
        mixed = (mid[...] + result[...] + vec_ref[3:4]).astype(BF)
        h2[...] = mixed

        def restore(index, carry):
            mixed_ref[:, lanes(index * LANES, LANES)] = dot(h2[...], unmix(index)).astype(BF)
            return carry

        lax.fori_loop(0, 9, restore, 0)
        g_t[...] = jnp.transpose(o_perm[...])
        h2[...] = dlow

        def outer(index, carry):
            rows = pl.ds(index * LANES, LANES)
            gout_ref[rows, :] = dot(g_t[rows, :], h2[...]).astype(BF)
            return carry

        lax.fori_loop(0, 9, outer, 0)
        o_perm[:, :LEAD] = dot_nt(h2[...], out_a_ref[...]).astype(BF)
        o_perm[:, LEAD:] = dot_nt(h2[...], out_b_ref[...]).astype(BF)

        def split_head(head, carry):
            do_ref[head] = dot_nt(o_perm[...], head_place(head)).astype(BF)
            return carry

        lax.fori_loop(0, HEADS, split_head, 0)
        leave_pack.wait()


def middle(o, x, g, attn, attn_tail, vec, bias, mlp):
    def whole(*shape):
        return pl.BlockSpec(shape, lambda i: (0,) * len(shape))

    return pl.pallas_call(
        middle_kernel,
        grid=(STEPS,),
        out_shape=(
            jax.ShapeDtypeStruct((256, D), BF),
            jax.ShapeDtypeStruct((HEADS, 256, LANES), BF),
            jax.ShapeDtypeStruct((256, D), F32),
            jax.ShapeDtypeStruct((D, D), BF),
            jax.ShapeDtypeStruct((8, D), F32),
            jax.ShapeDtypeStruct((1, FF_PAD), F32),
            jax.ShapeDtypeStruct((LEAD, MLP_TOTAL), BF),
        ),
        in_specs=[
            whole(HEADS, 256, LANES),
            whole(256, D),
            whole(256, D),
            pl.BlockSpec((LEAD, D), lambda i: (0, 3)),
            pl.BlockSpec((TAIL, D), lambda i: (0, 3)),
            whole(8, D),
            pl.BlockSpec((1, STEP), lambda i: (0, i)),
            pl.BlockSpec((LEAD, STEP), lambda i: (0, i)),
            pl.BlockSpec((LEAD, STEP), lambda i: (0, STEPS + i)),
            pl.BlockSpec(memory_space=pl.ANY),
        ],
        out_specs=(
            whole(256, D),
            whole(HEADS, 256, LANES),
            whole(256, D),
            whole(D, D),
            whole(8, D),
            pl.BlockSpec((1, STEP), lambda i: (0, i)),
            pl.BlockSpec(memory_space=pl.ANY),
        ),
        scratch_shapes=[
            pltpu.VMEM((256, D), BF),
            pltpu.VMEM((256, D), F32),
            pltpu.VMEM((256, D), BF),
            pltpu.VMEM((D, 256), BF),
            pltpu.VMEM((D, 256), BF),
            pltpu.VMEM((256, D), F32),
            pltpu.VMEM((256, D), F32),
            pltpu.VMEM((LEAD, MLP_CHUNK), BF),
            pltpu.VMEM((TAIL, 8 * MLP_CHUNK), BF),
            pltpu.VMEM((TAIL, 8 * MLP_CHUNK), BF),
            pltpu.VMEM((2, LEAD, STEP), BF),
            pltpu.VMEM((2, LEAD, STEP), BF),
            pltpu.VMEM((LEAD, MLP_TOTAL - MLP_MAIN), BF),
            pltpu.SemaphoreType.DMA((5,)),
        ],
        compiler_params=params(),
        name="middle",
    )(o, x, g, attn, attn_tail, vec, bias, mlp, mlp, mlp)


def finish_kernel(
    dheads_ref,
    weight_ref,
    tail_ref,
    h_ref,
    x_ref,
    dmid_ref,
    gout_ref,
    vec_ref,
    tokens_ref,
    gvec_ref,
    gbias_ref,
    gw_ref,
    flat,
    h_t,
    gtail,
    dh,
):
    for head in range(HEADS):
        flat[:, PACK * head : PACK * head + PACK] = dheads_ref[head, :, :PACK]
    h_t[...] = jnp.transpose(h_ref[...])
    dh[...] = jnp.zeros_like(dh)
    gtail[:, QKV:ATTN_MAIN] = gout_ref[LEAD:, :]
    gtail[:, ATTN_MAIN:] = jnp.zeros((TAIL, 8 * ATTN_CHUNK - ATTN_MAIN), BF)
    gw_ref[:, QKV:ATTN_MAIN] = gout_ref[:LEAD, :]
    gw_ref[:, ATTN_MAIN + ATTN_CHUNK :] = jnp.zeros(
        (LEAD, ATTN_TOTAL - ATTN_MAIN - ATTN_CHUNK), BF
    )

    def columns(index, carry):
        place = lanes(index * 384, 384)
        value = flat[:, place]
        gbias_ref[:, place] = column_total(value.astype(F32))
        dh[:, :LEAD] += dot_nt(value, weight_ref[:, place])
        dh[:, LEAD:] += dot_nt(value, tail_ref[:, place])
        gw_ref[:, place] = dot(h_t[:LEAD], value).astype(BF)
        gtail[:, place] = dot(h_t[LEAD:], value).astype(BF)
        return carry

    lax.fori_loop(0, QKV // 384, columns, 0)

    def collect(part, carry):
        total = jnp.zeros((LEAD, LANES), F32)
        for chunk in range(8):
            place = lanes(chunk * ATTN_CHUNK + part * LANES, LANES)
            total = total + dot_tn(pick_rows(chunk, LEAD), gtail[:, place])
        gw_ref[:, lanes(ATTN_MAIN + part * LANES, LANES)] = total.astype(BF)
        return carry

    lax.fori_loop(0, ATTN_CHUNK // LANES, collect, 0)
    unit, rate = normal(x_ref[...].astype(F32))
    grad = dh[...]
    gvec_ref[...] = jnp.zeros_like(gvec_ref)
    gvec_ref[0:1] = column_total(grad * unit)
    gvec_ref[1:2] = column_total(grad)
    total = dmid_ref[...] + normal_back(unit, rate, vec_ref[0:1], grad)
    flat[:, :D] = total.astype(BF)

    def restore(index, carry):
        tokens_ref[:, lanes(index * LANES, LANES)] = dot(flat[:, :D], unmix(index)).astype(BF)
        return carry

    lax.fori_loop(0, 9, restore, 0)


def finish(dheads, weight, tail, h, x, dmid, gout, vec):
    return pl.pallas_call(
        finish_kernel,
        out_shape=(
            jax.ShapeDtypeStruct((256, D), BF),
            jax.ShapeDtypeStruct((8, D), F32),
            jax.ShapeDtypeStruct((1, QKV), F32),
            jax.ShapeDtypeStruct((LEAD, ATTN_TOTAL), BF),
        ),
        scratch_shapes=[
            pltpu.VMEM((256, QKV), BF),
            pltpu.VMEM((D, 256), BF),
            pltpu.VMEM((TAIL, 8 * ATTN_CHUNK), BF),
            pltpu.VMEM((256, D), F32),
        ],
        compiler_params=params(),
        name="finish",
    )(dheads, weight, tail, h, x, dmid, gout, vec)


def pack_slab(weight, chunk, total):
    width = weight.shape[1]
    rest = jnp.pad(weight[16:], ((0, 0), (0, 8 * chunk - width))).reshape(16, chunk)
    return jnp.concatenate(
        [weight[:16], rest, jnp.zeros((16, total - width - chunk), weight.dtype)], axis=1
    )


def unpack_slab(slab, width, chunk):
    rest = slab[:, width : width + chunk].reshape(2, 8 * chunk)[:, :width]
    return jnp.concatenate([slab[:, :width], rest], axis=0).astype(F32)


def by_head(key, query, value):
    rows = key.shape[0]
    parts = [item.reshape(rows, HEADS, 1, HEAD_DIM) for item in (key, query, value)]
    return jnp.concatenate(parts, axis=2).reshape(rows, QKV)


def from_heads(value):
    parts = value.reshape(value.shape[0], HEADS, 3, HEAD_DIM)
    return [parts[:, :, i].reshape(value.shape[0], D) for i in range(3)]


def mixing():
    return onehot(iota((D, D), 0) == origin(iota((D, D), 1)))


def mix_exact(value, back=False):
    matrix = mixing().astype(F32)
    if back:
        matrix = matrix.T
    return jnp.dot(value, matrix, precision=lax.Precision.HIGHEST)


def body(
    tokens,
    picture,
    cotangent,
    ln1_gain,
    ln1_bias,
    w_query,
    b_query,
    w_key,
    w_value,
    b_value,
    w_out,
    b_out,
    ln2_gain,
    ln2_bias,
    w_fc1,
    b_fc1,
    w_fc2,
    b_fc2,
):
    mix = mixing()
    out_cols = dot(w_out, mix).astype(BF)
    attn_slab = pack_slab(
        jnp.concatenate([by_head(w_key, w_query, w_value), out_cols], axis=1),
        ATTN_CHUNK,
        ATTN_TOTAL,
    )
    gap = ((0, 0), (0, FF_PAD - FF))
    mlp_slab = pack_slab(
        jnp.concatenate([jnp.pad(w_fc1, gap), jnp.pad(w_fc2.T, gap)], axis=1),
        MLP_CHUNK,
        MLP_TOTAL,
    )
    attn = gather_slab(attn_slab, 0)
    mlp = gather_slab(mlp_slab, 1)

    both = jnp.concatenate([tokens.reshape(256, D), cotangent.reshape(256, D)], axis=0)
    both = dot(both, mix).astype(BF)
    x, g = both[:256], both[256:]
    vec = mix_exact(jnp.stack([ln1_gain, ln1_bias, ln2_gain, ln2_bias, b_out, b_fc2]))
    vec1 = jnp.pad(vec[:2], ((0, 6), (0, 0)))
    vec2 = jnp.pad(vec[2:], ((0, 4), (0, 0)))
    bias = by_head(jnp.zeros((1, D), F32), b_query[None], b_value[None])

    group = lax.div(lax.axis_index("fsdp"), 8)
    ids = lax.dynamic_slice(picture, (0, group * ROW), (2, ROW))
    first = ids[:, 0::256]
    last = ids[:, 255::256]
    spot = jnp.arange(ROW, dtype=jnp.int32)[None, None, :]
    begin = jnp.min(jnp.where(ids[:, None, :] == first[:, :, None], spot, ROW), axis=2) // 256
    end = jnp.max(jnp.where(ids[:, None, :] == last[:, :, None], spot, -1), axis=2) // 256 + 1
    spans = jnp.concatenate([begin, end], axis=1).reshape(32).astype(jnp.int32)
    row_ids = ids[:, None, :]
    col_ids = ids[:, :, None]

    heads, h1, attn_tail = project_heads(x, attn, vec1, bias)
    packed = swap_heads(heads, 2)
    o, keep = attend(spans, packed, row_ids, col_ids)
    o = swap_heads(o, 3)
    mixed, go, dmid, gout, gvec2, gbias1, gmlp = middle(
        o, x, g, attn, attn_tail, vec2, jnp.pad(b_fc1, (0, FF_PAD - FF))[None], mlp
    )
    go = swap_heads(go, 4)
    dheads = attend_back(spans, packed, go, keep, row_ids, col_ids)
    dheads = swap_heads(dheads, 5)
    gtokens, gvec1, gbias, gattn = finish(dheads, attn, attn_tail, h1, x, dmid, gout, vec1)
    mlp_share = unpack_slab(reduce_slab(gmlp, 6), MLP_MAIN, MLP_CHUNK)
    attn_share = unpack_slab(reduce_slab(gattn, 7), ATTN_MAIN, ATTN_CHUNK)
    vectors, gbias, gbias1 = lax.psum(
        (jnp.concatenate([gvec1[:2], gvec2[:4]]), gbias, gbias1), ("fsdp", "rep")
    )
    vectors = mix_exact(vectors, True)
    grad_key, grad_query, grad_value = from_heads(attn_share[:, :QKV])
    _, bias_query, bias_value = from_heads(gbias)
    grad_out = mix_exact(attn_share[:, QKV:], True)
    grad_up = mlp_share[:, :FF]
    grad_down = mlp_share[:, FF_PAD : FF_PAD + FF].T
    return (
        mixed.reshape(2, 128, D),
        gtokens.reshape(2, 128, D),
        vectors[0],
        vectors[1],
        grad_query,
        bias_query[0],
        grad_key,
        grad_value,
        bias_value[0],
        grad_out,
        vectors[4],
        vectors[2],
        vectors[3],
        grad_up,
        gbias1[0, :FF],
        grad_down,
        vectors[5],
    )


def solution(mesh):
    placed = (
        P(None, ("fsdp", "rep"), None),
        P(),
        P(None, ("fsdp", "rep"), None),
        P(),
        P(),
        P("fsdp", None),
        P(),
        P("fsdp", None),
        P("fsdp", None),
        P(),
        P("fsdp", None),
        P(),
        P(),
        P(),
        P("fsdp", None),
        P(),
        P(None, "fsdp"),
        P(),
    )
    return jax.shard_map(
        body,
        mesh=mesh,
        in_specs=placed,
        out_specs=(
            P(None, ("fsdp", "rep"), None),
            P(None, ("fsdp", "rep"), None),
            P(),
            P(),
            P("fsdp", None),
            P(),
            P("fsdp", None),
            P("fsdp", None),
            P(),
            P("fsdp", None),
            P(),
            P(),
            P(),
            P("fsdp", None),
            P(),
            P(None, "fsdp"),
            P(),
        ),
        check_vma=False,
    )
```

```python
import functools

import jax
import jax.numpy as jnp
import numpy as np
from jax import lax
from jax.experimental import pallas as pl
from jax.experimental.pallas import tpu as pltpu
from jax.sharding import PartitionSpec as P

MESH = pl.DeviceIdType.MESH
BF = jnp.bfloat16
F32 = jnp.float32
LANES = 128
ORDERS = (("x", "y", "z"), ("y", "z", "x"), ("z", "x", "y"))
AXES = ("x", "y", "z")


def here():
    shard = lax.axis_index("fsdp")
    low = lax.axis_index("rep")
    place = {
        "x": lax.div(shard, 16),
        "y": lax.rem(lax.div(shard, 8), 2) * 2 + low,
        "z": lax.rem(lax.div(shard, 2), 4),
    }
    return place, lax.rem(shard, 2)


def moved(place, axis, steps):
    steps = steps % 4
    if steps == 0:
        return place
    other = dict(place)
    other[axis] = lax.rem(place[axis] + steps, 4)
    return other


def device_at(place, core):
    high = lax.div(place["y"], 2)
    return (((place["x"] * 2 + high) * 4 + place["z"]) * 2 + core, lax.rem(place["y"], 2))


def greet(peers):
    barrier = pltpu.get_barrier_semaphore()
    for peer in peers:
        pl.semaphore_signal(barrier, inc=1, device_id=peer, device_id_type=MESH)
    pl.semaphore_wait(barrier, len(peers))


def torus_peers(place, core):
    peers = [device_at(place, 1 - core)]
    for axis in AXES:
        for steps in (1, 2, 3):
            peers.append(device_at(moved(place, axis, steps), core))
    return peers


def part_columns(part, half, width):
    return pl.ds(pl.multiple_of(part * 2 * width + half * width, LANES), width)


def piece_of(ref, part, width, place, core):
    return ref.at[
        place["x"],
        lax.div(place["y"], 2),
        place["z"],
        core,
        :,
        part_columns(part, lax.rem(place["y"], 2), width),
    ]


def block_of(ref, part, width, place, core, axis, half=None):
    where = {"x": place["x"], "y": lax.div(place["y"], 2), "z": place["z"]}
    if axis == "y":
        where["y"] = pl.ds(0, 2) if half is None else pl.ds(half, 1)
        columns = pl.ds(part * 2 * width, 2 * width)
    else:
        where[axis] = pl.ds(0, 4) if half is None else pl.ds(2 * half, 2)
        columns = part_columns(part, lax.rem(place["y"], 2), width)
    return ref.at[where["x"], where["y"], where["z"], core, :, columns]


GATHER_SEMS = 3 + 3 + 8 + 8 + 16


def gather_kernel(width, own, full, send, recv, local):
    place, core = here()
    greet(torus_peers(place, core))
    twin = device_at(place, 1 - core)
    started = []

    def sem_index(part, kind, index):
        return part * GATHER_SEMS + {"a": 0, "b": 3, "c": 6, "d": 14, "s": 22}[kind] + index

    def push(source, target, slot, device):
        copy = pltpu.make_async_remote_copy(
            src_ref=source,
            dst_ref=target,
            send_sem=send.at[slot],
            recv_sem=recv.at[slot],
            device_id=device,
            device_id_type=MESH,
        )
        copy.start()
        started.append(copy)

    def arrived(region, slot):
        pltpu.make_async_remote_copy(
            src_ref=region,
            dst_ref=region,
            send_sem=send.at[slot],
            recv_sem=recv.at[slot],
            device_id=twin,
            device_id_type=MESH,
        ).wait_recv()

    low = lax.rem(place["y"], 2)
    locals_ = []
    for part, (one, two, three) in enumerate(ORDERS):
        source = own.at[:, part_columns(part, low, width)]
        target = piece_of(full, part, width, place, core)
        copy = pltpu.make_async_copy(source, target, local.at[part])
        copy.start()
        locals_.append(copy)
        for steps in (1, 3, 2):
            push(
                source,
                target,
                sem_index(part, "a", steps - 1),
                device_at(moved(place, one, steps), core),
            )
    for part, (one, two, three) in enumerate(ORDERS):
        locals_[part].wait()
        for steps in (1, 3, 2):
            arrived(
                piece_of(full, part, width, moved(place, one, -steps), core),
                sem_index(part, "a", steps - 1),
            )
        block = block_of(full, part, width, place, core, one)
        for steps in (1, 3, 2):
            push(block, block, sem_index(part, "b", steps - 1), device_at(moved(place, two, steps), core))
        for way in (1, 3):
            push(block, block, sem_index(part, "c", (way // 2) * 4), device_at(moved(place, three, way), core))
        push(block, block, sem_index(part, "s", 0), twin)
    for steps in (1, 3, 2):
        for part, (one, two, three) in enumerate(ORDERS):
            block = block_of(full, part, width, moved(place, two, -steps), core, one)
            arrived(block, sem_index(part, "b", steps - 1))
            for way in (1, 3):
                push(
                    block,
                    block,
                    sem_index(part, "c", (way // 2) * 4 + steps),
                    device_at(moved(place, three, way), core),
                )
            push(block, block, sem_index(part, "s", steps), twin)
    for steps in (0, 1, 3, 2):
        for part, (one, two, three) in enumerate(ORDERS):
            for way in (1, 3):
                origin = moved(moved(place, two, -steps), three, -way)
                block = block_of(full, part, width, origin, core, one)
                arrived(block, sem_index(part, "c", (way // 2) * 4 + steps))
                piece = block_of(full, part, width, origin, core, one, way // 2)
                push(
                    piece,
                    piece,
                    sem_index(part, "d", (way // 2) * 4 + steps),
                    device_at(moved(place, three, way), core),
                )
                push(block, block, sem_index(part, "s", way * 4 + steps), twin)
    for steps in (0, 1, 3, 2):
        for part, (one, two, three) in enumerate(ORDERS):
            origin = moved(moved(place, two, -steps), three, 2)
            for way in (1, 3):
                arrived(
                    block_of(full, part, width, origin, core, one, way // 2),
                    sem_index(part, "d", (way // 2) * 4 + steps),
                )
            block = block_of(full, part, width, origin, core, one)
            push(block, block, sem_index(part, "s", 8 + steps), twin)
    for part, (one, two, three) in enumerate(ORDERS):
        for way in range(4):
            for steps in range(4):
                origin = moved(moved(place, two, -steps), three, -way)
                arrived(
                    block_of(full, part, width, origin, 1 - core, one),
                    sem_index(part, "s", way * 4 + steps),
                )
    for copy in started:
        copy.wait_send()


def gather_slab(slab, tag):
    total = slab.shape[1]
    width = total // 6
    full = pl.pallas_call(
        functools.partial(gather_kernel, width),
        out_shape=jax.ShapeDtypeStruct((4, 2, 4, 2, 16, total), slab.dtype),
        in_specs=[pl.BlockSpec(memory_space=pl.ANY)],
        out_specs=pl.BlockSpec(memory_space=pl.ANY),
        scratch_shapes=[
            pltpu.SemaphoreType.DMA((3 * GATHER_SEMS,)),
            pltpu.SemaphoreType.DMA((3 * GATHER_SEMS,)),
            pltpu.SemaphoreType.DMA((3,)),
        ],
        compiler_params=pltpu.CompilerParams(collective_id=tag, has_side_effects=True),
        name="gather_slab",
    )(slab)
    return full.reshape(1024, total)


def swap_kernel(own, full, send, recv, local):
    place, core = here()
    low = lax.rem(place["y"], 2)
    mine = (place["z"] * 2 + core) * 2 + low
    base = lax.div(lax.axis_index("fsdp"), 8) * 8

    def peer(index):
        return (base + lax.div(index, 2), lax.rem(index, 2))

    def partner(k):
        zz = lax.rem(place["z"] + k // 4, 4)
        cc = lax.rem(core + (k // 2) % 2, 2)
        ll = lax.rem(low + k % 2, 2)
        return (zz * 2 + cc) * 2 + ll

    def source(k):
        zz = lax.rem(place["z"] + 4 - k // 4, 4)
        cc = lax.rem(core + (k // 2) % 2, 2)
        ll = lax.rem(low + k % 2, 2)
        return (zz * 2 + cc) * 2 + ll

    greet([peer(partner(k)) for k in range(1, 16)])
    keep = pltpu.make_async_copy(own.at[mine], full.at[mine], local.at[0])
    keep.start()
    copies = []
    for k in (9, 11, 5, 13, 7, 15, 1, 3, 8, 10, 4, 12, 6, 14, 2):
        target = partner(k)
        copy = pltpu.make_async_remote_copy(
            src_ref=own.at[target],
            dst_ref=full.at[mine],
            send_sem=send.at[k],
            recv_sem=recv.at[k],
            device_id=peer(target),
            device_id_type=MESH,
        )
        copy.start()
        copies.append(copy)
    for k in range(1, 16):
        region = full.at[source(k)]
        pltpu.make_async_remote_copy(
            src_ref=region,
            dst_ref=region,
            send_sem=send.at[k],
            recv_sem=recv.at[k],
            device_id=peer(partner(k)),
            device_id_type=MESH,
        ).wait_recv()
    keep.wait()
    for copy in copies:
        copy.wait_send()


def swap_heads(blocks, tag):
    return pl.pallas_call(
        swap_kernel,
        out_shape=jax.ShapeDtypeStruct(blocks.shape, blocks.dtype),
        in_specs=[pl.BlockSpec(memory_space=pl.ANY)],
        out_specs=pl.BlockSpec(memory_space=pl.ANY),
        scratch_shapes=[
            pltpu.SemaphoreType.DMA((16,)),
            pltpu.SemaphoreType.DMA((16,)),
            pltpu.SemaphoreType.DMA((1,)),
        ],
        compiler_params=pltpu.CompilerParams(collective_id=tag, has_side_effects=True),
        name="swap_heads",
    )(blocks)


def remote(source, target, send, recv, device):
    return pltpu.make_async_remote_copy(
        src_ref=source,
        dst_ref=target,
        send_sem=send,
        recv_sem=recv,
        device_id=device,
        device_id_type=MESH,
    )


def cycle(value, steps):
    return lax.rem(value + steps, 4)


class Reducer:
    SEMS = 8 + 8 + 3 + 3 + 1
    KINDS = {"mid": 0, "far": 8, "side": 16, "line": 19, "done": 22}

    def __init__(self, width, place, core, buffers, out, send, recv):
        self.width, self.place, self.core = width, place, core
        self.acc, self.mid, self.far, self.side, self.line, self.done = [
            buffers[3 * i : 3 * i + 3] for i in range(6)
        ]
        self.out, self.send, self.recv = out, send, recv
        self.me = device_at(place, core)

    @staticmethod
    def scratch(width):
        found = []
        for lead, half in (((4, 4), 1), ((2, 4), 2), ((2, 4), 1), ((3,), 1)):
            for one, two, three in ORDERS:
                if one == "y":
                    found.append(pltpu.VMEM(lead + (2 // half, 16, 2 * width), BF))
                else:
                    found.append(pltpu.VMEM(lead + (4 // half, 16, width), BF))
        found += [pltpu.VMEM((3, 16, width), BF)] * 3
        found += [pltpu.VMEM((16, width), BF)] * 3
        return found

    def slot(self, part, kind, index):
        return part * self.SEMS + self.KINDS[kind] + index

    def push(self, source, target, slot, device):
        remote(source, target, self.send.at[slot], self.recv.at[slot], device).start()

    def arrived(self, region, slot):
        remote(region, region, self.send.at[slot], self.recv.at[slot], self.me).wait_recv()

    def sent(self, region, slot):
        remote(region, region, self.send.at[slot], self.recv.at[slot], self.me).wait_send()

    def add(self, target, *terms):
        for index in range(target.shape[0]):
            total = target[index].astype(F32)
            for term in terms:
                total = total + term[index].astype(F32)
            target[index] = total.astype(BF)

    def half_of(self, ref, half):
        size = ref.shape[0] // 2
        return ref.at[pl.ds(half * size, size)]

    def far_out(self):
        for spot in range(4):
            for part, (one, two, three) in enumerate(ORDERS):
                for half, way in ((0, 3), (1, 1)):
                    self.push(
                        self.half_of(self.acc[part].at[2, spot], half),
                        self.mid[part].at[half, spot],
                        self.slot(part, "mid", half * 4 + spot),
                        device_at(moved(self.place, three, way), self.core),
                    )

    def pass_on(self, spot):
        for part, (one, two, three) in enumerate(ORDERS):
            for half, way in ((0, 3), (1, 1)):
                self.arrived(
                    self.mid[part].at[half, spot], self.slot(part, "mid", half * 4 + spot)
                )
                self.add(
                    self.half_of(self.acc[part].at[way, spot], half), self.mid[part].at[half, spot]
                )
                self.push(
                    self.acc[part].at[way, spot],
                    self.far[part].at[half, spot],
                    self.slot(part, "far", half * 4 + spot),
                    device_at(moved(self.place, three, way), self.core),
                )

    def gather_side(self, over, last):
        for part, (one, two, three) in enumerate(ORDERS):
            spot = cycle(self.place[two], over)
            for half in range(2):
                self.arrived(
                    self.far[part].at[half, spot], self.slot(part, "far", half * 4 + spot)
                )
            self.add(
                self.acc[part].at[0, spot], self.far[part].at[0, spot], self.far[part].at[1, spot]
            )

            def give(part=part, two=two, spot=spot):
                other = dict(self.place)
                other[two] = spot
                self.push(
                    self.acc[part].at[0, spot],
                    self.side[part].at[over - 1],
                    self.slot(part, "side", over - 1),
                    device_at(other, self.core),
                )

            if last is False:
                give()
            elif last is not True:
                pl.when(jnp.logical_not(last))(give)

    def piece(self, part, axis, spot):
        own = self.acc[part].at[0, self.place[ORDERS[part][1]]]
        if axis == "y":
            start = pl.multiple_of(lax.rem(spot["y"], 2) * self.width, LANES)
            return own.at[lax.div(spot["y"], 2), :, pl.ds(start, self.width)]
        return own.at[spot[axis]]

    def line_up(self):
        for part, (one, two, three) in enumerate(ORDERS):
            for over in range(3):
                self.arrived(self.side[part].at[over], self.slot(part, "side", over))
            own = self.acc[part].at[0, self.place[two]]
            self.add(own, self.side[part].at[0], self.side[part].at[1], self.side[part].at[2])
            for over in (2, 1, 3):
                spot = moved(self.place, one, over)
                self.push(
                    self.piece(part, one, spot),
                    self.line[part].at[over - 1],
                    self.slot(part, "line", over - 1),
                    device_at(spot, self.core),
                )

    def share(self):
        low = lax.rem(self.place["y"], 2)
        partner = (lax.axis_index("fsdp"), 1 - low)
        for part, (one, two, three) in enumerate(ORDERS):
            for over in range(3):
                self.arrived(self.line[part].at[over], self.slot(part, "line", over))
            total = self.piece(part, one, self.place)[...].astype(F32)
            for over in range(3):
                total = total + self.line[part][over].astype(F32)
            self.done[part][...] = total.astype(BF)
            columns = part_columns(part, low, self.width)
            self.push(
                self.done[part], self.out.at[:, columns], self.slot(part, "done", 0), partner
            )
            self.out[:, columns] = self.done[part][...]

    def close(self):
        low = lax.rem(self.place["y"], 2)
        for part, (one, two, three) in enumerate(ORDERS):
            self.arrived(
                self.out.at[:, part_columns(part, 1 - low, self.width)],
                self.slot(part, "done", 0),
            )
            for half in range(2):
                for spot in range(4):
                    index = half * 4 + spot
                    self.sent(self.mid[part].at[half, spot], self.slot(part, "mid", index))
                    self.sent(self.far[part].at[half, spot], self.slot(part, "far", index))
            for over in range(3):
                self.sent(self.side[part].at[over], self.slot(part, "side", over))
                self.sent(self.line[part].at[over], self.slot(part, "line", over))
            self.sent(self.done[part], self.slot(part, "done", 0))


class Maker:
    def __init__(self, reducer, sources, extra, chunk):
        self.red, self.sources, self.extra, self.chunk = reducer, sources, extra, chunk
        self.main = sum(item[1].shape[1] for item in sources)

    def pack_tail(self):
        start = 0
        pieces = []
        for turned, right in self.sources:
            pieces.append((start, start + right.shape[1], turned, right))
            start += right.shape[1]
        for index in range(8):
            low, high = index * self.chunk, (index + 1) * self.chunk
            for first, last, turned, right in pieces:
                a, b = max(low, first), min(high, last)
                if a < b:
                    value = dot(turned[1][...], right[:, a - first : b - first])
                    self.scatter(index, a - low, value)
            if high > self.main:
                a = max(low, self.main)
                self.scatter(index, a - low, jnp.zeros((TAIL, high - a), F32))

    def scatter(self, index, start, value):
        for tile in range(value.shape[1] // LANES):
            self.extra[start // LANES + tile, pl.ds(index, TAIL, stride=8), :] = value[
                :, tile * LANES : (tile + 1) * LANES
            ]

    def rows(self, ref, part, ahead):
        place, core = self.red.place, self.red.core
        three = ORDERS[part][2]
        spot = cycle(place[three], ahead)
        if len(ref.shape) == 2:
            if three == "z":
                groups = [outer * 8 + spot * 2 + core for outer in range(8)]
            elif three == "x":
                groups = [spot * 16 + inner * 2 + core for inner in range(8)]
            else:
                high = lax.div(spot, 2) * 8
                groups = [x * 16 + high + z * 2 + core for x in range(4) for z in range(4)]
            found = [ref[pl.ds(pl.multiple_of(group * 16, 16), 16)] for group in groups]
            return jnp.concatenate(found, axis=0)
        if three == "z":
            value = ref[:, :, spot, core]
        elif three == "x":
            value = ref[spot, :, :, core]
        else:
            value = ref[:, lax.div(spot, 2), :, core]
        return value.reshape(-1, ref.shape[-1])

    def columns(self, part, half, ahead):
        width = self.red.width
        low = (2 * part + half) * width
        high = low + width
        first = 0
        found = []
        for turned, right in self.sources:
            last = first + right.shape[1]
            a, b = max(low, first), min(high, last)
            if a < b:
                left = self.rows(turned[0], part, ahead)
                found.append(dot(left, right[:, a - first : b - first]).astype(BF))
            first = last
        a, b = max(low, first), min(high, first + self.chunk)
        if a < b:
            for tile in range((a - first) // LANES, (b - first) // LANES):
                found.append(self.rows(self.extra.at[tile], part, ahead).astype(BF))
        a = max(low, first + self.chunk)
        if a < high:
            found.append(jnp.zeros((found[0].shape[0], high - a), BF))
        return found[0] if len(found) == 1 else jnp.concatenate(found, axis=1)

    def make(self, part, ahead):
        red, width = self.red, self.red.width
        acc = red.acc[part]
        three = ORDERS[part][2]
        if three == "z":
            for half in range(2):
                value = self.columns(part, half, ahead).reshape(4, 2, 16, width)
                for high in range(2):
                    acc[ahead, 2 * high + half] = value[:, high]
        elif three == "x":
            for half in range(2):
                value = self.columns(part, half, ahead).reshape(2, 4, 16, width)
                for spot in range(4):
                    acc[ahead, spot, :, :, half * width : (half + 1) * width] = value[:, spot]
        else:
            low = lax.rem(cycle(red.place["y"], ahead), 2)
            for half in range(2):

                @pl.when(low == half)
                def _(half=half):
                    value = self.columns(part, half, ahead).reshape(4, 4, 16, width)
                    for spot in range(4):
                        acc[ahead, spot] = value[spot]


SWAP_ORDER = (9, 11, 5, 13, 7, 15, 1, 3, 8, 10, 4, 12, 6, 14, 2)


class Swapper:
    def __init__(self, place, core, own, full, send, recv, base):
        self.place, self.core = place, core
        self.own, self.full, self.send, self.recv, self.base = own, full, send, recv, base
        self.low = lax.rem(place["y"], 2)
        self.mine = (place["z"] * 2 + core) * 2 + self.low
        self.group = lax.div(lax.axis_index("fsdp"), 8) * 8

    def member(self, k, sign=1):
        z = lax.rem(self.place["z"] + (4 + sign * (k // 4)), 4)
        core = lax.rem(self.core + (k // 2) % 2, 2)
        low = lax.rem(self.low + k % 2, 2)
        return (z * 2 + core) * 2 + low

    def device(self, index):
        return (self.group + lax.div(index, 2), lax.rem(index, 2))

    def peers(self):
        return [self.device(self.member(k)) for k in range(1, 16)]

    def view(self, ref, index, micro):
        if micro is None:
            return ref.at[index]
        return ref.at[index, pl.ds(micro * 128, 128)]

    def start(self, micro=None):
        for k in SWAP_ORDER:
            target = self.member(k)
            remote(
                self.view(self.own, target, micro),
                self.view(self.full, self.mine, micro),
                self.send.at[self.base + k],
                self.recv.at[self.base + k],
                self.device(target),
            ).start()
        pltpu.make_async_copy(
            self.view(self.own, self.mine, micro),
            self.view(self.full, self.mine, micro),
            self.send.at[self.base],
        ).start()

    def finish(self, micro=None):
        pltpu.make_async_copy(
            self.view(self.own, self.mine, micro),
            self.view(self.full, self.mine, micro),
            self.send.at[self.base],
        ).wait()
        for k in range(1, 16):
            region = self.view(self.full, self.member(k, -1), micro)
            remote(
                region,
                region,
                self.send.at[self.base + k],
                self.recv.at[self.base + k],
                self.device(self.mine),
            ).wait_recv()

    def drain(self, micro=None):
        for k in range(1, 16):
            region = self.view(self.own, self.member(k), micro)
            remote(
                region,
                region,
                self.send.at[self.base + k],
                self.recv.at[self.base + k],
                self.device(self.mine),
            ).wait_send()


def union(*lists):
    return [peer for peers in lists for peer in peers]


def line_peers(place, core):
    peers = []
    for axis in AXES:
        for steps in (1, 2, 3):
            peers.append(device_at(moved(place, axis, steps), core))
    return peers


D = 1152
HEADS = 16
HEAD_DIM = 72
FF = 4304
ROW = 2048
EPS = 1e-06
NEG = -1e30
SCALE = HEAD_DIM**-0.5
LEAD = 1024
TAIL = 128
PACK = 3 * HEAD_DIM
WIDE = 256
VALUE_LANE = 16
FF_PAD = 4352
STEP = 256
STEPS = FF_PAD // STEP
QKV = HEADS * PACK
ATTN_MAIN = QKV + D
ATTN_CHUNK = 640
ATTN_TOTAL = 5376
MLP_MAIN = 2 * FF_PAD
MLP_CHUNK = 1152
MLP_TOTAL = 9984
LOG2E = 1.4426950408889634
QUERIES = 512
KEYS = 512
BLOCKS = ROW // QUERIES
TANH_A = 0.7978845608028654
TANH_B = 0.044715


def dot(left, right):
    return jnp.dot(left, right, preferred_element_type=F32)


def dot_nt(left, right):
    return lax.dot_general(left, right, (((1,), (1,)), ((), ())), preferred_element_type=F32)


def dot_tn(left, right):
    return lax.dot_general(left, right, (((0,), (0,)), ((), ())), preferred_element_type=F32)


def origin(index):
    lead = (index >> 4) * 18 + (index & 15)
    rest = index - LEAD
    tail = (rest >> 1) * 18 + 16 + (rest & 1)
    return jnp.where(index < LEAD, lead, tail)


def iota(shape, axis):
    return lax.broadcasted_iota(jnp.int32, shape, axis)


def onehot(mask):
    return mask.astype(F32).astype(BF)


def normal(values):
    center = values - jnp.mean(values, axis=-1, keepdims=True)
    rate = lax.rsqrt(jnp.mean(center * center, axis=-1, keepdims=True) + EPS)
    return center * rate, rate


def normal_back(unit, rate, gain, grad):
    inner = grad * gain
    first = jnp.mean(inner, axis=-1, keepdims=True)
    second = jnp.mean(inner * unit, axis=-1, keepdims=True)
    return rate * (inner - first - unit * second)


def column_total(values):
    return jnp.sum(values, axis=0, keepdims=True)


def lanes(start, size):
    return pl.ds(pl.multiple_of(start, LANES), size)


def params(limit=60):
    return pltpu.CompilerParams(vmem_limit_bytes=limit << 20)


def project_kernel(x_ref, weight_ref, vec_ref, bias_ref, heads_ref, h_ref, tail_ref, flat, wide):
    unit, _ = normal(x_ref[...].astype(F32))
    h_ref[...] = (unit * vec_ref[0:1] + vec_ref[1:2]).astype(BF)
    for tile in range(ATTN_CHUNK // LANES):
        start = ATTN_MAIN + tile * LANES
        wide[tile] = weight_ref[:, start : start + LANES].astype(F32)
        for chunk in range(8):
            start = chunk * ATTN_CHUNK + tile * LANES
            picked = wide[tile, pl.ds(chunk, TAIL, stride=8), :]
            tail_ref[:, start : start + LANES] = picked.astype(BF)

    def columns(index, carry):
        place = lanes(index * 384, 384)
        value = dot(h_ref[:, :LEAD], weight_ref[:, place]) + dot(h_ref[:, LEAD:], tail_ref[:, place])
        flat[:, place] = (value + bias_ref[:, place]).astype(BF)
        return carry

    lax.fori_loop(0, QKV // 384, columns, 0)
    for head in range(HEADS):
        block = flat[:, PACK * head : PACK * head + PACK]
        heads_ref[head] = jnp.concatenate([block, jnp.zeros((256, WIDE - PACK), BF)], axis=1)


def project_heads(x, weight, vec, bias):
    return pl.pallas_call(
        project_kernel,
        out_shape=(
            jax.ShapeDtypeStruct((HEADS, 256, WIDE), BF),
            jax.ShapeDtypeStruct((256, D), BF),
            jax.ShapeDtypeStruct((TAIL, 8 * ATTN_CHUNK), BF),
        ),
        scratch_shapes=[pltpu.VMEM((256, QKV), BF), pltpu.VMEM((ATTN_CHUNK // LANES, LEAD, LANES), F32)],
        compiler_params=params(),
        name="project_heads",
    )(x, weight, vec, bias)


def attend_kernel(packed_ref, row_ref, col_ref, o_ref, keep_ref, keys, queries, values, scores):
    packed = packed_ref[...].reshape(ROW, WIDE)
    lane = iota((ROW, LANES), 1)
    zero = jnp.zeros((ROW, LANES), BF)
    keys[...] = jnp.where(lane < HEAD_DIM, packed[:, :LANES], zero)
    queries[...] = jnp.concatenate(
        [packed[:, HEAD_DIM : 2 * HEAD_DIM], jnp.zeros((ROW, LANES - HEAD_DIM), BF)], axis=1
    )
    values[...] = jnp.where(lane == LANES - 1, jnp.ones((ROW, LANES), BF), packed[:, LANES:])

    def block(index, carry):
        rows = pl.ds(index * 256, 256)
        query = queries[rows, :]
        mine = col_ref[0, rows, :]
        top = jnp.full((256, LANES), NEG, F32)
        for part in range(ROW // KEYS):
            span = slice(part * KEYS, (part + 1) * KEYS)
            score = dot_nt(query, keys[span, :])
            score = jnp.where(mine == row_ref[0, :, span], score, NEG)
            scores[:, span] = score
            for lane_block in range(KEYS // LANES):
                top = jnp.maximum(top, score[:, lane_block * LANES : (lane_block + 1) * LANES])
        top = jnp.max(top, axis=1, keepdims=True)
        total = jnp.zeros((256, LANES), F32)
        for part in range(ROW // KEYS):
            span = slice(part * KEYS, (part + 1) * KEYS)
            expo = jnp.exp2((scores[:, span] - top) * (SCALE * LOG2E))
            total = total + dot(expo.astype(BF), values[span, :])
        mass = total[:, LANES - 1 :]
        total = total / mass
        o_ref[pl.ds(index * 2, 2)] = total.astype(BF).reshape(2, 128, LANES)
        lane = iota((256, LANES), 1)
        logsum = top * (SCALE * LOG2E) + jnp.log2(mass)
        keep_ref[0, rows, :] = jnp.where(lane == 0, logsum, total)
        return carry

    lax.fori_loop(0, 8, block, 0)


def attend(packed, row_ids, col_ids):
    return pl.pallas_call(
        attend_kernel,
        out_shape=(
            jax.ShapeDtypeStruct((16, 256, LANES), BF),
            jax.ShapeDtypeStruct((2, ROW, LANES), F32),
        ),
        grid=(2,),
        in_specs=[
            pl.BlockSpec((16, 128, WIDE), lambda m: (0, m, 0)),
            pl.BlockSpec((1, 1, ROW), lambda m: (m, 0, 0)),
            pl.BlockSpec((1, ROW, 1), lambda m: (m, 0, 0)),
        ],
        out_specs=(
            pl.BlockSpec((16, 128, LANES), lambda m: (0, m, 0)),
            pl.BlockSpec((1, ROW, LANES), lambda m: (m, 0, 0)),
        ),
        scratch_shapes=[pltpu.VMEM((ROW, LANES), BF)] * 3 + [pltpu.VMEM((256, ROW), F32)],
        compiler_params=params(),
        name="attend",
    )(packed, row_ids, col_ids)


def head_place(head):
    spot = iota((LANES, D), 0) - VALUE_LANE
    inside = (spot >= 0) & (spot < HEAD_DIM)
    return onehot(inside & (origin(iota((LANES, D), 1)) == HEAD_DIM * head + spot))


def unmix(value):
    return onehot(origin(iota((D, LANES), 0)) == value * LANES + iota((D, LANES), 1))


def middle_kernel(
    o_ref,
    x_ref,
    g_ref,
    out_a_ref,
    out_b_ref,
    vec_ref,
    bias_ref,
    up_ref,
    down_ref,
    whole_ref,
    mixed_ref,
    do_ref,
    dmid_ref,
    dy_ref,
    gvec_ref,
    gbias_ref,
    dpre_ref,
    active_ref,
    h_main_ref,
    h_tail_ref,
    g_main_ref,
    g_tail_ref,
    o_main_ref,
    o_tail_ref,
    o_perm,
    mid,
    h2,
    result,
    dh2,
    packed,
    wide,
    tail,
    sem,
):
    step = pl.program_id(0)

    def turn(value, main, rest):
        turned = jnp.transpose(value)
        main[...] = turned[:LEAD]
        rest[...] = turned[LEAD:]

    @pl.when(step == 0)
    def _():
        fetch = pltpu.make_async_copy(whole_ref.at[:, pl.ds(MLP_MAIN, MLP_CHUNK)], packed, sem.at[0])
        fetch.start()
        mid[...] = jnp.zeros_like(mid)

        def gather_head(head, carry):
            mid[...] += dot(o_ref[head], head_place(head))
            return carry

        lax.fori_loop(0, HEADS, gather_head, 0)
        o_perm[...] = mid[...].astype(BF)
        for part in range(3):
            place = slice(384 * part, 384 * part + 384)
            value = dot(o_perm[:, :LEAD], out_a_ref[:, place])
            value = value + dot(o_perm[:, LEAD:], out_b_ref[:, place])
            mid[:, place] = x_ref[:, place].astype(F32) + value + vec_ref[2:3, place]
        unit, _ = normal(mid[...])
        h2[...] = (unit * vec_ref[0:1] + vec_ref[1:2]).astype(BF)
        turn(o_perm[...], o_main_ref, o_tail_ref)
        turn(h2[...], h_main_ref, h_tail_ref)
        turn(g_ref[...], g_main_ref, g_tail_ref)
        result[...] = jnp.zeros_like(result)
        dh2[...] = jnp.zeros_like(dh2)
        fetch.wait()
        for tile in range(MLP_CHUNK // LANES):
            wide[tile] = packed[:, tile * LANES : (tile + 1) * LANES].astype(F32)
            for chunk in range(8):
                start = chunk * MLP_CHUNK + tile * LANES
                picked = wide[tile, pl.ds(chunk, TAIL, stride=8), :]
                tail[:, start : start + LANES] = picked.astype(BF)

    up = up_ref[...]
    down = down_ref[...]
    up_tail = tail[:, lanes(step * STEP, STEP)]
    down_tail = tail[:, lanes(FF_PAD + step * STEP, STEP)]
    pre = dot(h2[:, :LEAD], up) + dot(h2[:, LEAD:], up_tail) + bias_ref[...]
    square = pre * pre
    bend = jnp.tanh(TANH_A * pre * (1.0 + TANH_B * square))
    half = 0.5 * (1.0 + bend)
    active = (pre * half).astype(BF)
    slope = half + 0.5 * pre * (1.0 - bend * bend) * (TANH_A * (1.0 + 3.0 * TANH_B * square))
    back = dot(g_ref[:, :LEAD], down) + dot(g_ref[:, LEAD:], down_tail)
    dpre = (back * slope).astype(BF)
    active_ref[...] = active
    dpre_ref[...] = dpre
    result[:, :LEAD] += dot_nt(active, down)
    result[:, LEAD:] += dot_nt(active, down_tail)
    dh2[:, :LEAD] += dot_nt(dpre, up)
    dh2[:, LEAD:] += dot_nt(dpre, up_tail)
    gbias_ref[...] = column_total(dpre.astype(F32))

    @pl.when(step == STEPS - 1)
    def _():
        gain = vec_ref[0:1]
        unit, rate = normal(mid[...])
        grad = dh2[...]
        gvec_ref[...] = jnp.zeros_like(gvec_ref)
        gvec_ref[0:1] = column_total(grad * unit)
        gvec_ref[1:2] = column_total(grad)
        gvec_ref[3:4] = column_total(g_ref[...].astype(F32))
        dmid = g_ref[...].astype(F32) + normal_back(unit, rate, gain, grad)
        dmid_ref[...] = dmid
        dlow = dmid.astype(BF)
        dy_ref[...] = dlow
        gvec_ref[2:3] = column_total(dlow.astype(F32))
        h2[...] = (mid[...] + result[...] + vec_ref[3:4]).astype(BF)

        def restore(index, carry):
            mixed_ref[:, lanes(index * LANES, LANES)] = dot(h2[...], unmix(index)).astype(BF)
            return carry

        lax.fori_loop(0, 9, restore, 0)
        o_perm[:, :LEAD] = dot_nt(dlow, out_a_ref[...]).astype(BF)
        o_perm[:, LEAD:] = dot_nt(dlow, out_b_ref[...]).astype(BF)

        def split_head(head, carry):
            do_ref[head] = dot_nt(o_perm[...], head_place(head)).astype(BF)
            return carry

        lax.fori_loop(0, HEADS, split_head, 0)


def middle(o, x, g, attn, attn_tail, vec, bias, mlp):
    def whole(*shape):
        return pl.BlockSpec(shape, lambda i: (0,) * len(shape))

    turned = [(LEAD, 256), (TAIL, 256)] * 3
    found = pl.pallas_call(
        middle_kernel,
        grid=(STEPS,),
        out_shape=tuple(
            [
                jax.ShapeDtypeStruct((256, D), BF),
                jax.ShapeDtypeStruct((HEADS, 256, LANES), BF),
                jax.ShapeDtypeStruct((256, D), F32),
                jax.ShapeDtypeStruct((256, D), BF),
                jax.ShapeDtypeStruct((8, D), F32),
                jax.ShapeDtypeStruct((1, FF_PAD), F32),
                jax.ShapeDtypeStruct((256, FF_PAD), BF),
                jax.ShapeDtypeStruct((256, FF_PAD), BF),
            ]
            + [jax.ShapeDtypeStruct(shape, BF) for shape in turned]
        ),
        in_specs=[
            whole(HEADS, 256, LANES),
            whole(256, D),
            whole(256, D),
            pl.BlockSpec((LEAD, D), lambda i: (0, 3)),
            pl.BlockSpec((TAIL, D), lambda i: (0, 3)),
            whole(8, D),
            pl.BlockSpec((1, STEP), lambda i: (0, i)),
            pl.BlockSpec((LEAD, STEP), lambda i: (0, i)),
            pl.BlockSpec((LEAD, STEP), lambda i: (0, STEPS + i)),
            pl.BlockSpec(memory_space=pl.ANY),
        ],
        out_specs=tuple(
            [
                whole(256, D),
                whole(HEADS, 256, LANES),
                whole(256, D),
                whole(256, D),
                whole(8, D),
                pl.BlockSpec((1, STEP), lambda i: (0, i)),
                pl.BlockSpec((256, STEP), lambda i: (0, i)),
                pl.BlockSpec((256, STEP), lambda i: (0, i)),
            ]
            + [whole(*shape) for shape in turned]
        ),
        scratch_shapes=[
            pltpu.VMEM((256, D), BF),
            pltpu.VMEM((256, D), F32),
            pltpu.VMEM((256, D), BF),
            pltpu.VMEM((256, D), F32),
            pltpu.VMEM((256, D), F32),
            pltpu.VMEM((LEAD, MLP_CHUNK), BF),
            pltpu.VMEM((MLP_CHUNK // LANES, LEAD, LANES), F32),
            pltpu.VMEM((TAIL, 8 * MLP_CHUNK), BF),
            pltpu.SemaphoreType.DMA((1,)),
        ],
        compiler_params=params(),
        name="middle",
    )(o, x, g, attn, attn_tail, vec, bias, mlp, mlp, mlp)
    grouped = [
        item.reshape(4, 2, 4, 2, 16, 256) if item.shape[0] == LEAD else item for item in found[8:]
    ]
    return found[:8], grouped[4:6], grouped[0:2], grouped[2:4]


def mesh_params(tag, limit=62):
    return pltpu.CompilerParams(
        collective_id=tag, has_side_effects=True, vmem_limit_bytes=limit << 20
    )


class Twin:
    def __init__(self, place, core, send, recv, base):
        self.core, self.device = core, device_at(place, 1 - core)
        self.send, self.recv, self.base = send, recv, base
        self.items = []

    def half(self, ref, axis, core):
        size = ref.shape[axis] // 2
        if axis == 0:
            return ref.at[pl.ds(pl.multiple_of(core * size, size), size)]
        lead = (slice(None),) * (len(ref.shape) - 1)
        return ref.at[lead + (pl.ds(pl.multiple_of(core * size, LANES), size),)]

    def give(self, source, target, axis):
        index = self.base + 2 * len(self.items)
        place = self.half(target, axis, self.core)
        pltpu.make_async_copy(source, place, self.recv.at[index + 1]).start()
        remote(source, place, self.send.at[index], self.recv.at[index], self.device).start()
        self.items.append((source, target, axis, index))

    def ready(self):
        for source, target, axis, index in self.items:
            place = self.half(target, axis, self.core)
            pltpu.make_async_copy(source, place, self.recv.at[index + 1]).wait()
            other = self.half(target, axis, 1 - self.core)
            remote(
                other, other, self.send.at[index], self.recv.at[index], self.device
            ).wait_recv()

    def drain(self):
        for source, target, axis, index in self.items:
            place = self.half(target, axis, self.core)
            remote(
                place, place, self.send.at[index], self.recv.at[index], self.device
            ).wait_send()


def back_kernel(
    go,
    dpre,
    active,
    h_main,
    h_tail,
    g_main,
    g_tail,
    packed_ref,
    keep_ref,
    row_ref,
    col_ref,
    share_ref,
    dheads,
    go_all,
    grads,
    dpre_all,
    active_all,
    h_main_all,
    h_tail_all,
    g_main_all,
    g_tail_all,
    extra,
    keys,
    queries,
    dkeys,
    dvalues,
    *rest,
):
    buffers, (send, recv) = rest[:-2], rest[-2:]
    place, core = here()
    width = MLP_TOTAL // 6
    red = Reducer(width, place, core, buffers, share_ref, send, recv)
    base = 3 * Reducer.SEMS
    swap_in = Swapper(place, core, go, go_all, send, recv, base)
    outs = [Swapper(place, core, grads, dheads, send, recv, base + 16 + 16 * m) for m in range(2)]
    twin = Twin(place, core, send, recv, base + 48)
    greet(line_peers(place, core) + [swap_in.device(swap_in.member(k)) for k in range(1, 16) if k not in (1, 4, 8, 12)])
    swap_in.start()
    for source, target, axis in (
        (h_main, h_main_all, 5),
        (h_tail, h_tail_all, 1),
        (g_main, g_main_all, 5),
        (g_tail, g_tail_all, 1),
        (dpre, dpre_all, 0),
        (active, active_all, 0),
    ):
        twin.give(source, target, axis)
    maker = Maker(
        red,
        [((h_main_all, h_tail_all), dpre_all), ((g_main_all, g_tail_all), active_all)],
        extra,
        MLP_CHUNK,
    )
    twin.ready()
    maker.pack_tail()
    for part in range(3):
        maker.make(part, 2)
    red.far_out()

    def others(index, carry):
        ahead = cycle(index, 3)
        for part in range(3):
            maker.make(part, ahead)
        return carry

    lax.fori_loop(0, 3, others, 0)
    swap_in.finish()

    def block(step, carry):
        row = lax.div(step, BLOCKS)
        index = lax.rem(step, BLOCKS)
        tokens = pl.ds(pl.multiple_of(row * 128, 128), 128)

        @pl.when(index == 0)
        def _():
            packed = packed_ref[:, tokens, :].reshape(ROW, WIDE)
            lane = iota((ROW, LANES), 1)
            zero = jnp.zeros((ROW, LANES), BF)
            keys[...] = jnp.where(lane < HEAD_DIM, packed[:, :LANES], zero)
            queries[...] = jnp.concatenate(
                [packed[:, HEAD_DIM : 2 * HEAD_DIM], jnp.zeros((ROW, LANES - HEAD_DIM), BF)],
                axis=1,
            )
            dkeys[...] = jnp.zeros_like(dkeys)
            dvalues[...] = jnp.zeros_like(dvalues)

        rows = pl.ds(pl.multiple_of(index * QUERIES, QUERIES), QUERIES)
        groups = pl.ds(index * (QUERIES // 128), QUERIES // 128)
        query = queries[rows, :]
        back = go_all[groups, tokens, :].reshape(QUERIES, LANES)
        mine = row_ref[row, :, lanes(index * QUERIES, QUERIES)]
        kept = keep_ref[row, rows, :]
        inner = jnp.sum(back.astype(F32) * kept, axis=1, keepdims=True)
        lane = iota((QUERIES, LANES), 1)
        stats = jnp.transpose(jnp.where(lane == 0, kept, inner))
        logsum = stats[0:1]
        inner = stats[1:2]
        total = jnp.zeros((QUERIES, LANES), F32)
        for part in range(ROW // KEYS):
            span = slice(part * KEYS, (part + 1) * KEYS)
            blocks = slice(part * KEYS // 128, (part + 1) * KEYS // 128)
            value = packed_ref[blocks, tokens, LANES:].reshape(KEYS, LANES)
            score = dot_nt(keys[span, :], query) * (SCALE * LOG2E) - logsum
            prob = jnp.exp2(jnp.where(col_ref[row, span, :] == mine, score, NEG))
            grad = (prob * (dot_nt(value, back) - inner)).astype(BF)
            dvalues[span, :] += dot(prob.astype(BF), back)
            dkeys[span, :] += dot(grad, query)
            total = total + dot_tn(grad, keys[span, :])
        total = total * SCALE
        moved_q = jnp.concatenate(
            [
                jnp.zeros((QUERIES, HEAD_DIM), F32),
                total[:, :HEAD_DIM],
                jnp.zeros((QUERIES, WIDE - 2 * HEAD_DIM), F32),
            ],
            axis=1,
        )
        grads[groups, tokens, :] = moved_q.astype(BF).reshape(QUERIES // 128, 128, WIDE)

        @pl.when(index == BLOCKS - 1)
        def _():
            wide = jnp.concatenate([dkeys[...] * SCALE, dvalues[...]], axis=1)
            lane = iota((ROW, WIDE), 1)
            old = grads[:, tokens, :].reshape(ROW, WIDE)
            inside = (lane >= HEAD_DIM) & (lane < 2 * HEAD_DIM)
            grads[:, tokens, :] = jnp.where(inside, old, wide.astype(BF)).reshape(16, 128, WIDE)
            for micro in range(2):
                pl.when(row == micro)(functools.partial(outs[micro].start, micro))

        @pl.when(step < 4)
        def _():
            red.pass_on(step)

        @pl.when(step >= 4)
        def _():
            red.gather_side(lax.rem(step - 4 + 1, 4), step == 7)

        return carry

    lax.fori_loop(0, 2 * BLOCKS, block, 0)
    red.line_up()
    red.share()
    red.close()
    for micro in range(2):
        outs[micro].finish(micro)
    swap_in.drain()
    for micro in range(2):
        outs[micro].drain(micro)
    twin.drain()


def attend_back_reduce(go, dpre, active, turned, packed, keep, row_ids, col_ids, tag):
    any_ = pl.BlockSpec(memory_space=pl.ANY)
    vmem = pl.BlockSpec(memory_space=pltpu.VMEM)
    sems = 3 * Reducer.SEMS + 48 + 12
    return pl.pallas_call(
        back_kernel,
        out_shape=(
            jax.ShapeDtypeStruct((16, MLP_TOTAL), BF),
            jax.ShapeDtypeStruct((16, 256, WIDE), BF),
        ),
        in_specs=[any_] * 7 + [vmem] * 4,
        out_specs=(vmem, any_),
        scratch_shapes=[
            pltpu.VMEM((16, 256, LANES), BF),
            pltpu.VMEM((16, 256, WIDE), BF),
            pltpu.VMEM((512, FF_PAD), BF),
            pltpu.VMEM((512, FF_PAD), BF),
            pltpu.VMEM((4, 2, 4, 2, 16, 512), BF),
            pltpu.VMEM((TAIL, 512), BF),
            pltpu.VMEM((4, 2, 4, 2, 16, 512), BF),
            pltpu.VMEM((TAIL, 512), BF),
            pltpu.VMEM((MLP_CHUNK // LANES, LEAD, LANES), F32),
            pltpu.VMEM((ROW, LANES), BF),
            pltpu.VMEM((ROW, LANES), BF),
            pltpu.VMEM((ROW, LANES), F32),
            pltpu.VMEM((ROW, LANES), F32),
        ]
        + Reducer.scratch(MLP_TOTAL // 6)
        + [pltpu.SemaphoreType.DMA((sems,)), pltpu.SemaphoreType.DMA((sems,))],
        compiler_params=mesh_params(tag),
        name="attend_back_reduce",
    )(go, dpre, active, *turned, packed, keep, row_ids, col_ids)


VEC_ROWS = 16
VEC_QKV = 6
VEC_UP = 9


class Everyone:
    def __init__(self, place, core, slots, send, recv, base):
        self.place, self.core = place, core
        self.slots, self.send, self.recv, self.base = slots, send, recv, base

    def start(self, stage, value):
        if stage == 3:
            spot, targets = self.core, [(1, device_at(self.place, 1 - self.core))]
        else:
            axis = AXES[stage]
            spot = self.place[axis]
            targets = [
                (over, device_at(moved(self.place, axis, over), self.core)) for over in (2, 1, 3)
            ]
        self.slots[stage, spot] = value
        for over, device in targets:
            index = self.base + stage * 3 + over - 1
            slot = self.slots.at[stage, spot]
            remote(slot, slot, self.send.at[index], self.recv.at[index], device).start()

    def finish(self, stage):
        count = 2 if stage == 3 else 4
        for over in range(1, count):
            index = self.base + stage * 3 + over - 1
            spot = 1 - self.core if stage == 3 else cycle(self.place[AXES[stage]], 4 - over)
            slot = self.slots.at[stage, spot]
            remote(
                slot, slot, self.send.at[index], self.recv.at[index], device_at(self.place, self.core)
            ).wait_recv()
        total = self.slots[stage, 0]
        for spot in range(1, count):
            total = total + self.slots[stage, spot]
        return total

    def drain(self):
        for stage in range(4):
            for over in range(1, 2 if stage == 3 else 4):
                index = self.base + stage * 3 + over - 1
                slot = self.slots.at[stage, 0]
                remote(
                    slot,
                    slot,
                    self.send.at[index],
                    self.recv.at[index],
                    device_at(self.place, self.core),
                ).wait_send()


def finish_kernel(
    dheads,
    weight,
    dy,
    h_main,
    h_tail,
    o_main,
    o_tail,
    tail_ref,
    x_ref,
    dmid_ref,
    vec_ref,
    gvec_ref,
    gup_ref,
    tokens_ref,
    total_ref,
    share_ref,
    dheads_all,
    weight_all,
    flat,
    flat_all,
    dy_all,
    h_main_all,
    h_tail_all,
    o_main_all,
    o_tail_all,
    extra,
    dh,
    low,
    vectors,
    slots,
    *rest,
):
    buffers, (send, recv, local) = rest[:-3], rest[-3:]
    place, core = here()
    width = ATTN_TOTAL // 6
    red = Reducer(width, place, core, buffers, share_ref, send, recv)
    base = 3 * Reducer.SEMS
    twin = Twin(place, core, send, recv, base)
    every = Everyone(place, core, slots, send, recv, base + 12)
    heads_in = pltpu.make_async_copy(dheads, dheads_all, local.at[0])
    heads_in.start()
    weight_in = pltpu.make_async_copy(weight.at[:, pl.ds(0, QKV)], weight_all, local.at[1])
    weight_in.start()
    greet(line_peers(place, core) + [device_at(place, 1 - core)])
    for source, target, axis in (
        (h_main, h_main_all, 5),
        (h_tail, h_tail_all, 1),
        (o_main, o_main_all, 5),
        (o_tail, o_tail_all, 1),
        (dy, dy_all, 0),
    ):
        twin.give(source, target, axis)
    heads_in.wait()
    for head in range(HEADS):
        flat[:, PACK * head : PACK * head + PACK] = dheads_all[head, :, :PACK]
    twin.give(flat, flat_all, 0)
    maker = Maker(
        red,
        [((h_main_all, h_tail_all), flat_all), ((o_main_all, o_tail_all), dy_all)],
        extra,
        ATTN_CHUNK,
    )
    twin.ready()
    maker.pack_tail()
    for part in range(3):
        maker.make(part, 2)
    red.far_out()

    def others(index, carry):
        ahead = cycle(index, 3)
        for part in range(3):
            maker.make(part, ahead)
        return carry

    lax.fori_loop(0, 3, others, 0)
    dh[...] = jnp.zeros_like(dh)
    vectors[...] = jnp.zeros((VEC_ROWS, D), F32)
    vectors[2:6] = gvec_ref[:4]
    for row in range(4):
        span = slice(row * D, min((row + 1) * D, FF_PAD))
        vectors[VEC_UP + row : VEC_UP + row + 1, : span.stop - span.start] = gup_ref[:, span]
    weight_in.wait()

    for row in range(3):

        def columns(index, carry):
            columns_ = lanes(row * D + index * 384, 384)
            value = flat[:, columns_]
            vectors[VEC_QKV + row : VEC_QKV + row + 1, lanes(index * 384, 384)] = column_total(
                value.astype(F32)
            )
            dh[:, :LEAD] += dot_nt(value, weight_all[:, columns_])
            dh[:, LEAD:] += dot_nt(value, tail_ref[:, columns_])
            return carry

        lax.fori_loop(0, 3, columns, 0)
    unit, rate = normal(x_ref[...].astype(F32))
    grad = dh[...]
    vectors[0:1] = column_total(grad * unit)
    vectors[1:2] = column_total(grad)
    every.start(0, vectors[...])
    red.pass_on(0)
    red.pass_on(1)
    total = dmid_ref[...] + normal_back(unit, rate, vec_ref[0:1], grad)
    low[...] = total.astype(BF)
    red.pass_on(2)
    red.pass_on(3)
    every.start(1, every.finish(0))

    def restore(index, carry):
        tokens_ref[:, lanes(index * LANES, LANES)] = dot(low[...], unmix(index)).astype(BF)
        return carry

    lax.fori_loop(0, 9, restore, 0)
    for over in (2, 1, 3):
        red.gather_side(over, False)
    every.start(2, every.finish(1))
    red.gather_side(0, True)
    every.start(3, every.finish(2))
    red.line_up()
    total_ref[...] = every.finish(3)
    red.share()
    red.close()
    twin.drain()
    every.drain()


def finish(dheads, weight, dy, turned, tail, x, dmid, vec, gvec, gup, tag):
    any_ = pl.BlockSpec(memory_space=pl.ANY)
    vmem = pl.BlockSpec(memory_space=pltpu.VMEM)
    sems = 3 * Reducer.SEMS + 12 + 12
    return pl.pallas_call(
        finish_kernel,
        out_shape=(
            jax.ShapeDtypeStruct((256, D), BF),
            jax.ShapeDtypeStruct((VEC_ROWS, D), F32),
            jax.ShapeDtypeStruct((16, ATTN_TOTAL), BF),
        ),
        in_specs=[any_] * 7 + [vmem] * 6,
        out_specs=(vmem, vmem, vmem),
        scratch_shapes=[
            pltpu.VMEM((HEADS, 256, WIDE), BF),
            pltpu.VMEM((LEAD, QKV), BF),
            pltpu.VMEM((256, QKV), BF),
            pltpu.VMEM((512, QKV), BF),
            pltpu.VMEM((512, D), BF),
            pltpu.VMEM((4, 2, 4, 2, 16, 512), BF),
            pltpu.VMEM((TAIL, 512), BF),
            pltpu.VMEM((4, 2, 4, 2, 16, 512), BF),
            pltpu.VMEM((TAIL, 512), BF),
            pltpu.VMEM((ATTN_CHUNK // LANES, LEAD, LANES), F32),
            pltpu.VMEM((256, D), F32),
            pltpu.VMEM((256, D), BF),
            pltpu.VMEM((VEC_ROWS, D), F32),
            pltpu.VMEM((4, 4, VEC_ROWS, D), F32),
        ]
        + Reducer.scratch(ATTN_TOTAL // 6)
        + [
            pltpu.SemaphoreType.DMA((sems,)),
            pltpu.SemaphoreType.DMA((sems,)),
            pltpu.SemaphoreType.DMA((2,)),
        ],
        compiler_params=mesh_params(tag),
        name="finish",
    )(dheads, weight, dy, *turned, tail, x, dmid, vec, gvec, gup)
def pack_slab(weight, chunk, total):
    width = weight.shape[1]
    rest = jnp.pad(weight[16:], ((0, 0), (0, 8 * chunk - width))).reshape(16, chunk)
    return jnp.concatenate(
        [weight[:16], rest, jnp.zeros((16, total - width - chunk), weight.dtype)], axis=1
    )


def unpack_slab(slab, width, chunk):
    rest = slab[:, width : width + chunk].reshape(2, 8 * chunk)[:, :width]
    return jnp.concatenate([slab[:, :width], rest], axis=0).astype(F32)


def by_head(key, query, value):
    rows = key.shape[0]
    parts = [item.reshape(rows, HEADS, 1, HEAD_DIM) for item in (key, query, value)]
    return jnp.concatenate(parts, axis=2).reshape(rows, QKV)


def from_heads(value):
    parts = value.reshape(value.shape[0], HEADS, 3, HEAD_DIM)
    return [parts[:, :, i].reshape(value.shape[0], D) for i in range(3)]


def mixing():
    return onehot(iota((D, D), 0) == origin(iota((D, D), 1)))


def mix_exact(value, back=False):
    matrix = mixing().astype(F32)
    if back:
        matrix = matrix.T
    return jnp.dot(value, matrix, precision=lax.Precision.HIGHEST)


def body(
    tokens,
    picture,
    cotangent,
    ln1_gain,
    ln1_bias,
    w_query,
    b_query,
    w_key,
    w_value,
    b_value,
    w_out,
    b_out,
    ln2_gain,
    ln2_bias,
    w_fc1,
    b_fc1,
    w_fc2,
    b_fc2,
):
    mix = mixing()
    out_cols = dot(w_out, mix).astype(BF)
    attn_slab = pack_slab(
        jnp.concatenate([by_head(w_key, w_query, w_value), out_cols], axis=1),
        ATTN_CHUNK,
        ATTN_TOTAL,
    )
    gap = ((0, 0), (0, FF_PAD - FF))
    mlp_slab = pack_slab(
        jnp.concatenate([jnp.pad(w_fc1, gap), jnp.pad(w_fc2.T, gap)], axis=1),
        MLP_CHUNK,
        MLP_TOTAL,
    )
    attn = gather_slab(attn_slab, 0)
    mlp = gather_slab(mlp_slab, 1)

    both = jnp.concatenate([tokens.reshape(256, D), cotangent.reshape(256, D)], axis=0)
    both = dot(both, mix).astype(BF)
    x, g = both[:256], both[256:]
    vec = mix_exact(jnp.stack([ln1_gain, ln1_bias, ln2_gain, ln2_bias, b_out, b_fc2]))
    vec1 = jnp.pad(vec[:2], ((0, 6), (0, 0)))
    vec2 = jnp.pad(vec[2:], ((0, 4), (0, 0)))
    bias = by_head(jnp.zeros((1, D), F32), b_query[None], b_value[None])

    group = lax.div(lax.axis_index("fsdp"), 8)
    ids = lax.dynamic_slice(picture, (0, group * ROW), (2, ROW))
    row_ids = ids[:, None, :]
    col_ids = ids[:, :, None]

    heads, h1, attn_tail = project_heads(x, attn, vec1, bias)
    packed = swap_heads(heads, 2)
    o, keep = attend(packed, row_ids, col_ids)
    o = swap_heads(o, 3)
    (mixed, go, dmid, dy, gvec2, gbias1, dpre, active), o_turned, h_turned, g_turned = middle(
        o, x, g, attn, attn_tail, vec2, jnp.pad(b_fc1, (0, FF_PAD - FF))[None], mlp
    )
    mlp_share, dheads = attend_back_reduce(
        go, dpre, active, (*h_turned, *g_turned), packed, keep, row_ids, col_ids, 4
    )
    h_main = h1.T[:LEAD].reshape(4, 2, 4, 2, 16, 256)
    gtokens, totals, attn_share = finish(
        dheads,
        attn,
        dy,
        (h_main, h1.T[LEAD:], *o_turned),
        attn_tail,
        x,
        dmid,
        vec1,
        gvec2,
        gbias1,
        5,
    )
    mlp_share = unpack_slab(mlp_share, MLP_MAIN, MLP_CHUNK)
    attn_share = unpack_slab(attn_share, ATTN_MAIN, ATTN_CHUNK)
    vectors = totals[:VEC_QKV]
    gbias = totals[VEC_QKV:VEC_UP].reshape(1, QKV)
    gbias1 = totals[VEC_UP : VEC_UP + 4].reshape(1, 4 * D)
    vectors = mix_exact(vectors, True)
    grad_key, grad_query, grad_value = from_heads(attn_share[:, :QKV])
    _, bias_query, bias_value = from_heads(gbias)
    grad_out = mix_exact(attn_share[:, QKV:], True)
    grad_up = mlp_share[:, :FF]
    grad_down = mlp_share[:, FF_PAD : FF_PAD + FF].T
    return (
        mixed.reshape(2, 128, D),
        gtokens.reshape(2, 128, D),
        vectors[0],
        vectors[1],
        grad_query,
        bias_query[0],
        grad_key,
        grad_value,
        bias_value[0],
        grad_out,
        vectors[4],
        vectors[2],
        vectors[3],
        grad_up,
        gbias1[0, :FF],
        grad_down,
        vectors[5],
    )


def solution(mesh):
    placed = (
        P(None, ("fsdp", "rep"), None),
        P(),
        P(None, ("fsdp", "rep"), None),
        P(),
        P(),
        P("fsdp", None),
        P(),
        P("fsdp", None),
        P("fsdp", None),
        P(),
        P("fsdp", None),
        P(),
        P(),
        P(),
        P("fsdp", None),
        P(),
        P(None, "fsdp"),
        P(),
    )
    return jax.shard_map(
        body,
        mesh=mesh,
        in_specs=placed,
        out_specs=(
            P(None, ("fsdp", "rep"), None),
            P(None, ("fsdp", "rep"), None),
            P(),
            P(),
            P("fsdp", None),
            P(),
            P("fsdp", None),
            P("fsdp", None),
            P(),
            P("fsdp", None),
            P(),
            P(),
            P(),
            P("fsdp", None),
            P(),
            P(None, "fsdp"),
            P(),
        ),
        check_vma=False,
    )
```

```python
import functools

import jax
import jax.numpy as jnp
import numpy as np
from jax import lax
from jax.experimental import pallas as pl
from jax.experimental.pallas import tpu as pltpu
from jax.sharding import PartitionSpec as P

MESH = pl.DeviceIdType.MESH
BF = jnp.bfloat16
F32 = jnp.float32
LANES = 128
ORDERS = (("x", "y", "z"), ("y", "z", "x"), ("z", "x", "y"))
AXES = ("x", "y", "z")


def here():
    shard = lax.axis_index("fsdp")
    low = lax.axis_index("rep")
    place = {
        "x": lax.div(shard, 16),
        "y": lax.rem(lax.div(shard, 8), 2) * 2 + low,
        "z": lax.rem(lax.div(shard, 2), 4),
    }
    return place, lax.rem(shard, 2)


def moved(place, axis, steps):
    steps = steps % 4
    if steps == 0:
        return place
    other = dict(place)
    other[axis] = lax.rem(place[axis] + steps, 4)
    return other


def device_at(place, core):
    high = lax.div(place["y"], 2)
    return (((place["x"] * 2 + high) * 4 + place["z"]) * 2 + core, lax.rem(place["y"], 2))


def greet(peers):
    barrier = pltpu.get_barrier_semaphore()
    for peer in peers:
        pl.semaphore_signal(barrier, inc=1, device_id=peer, device_id_type=MESH)
    pl.semaphore_wait(barrier, len(peers))


def part_columns(part, half, widths):
    start = 2 * sum(widths[:part]) + half * widths[part]
    return pl.ds(pl.multiple_of(start, LANES), widths[part])


def piece_of(ref, part, widths, place, core):
    return ref.at[
        place["x"],
        lax.div(place["y"], 2),
        place["z"],
        core,
        :,
        part_columns(part, lax.rem(place["y"], 2), widths),
    ]


def block_of(ref, part, widths, place, core, axis, half=None):
    where = {"x": place["x"], "y": lax.div(place["y"], 2), "z": place["z"]}
    if axis == "y":
        where["y"] = pl.ds(0, 2) if half is None else pl.ds(half, 1)
        columns = pl.ds(2 * sum(widths[:part]), 2 * widths[part])
    else:
        where[axis] = pl.ds(0, 4) if half is None else pl.ds(2 * half, 2)
        columns = part_columns(part, lax.rem(place["y"], 2), widths)
    return ref.at[where["x"], where["y"], where["z"], core, :, columns]


def remote(source, target, send, recv, device):
    return pltpu.make_async_remote_copy(
        src_ref=source,
        dst_ref=target,
        send_sem=send,
        recv_sem=recv,
        device_id=device,
        device_id_type=MESH,
    )


def cycle(value, steps):
    return lax.rem(value + steps, 4)


def turned_by(place, axis, steps):
    other = dict(place)
    other[axis] = cycle(place[axis], steps)
    return other


class Gatherer:
    SEMS = 3 + 3 + 8 + 8 + 16
    KINDS = {"one": 0, "two": 3, "three": 6, "four": 14, "twin": 22}

    def __init__(self, widths, place, core, own, full, send, recv, base):
        self.widths, self.place, self.core = widths, place, core
        self.own, self.full, self.send, self.recv, self.base = own, full, send, recv, base
        self.twin = device_at(place, 1 - core)

    def slot(self, part, kind, index):
        return self.base + part * self.SEMS + self.KINDS[kind] + index

    def push(self, source, target, slot, device):
        remote(source, target, self.send.at[slot], self.recv.at[slot], device).start()

    def arrived(self, region, slot):
        remote(region, region, self.send.at[slot], self.recv.at[slot], self.twin).wait_recv()

    def sent(self, region, slot):
        remote(region, region, self.send.at[slot], self.recv.at[slot], self.twin).wait_send()

    def block(self, part, place, half=None, core=None):
        core = self.core if core is None else core
        return block_of(self.full, part, self.widths, place, core, ORDERS[part][0], half)

    def keep(self, part):
        low = lax.rem(self.place["y"], 2)
        source = self.own.at[:, part_columns(part, low, self.widths)]
        target = piece_of(self.full, part, self.widths, self.place, self.core)
        return source, target, pltpu.make_async_copy(
            source, target, self.recv.at[self.base + 3 * self.SEMS + part]
        )

    def start(self):
        for part, (one, two, three) in enumerate(ORDERS):
            source, target, copy = self.keep(part)
            copy.start()
            for steps in (1, 3, 2):
                device = device_at(turned_by(self.place, one, steps), self.core)
                self.push(source, target, self.slot(part, "one", steps - 1), device)

    def second(self):
        for part, (one, two, three) in enumerate(ORDERS):
            self.keep(part)[2].wait()
            for steps in (1, 3, 2):
                origin = turned_by(self.place, one, 4 - steps)
                region = piece_of(self.full, part, self.widths, origin, self.core)
                self.arrived(region, self.slot(part, "one", steps - 1))
            block = self.block(part, self.place)
            for steps in (1, 3, 2):
                device = device_at(turned_by(self.place, two, steps), self.core)
                self.push(block, block, self.slot(part, "two", steps - 1), device)
        self.spread(0)

    def spread(self, steps):
        for part, (one, two, three) in enumerate(ORDERS):
            block = self.block(part, turned_by(self.place, two, 4 - steps))
            for index, way in enumerate((1, 3)):
                device = device_at(turned_by(self.place, three, way), self.core)
                self.push(block, block, self.slot(part, "three", index * 4 + steps), device)
            self.push(block, block, self.slot(part, "twin", steps), self.twin)

    def third(self, steps):
        for part, (one, two, three) in enumerate(ORDERS):
            block = self.block(part, turned_by(self.place, two, 4 - steps))
            self.arrived(block, self.slot(part, "two", steps - 1))
        self.spread(steps)

    def fourth(self, steps):
        for part, (one, two, three) in enumerate(ORDERS):
            side = turned_by(self.place, two, 4 - steps)
            for index, way in enumerate((1, 3)):
                origin = turned_by(side, three, 4 - way)
                block = self.block(part, origin)
                self.arrived(block, self.slot(part, "three", index * 4 + steps))
                half = self.block(part, origin, index)
                device = device_at(turned_by(self.place, three, way), self.core)
                self.push(half, half, self.slot(part, "four", index * 4 + steps), device)
                self.push(block, block, self.slot(part, "twin", way * 4 + steps), self.twin)

    def fifth(self, steps):
        for part, (one, two, three) in enumerate(ORDERS):
            origin = turned_by(turned_by(self.place, two, 4 - steps), three, 2)
            for index in range(2):
                half = self.block(part, origin, index)
                self.arrived(half, self.slot(part, "four", index * 4 + steps))
            block = self.block(part, origin)
            self.push(block, block, self.slot(part, "twin", 8 + steps), self.twin)

    def close(self):
        for part, (one, two, three) in enumerate(ORDERS):
            for way in range(4):
                for steps in range(4):
                    origin = moved(moved(self.place, two, -steps), three, -way)
                    region = self.block(part, origin, core=1 - self.core)
                    self.arrived(region, self.slot(part, "twin", way * 4 + steps))

    def drain(self):
        for part in range(3):
            piece = piece_of(self.full, part, self.widths, self.place, self.core)
            block = self.block(part, self.place)
            half = self.block(part, self.place, 0)
            for kind, region, count in (
                ("one", piece, 3),
                ("two", block, 3),
                ("three", block, 8),
                ("four", half, 8),
                ("twin", block, 16),
            ):
                for index in range(count):
                    self.sent(region, self.slot(part, kind, index))


class Reducer:
    SEMS = 8 + 8 + 3 + 3 + 1
    KINDS = {"mid": 0, "far": 8, "side": 16, "line": 19, "done": 22}

    def __init__(self, widths, place, core, buffers, out, send, recv, base=0):
        self.widths, self.place, self.core, self.base = widths, place, core, base
        self.acc, self.mid, self.far, self.side, self.line, self.done = [
            buffers[3 * i : 3 * i + 3] for i in range(6)
        ]
        self.out, self.send, self.recv = out, send, recv
        self.me = device_at(place, core)

    @staticmethod
    def scratch(widths):
        found = []
        for lead, half in (((4, 4), 1), ((2, 4), 2), ((2, 4), 1), ((3,), 1)):
            for width, (one, two, three) in zip(widths, ORDERS):
                if one == "y":
                    found.append(pltpu.VMEM(lead + (2 // half, 16, 2 * width), BF))
                else:
                    found.append(pltpu.VMEM(lead + (4 // half, 16, width), BF))
        found += [pltpu.VMEM((3, 16, width), BF) for width in widths]
        found += [pltpu.VMEM((16, width), BF) for width in widths]
        return found

    def slot(self, part, kind, index):
        return self.base + part * self.SEMS + self.KINDS[kind] + index

    def push(self, source, target, slot, device):
        remote(source, target, self.send.at[slot], self.recv.at[slot], device).start()

    def arrived(self, region, slot):
        remote(region, region, self.send.at[slot], self.recv.at[slot], self.me).wait_recv()

    def sent(self, region, slot):
        remote(region, region, self.send.at[slot], self.recv.at[slot], self.me).wait_send()

    def add(self, target, *terms):
        for index in range(target.shape[0]):
            total = target[index].astype(F32)
            for term in terms:
                total = total + term[index].astype(F32)
            target[index] = total.astype(BF)

    def half_of(self, ref, half):
        size = ref.shape[0] // 2
        return ref.at[pl.ds(half * size, size)]

    def far_out(self):
        for spot in range(4):
            for part, (one, two, three) in enumerate(ORDERS):
                for half, way in ((0, 3), (1, 1)):
                    self.push(
                        self.half_of(self.acc[part].at[2, spot], half),
                        self.mid[part].at[half, spot],
                        self.slot(part, "mid", half * 4 + spot),
                        device_at(moved(self.place, three, way), self.core),
                    )

    def pass_on(self, spot):
        for part, (one, two, three) in enumerate(ORDERS):
            for half, way in ((0, 3), (1, 1)):
                self.arrived(
                    self.mid[part].at[half, spot], self.slot(part, "mid", half * 4 + spot)
                )
                self.add(
                    self.half_of(self.acc[part].at[way, spot], half), self.mid[part].at[half, spot]
                )
                self.push(
                    self.acc[part].at[way, spot],
                    self.far[part].at[half, spot],
                    self.slot(part, "far", half * 4 + spot),
                    device_at(moved(self.place, three, way), self.core),
                )

    def gather_side(self, over, last):
        for part, (one, two, three) in enumerate(ORDERS):
            spot = cycle(self.place[two], over)
            for half in range(2):
                self.arrived(
                    self.far[part].at[half, spot], self.slot(part, "far", half * 4 + spot)
                )
            self.add(
                self.acc[part].at[0, spot], self.far[part].at[0, spot], self.far[part].at[1, spot]
            )

            def give(part=part, two=two, spot=spot):
                other = dict(self.place)
                other[two] = spot
                self.push(
                    self.acc[part].at[0, spot],
                    self.side[part].at[over - 1],
                    self.slot(part, "side", over - 1),
                    device_at(other, self.core),
                )

            if last is False:
                give()
            elif last is not True:
                pl.when(jnp.logical_not(last))(give)

    def piece(self, part, axis, spot):
        own = self.acc[part].at[0, self.place[ORDERS[part][1]]]
        if axis == "y":
            start = pl.multiple_of(lax.rem(spot["y"], 2) * self.widths[part], LANES)
            return own.at[lax.div(spot["y"], 2), :, pl.ds(start, self.widths[part])]
        return own.at[spot[axis]]

    def line_up(self):
        for part, (one, two, three) in enumerate(ORDERS):
            for over in range(3):
                self.arrived(self.side[part].at[over], self.slot(part, "side", over))
            own = self.acc[part].at[0, self.place[two]]
            self.add(own, self.side[part].at[0], self.side[part].at[1], self.side[part].at[2])
            for over in (2, 1, 3):
                spot = moved(self.place, one, over)
                self.push(
                    self.piece(part, one, spot),
                    self.line[part].at[over - 1],
                    self.slot(part, "line", over - 1),
                    device_at(spot, self.core),
                )

    def share(self):
        low = lax.rem(self.place["y"], 2)
        partner = (lax.axis_index("fsdp"), 1 - low)
        for part, (one, two, three) in enumerate(ORDERS):
            for over in range(3):
                self.arrived(self.line[part].at[over], self.slot(part, "line", over))
            total = self.piece(part, one, self.place)[...].astype(F32)
            for over in range(3):
                total = total + self.line[part][over].astype(F32)
            self.done[part][...] = total.astype(BF)
            columns = part_columns(part, low, self.widths)
            self.push(
                self.done[part], self.out.at[:, columns], self.slot(part, "done", 0), partner
            )
            self.out[:, columns] = self.done[part][...]

    def close(self):
        low = lax.rem(self.place["y"], 2)
        for part, (one, two, three) in enumerate(ORDERS):
            self.arrived(
                self.out.at[:, part_columns(part, 1 - low, self.widths)],
                self.slot(part, "done", 0),
            )
            for half in range(2):
                for spot in range(4):
                    index = half * 4 + spot
                    self.sent(self.mid[part].at[half, spot], self.slot(part, "mid", index))
                    self.sent(self.far[part].at[half, spot], self.slot(part, "far", index))
            for over in range(3):
                self.sent(self.side[part].at[over], self.slot(part, "side", over))
                self.sent(self.line[part].at[over], self.slot(part, "line", over))
            self.sent(self.done[part], self.slot(part, "done", 0))


class Maker:
    def __init__(self, reducer, sources, extra, chunk):
        self.red, self.sources, self.extra, self.chunk = reducer, sources, extra, chunk
        self.main = sum(item[1].shape[1] for item in sources)

    def pack_tail(self):
        start = 0
        pieces = []
        for turned, right in self.sources:
            pieces.append((start, start + right.shape[1], turned, right))
            start += right.shape[1]
        for index in range(8):
            low, high = index * self.chunk, (index + 1) * self.chunk
            for first, last, turned, right in pieces:
                a, b = max(low, first), min(high, last)
                if a < b:
                    value = dot(turned[1][...], right[:, a - first : b - first])
                    self.scatter(index, a - low, value)
            if high > self.main:
                a = max(low, self.main)
                self.scatter(index, a - low, jnp.zeros((TAIL, high - a), F32))

    def scatter(self, index, start, value):
        for tile in range(value.shape[1] // LANES):
            self.extra[start // LANES + tile, pl.ds(index, TAIL, stride=8), :] = value[
                :, tile * LANES : (tile + 1) * LANES
            ]

    def rows(self, ref, part, ahead):
        place, core = self.red.place, self.red.core
        three = ORDERS[part][2]
        spot = cycle(place[three], ahead)
        if len(ref.shape) == 2:
            if three == "z":
                groups = [outer * 8 + spot * 2 + core for outer in range(8)]
            elif three == "x":
                groups = [spot * 16 + inner * 2 + core for inner in range(8)]
            else:
                high = lax.div(spot, 2) * 8
                groups = [x * 16 + high + z * 2 + core for x in range(4) for z in range(4)]
            found = [ref[pl.ds(pl.multiple_of(group * 16, 16), 16)] for group in groups]
            return jnp.concatenate(found, axis=0)
        if three == "z":
            value = ref[:, :, spot, core]
        elif three == "x":
            value = ref[spot, :, :, core]
        else:
            value = ref[:, lax.div(spot, 2), :, core]
        return value.reshape(-1, ref.shape[-1])

    def columns(self, part, half, ahead):
        width = self.red.widths[part]
        low = 2 * sum(self.red.widths[:part]) + half * width
        high = low + width
        first = 0
        found = []
        for turned, right in self.sources:
            last = first + right.shape[1]
            a, b = max(low, first), min(high, last)
            if a < b:
                left = self.rows(turned[0], part, ahead)
                found.append(dot(left, right[:, a - first : b - first]).astype(BF))
            first = last
        a, b = max(low, first), min(high, first + self.chunk)
        if a < b:
            for tile in range((a - first) // LANES, (b - first) // LANES):
                found.append(self.rows(self.extra.at[tile], part, ahead).astype(BF))
        a = max(low, first + self.chunk)
        if a < high:
            found.append(jnp.zeros((found[0].shape[0], high - a), BF))
        return found[0] if len(found) == 1 else jnp.concatenate(found, axis=1)

    def make(self, part, ahead):
        red, width = self.red, self.red.widths[part]
        acc = red.acc[part]
        three = ORDERS[part][2]
        if three == "z":
            for half in range(2):
                value = self.columns(part, half, ahead).reshape(4, 2, 16, width)
                for high in range(2):
                    acc[ahead, 2 * high + half] = value[:, high]
        elif three == "x":
            for half in range(2):
                value = self.columns(part, half, ahead).reshape(2, 4, 16, width)
                for spot in range(4):
                    acc[ahead, spot, :, :, half * width : (half + 1) * width] = value[:, spot]
        else:
            low = lax.rem(cycle(red.place["y"], ahead), 2)
            for half in range(2):

                @pl.when(low == half)
                def _(half=half):
                    value = self.columns(part, half, ahead).reshape(4, 4, 16, width)
                    for spot in range(4):
                        acc[ahead, spot] = value[spot]


SWAP_ORDER = (9, 11, 5, 13, 7, 15, 1, 3, 8, 10, 4, 12, 6, 14, 2)


class Swapper:
    def __init__(self, place, core, own, full, send, recv, base):
        self.place, self.core = place, core
        self.own, self.full, self.send, self.recv, self.base = own, full, send, recv, base
        self.low = lax.rem(place["y"], 2)
        self.mine = (place["z"] * 2 + core) * 2 + self.low
        self.group = lax.div(lax.axis_index("fsdp"), 8) * 8

    def member(self, k, sign=1):
        z = lax.rem(self.place["z"] + (4 + sign * (k // 4)), 4)
        core = lax.rem(self.core + (k // 2) % 2, 2)
        low = lax.rem(self.low + k % 2, 2)
        return (z * 2 + core) * 2 + low

    def device(self, index):
        return (self.group + lax.div(index, 2), lax.rem(index, 2))

    def peers(self):
        return [self.device(self.member(k)) for k in range(1, 16)]

    def view(self, ref, index, micro):
        if micro is None:
            return ref.at[index]
        return ref.at[index, pl.ds(micro * 128, 128)]

    def start(self, micro=None):
        for k in SWAP_ORDER:
            target = self.member(k)
            remote(
                self.view(self.own, target, micro),
                self.view(self.full, self.mine, micro),
                self.send.at[self.base + k],
                self.recv.at[self.base + k],
                self.device(target),
            ).start()
        pltpu.make_async_copy(
            self.view(self.own, self.mine, micro),
            self.view(self.full, self.mine, micro),
            self.send.at[self.base],
        ).start()

    def finish(self, micro=None):
        pltpu.make_async_copy(
            self.view(self.own, self.mine, micro),
            self.view(self.full, self.mine, micro),
            self.send.at[self.base],
        ).wait()
        for k in range(1, 16):
            region = self.view(self.full, self.member(k, -1), micro)
            remote(
                region,
                region,
                self.send.at[self.base + k],
                self.recv.at[self.base + k],
                self.device(self.mine),
            ).wait_recv()

    def drain(self, micro=None):
        for k in range(1, 16):
            region = self.view(self.own, self.member(k), micro)
            remote(
                region,
                region,
                self.send.at[self.base + k],
                self.recv.at[self.base + k],
                self.device(self.mine),
            ).wait_send()


def line_peers(place, core):
    peers = []
    for axis in AXES:
        for steps in (1, 2, 3):
            peers.append(device_at(moved(place, axis, steps), core))
    return peers


D = 1152
HEADS = 16
HEAD_DIM = 72
FF = 4304
ROW = 2048
EPS = 1e-06
NEG = -1e30
SCALE = HEAD_DIM**-0.5
LEAD = 1024
TAIL = 128
PACK = 3 * HEAD_DIM
WIDE = 256
VALUE_LANE = 16
FF_PAD = 4352
QKV = HEADS * PACK
ATTN_MAIN = QKV + D
ATTN_CHUNK = 640
ATTN_TOTAL = 5376
MLP_MAIN = 2 * FF_PAD
MLP_CHUNK = 1152
MLP_TOTAL = 9984
ATTN_WIDTHS = (896, 896, 896)
MLP_WIDTHS = (1664, 1664, 1664)
FIRST = 2304
FIRST_CHUNK = 640
FIRST_TOTAL = 5376
FIRST_WIDTHS = (896, 896, 896)
FIRST_STEP = 768
SECOND = FF_PAD - FIRST
SECOND_CHUNK = 512
SECOND_TOTAL = 4608
SECOND_WIDTHS = (768, 768, 768)
SECOND_STEP = 512
LOG2E = 1.4426950408889634
QUERIES = 512
KEYS = 512
BLOCKS = ROW // QUERIES
TANH_A = 0.7978845608028654
TANH_B = 0.044715


def dot(left, right):
    return jnp.dot(left, right, preferred_element_type=F32)


def dot_nt(left, right):
    return lax.dot_general(left, right, (((1,), (1,)), ((), ())), preferred_element_type=F32)


def dot_tn(left, right):
    return lax.dot_general(left, right, (((0,), (0,)), ((), ())), preferred_element_type=F32)


def origin(index):
    lead = (index >> 4) * 18 + (index & 15)
    rest = index - LEAD
    tail = (rest >> 1) * 18 + 16 + (rest & 1)
    return jnp.where(index < LEAD, lead, tail)


def iota(shape, axis):
    return lax.broadcasted_iota(jnp.int32, shape, axis)


def onehot(mask):
    return mask.astype(F32).astype(BF)


def normal(values):
    center = values - jnp.mean(values, axis=-1, keepdims=True)
    rate = lax.rsqrt(jnp.mean(center * center, axis=-1, keepdims=True) + EPS)
    return center * rate, rate


def normal_back(unit, rate, gain, grad):
    inner = grad * gain
    first = jnp.mean(inner, axis=-1, keepdims=True)
    second = jnp.mean(inner * unit, axis=-1, keepdims=True)
    return rate * (inner - first - unit * second)


def column_total(values):
    return jnp.sum(values, axis=0, keepdims=True)


def lanes(start, size):
    return pl.ds(pl.multiple_of(start, LANES), size)


def params(limit=60):
    return pltpu.CompilerParams(vmem_limit_bytes=limit << 20)


def head_place(head):
    spot = iota((LANES, D), 0) - VALUE_LANE
    inside = (spot >= 0) & (spot < HEAD_DIM)
    return onehot(inside & (origin(iota((LANES, D), 1)) == HEAD_DIM * head + spot))


def head_pick(head):
    spot = iota((D, LANES), 1) - VALUE_LANE
    inside = (spot >= 0) & (spot < HEAD_DIM)
    return onehot(inside & (origin(iota((D, LANES), 0)) == HEAD_DIM * head + spot))


def unmix(value):
    return onehot(origin(iota((D, LANES), 0)) == value * LANES + iota((D, LANES), 1))


def mesh_params(tag, limit=62):
    return pltpu.CompilerParams(
        collective_id=tag, has_side_effects=True, vmem_limit_bytes=limit << 20
    )


class Twin:
    def __init__(self, place, core, send, recv, base):
        self.core, self.device = core, device_at(place, 1 - core)
        self.send, self.recv, self.base = send, recv, base
        self.items = []

    def half(self, ref, axis, core):
        size = ref.shape[axis] // 2
        if axis == 0:
            return ref.at[pl.ds(pl.multiple_of(core * size, size), size)]
        lead = (slice(None),) * (len(ref.shape) - 1)
        return ref.at[lead + (pl.ds(pl.multiple_of(core * size, LANES), size),)]

    def give(self, source, target, axis):
        index = self.base + 2 * len(self.items)
        place = self.half(target, axis, self.core)
        pltpu.make_async_copy(source, place, self.recv.at[index + 1]).start()
        remote(source, place, self.send.at[index], self.recv.at[index], self.device).start()
        self.items.append((source, target, axis, index))

    def ready(self):
        for source, target, axis, index in self.items:
            place = self.half(target, axis, self.core)
            pltpu.make_async_copy(source, place, self.recv.at[index + 1]).wait()
            other = self.half(target, axis, 1 - self.core)
            remote(
                other, other, self.send.at[index], self.recv.at[index], self.device
            ).wait_recv()

    def drain(self):
        for source, target, axis, index in self.items:
            place = self.half(target, axis, self.core)
            remote(
                place, place, self.send.at[index], self.recv.at[index], self.device
            ).wait_send()


def back_kernel(
    go,
    dpre,
    active,
    h_main,
    h_tail,
    g_main,
    g_tail,
    picture,
    packed_ref,
    keep_ref,
    share_ref,
    dheads,
    go_all,
    grads,
    dpre_all,
    active_all,
    h_main_all,
    h_tail_all,
    g_main_all,
    g_tail_all,
    extra,
    keys,
    queries,
    ids,
    dkeys,
    dvalues,
    found,
    row_ref,
    *rest,
):
    buffers, (send, recv, local) = rest[:-3], rest[-3:]
    place, core = here()
    red = Reducer(FIRST_WIDTHS, place, core, buffers, share_ref, send, recv)
    base = 3 * Reducer.SEMS
    swap_in = Swapper(place, core, go, go_all, send, recv, base)
    outs = [Swapper(place, core, grads, dheads, send, recv, base + 16 + 16 * m) for m in range(2)]
    twin = Twin(place, core, send, recv, base + 48)
    greet(line_peers(place, core) + swap_only(swap_in))
    swap_in.start()
    for source, target, axis in (
        (h_main, h_main_all, 5),
        (h_tail, h_tail_all, 1),
        (g_main, g_main_all, 5),
        (g_tail, g_tail_all, 1),
        (dpre.at[:, pl.ds(0, FIRST)], dpre_all, 0),
        (active.at[:, pl.ds(0, FIRST)], active_all, 0),
    ):
        twin.give(source, target, axis)
    maker = Maker(
        red,
        [((h_main_all, h_tail_all), dpre_all), ((g_main_all, g_tail_all), active_all)],
        extra,
        FIRST_CHUNK,
    )
    ids_in = fetch_ids(picture, found, local.at[0])
    ids_in.start()
    ids_in.wait()
    for micro in range(2):
        row_ref[micro] = found[micro : micro + 1].astype(F32)
    twin.ready()
    maker.pack_tail()
    for part in range(3):
        maker.make(part, 2)
    red.far_out()

    def others(index, carry):
        ahead = cycle(index, 3)
        for part in range(3):
            maker.make(part, ahead)
        return carry

    lax.fori_loop(0, 3, others, 0)
    swap_in.finish()

    def block(step, carry):
        row = lax.div(step, BLOCKS)
        index = lax.rem(step, BLOCKS)
        tokens = pl.ds(pl.multiple_of(row * 128, 128), 128)

        @pl.when(index == 0)
        def _():
            packed = packed_ref[:, tokens, :].reshape(ROW, WIDE)
            split_packed(packed, keys, queries)
            for part in range(ROW // LANES):
                span = slice(part * LANES, (part + 1) * LANES)
                ids[span, :] = column_ids(row_ref[row, :, span])
            dkeys[...] = jnp.zeros_like(dkeys)
            dvalues[...] = jnp.zeros_like(dvalues)

        rows = pl.ds(pl.multiple_of(index * QUERIES, QUERIES), QUERIES)
        groups = pl.ds(index * (QUERIES // 128), QUERIES // 128)
        query = queries[rows, :]
        back = go_all[groups, tokens, :].reshape(QUERIES, LANES)
        mine = row_ref[row, :, lanes(index * QUERIES, QUERIES)]
        kept = keep_ref[row, rows, :]
        inner = jnp.sum(back.astype(F32) * kept, axis=1, keepdims=True)
        lane = iota((QUERIES, LANES), 1)
        stats = jnp.transpose(jnp.where(lane == 0, kept, inner))
        logsum = stats[0:1]
        inner = stats[1:2]
        total = jnp.zeros((QUERIES, LANES), F32)
        for part in range(ROW // KEYS):
            span = slice(part * KEYS, (part + 1) * KEYS)
            blocks = slice(part * KEYS // 128, (part + 1) * KEYS // 128)
            value = packed_ref[blocks, tokens, LANES:].reshape(KEYS, LANES)
            allowed = jnp.concatenate([ids[span, :]] * (QUERIES // LANES), axis=1)
            score = dot_nt(keys[span, :], query) * (SCALE * LOG2E) - logsum
            prob = jnp.exp2(jnp.where(allowed == mine, score, NEG))
            grad = (prob * (dot_nt(value, back) - inner)).astype(BF)
            dvalues[span, :] += dot(prob.astype(BF), back)
            dkeys[span, :] += dot(grad, query)
            total = total + dot_tn(grad, keys[span, :])
        total = total * SCALE
        moved_q = jnp.concatenate(
            [
                jnp.zeros((QUERIES, HEAD_DIM), F32),
                total[:, :HEAD_DIM],
                jnp.zeros((QUERIES, WIDE - 2 * HEAD_DIM), F32),
            ],
            axis=1,
        )
        grads[groups, tokens, :] = moved_q.astype(BF).reshape(QUERIES // 128, 128, WIDE)

        @pl.when(index == BLOCKS - 1)
        def _():
            wide = jnp.concatenate([dkeys[...] * SCALE, dvalues[...]], axis=1)
            lane = iota((ROW, WIDE), 1)
            old = grads[:, tokens, :].reshape(ROW, WIDE)
            inside = (lane >= HEAD_DIM) & (lane < 2 * HEAD_DIM)
            grads[:, tokens, :] = jnp.where(inside, old, wide.astype(BF)).reshape(16, 128, WIDE)
            for micro in range(2):
                pl.when(row == micro)(functools.partial(outs[micro].start, micro))

        @pl.when(step < 4)
        def _():
            red.pass_on(step)

        @pl.when(step >= 4)
        def _():
            red.gather_side(lax.rem(step - 4 + 1, 4), step == 7)

        return carry

    lax.fori_loop(0, 2 * BLOCKS, block, 0)
    red.line_up()
    red.share()
    red.close()
    for micro in range(2):
        outs[micro].finish(micro)
    swap_in.drain()
    for micro in range(2):
        outs[micro].drain(micro)
    twin.drain()


def attend_back_reduce(go, dpre, active, turned, packed, keep, picture, tag):
    any_ = pl.BlockSpec(memory_space=pl.ANY)
    vmem = pl.BlockSpec(memory_space=pltpu.VMEM)
    sems = 3 * Reducer.SEMS + 48 + 12
    return pl.pallas_call(
        back_kernel,
        out_shape=(
            jax.ShapeDtypeStruct((16, FIRST_TOTAL), BF),
            jax.ShapeDtypeStruct((16, 256, WIDE), BF),
        ),
        in_specs=[any_] * 8 + [vmem] * 2,
        out_specs=(vmem, any_),
        scratch_shapes=[
            pltpu.VMEM((16, 256, LANES), BF),
            pltpu.VMEM((16, 256, WIDE), BF),
            pltpu.VMEM((512, FIRST), BF),
            pltpu.VMEM((512, FIRST), BF),
            pltpu.VMEM((4, 2, 4, 2, 16, 512), BF),
            pltpu.VMEM((TAIL, 512), BF),
            pltpu.VMEM((4, 2, 4, 2, 16, 512), BF),
            pltpu.VMEM((TAIL, 512), BF),
            pltpu.VMEM((FIRST_CHUNK // LANES, LEAD, LANES), F32),
            pltpu.VMEM((ROW, LANES), BF),
            pltpu.VMEM((ROW, LANES), BF),
            pltpu.VMEM((ROW, LANES), F32),
            pltpu.VMEM((ROW, LANES), F32),
            pltpu.VMEM((ROW, LANES), F32),
            pltpu.VMEM((2, ROW), jnp.int32),
            pltpu.VMEM((2, 1, ROW), F32),
        ]
        + Reducer.scratch(FIRST_WIDTHS)
        + [
            pltpu.SemaphoreType.DMA((sems,)),
            pltpu.SemaphoreType.DMA((sems,)),
            pltpu.SemaphoreType.DMA((1,)),
        ],
        compiler_params=mesh_params(tag),
        name="attend_back_reduce",
    )(go, dpre, active, *turned, picture, packed, keep)


VEC_ROWS = 16
VEC_QKV = 6
VEC_UP = 9


def spread_tail(source, chunk, wide, tail):
    for tile in range(chunk // LANES):
        wide[tile] = source(tile).astype(F32)
        for index in range(8):
            start = index * chunk + tile * LANES
            picked = wide[tile, pl.ds(index, TAIL, stride=8), :]
            tail[:, start : start + LANES] = picked.astype(BF)


def open_kernel(
    slab,
    tokens_ref,
    cotangent_ref,
    *refs,
):
    lines, rest = refs[:8], refs[8:]
    run_open(slab, tokens_ref, cotangent_ref, lines, *rest)


def run_open(
    slab,
    tokens_ref,
    cotangent_ref,
    lines,
    heads_ref,
    x_ref,
    g_ref,
    h_main_ref,
    h_tail_ref,
    tail_ref,
    out_tail_ref,
    mixed_vec_ref,
    weight_out,
    full,
    low,
    flat,
    wide,
    tail,
    vec_ref,
    send,
    recv,
    local,
):
    place, core = here()
    red = Gatherer(ATTN_WIDTHS, place, core, slab, full, send, recv, 0)
    greet(line_peers(place, core) + [device_at(place, 1 - core)])
    red.start()
    for index, line in enumerate(lines):
        vec_ref[index : index + 1, :] = line[...].reshape(1, D)

    def mix(index, carry):
        columns = lanes(index * LANES, LANES)
        column = onehot(iota((D, LANES), 0) == origin(index * LANES + iota((D, LANES), 1)))
        x_ref[:, columns] = dot(tokens_ref[...], column).astype(BF)
        g_ref[:, columns] = dot(cotangent_ref[...], column).astype(BF)
        mixed_vec_ref[:, columns] = jnp.dot(
            vec_ref[...],
            column.astype(F32),
            precision=lax.Precision.HIGHEST,
            preferred_element_type=F32,
        )
        return carry

    lax.fori_loop(0, 9, mix, 0)
    red.second()
    unit, _ = normal(x_ref[...].astype(F32))
    low[...] = (unit * mixed_vec_ref[0:1] + mixed_vec_ref[1:2]).astype(BF)
    for steps in (1, 2, 3):
        red.third(steps)
    turned = jnp.transpose(low[...])
    h_main_ref[...] = turned[:LEAD].reshape(4, 2, 4, 2, 16, 256)
    h_tail_ref[...] = turned[LEAD:]
    for steps in range(4):
        red.fourth(steps)
    for steps in range(4):
        red.fifth(steps)
    red.close()
    leave = pltpu.make_async_copy(full, weight_out, local.at[0])
    leave.start()

    def packed(tile):
        start = ATTN_MAIN + tile * LANES
        return full[:, :, :, :, :, start : start + LANES].reshape(LEAD, LANES)

    spread_tail(packed, ATTN_CHUNK, wide, tail)
    tail_ref[...] = tail[:, :QKV]
    out_tail_ref[...] = tail[:, QKV:ATTN_MAIN]

    def columns(index, carry):
        span = lanes(index * 384, 384)
        weight = full[:, :, :, :, :, span].reshape(LEAD, 384)
        flat[:, span] = dot(low[:, :LEAD], weight) + dot(low[:, LEAD:], tail[:, span])
        return carry

    lax.fori_loop(0, QKV // 384, columns, 0)
    for head in range(HEADS):
        span = slice(head * HEAD_DIM, (head + 1) * HEAD_DIM)
        bias = jnp.concatenate(
            [jnp.zeros((1, HEAD_DIM), F32), vec_ref[6:7, span], vec_ref[7:8, span]], axis=1
        )
        block = flat[:, PACK * head : PACK * head + PACK] + bias
        heads_ref[head] = jnp.concatenate(
            [block, jnp.zeros((256, WIDE - PACK), F32)], axis=1
        ).astype(BF)
    red.drain()
    leave.wait()


def open_layer(slab, tokens, cotangent, lines, tag):
    any_ = pl.BlockSpec(memory_space=pl.ANY)
    vmem = pl.BlockSpec(memory_space=pltpu.VMEM)
    sems = 3 * Gatherer.SEMS + 3
    full = (4, 2, 4, 2, 16, ATTN_TOTAL)
    return pl.pallas_call(
        open_kernel,
        out_shape=(
            jax.ShapeDtypeStruct((HEADS, 256, WIDE), BF),
            jax.ShapeDtypeStruct((256, D), BF),
            jax.ShapeDtypeStruct((256, D), BF),
            jax.ShapeDtypeStruct((4, 2, 4, 2, 16, 256), BF),
            jax.ShapeDtypeStruct((TAIL, 256), BF),
            jax.ShapeDtypeStruct((TAIL, QKV), BF),
            jax.ShapeDtypeStruct((TAIL, D), BF),
            jax.ShapeDtypeStruct((8, D), F32),
            jax.ShapeDtypeStruct(full, BF),
        ),
        in_specs=[any_] + [vmem] * 10,
        out_specs=(vmem,) * 8 + (any_,),
        scratch_shapes=[
            pltpu.VMEM(full, BF),
            pltpu.VMEM((256, D), BF),
            pltpu.VMEM((256, QKV), F32),
            pltpu.VMEM((ATTN_CHUNK // LANES, LEAD, LANES), F32),
            pltpu.VMEM((TAIL, 8 * ATTN_CHUNK), BF),
            pltpu.VMEM((8, D), F32),
            pltpu.SemaphoreType.DMA((sems,)),
            pltpu.SemaphoreType.DMA((sems,)),
            pltpu.SemaphoreType.DMA((1,)),
        ],
        compiler_params=mesh_params(tag),
        name="open_layer",
    )(slab, tokens, cotangent, *lines)


def column_ids(row_ids):
    size = row_ids.shape[1]
    return jnp.transpose(jnp.broadcast_to(row_ids, (LANES, size)))


def fetch_ids(picture, found, sem):
    start = pl.multiple_of(lax.div(lax.axis_index("fsdp"), 8) * ROW, ROW)
    return pltpu.make_async_copy(picture.at[:, pl.ds(start, ROW)], found, sem)


def split_packed(packed, keys, queries):
    lane = iota((ROW, LANES), 1)
    zero = jnp.zeros((ROW, LANES), BF)
    keys[...] = jnp.where(lane < HEAD_DIM, packed[:, :LANES], zero)
    queries[...] = jnp.concatenate(
        [packed[:, HEAD_DIM : 2 * HEAD_DIM], jnp.zeros((ROW, LANES - HEAD_DIM), BF)], axis=1
    )


def swap_only(swapper):
    return [swapper.device(swapper.member(k)) for k in range(1, 16) if k not in (1, 4, 8, 12)]


def attend_kernel(
    heads,
    slab,
    picture,
    packed_ref,
    keep_ref,
    o_all,
    full,
    o_own,
    keys,
    queries,
    values,
    scores,
    found,
    row_ref,
    send,
    recv,
    local,
):
    place, core = here()
    red = Gatherer(FIRST_WIDTHS, place, core, slab, full, send, recv, 0)
    base = 3 * Gatherer.SEMS + 3
    swap_in = Swapper(place, core, heads, packed_ref, send, recv, base)
    outs = [Swapper(place, core, o_own, o_all, send, recv, base + 16 + 16 * m) for m in range(2)]
    greet(line_peers(place, core) + swap_only(swap_in))
    red.start()
    swap_in.start()
    ids_in = fetch_ids(picture, found, local.at[0])
    ids_in.start()
    ids_in.wait()
    for micro in range(2):
        row_ref[micro] = found[micro : micro + 1].astype(F32)
    red.second()
    for steps in (1, 2, 3):
        red.third(steps)
    swap_in.finish()

    def block(step, carry):
        row = lax.div(step, 8)
        index = lax.rem(step, 8)
        tokens = pl.ds(pl.multiple_of(row * 128, 128), 128)

        @pl.when(index == 0)
        def _():
            packed = packed_ref[:, tokens, :].reshape(ROW, WIDE)
            split_packed(packed, keys, queries)
            lane = iota((ROW, LANES), 1)
            values[...] = jnp.where(
                lane == LANES - 1, jnp.ones((ROW, LANES), BF), packed[:, LANES:]
            )

        rows = pl.ds(pl.multiple_of(index * 256, 256), 256)
        query = queries[rows, :]
        mine = column_ids(row_ref[row, :, lanes(index * 256, 256)])
        mine = jnp.concatenate([mine] * (KEYS // LANES), axis=1)
        top = jnp.full((256, LANES), NEG, F32)
        for part in range(ROW // KEYS):
            span = slice(part * KEYS, (part + 1) * KEYS)
            score = dot_nt(query, keys[span, :])
            score = jnp.where(mine == row_ref[row, :, span], score, NEG)
            scores[:, span] = score
            for lane_block in range(KEYS // LANES):
                top = jnp.maximum(top, score[:, lane_block * LANES : (lane_block + 1) * LANES])
        top = jnp.max(top, axis=1, keepdims=True)
        total = jnp.zeros((256, LANES), F32)
        for part in range(ROW // KEYS):
            span = slice(part * KEYS, (part + 1) * KEYS)
            expo = jnp.exp2((scores[:, span] - top) * (SCALE * LOG2E))
            total = total + dot(expo.astype(BF), values[span, :])
        mass = total[:, LANES - 1 :]
        total = total / mass
        o_own[pl.ds(index * 2, 2), tokens, :] = total.astype(BF).reshape(2, 128, LANES)
        lane = iota((256, LANES), 1)
        logsum = top * (SCALE * LOG2E) + jnp.log2(mass)
        keep_ref[row, rows, :] = jnp.where(lane == 0, logsum, total)

        @pl.when(lax.rem(step, 4) == 0)
        def _():
            red.fourth(lax.div(step, 4))

        for micro in range(2):
            pl.when(step == 8 * micro + 7)(functools.partial(outs[micro].start, micro))
        return carry

    lax.fori_loop(0, 16, block, 0)
    for steps in range(4):
        red.fifth(steps)
    red.close()
    for micro in range(2):
        outs[micro].finish(micro)
    red.drain()
    swap_in.drain()
    for micro in range(2):
        outs[micro].drain(micro)


def attend_gather(heads, slab, picture, tag):
    any_ = pl.BlockSpec(memory_space=pl.ANY)
    vmem = pl.BlockSpec(memory_space=pltpu.VMEM)
    sems = 3 * Gatherer.SEMS + 3 + 48
    return pl.pallas_call(
        attend_kernel,
        out_shape=(
            jax.ShapeDtypeStruct((16, 256, WIDE), BF),
            jax.ShapeDtypeStruct((2, ROW, LANES), F32),
            jax.ShapeDtypeStruct((16, 256, LANES), BF),
            jax.ShapeDtypeStruct((4, 2, 4, 2, 16, FIRST_TOTAL), BF),
        ),
        in_specs=[any_] * 3,
        out_specs=(vmem, vmem, any_, any_),
        scratch_shapes=[pltpu.VMEM((16, 256, LANES), BF)]
        + [pltpu.VMEM((ROW, LANES), BF)] * 3
        + [
            pltpu.VMEM((256, ROW), F32),
            pltpu.VMEM((2, ROW), jnp.int32),
            pltpu.VMEM((2, 1, ROW), F32),
            pltpu.SemaphoreType.DMA((sems,)),
            pltpu.SemaphoreType.DMA((sems,)),
            pltpu.SemaphoreType.DMA((1,)),
        ],
        compiler_params=mesh_params(tag),
        name="attend_gather",
    )(heads, slab, picture)


def middle_kernel(
    attn,
    first,
    slab,
    o_ref,
    x_ref,
    g_ref,
    out_b_ref,
    vec_ref,
    bias_ref,
    mixed_ref,
    do_ref,
    dmid_ref,
    dy_ref,
    gvec_ref,
    gbias_ref,
    dpre_ref,
    active_ref,
    h_main_ref,
    h_tail_ref,
    g_main_ref,
    g_tail_ref,
    o_main_ref,
    o_tail_ref,
    out_a,
    weights,
    full,
    o_perm,
    mid,
    h2,
    result,
    dh2,
    wide,
    tail,
    bias,
    send,
    recv,
    local,
):
    place, core = here()
    red = Gatherer(SECOND_WIDTHS, place, core, slab, full, send, recv, 0)
    out_in = pltpu.make_async_copy(attn.at[:, pl.ds(QKV, D)], out_a, local.at[0])
    out_in.start()
    first_in = pltpu.make_async_copy(first, weights, local.at[1])
    first_in.start()
    greet(line_peers(place, core) + [device_at(place, 1 - core)])
    red.start()
    bias[...] = jnp.zeros_like(bias)
    bias[:, :FF] = bias_ref[...].reshape(1, FF)
    mid[...] = jnp.zeros_like(mid)

    def gather_head(head, carry):
        mid[...] += dot(o_ref[head], head_place(head))
        return carry

    lax.fori_loop(0, HEADS, gather_head, 0)
    o_perm[...] = mid[...].astype(BF)
    red.second()
    out_in.wait()
    for part in range(3):
        columns = slice(384 * part, 384 * part + 384)
        value = dot(o_perm[:, :LEAD], out_a[:, columns])
        value = value + dot(o_perm[:, LEAD:], out_b_ref[:, columns])
        mid[:, columns] = x_ref[:, columns].astype(F32) + value + vec_ref[4:5, columns]
    unit, _ = normal(mid[...])
    h2[...] = (unit * vec_ref[2:3] + vec_ref[3:4]).astype(BF)
    for steps in (1, 2, 3):
        red.third(steps)

    def turn(value, main, rest):
        turned = jnp.transpose(value)
        main[...] = turned[:LEAD].reshape(4, 2, 4, 2, 16, 256)
        rest[...] = turned[LEAD:]

    turn(o_perm[...], o_main_ref, o_tail_ref)
    turn(h2[...], h_main_ref, h_tail_ref)
    turn(g_ref[...], g_main_ref, g_tail_ref)
    result[...] = jnp.zeros_like(result)
    dh2[...] = jnp.zeros_like(dh2)
    first_in.wait()

    def tile_of(ref, main):
        def read(tile):
            start = main + tile * LANES
            return ref[:, :, :, :, :, start : start + LANES].reshape(LEAD, LANES)

        return read

    spread_tail(tile_of(weights, 2 * FIRST), FIRST_CHUNK, wide, tail)
    red.fourth(0)
    red.fourth(1)

    def chunk(ref, span, width, index, size):
        up_place = lanes(index * size, size)
        down_place = lanes(width + index * size, size)
        place_all = lanes(span + index * size, size)
        up = ref[:, :, :, :, :, up_place].reshape(LEAD, size)
        down = ref[:, :, :, :, :, down_place].reshape(LEAD, size)
        up_tail = tail[:, up_place]
        down_tail = tail[:, down_place]
        pre = dot(h2[:, :LEAD], up) + dot(h2[:, LEAD:], up_tail) + bias[:, place_all]
        square = pre * pre
        bend = jnp.tanh(TANH_A * pre * (1.0 + TANH_B * square))
        half = 0.5 * (1.0 + bend)
        active = (pre * half).astype(BF)
        slope = half + 0.5 * pre * (1.0 - bend * bend) * (TANH_A * (1.0 + 3.0 * TANH_B * square))
        back = dot(g_ref[:, :LEAD], down) + dot(g_ref[:, LEAD:], down_tail)
        dpre = (back * slope).astype(BF)
        active_ref[:, place_all] = active
        dpre_ref[:, place_all] = dpre
        active_t = jnp.transpose(active)
        dpre_t = jnp.transpose(dpre)
        result[:LEAD] += dot(down, active_t)
        result[LEAD:] += dot(down_tail, active_t)
        dh2[:LEAD] += dot(up, dpre_t)
        dh2[LEAD:] += dot(up_tail, dpre_t)
        gbias_ref[:, place_all] = column_total(dpre.astype(F32))

    def early(index, carry):
        chunk(weights, 0, FIRST, index, FIRST_STEP)

        @pl.when(index == 0)
        def _():
            red.fourth(2)
            red.fourth(3)

        @pl.when(index == 1)
        def _():
            for steps in range(4):
                red.fifth(steps)

        return carry

    lax.fori_loop(0, FIRST // FIRST_STEP, early, 0)
    red.close()
    spread_tail(tile_of(full, 2 * SECOND), SECOND_CHUNK, wide, tail)

    def late(index, carry):
        chunk(full, FIRST, SECOND, index, SECOND_STEP)
        return carry

    lax.fori_loop(0, SECOND // SECOND_STEP, late, 0)
    red.drain()
    gain = vec_ref[2:3]
    unit, rate = normal(mid[...])
    grad = jnp.transpose(dh2[...])
    gvec_ref[...] = jnp.zeros_like(gvec_ref)
    gvec_ref[0:1] = column_total(grad * unit)
    gvec_ref[1:2] = column_total(grad)
    gvec_ref[3:4] = column_total(g_ref[...].astype(F32))
    dmid = g_ref[...].astype(F32) + normal_back(unit, rate, gain, grad)
    dmid_ref[...] = dmid
    dlow = dmid.astype(BF)
    dy_ref[...] = dlow
    gvec_ref[2:3] = column_total(dlow.astype(F32))
    mixed_ref[...] = (mid[...] + jnp.transpose(result[...]) + vec_ref[5:6]).astype(BF)
    low_t = jnp.transpose(dlow)
    result[:LEAD] = dot(out_a[...], low_t)
    result[LEAD:] = dot(out_b_ref[...], low_t)
    o_perm[...] = jnp.transpose(result[...].astype(BF))

    def split_head(head, carry):
        do_ref[head] = dot(o_perm[...], head_pick(head)).astype(BF)
        return carry

    lax.fori_loop(0, HEADS, split_head, 0)


def middle(attn, first, slab, o, x, g, out_tail, vec, bias, tag):
    any_ = pl.BlockSpec(memory_space=pl.ANY)
    vmem = pl.BlockSpec(memory_space=pltpu.VMEM)
    sems = 3 * Gatherer.SEMS + 3
    turned = [(4, 2, 4, 2, 16, 256), (TAIL, 256)] * 3
    found = pl.pallas_call(
        middle_kernel,
        out_shape=tuple(
            [
                jax.ShapeDtypeStruct((256, D), BF),
                jax.ShapeDtypeStruct((HEADS, 256, LANES), BF),
                jax.ShapeDtypeStruct((256, D), F32),
                jax.ShapeDtypeStruct((256, D), BF),
                jax.ShapeDtypeStruct((8, D), F32),
                jax.ShapeDtypeStruct((1, FF_PAD), F32),
                jax.ShapeDtypeStruct((256, FF_PAD), BF),
                jax.ShapeDtypeStruct((256, FF_PAD), BF),
            ]
            + [jax.ShapeDtypeStruct(shape, BF) for shape in turned]
        ),
        in_specs=[any_] * 3 + [vmem] * 6,
        out_specs=(vmem,) * 14,
        scratch_shapes=[
            pltpu.VMEM((LEAD, D), BF),
            pltpu.VMEM((4, 2, 4, 2, 16, FIRST_TOTAL), BF),
            pltpu.VMEM((4, 2, 4, 2, 16, SECOND_TOTAL), BF),
            pltpu.VMEM((256, D), BF),
            pltpu.VMEM((256, D), F32),
            pltpu.VMEM((256, D), BF),
            pltpu.VMEM((D, 256), F32),
            pltpu.VMEM((D, 256), F32),
            pltpu.VMEM((FIRST_CHUNK // LANES, LEAD, LANES), F32),
            pltpu.VMEM((TAIL, 8 * FIRST_CHUNK), BF),
            pltpu.VMEM((1, FF_PAD), F32),
            pltpu.SemaphoreType.DMA((sems,)),
            pltpu.SemaphoreType.DMA((sems,)),
            pltpu.SemaphoreType.DMA((2,)),
        ],
        compiler_params=mesh_params(tag),
        name="middle",
    )(attn, first, slab, o, x, g, out_tail, vec, bias)
    return found[:8], found[12:14], found[8:10], found[10:12]


class Everyone:
    def __init__(self, place, core, slots, send, recv, base):
        self.place, self.core = place, core
        self.slots, self.send, self.recv, self.base = slots, send, recv, base

    def start(self, stage, value):
        if stage == 3:
            spot, targets = self.core, [(1, device_at(self.place, 1 - self.core))]
        else:
            axis = AXES[stage]
            spot = self.place[axis]
            targets = [
                (over, device_at(moved(self.place, axis, over), self.core)) for over in (2, 1, 3)
            ]
        self.slots[stage, spot] = value
        for over, device in targets:
            index = self.base + stage * 3 + over - 1
            slot = self.slots.at[stage, spot]
            remote(slot, slot, self.send.at[index], self.recv.at[index], device).start()

    def finish(self, stage):
        count = 2 if stage == 3 else 4
        for over in range(1, count):
            index = self.base + stage * 3 + over - 1
            spot = 1 - self.core if stage == 3 else cycle(self.place[AXES[stage]], 4 - over)
            slot = self.slots.at[stage, spot]
            remote(
                slot, slot, self.send.at[index], self.recv.at[index], device_at(self.place, self.core)
            ).wait_recv()
        total = self.slots[stage, 0]
        for spot in range(1, count):
            total = total + self.slots[stage, spot]
        return total

    def drain(self):
        for stage in range(4):
            for over in range(1, 2 if stage == 3 else 4):
                index = self.base + stage * 3 + over - 1
                slot = self.slots.at[stage, 0]
                remote(
                    slot,
                    slot,
                    self.send.at[index],
                    self.recv.at[index],
                    device_at(self.place, self.core),
                ).wait_send()


def finish_kernel(
    dheads,
    weight,
    dy,
    dpre,
    active,
    h_main,
    h_tail,
    o_main,
    o_tail,
    h2_main,
    h2_tail,
    g_main,
    g_tail,
    tail_ref,
    x_ref,
    dmid_ref,
    vec_ref,
    gvec_ref,
    gup_ref,
    tokens_ref,
    total_ref,
    share_ref,
    second_ref,
    dheads_all,
    weight_all,
    flat,
    flat_all,
    dy_all,
    dpre_all,
    active_all,
    h_main_all,
    h_tail_all,
    o_main_all,
    o_tail_all,
    h2_main_all,
    h2_tail_all,
    g_main_all,
    g_tail_all,
    extra,
    dh,
    vectors,
    slots,
    *rest,
):
    buffers, (send, recv, local) = rest[:-3], rest[-3:]
    place, core = here()
    red = Reducer(ATTN_WIDTHS, place, core, buffers[:18], share_ref, send, recv)
    base = 3 * Reducer.SEMS
    late = Reducer(SECOND_WIDTHS, place, core, buffers[18:], second_ref, send, recv, base)
    base = 2 * base
    twin = Twin(place, core, send, recv, base)
    late_twin = Twin(place, core, send, recv, base + 12)
    every = Everyone(place, core, slots, send, recv, base + 24)
    heads_in = pltpu.make_async_copy(dheads, dheads_all, local.at[0])
    heads_in.start()
    weight_in = pltpu.make_async_copy(weight.at[:, pl.ds(0, QKV)], weight_all, local.at[1])
    weight_in.start()
    greet(line_peers(place, core) + [device_at(place, 1 - core)])
    for source, target, axis in (
        (h2_main, h2_main_all, 5),
        (h2_tail, h2_tail_all, 1),
        (dpre.at[:, pl.ds(FIRST, SECOND)], dpre_all, 0),
        (g_main, g_main_all, 5),
        (g_tail, g_tail_all, 1),
        (active.at[:, pl.ds(FIRST, SECOND)], active_all, 0),
    ):
        late_twin.give(source, target, axis)
    for source, target, axis in (
        (h_main, h_main_all, 5),
        (h_tail, h_tail_all, 1),
        (o_main, o_main_all, 5),
        (o_tail, o_tail_all, 1),
        (dy, dy_all, 0),
    ):
        twin.give(source, target, axis)
    heads_in.wait()
    for head in range(HEADS):
        flat[:, PACK * head : PACK * head + PACK] = dheads_all[head, :, :PACK]
    twin.give(flat, flat_all, 0)

    def make_all(reducer, maker):
        maker.pack_tail()
        for part in range(3):
            maker.make(part, 2)
        reducer.far_out()

        def others(index, carry):
            ahead = cycle(index, 3)
            for part in range(3):
                maker.make(part, ahead)
            return carry

        lax.fori_loop(0, 3, others, 0)

    late_twin.ready()
    make_all(
        late,
        Maker(
            late,
            [((h2_main_all, h2_tail_all), dpre_all), ((g_main_all, g_tail_all), active_all)],
            extra.at[pl.ds(0, SECOND_CHUNK // LANES)],
            SECOND_CHUNK,
        ),
    )
    twin.ready()
    make_all(
        red,
        Maker(
            red,
            [((h_main_all, h_tail_all), flat_all), ((o_main_all, o_tail_all), dy_all)],
            extra,
            ATTN_CHUNK,
        ),
    )
    for spot in range(4):
        late.pass_on(spot)
    dh[...] = jnp.zeros_like(dh)
    vectors[...] = jnp.zeros((VEC_ROWS, D), F32)
    vectors[2:6] = gvec_ref[:4]
    for row in range(4):
        span = slice(row * D, min((row + 1) * D, FF_PAD))
        vectors[VEC_UP + row : VEC_UP + row + 1, : span.stop - span.start] = gup_ref[:, span]
    weight_in.wait()

    for row in range(3):

        def columns(index, carry):
            span = lanes(row * D + index * 384, 384)
            value = flat[:, span]
            vectors[VEC_QKV + row : VEC_QKV + row + 1, lanes(index * 384, 384)] = column_total(
                value.astype(F32)
            )
            value_t = jnp.transpose(value)
            dh[:LEAD] += dot(weight_all[:, span], value_t)
            dh[LEAD:] += dot(tail_ref[:, span], value_t)
            return carry

        lax.fori_loop(0, 3, columns, 0)
    for spot in range(4):
        red.pass_on(spot)
    unit, rate = normal(x_ref[...].astype(F32))
    grad = jnp.transpose(dh[...])
    vectors[0:1] = column_total(grad * unit)
    vectors[1:2] = column_total(grad)
    every.start(0, vectors[...])
    total = dmid_ref[...] + normal_back(unit, rate, vec_ref[0:1], grad)
    tokens_ref[...] = total.astype(BF)
    for over in (2, 1, 3):
        late.gather_side(over, False)
    every.start(1, every.finish(0))
    late.gather_side(0, True)
    for over in (2, 1, 3):
        red.gather_side(over, False)
    every.start(2, every.finish(1))
    red.gather_side(0, True)
    late.line_up()
    every.start(3, every.finish(2))
    red.line_up()
    late.share()
    total_ref[...] = every.finish(3)
    red.share()
    late.close()
    red.close()
    twin.drain()
    late_twin.drain()
    every.drain()


def finish(dheads, weight, dy, dpre, active, turned, tail, x, dmid, vec, gvec, gup, tag):
    any_ = pl.BlockSpec(memory_space=pl.ANY)
    vmem = pl.BlockSpec(memory_space=pltpu.VMEM)
    sems = 6 * Reducer.SEMS + 24 + 12
    rows = [pltpu.VMEM((4, 2, 4, 2, 16, 512), BF), pltpu.VMEM((TAIL, 512), BF)]
    return pl.pallas_call(
        finish_kernel,
        out_shape=(
            jax.ShapeDtypeStruct((256, D), BF),
            jax.ShapeDtypeStruct((VEC_ROWS, D), F32),
            jax.ShapeDtypeStruct((16, ATTN_TOTAL), BF),
            jax.ShapeDtypeStruct((16, SECOND_TOTAL), BF),
        ),
        in_specs=[any_] * 13 + [vmem] * 6,
        out_specs=(vmem,) * 4,
        scratch_shapes=[
            pltpu.VMEM((HEADS, 256, WIDE), BF),
            pltpu.VMEM((LEAD, QKV), BF),
            pltpu.VMEM((256, QKV), BF),
            pltpu.VMEM((512, QKV), BF),
            pltpu.VMEM((512, D), BF),
            pltpu.VMEM((512, SECOND), BF),
            pltpu.VMEM((512, SECOND), BF),
        ]
        + rows * 4
        + [
            pltpu.VMEM((ATTN_CHUNK // LANES, LEAD, LANES), F32),
            pltpu.VMEM((D, 256), F32),
            pltpu.VMEM((VEC_ROWS, D), F32),
            pltpu.VMEM((4, 4, VEC_ROWS, D), F32),
        ]
        + Reducer.scratch(ATTN_WIDTHS)
        + Reducer.scratch(SECOND_WIDTHS)
        + [
            pltpu.SemaphoreType.DMA((sems,)),
            pltpu.SemaphoreType.DMA((sems,)),
            pltpu.SemaphoreType.DMA((2,)),
        ],
        compiler_params=mesh_params(tag),
        name="finish",
    )(dheads, weight, dy, dpre, active, *turned, tail, x, dmid, vec, gvec, gup)


def close_kernel(
    totals_ref,
    attn_ref,
    first_ref,
    second_ref,
    mixed_in,
    tokens_in,
    mixed_ref,
    tokens_ref,
    query_ref,
    key_ref,
    value_ref,
    out_ref,
    up_ref,
    down_ref,
    gain1_ref,
    bias1_ref,
    gain2_ref,
    bias2_ref,
    bias_out_ref,
    bias_down_ref,
    bias_query_ref,
    bias_value_ref,
    bias_up_ref,
    attn,
    first,
    second,
    vec,
):
    def unpack(share, full, main, chunk):
        full[0:16, :] = share[:, :main].astype(F32)
        rest = share[:, main : main + chunk].astype(F32)
        for row in range(2):
            for index in range(8):
                size = min(main - index * chunk, chunk)
                if size > 0:
                    start = index * chunk
                    spot = row * 8 + index
                    full[16 + row : 17 + row, start : start + size] = rest[
                        spot : spot + 1, :size
                    ]

    unpack(attn_ref, attn, ATTN_MAIN, ATTN_CHUNK)
    unpack(first_ref, first, 2 * FIRST, FIRST_CHUNK)
    unpack(second_ref, second, 2 * SECOND, SECOND_CHUNK)
    for head in range(HEADS):
        span = slice(head * HEAD_DIM, (head + 1) * HEAD_DIM)
        for index, ref in enumerate((key_ref, query_ref, value_ref)):
            start = head * PACK + index * HEAD_DIM
            ref[:, span] = attn[:18, start : start + HEAD_DIM]
    low = attn[:, QKV:ATTN_MAIN].astype(BF)

    def restore(index, carry):
        columns = lanes(index * LANES, LANES)
        matrix = unmix(index)
        out_ref[:, columns] = dot(low, matrix)[:18]
        mixed_ref[:, columns] = dot(mixed_in[...], matrix).astype(BF)
        tokens_ref[:, columns] = dot(tokens_in[...], matrix).astype(BF)
        vec[0:8, columns] = jnp.dot(
            totals_ref[0:8, :],
            matrix.astype(F32),
            precision=lax.Precision.HIGHEST,
            preferred_element_type=F32,
        )
        return carry

    lax.fori_loop(0, 9, restore, 0)
    lines = (gain1_ref, bias1_ref, gain2_ref, bias2_ref, bias_out_ref, bias_down_ref)
    for index, ref in enumerate(lines):
        ref[...] = vec[index : index + 1, :D].reshape(D)
    for row in range(3):
        vec[8:9, row * D : (row + 1) * D] = totals_ref[VEC_QKV + row : VEC_QKV + row + 1, :]
    for head in range(HEADS):
        span = slice(head * HEAD_DIM, (head + 1) * HEAD_DIM)
        for index, row in ((1, 9), (2, 10)):
            start = head * PACK + index * HEAD_DIM
            vec[row : row + 1, span] = vec[8:9, start : start + HEAD_DIM]
    bias_query_ref[...] = vec[9:10, :D].reshape(D)
    bias_value_ref[...] = vec[10:11, :D].reshape(D)
    for row in range(4):
        size = min(FF - row * D, D)
        vec[11:12, row * D : row * D + size] = totals_ref[
            VEC_UP + row : VEC_UP + row + 1, :size
        ]
    bias_up_ref[...] = vec[11:12, :FF].reshape(FF)
    up_ref[:, :FIRST] = first[:18, :FIRST]
    up_ref[:, FIRST:] = second[:18, : FF - FIRST]
    down_ref[:, :FIRST] = first[:18, FIRST : 2 * FIRST]
    down_ref[:, FIRST:] = second[:18, SECOND : SECOND + FF - FIRST]


def close_layer(totals, attn, first, second, mixed, tokens):
    line = jax.ShapeDtypeStruct((D,), F32)
    square = jax.ShapeDtypeStruct((18, D), F32)
    return pl.pallas_call(
        close_kernel,
        out_shape=(
            jax.ShapeDtypeStruct((256, D), BF),
            jax.ShapeDtypeStruct((256, D), BF),
            square,
            square,
            square,
            square,
            jax.ShapeDtypeStruct((18, FF), F32),
            jax.ShapeDtypeStruct((18, FF), F32),
            *([line] * 8),
            jax.ShapeDtypeStruct((FF,), F32),
        ),
        scratch_shapes=[
            pltpu.VMEM((24, ATTN_MAIN), F32),
            pltpu.VMEM((24, 2 * FIRST), F32),
            pltpu.VMEM((24, 2 * SECOND), F32),
            pltpu.VMEM((16, 4 * D), F32),
        ],
        compiler_params=params(),
        name="close_layer",
    )(totals, attn, first, second, mixed, tokens)


def pack_slab(weight, chunk, total):
    width = weight.shape[1]
    rest = jnp.pad(weight[16:], ((0, 0), (0, 8 * chunk - width))).reshape(16, chunk)
    return jnp.concatenate(
        [weight[:16], rest, jnp.zeros((16, total - width - chunk), weight.dtype)], axis=1
    )


def by_head(key, query, value):
    rows = key.shape[0]
    parts = [item.reshape(rows, HEADS, 1, HEAD_DIM) for item in (key, query, value)]
    return jnp.concatenate(parts, axis=2).reshape(rows, QKV)


def mixing():
    return onehot(iota((D, D), 0) == origin(iota((D, D), 1)))


def body(
    tokens,
    picture,
    cotangent,
    ln1_gain,
    ln1_bias,
    w_query,
    b_query,
    w_key,
    w_value,
    b_value,
    w_out,
    b_out,
    ln2_gain,
    ln2_bias,
    w_fc1,
    b_fc1,
    w_fc2,
    b_fc2,
):
    mix = mixing()
    out_cols = dot(w_out, mix).astype(BF)
    attn_slab = pack_slab(
        jnp.concatenate([by_head(w_key, w_query, w_value), out_cols], axis=1),
        ATTN_CHUNK,
        ATTN_TOTAL,
    )
    gap = ((0, 0), (0, FF_PAD - FF))
    up, down = jnp.pad(w_fc1, gap), jnp.pad(w_fc2.T, gap)
    first_slab = pack_slab(
        jnp.concatenate([up[:, :FIRST], down[:, :FIRST]], axis=1), FIRST_CHUNK, FIRST_TOTAL
    )
    second_slab = pack_slab(
        jnp.concatenate([up[:, FIRST:], down[:, FIRST:]], axis=1), SECOND_CHUNK, SECOND_TOTAL
    )
    lines = (ln1_gain, ln1_bias, ln2_gain, ln2_bias, b_out, b_fc2, b_query, b_value)
    heads, x, g, h_main, h_tail, attn_tail, out_tail, vec, attn = open_layer(
        attn_slab, tokens.reshape(256, D), cotangent.reshape(256, D), lines, 0
    )
    attn = attn.reshape(LEAD, ATTN_TOTAL)
    packed, keep, o, first = attend_gather(heads, first_slab, picture, 1)
    (mixed, go, dmid, dy, gvec2, gbias1, dpre, active), o_turned, h_turned, g_turned = middle(
        attn, first, second_slab, o, x, g, out_tail, vec, b_fc1, 2
    )
    first_share, dheads = attend_back_reduce(
        go, dpre, active, (*h_turned, *g_turned), packed, keep, picture, 3
    )
    gtokens, totals, attn_share, second_share = finish(
        dheads,
        attn,
        dy,
        dpre,
        active,
        (h_main, h_tail, *o_turned, *h_turned, *g_turned),
        attn_tail,
        x,
        dmid,
        vec,
        gvec2,
        gbias1,
        4,
    )
    (
        mixed,
        gtokens,
        grad_query,
        grad_key,
        grad_value,
        grad_out,
        grad_up,
        grad_down,
        grad_gain1,
        grad_bias1,
        grad_gain2,
        grad_bias2,
        grad_b_out,
        grad_b_fc2,
        grad_b_query,
        grad_b_value,
        grad_b_fc1,
    ) = close_layer(totals, attn_share, first_share, second_share, mixed, gtokens)
    return (
        mixed.reshape(2, 128, D),
        gtokens.reshape(2, 128, D),
        grad_gain1,
        grad_bias1,
        grad_query,
        grad_b_query,
        grad_key,
        grad_value,
        grad_b_value,
        grad_out,
        grad_b_out,
        grad_gain2,
        grad_bias2,
        grad_up,
        grad_b_fc1,
        grad_down.T,
        grad_b_fc2,
    )


def solution(mesh):
    placed = (
        P(None, ("fsdp", "rep"), None),
        P(),
        P(None, ("fsdp", "rep"), None),
        P(),
        P(),
        P("fsdp", None),
        P(),
        P("fsdp", None),
        P("fsdp", None),
        P(),
        P("fsdp", None),
        P(),
        P(),
        P(),
        P("fsdp", None),
        P(),
        P(None, "fsdp"),
        P(),
    )
    return jax.shard_map(
        body,
        mesh=mesh,
        in_specs=placed,
        out_specs=(
            P(None, ("fsdp", "rep"), None),
            P(None, ("fsdp", "rep"), None),
            P(),
            P(),
            P("fsdp", None),
            P(),
            P("fsdp", None),
            P("fsdp", None),
            P(),
            P("fsdp", None),
            P(),
            P(),
            P(),
            P("fsdp", None),
            P(),
            P(None, "fsdp"),
            P(),
        ),
        check_vma=False,
    )
```

```python
import functools

import jax
import jax.numpy as jnp
import numpy as np
from jax import lax
from jax.experimental import pallas as pl
from jax.experimental.pallas import tpu as pltpu
from jax.sharding import PartitionSpec as P

MESH = pl.DeviceIdType.MESH
BF = jnp.bfloat16
F32 = jnp.float32
LANES = 128
ORDERS = (("x", "y", "z"), ("y", "z", "x"), ("z", "x", "y"))
AXES = ("x", "y", "z")


def here():
    shard = lax.axis_index("fsdp")
    low = lax.axis_index("rep")
    place = {
        "x": lax.div(shard, 16),
        "y": lax.rem(lax.div(shard, 8), 2) * 2 + low,
        "z": lax.rem(lax.div(shard, 2), 4),
    }
    return place, lax.rem(shard, 2)


def moved(place, axis, steps):
    steps = steps % 4
    if steps == 0:
        return place
    other = dict(place)
    other[axis] = lax.rem(place[axis] + steps, 4)
    return other


def device_at(place, core):
    high = lax.div(place["y"], 2)
    return (((place["x"] * 2 + high) * 4 + place["z"]) * 2 + core, lax.rem(place["y"], 2))


def greet(peers):
    barrier = pltpu.get_barrier_semaphore()
    for peer in peers:
        pl.semaphore_signal(barrier, inc=1, device_id=peer, device_id_type=MESH)
    pl.semaphore_wait(barrier, len(peers))


def part_columns(part, half, widths):
    start = 2 * sum(widths[:part]) + half * widths[part]
    return pl.ds(pl.multiple_of(start, LANES), widths[part])


def piece_of(ref, part, widths, place, core):
    return ref.at[
        place["x"],
        lax.div(place["y"], 2),
        place["z"],
        core,
        :,
        part_columns(part, lax.rem(place["y"], 2), widths),
    ]


def block_of(ref, part, widths, place, core, axis, half=None):
    where = {"x": place["x"], "y": lax.div(place["y"], 2), "z": place["z"]}
    if axis == "y":
        where["y"] = pl.ds(0, 2) if half is None else pl.ds(half, 1)
        columns = pl.ds(2 * sum(widths[:part]), 2 * widths[part])
    else:
        where[axis] = pl.ds(0, 4) if half is None else pl.ds(2 * half, 2)
        columns = part_columns(part, lax.rem(place["y"], 2), widths)
    return ref.at[where["x"], where["y"], where["z"], core, :, columns]


def remote(source, target, send, recv, device):
    return pltpu.make_async_remote_copy(
        src_ref=source,
        dst_ref=target,
        send_sem=send,
        recv_sem=recv,
        device_id=device,
        device_id_type=MESH,
    )


def cycle(value, steps):
    return lax.rem(value + steps, 4)


def turned_by(place, axis, steps):
    other = dict(place)
    other[axis] = cycle(place[axis], steps)
    return other


class Gatherer:
    SEMS = 3 + 3 + 8 + 8 + 16
    KINDS = {"one": 0, "two": 3, "three": 6, "four": 14, "twin": 22}

    def __init__(self, widths, place, core, own, full, send, recv, base):
        self.widths, self.place, self.core = widths, place, core
        self.own, self.full, self.send, self.recv, self.base = own, full, send, recv, base
        self.twin = device_at(place, 1 - core)

    def slot(self, part, kind, index):
        return self.base + part * self.SEMS + self.KINDS[kind] + index

    def push(self, source, target, slot, device):
        remote(source, target, self.send.at[slot], self.recv.at[slot], device).start()

    def arrived(self, region, slot):
        remote(region, region, self.send.at[slot], self.recv.at[slot], self.twin).wait_recv()

    def sent(self, region, slot):
        remote(region, region, self.send.at[slot], self.recv.at[slot], self.twin).wait_send()

    def block(self, part, place, half=None, core=None):
        core = self.core if core is None else core
        return block_of(self.full, part, self.widths, place, core, ORDERS[part][0], half)

    def keep(self, part):
        low = lax.rem(self.place["y"], 2)
        source = self.own.at[:, part_columns(part, low, self.widths)]
        target = piece_of(self.full, part, self.widths, self.place, self.core)
        return source, target, pltpu.make_async_copy(
            source, target, self.recv.at[self.base + 3 * self.SEMS + part]
        )

    def start(self):
        for part, (one, two, three) in enumerate(ORDERS):
            source, target, copy = self.keep(part)
            copy.start()
            for steps in (1, 3, 2):
                device = device_at(turned_by(self.place, one, steps), self.core)
                self.push(source, target, self.slot(part, "one", steps - 1), device)

    def second(self):
        for part, (one, two, three) in enumerate(ORDERS):
            self.keep(part)[2].wait()
            for steps in (1, 3, 2):
                origin = turned_by(self.place, one, 4 - steps)
                region = piece_of(self.full, part, self.widths, origin, self.core)
                self.arrived(region, self.slot(part, "one", steps - 1))
            block = self.block(part, self.place)
            for steps in (1, 3, 2):
                device = device_at(turned_by(self.place, two, steps), self.core)
                self.push(block, block, self.slot(part, "two", steps - 1), device)
        self.spread(0)

    def spread(self, steps):
        for part, (one, two, three) in enumerate(ORDERS):
            block = self.block(part, turned_by(self.place, two, 4 - steps))
            for index, way in enumerate((1, 3)):
                device = device_at(turned_by(self.place, three, way), self.core)
                self.push(block, block, self.slot(part, "three", index * 4 + steps), device)
            self.push(block, block, self.slot(part, "twin", steps), self.twin)

    def third(self, steps):
        for part, (one, two, three) in enumerate(ORDERS):
            block = self.block(part, turned_by(self.place, two, 4 - steps))
            self.arrived(block, self.slot(part, "two", steps - 1))
        self.spread(steps)

    def fourth(self, steps):
        for part, (one, two, three) in enumerate(ORDERS):
            side = turned_by(self.place, two, 4 - steps)
            for index, way in enumerate((1, 3)):
                origin = turned_by(side, three, 4 - way)
                block = self.block(part, origin)
                self.arrived(block, self.slot(part, "three", index * 4 + steps))
                half = self.block(part, origin, index)
                device = device_at(turned_by(self.place, three, way), self.core)
                self.push(half, half, self.slot(part, "four", index * 4 + steps), device)
                self.push(block, block, self.slot(part, "twin", way * 4 + steps), self.twin)

    def fifth(self, steps):
        for part, (one, two, three) in enumerate(ORDERS):
            origin = turned_by(turned_by(self.place, two, 4 - steps), three, 2)
            for index in range(2):
                half = self.block(part, origin, index)
                self.arrived(half, self.slot(part, "four", index * 4 + steps))
            block = self.block(part, origin)
            self.push(block, block, self.slot(part, "twin", 8 + steps), self.twin)

    def close(self):
        for part, (one, two, three) in enumerate(ORDERS):
            for way in range(4):
                for steps in range(4):
                    origin = moved(moved(self.place, two, -steps), three, -way)
                    region = self.block(part, origin, core=1 - self.core)
                    self.arrived(region, self.slot(part, "twin", way * 4 + steps))

    def drain(self):
        for part in range(3):
            piece = piece_of(self.full, part, self.widths, self.place, self.core)
            block = self.block(part, self.place)
            half = self.block(part, self.place, 0)
            for kind, region, count in (
                ("one", piece, 3),
                ("two", block, 3),
                ("three", block, 8),
                ("four", half, 8),
                ("twin", block, 16),
            ):
                for index in range(count):
                    self.sent(region, self.slot(part, kind, index))


class Reducer:
    SEMS = 8 + 8 + 3 + 3 + 1
    KINDS = {"mid": 0, "far": 8, "side": 16, "line": 19, "done": 22}

    def __init__(self, widths, place, core, buffers, out, send, recv, base=0):
        self.widths, self.place, self.core, self.base = widths, place, core, base
        self.acc, self.mid, self.far, self.side, self.line, self.done = [
            buffers[3 * i : 3 * i + 3] for i in range(6)
        ]
        self.out, self.send, self.recv = out, send, recv
        self.me = device_at(place, core)

    @staticmethod
    def scratch(widths):
        found = []
        for lead, half in (((4, 4), 1), ((2, 4), 2), ((2, 4), 1), ((3,), 1)):
            for width, (one, two, three) in zip(widths, ORDERS):
                if one == "y":
                    found.append(pltpu.VMEM(lead + (2 // half, 16, 2 * width), BF))
                else:
                    found.append(pltpu.VMEM(lead + (4 // half, 16, width), BF))
        found += [pltpu.VMEM((3, 16, width), BF) for width in widths]
        found += [pltpu.VMEM((16, width), BF) for width in widths]
        return found

    def slot(self, part, kind, index):
        return self.base + part * self.SEMS + self.KINDS[kind] + index

    def push(self, source, target, slot, device):
        remote(source, target, self.send.at[slot], self.recv.at[slot], device).start()

    def arrived(self, region, slot):
        remote(region, region, self.send.at[slot], self.recv.at[slot], self.me).wait_recv()

    def sent(self, region, slot):
        remote(region, region, self.send.at[slot], self.recv.at[slot], self.me).wait_send()

    def add(self, target, *terms):
        for index in range(target.shape[0]):
            total = target[index].astype(F32)
            for term in terms:
                total = total + term[index].astype(F32)
            target[index] = total.astype(BF)

    def half_of(self, ref, half):
        size = ref.shape[0] // 2
        return ref.at[pl.ds(half * size, size)]

    def far_out(self):
        for spot in range(4):
            for part, (one, two, three) in enumerate(ORDERS):
                for half, way in ((0, 3), (1, 1)):
                    self.push(
                        self.half_of(self.acc[part].at[2, spot], half),
                        self.mid[part].at[half, spot],
                        self.slot(part, "mid", half * 4 + spot),
                        device_at(moved(self.place, three, way), self.core),
                    )

    def pass_on(self, spot):
        for part, (one, two, three) in enumerate(ORDERS):
            for half, way in ((0, 3), (1, 1)):
                self.arrived(
                    self.mid[part].at[half, spot], self.slot(part, "mid", half * 4 + spot)
                )
                self.add(
                    self.half_of(self.acc[part].at[way, spot], half), self.mid[part].at[half, spot]
                )
                self.push(
                    self.acc[part].at[way, spot],
                    self.far[part].at[half, spot],
                    self.slot(part, "far", half * 4 + spot),
                    device_at(moved(self.place, three, way), self.core),
                )

    def gather_side(self, over, last):
        for part, (one, two, three) in enumerate(ORDERS):
            spot = cycle(self.place[two], over)
            for half in range(2):
                self.arrived(
                    self.far[part].at[half, spot], self.slot(part, "far", half * 4 + spot)
                )
            self.add(
                self.acc[part].at[0, spot], self.far[part].at[0, spot], self.far[part].at[1, spot]
            )

            def give(part=part, two=two, spot=spot):
                other = dict(self.place)
                other[two] = spot
                self.push(
                    self.acc[part].at[0, spot],
                    self.side[part].at[over - 1],
                    self.slot(part, "side", over - 1),
                    device_at(other, self.core),
                )

            if last is False:
                give()
            elif last is not True:
                pl.when(jnp.logical_not(last))(give)

    def piece(self, part, axis, spot):
        own = self.acc[part].at[0, self.place[ORDERS[part][1]]]
        if axis == "y":
            start = pl.multiple_of(lax.rem(spot["y"], 2) * self.widths[part], LANES)
            return own.at[lax.div(spot["y"], 2), :, pl.ds(start, self.widths[part])]
        return own.at[spot[axis]]

    def line_up(self):
        for part, (one, two, three) in enumerate(ORDERS):
            for over in range(3):
                self.arrived(self.side[part].at[over], self.slot(part, "side", over))
            own = self.acc[part].at[0, self.place[two]]
            self.add(own, self.side[part].at[0], self.side[part].at[1], self.side[part].at[2])
            for over in (2, 1, 3):
                spot = moved(self.place, one, over)
                self.push(
                    self.piece(part, one, spot),
                    self.line[part].at[over - 1],
                    self.slot(part, "line", over - 1),
                    device_at(spot, self.core),
                )

    def share(self):
        low = lax.rem(self.place["y"], 2)
        partner = (lax.axis_index("fsdp"), 1 - low)
        for part, (one, two, three) in enumerate(ORDERS):
            for over in range(3):
                self.arrived(self.line[part].at[over], self.slot(part, "line", over))
            total = self.piece(part, one, self.place)[...].astype(F32)
            for over in range(3):
                total = total + self.line[part][over].astype(F32)
            self.done[part][...] = total.astype(BF)
            columns = part_columns(part, low, self.widths)
            self.push(
                self.done[part], self.out.at[:, columns], self.slot(part, "done", 0), partner
            )
            self.out[:, columns] = self.done[part][...]

    def close(self):
        low = lax.rem(self.place["y"], 2)
        for part, (one, two, three) in enumerate(ORDERS):
            self.arrived(
                self.out.at[:, part_columns(part, 1 - low, self.widths)],
                self.slot(part, "done", 0),
            )
            for half in range(2):
                for spot in range(4):
                    index = half * 4 + spot
                    self.sent(self.mid[part].at[half, spot], self.slot(part, "mid", index))
                    self.sent(self.far[part].at[half, spot], self.slot(part, "far", index))
            for over in range(3):
                self.sent(self.side[part].at[over], self.slot(part, "side", over))
                self.sent(self.line[part].at[over], self.slot(part, "line", over))
            self.sent(self.done[part], self.slot(part, "done", 0))


class Maker:
    def __init__(self, reducer, sources, extra, chunk):
        self.red, self.sources, self.extra, self.chunk = reducer, sources, extra, chunk
        self.main = sum(item[1].shape[1] for item in sources)

    def pack_tail(self):
        start = 0
        pieces = []
        for turned, right in self.sources:
            pieces.append((start, start + right.shape[1], turned, right))
            start += right.shape[1]
        for index in range(8):
            low, high = index * self.chunk, (index + 1) * self.chunk
            for first, last, turned, right in pieces:
                a, b = max(low, first), min(high, last)
                if a < b:
                    value = dot(turned[1][...], right[:, a - first : b - first])
                    self.scatter(index, a - low, value)
            if high > self.main:
                a = max(low, self.main)
                self.scatter(index, a - low, jnp.zeros((TAIL, high - a), F32))

    def scatter(self, index, start, value):
        for tile in range(value.shape[1] // LANES):
            self.extra[start // LANES + tile, pl.ds(index, TAIL, stride=8), :] = value[
                :, tile * LANES : (tile + 1) * LANES
            ]

    def rows(self, ref):
        core = self.red.core
        if len(ref.shape) == 2:
            groups = [
                ref[pl.ds(pl.multiple_of((2 * index + core) * 16, 16), 16)] for index in range(32)
            ]
            return jnp.concatenate(groups, axis=0)
        return ref[:, :, :, core].reshape(512, ref.shape[-1])

    def columns(self, part, half):
        width = self.red.widths[part]
        low = 2 * sum(self.red.widths[:part]) + half * width
        high = low + width
        first = 0
        found = []
        for turned, right in self.sources:
            last = first + right.shape[1]
            a, b = max(low, first), min(high, last)
            if a < b:
                left = self.rows(turned[0])
                found.append(dot(left, right[:, a - first : b - first]).astype(BF))
            first = last
        a, b = max(low, first), min(high, first + self.chunk)
        if a < b:
            for tile in range((a - first) // LANES, (b - first) // LANES):
                found.append(self.rows(self.extra.at[tile]).astype(BF))
        a = max(low, first + self.chunk)
        if a < high:
            found.append(jnp.zeros((512, high - a), BF))
        return found[0] if len(found) == 1 else jnp.concatenate(found, axis=1)

    def make(self, part):
        red, width = self.red, self.red.widths[part]
        acc = red.acc[part]
        three = ORDERS[part][2]
        own = red.place[three]

        def ahead(spot):
            return cycle(spot + 4 - own, 0)

        for half in range(2):
            value = self.columns(part, half).reshape(4, 2, 4, 16, width)
            if three == "z":
                for spot in range(4):
                    for high in range(2):
                        acc[ahead(spot), 2 * high + half] = value[:, high, spot]
            elif three == "x":
                for spot in range(4):
                    for z in range(4):
                        acc[ahead(spot), z, :, :, half * width : (half + 1) * width] = value[
                            spot, :, z
                        ]
            else:
                for high in range(2):
                    for x in range(4):
                        acc[ahead(2 * high + half), x] = value[x, high]

    def run(self):
        self.pack_tail()
        for part in range(3):
            self.make(part)
        self.red.far_out()


SWAP_ORDER = (9, 11, 5, 13, 7, 15, 1, 3, 8, 10, 4, 12, 6, 14, 2)


class Swapper:
    def __init__(self, place, core, own, full, send, recv, base):
        self.place, self.core = place, core
        self.own, self.full, self.send, self.recv, self.base = own, full, send, recv, base
        self.low = lax.rem(place["y"], 2)
        self.mine = (place["z"] * 2 + core) * 2 + self.low
        self.group = lax.div(lax.axis_index("fsdp"), 8) * 8

    def member(self, k, sign=1):
        z = lax.rem(self.place["z"] + (4 + sign * (k // 4)), 4)
        core = lax.rem(self.core + (k // 2) % 2, 2)
        low = lax.rem(self.low + k % 2, 2)
        return (z * 2 + core) * 2 + low

    def device(self, index):
        return (self.group + lax.div(index, 2), lax.rem(index, 2))

    def peers(self):
        return [self.device(self.member(k)) for k in range(1, 16)]

    def view(self, ref, index, micro):
        if micro is None:
            return ref.at[index]
        return ref.at[index, pl.ds(micro * 128, 128)]

    def start(self, micro=None):
        for k in SWAP_ORDER:
            target = self.member(k)
            remote(
                self.view(self.own, target, micro),
                self.view(self.full, self.mine, micro),
                self.send.at[self.base + k],
                self.recv.at[self.base + k],
                self.device(target),
            ).start()
        pltpu.make_async_copy(
            self.view(self.own, self.mine, micro),
            self.view(self.full, self.mine, micro),
            self.send.at[self.base],
        ).start()

    def finish(self, micro=None):
        pltpu.make_async_copy(
            self.view(self.own, self.mine, micro),
            self.view(self.full, self.mine, micro),
            self.send.at[self.base],
        ).wait()
        for k in range(1, 16):
            region = self.view(self.full, self.member(k, -1), micro)
            remote(
                region,
                region,
                self.send.at[self.base + k],
                self.recv.at[self.base + k],
                self.device(self.mine),
            ).wait_recv()

    def drain(self, micro=None):
        for k in range(1, 16):
            region = self.view(self.own, self.member(k), micro)
            remote(
                region,
                region,
                self.send.at[self.base + k],
                self.recv.at[self.base + k],
                self.device(self.mine),
            ).wait_send()


def line_peers(place, core):
    peers = []
    for axis in AXES:
        for steps in (1, 2, 3):
            peers.append(device_at(moved(place, axis, steps), core))
    return peers


D = 1152
HEADS = 16
HEAD_DIM = 72
FF = 4304
ROW = 2048
EPS = 1e-06
NEG = -1e30
SCALE = HEAD_DIM**-0.5
LEAD = 1024
TAIL = 128
PACK = 3 * HEAD_DIM
WIDE = 256
VALUE_LANE = 16
FF_PAD = 4352
QKV = HEADS * PACK
ATTN_MAIN = QKV + D
ATTN_CHUNK = 640
ATTN_TOTAL = 5376
MLP_MAIN = 2 * FF_PAD
MLP_CHUNK = 1152
MLP_TOTAL = 9984
ATTN_WIDTHS = (896, 896, 896)
MLP_WIDTHS = (1664, 1664, 1664)
FIRST = 3072
FIRST_CHUNK = 768
FIRST_TOTAL = 6912
FIRST_WIDTHS = (1152, 1152, 1152)
FIRST_STEP = 768
SECOND = FF_PAD - FIRST
SECOND_CHUNK = 384
SECOND_TOTAL = 3072
SECOND_WIDTHS = (512, 512, 512)
SECOND_STEP = 640
LOG2E = 1.4426950408889634
QUERIES = 512
KEYS = 512
BLOCKS = ROW // QUERIES
TANH_A = 0.7978845608028654
TANH_B = 0.044715


def dot(left, right):
    return jnp.dot(left, right, preferred_element_type=F32)


def dot_nt(left, right):
    return lax.dot_general(left, right, (((1,), (1,)), ((), ())), preferred_element_type=F32)


def dot_tn(left, right):
    return lax.dot_general(left, right, (((0,), (0,)), ((), ())), preferred_element_type=F32)


def origin(index):
    lead = (index >> 4) * 18 + (index & 15)
    rest = index - LEAD
    tail = (rest >> 1) * 18 + 16 + (rest & 1)
    return jnp.where(index < LEAD, lead, tail)


def iota(shape, axis):
    return lax.broadcasted_iota(jnp.int32, shape, axis)


def onehot(mask):
    return mask.astype(F32).astype(BF)


def normal(values):
    center = values - jnp.mean(values, axis=-1, keepdims=True)
    rate = lax.rsqrt(jnp.mean(center * center, axis=-1, keepdims=True) + EPS)
    return center * rate, rate


def normal_back(unit, rate, gain, grad):
    inner = grad * gain
    first = jnp.mean(inner, axis=-1, keepdims=True)
    second = jnp.mean(inner * unit, axis=-1, keepdims=True)
    return rate * (inner - first - unit * second)


def exact_parts(values):
    high = values.astype(BF)
    rest = values - high.astype(F32)
    middle_part = rest.astype(BF)
    low = (rest - middle_part.astype(F32)).astype(BF)
    return jnp.concatenate([high, middle_part, low], axis=0)


def column_total(values):
    return jnp.sum(values, axis=0, keepdims=True)


def lanes(start, size):
    return pl.ds(pl.multiple_of(start, LANES), size)


def params(limit=60):
    return pltpu.CompilerParams(vmem_limit_bytes=limit << 20)


PERMUTED = np.concatenate(
    [np.arange(64)[:, None] * 18 + np.arange(16), np.arange(64)[:, None] * 18 + [16, 17]], axis=1
)
PERMUTED = np.concatenate([PERMUTED[:, :16].reshape(-1), PERMUTED[:, 16:].reshape(-1)])


def mix_matrix():
    matrix = np.zeros((D, D), np.float32)
    matrix[PERMUTED, np.arange(D)] = 1.0
    return matrix


def place_matrix():
    matrix = np.zeros((HEADS, LANES, D), np.float32)
    mixed = mix_matrix().reshape(HEADS, HEAD_DIM, D)
    matrix[:, VALUE_LANE : VALUE_LANE + HEAD_DIM] = mixed
    return matrix.reshape(HEADS * LANES, D)


def mesh_params(tag, limit=62):
    return pltpu.CompilerParams(
        collective_id=tag, has_side_effects=True, vmem_limit_bytes=limit << 20
    )


class Twin:
    def __init__(self, place, core, send, recv, base):
        self.core, self.device = core, device_at(place, 1 - core)
        self.send, self.recv, self.base = send, recv, base
        self.items = []

    def half(self, ref, axis, core):
        size = ref.shape[axis] // 2
        if axis == 0:
            return ref.at[pl.ds(pl.multiple_of(core * size, size), size)]
        lead = (slice(None),) * (len(ref.shape) - 1)
        return ref.at[lead + (pl.ds(pl.multiple_of(core * size, LANES), size),)]

    def give(self, source, target, axis):
        index = self.base + 2 * len(self.items)
        place = self.half(target, axis, self.core)
        pltpu.make_async_copy(source, place, self.recv.at[index + 1]).start()
        remote(source, place, self.send.at[index], self.recv.at[index], self.device).start()
        self.items.append((source, target, axis, index))

    def ready(self):
        for source, target, axis, index in self.items:
            place = self.half(target, axis, self.core)
            pltpu.make_async_copy(source, place, self.recv.at[index + 1]).wait()
            other = self.half(target, axis, 1 - self.core)
            remote(
                other, other, self.send.at[index], self.recv.at[index], self.device
            ).wait_recv()

    def drain(self):
        for source, target, axis, index in self.items:
            place = self.half(target, axis, self.core)
            remote(
                place, place, self.send.at[index], self.recv.at[index], self.device
            ).wait_send()


def back_kernel(
    go,
    dpre,
    active,
    h_main,
    h_tail,
    g_main,
    g_tail,
    picture,
    packed_ref,
    keep_ref,
    share_ref,
    dheads,
    go_all,
    grads,
    dpre_all,
    active_all,
    h_main_all,
    h_tail_all,
    g_main_all,
    g_tail_all,
    extra,
    keys,
    queries,
    ids,
    dkeys,
    dvalues,
    found,
    row_ref,
    *rest,
):
    buffers, (send, recv, local) = rest[:-3], rest[-3:]
    place, core = here()
    red = Reducer(FIRST_WIDTHS, place, core, buffers, share_ref, send, recv)
    base = 3 * Reducer.SEMS
    swap_in = Swapper(place, core, go, go_all, send, recv, base)
    outs = [Swapper(place, core, grads, dheads, send, recv, base + 16 + 16 * m) for m in range(2)]
    twin = Twin(place, core, send, recv, base + 48)
    greet(line_peers(place, core) + swap_only(swap_in))
    swap_in.start()
    for source, target, axis in (
        (h_main, h_main_all, 5),
        (h_tail, h_tail_all, 1),
        (g_main, g_main_all, 5),
        (g_tail, g_tail_all, 1),
        (dpre.at[:, pl.ds(0, FIRST)], dpre_all, 0),
        (active.at[:, pl.ds(0, FIRST)], active_all, 0),
    ):
        twin.give(source, target, axis)
    maker = Maker(
        red,
        [((h_main_all, h_tail_all), dpre_all), ((g_main_all, g_tail_all), active_all)],
        extra,
        FIRST_CHUNK,
    )
    ids_in = fetch_ids(picture, found, local.at[0])
    ids_in.start()
    ids_in.wait()
    for micro in range(2):
        row_ref[micro] = found[micro : micro + 1].astype(F32)
    twin.ready()
    maker.run()
    swap_in.finish()

    def block(step, carry):
        row = lax.div(step, BLOCKS)
        index = lax.rem(step, BLOCKS)
        tokens = pl.ds(pl.multiple_of(row * 128, 128), 128)

        @pl.when(index == 0)
        def _():
            packed = packed_ref[:, tokens, :].reshape(ROW, WIDE)
            split_packed(packed, keys, queries)
            for part in range(ROW // LANES):
                span = slice(part * LANES, (part + 1) * LANES)
                ids[span, :] = column_ids(row_ref[row, :, span])
            dkeys[...] = jnp.zeros_like(dkeys)
            dvalues[...] = jnp.zeros_like(dvalues)

        rows = pl.ds(pl.multiple_of(index * QUERIES, QUERIES), QUERIES)
        groups = pl.ds(index * (QUERIES // 128), QUERIES // 128)

        def scan(count):
            start = jnp.where(index < 2, 0, BLOCKS - count)
            query = queries[rows, :]
            back = go_all[groups, tokens, :].reshape(QUERIES, LANES)
            mine = row_ref[row, :, lanes(index * QUERIES, QUERIES)]
            kept = keep_ref[row, rows, :]
            inner = jnp.sum(back.astype(F32) * kept, axis=1, keepdims=True)
            lane = iota((QUERIES, LANES), 1)
            stats = jnp.transpose(jnp.where(lane == 0, kept, inner))
            logsum = stats[0:1]
            inner = stats[1:2]
            total = jnp.zeros((QUERIES, LANES), F32)
            for part in range(count):
                span = pl.ds(pl.multiple_of((start + part) * KEYS, KEYS), KEYS)
                blocks = pl.ds((start + part) * (KEYS // 128), KEYS // 128)
                value = packed_ref[blocks, tokens, LANES:].reshape(KEYS, LANES)
                allowed = jnp.concatenate([ids[span, :]] * (QUERIES // LANES), axis=1)
                score = dot_nt(keys[span, :], query) * (SCALE * LOG2E) - logsum
                prob = jnp.exp2(jnp.where(allowed == mine, score, NEG))
                grad = (prob * (dot_nt(value, back) - inner)).astype(BF)
                dvalues[span, :] += dot(prob.astype(BF), back)
                dkeys[span, :] += dot(grad, query)
                total = total + dot_tn(grad, keys[span, :])
            total = total * SCALE
            moved_q = jnp.concatenate(
                [
                    jnp.zeros((QUERIES, HEAD_DIM), F32),
                    total[:, :HEAD_DIM],
                    jnp.zeros((QUERIES, WIDE - 2 * HEAD_DIM), F32),
                ],
                axis=1,
            )
            grads[groups, tokens, :] = moved_q.astype(BF).reshape(QUERIES // 128, 128, WIDE)

        edge = (index == 0) | (index == BLOCKS - 1)
        pl.when(edge)(functools.partial(scan, 3))
        pl.when(jnp.logical_not(edge))(functools.partial(scan, 4))

        @pl.when(index == BLOCKS - 1)
        def _():
            wide = jnp.concatenate([dkeys[...] * SCALE, dvalues[...]], axis=1)
            lane = iota((ROW, WIDE), 1)
            old = grads[:, tokens, :].reshape(ROW, WIDE)
            inside = (lane >= HEAD_DIM) & (lane < 2 * HEAD_DIM)
            grads[:, tokens, :] = jnp.where(inside, old, wide.astype(BF)).reshape(16, 128, WIDE)
            for micro in range(2):
                pl.when(row == micro)(functools.partial(outs[micro].start, micro))

        @pl.when(step < 4)
        def _():
            red.pass_on(step)

        @pl.when(step >= 4)
        def _():
            red.gather_side(lax.rem(step - 4 + 1, 4), step == 7)

        return carry

    lax.fori_loop(0, 2 * BLOCKS, block, 0)
    red.line_up()
    red.share()
    red.close()
    for micro in range(2):
        outs[micro].finish(micro)
    swap_in.drain()
    for micro in range(2):
        outs[micro].drain(micro)
    twin.drain()


def attend_back_reduce(go, dpre, active, turned, packed, keep, picture, tag):
    any_ = pl.BlockSpec(memory_space=pl.ANY)
    vmem = pl.BlockSpec(memory_space=pltpu.VMEM)
    sems = 3 * Reducer.SEMS + 48 + 12
    return pl.pallas_call(
        back_kernel,
        out_shape=(
            jax.ShapeDtypeStruct((16, FIRST_TOTAL), BF),
            jax.ShapeDtypeStruct((16, 256, WIDE), BF),
        ),
        in_specs=[any_] * 8 + [vmem] * 2,
        out_specs=(vmem, any_),
        scratch_shapes=[
            pltpu.VMEM((16, 256, LANES), BF),
            pltpu.VMEM((16, 256, WIDE), BF),
            pltpu.VMEM((512, FIRST), BF),
            pltpu.VMEM((512, FIRST), BF),
            pltpu.VMEM((4, 2, 4, 2, 16, 512), BF),
            pltpu.VMEM((TAIL, 512), BF),
            pltpu.VMEM((4, 2, 4, 2, 16, 512), BF),
            pltpu.VMEM((TAIL, 512), BF),
            pltpu.VMEM((FIRST_CHUNK // LANES, LEAD, LANES), F32),
            pltpu.VMEM((ROW, LANES), BF),
            pltpu.VMEM((ROW, LANES), BF),
            pltpu.VMEM((ROW, LANES), F32),
            pltpu.VMEM((ROW, LANES), F32),
            pltpu.VMEM((ROW, LANES), F32),
            pltpu.VMEM((2, ROW), jnp.int32),
            pltpu.VMEM((2, 1, ROW), F32),
        ]
        + Reducer.scratch(FIRST_WIDTHS)
        + [
            pltpu.SemaphoreType.DMA((sems,)),
            pltpu.SemaphoreType.DMA((sems,)),
            pltpu.SemaphoreType.DMA((1,)),
        ],
        compiler_params=mesh_params(tag),
        name="attend_back_reduce",
    )(go, dpre, active, *turned, picture, packed, keep)


VEC_ROWS = 16
VEC_QKV = 6
VEC_UP = 9


def spread_tail(source, chunk, wide, tail):
    for tile in range(chunk // LANES):
        wide[tile] = source(tile).astype(F32)
        for index in range(8):
            start = index * chunk + tile * LANES
            picked = wide[tile, pl.ds(index, TAIL, stride=8), :]
            tail[:, start : start + LANES] = picked.astype(BF)


def column_ids(row_ids):
    size = row_ids.shape[1]
    return jnp.transpose(jnp.broadcast_to(row_ids, (LANES, size)))


def fetch_ids(picture, found, sem):
    start = pl.multiple_of(lax.div(lax.axis_index("fsdp"), 8) * ROW, ROW)
    return pltpu.make_async_copy(picture.at[:, pl.ds(start, ROW)], found, sem)


def split_packed(packed, keys, queries):
    lane = iota((ROW, LANES), 1)
    zero = jnp.zeros((ROW, LANES), BF)
    keys[...] = jnp.where(lane < HEAD_DIM, packed[:, :LANES], zero)
    queries[...] = jnp.concatenate(
        [packed[:, HEAD_DIM : 2 * HEAD_DIM], jnp.zeros((ROW, LANES - HEAD_DIM), BF)], axis=1
    )


def swap_only(swapper):
    return [swapper.device(swapper.member(k)) for k in range(1, 16) if k not in (1, 4, 8, 12)]


def front_kernel(
    slab,
    first_slab,
    picture,
    tokens_ref,
    cotangent_ref,
    *refs,
):
    lines, rest = refs[:8], refs[8:]
    run_front(slab, first_slab, picture, tokens_ref, cotangent_ref, lines, *rest)


def run_front(
    slab,
    first_slab,
    picture,
    tokens_ref,
    cotangent_ref,
    lines,
    x_ref,
    g_ref,
    h_main_ref,
    h_tail_ref,
    tail_ref,
    out_tail_ref,
    mixed_vec_ref,
    packed_ref,
    keep_ref,
    o_all,
    weight_out,
    first_out,
    full,
    low,
    flat,
    wide,
    tail,
    vec_ref,
    vec_parts,
    heads,
    o_own,
    keys,
    queries,
    values,
    scores,
    found,
    row_ref,
    send,
    recv,
    local,
):
    place, core = here()
    red = Gatherer(ATTN_WIDTHS, place, core, slab, full, send, recv, 0)
    base = 3 * Gatherer.SEMS + 3
    first = Gatherer(FIRST_WIDTHS, place, core, first_slab, first_out, send, recv, base)
    base = 2 * base
    ins = [Swapper(place, core, heads, packed_ref, send, recv, base + 16 * m) for m in range(2)]
    base = base + 32
    outs = [Swapper(place, core, o_own, o_all, send, recv, base + 16 * m) for m in range(2)]
    greet(line_peers(place, core) + swap_only(ins[0]))
    red.start()
    ids_in = fetch_ids(picture, found, local.at[0])
    ids_in.start()
    for index, line in enumerate(lines):
        vec_ref[index : index + 1, :] = line[...].reshape(1, D)
    vec_parts[...] = exact_parts(vec_ref[...])

    def mix(index, carry):
        columns = lanes(index * LANES, LANES)
        column = onehot(iota((D, LANES), 0) == origin(index * LANES + iota((D, LANES), 1)))
        x_ref[:, columns] = dot(tokens_ref[...], column).astype(BF)
        g_ref[:, columns] = dot(cotangent_ref[...], column).astype(BF)
        parts = dot(vec_parts[...], column)
        mixed_vec_ref[:, columns] = parts[0:8] + parts[8:16] + parts[16:24]
        return carry

    lax.fori_loop(0, 3, mix, 0)
    red.second()
    lax.fori_loop(3, 9, mix, 0)
    unit, _ = normal(x_ref[...].astype(F32))
    low[...] = (unit * mixed_vec_ref[0:1] + mixed_vec_ref[1:2]).astype(BF)
    for steps in (1, 2, 3):
        red.third(steps)
    turned = jnp.transpose(low[...])
    h_main_ref[...] = turned[:LEAD].reshape(4, 2, 4, 2, 16, 256)
    h_tail_ref[...] = turned[LEAD:]
    ids_in.wait()
    for micro in range(2):
        row_ref[micro] = found[micro : micro + 1].astype(F32)
    for steps in range(4):
        red.fourth(steps)
    first.start()
    for steps in range(4):
        red.fifth(steps)
    first.second()
    red.close()
    leave = pltpu.make_async_copy(full, weight_out, local.at[1])
    leave.start()

    def packed_tile(tile):
        start = ATTN_MAIN + tile * LANES
        return full[:, :, :, :, :, start : start + LANES].reshape(LEAD, LANES)

    spread_tail(packed_tile, ATTN_CHUNK, wide, tail)
    tail_ref[...] = tail[:, :QKV]
    out_tail_ref[...] = tail[:, QKV:ATTN_MAIN]
    first.third(1)
    first.third(2)

    def columns(index, carry):
        span = lanes(index * 384, 384)
        weight = full[:, :, :, :, :, span].reshape(LEAD, 384)
        flat[:, span] = dot(low[:, :LEAD], weight) + dot(low[:, LEAD:], tail[:, span])
        return carry

    lax.fori_loop(0, QKV // 384, columns, 0)
    first.third(3)
    for head in range(HEADS):
        span = slice(head * HEAD_DIM, (head + 1) * HEAD_DIM)
        bias = jnp.concatenate(
            [jnp.zeros((1, HEAD_DIM), F32), vec_ref[6:7, span], vec_ref[7:8, span]], axis=1
        )
        block = flat[:, PACK * head : PACK * head + PACK] + bias
        heads[head] = jnp.concatenate([block, jnp.zeros((256, WIDE - PACK), F32)], axis=1).astype(
            BF
        )
    ins[0].start(0)
    first.fourth(0)
    first.fourth(1)
    ins[1].start(1)
    ins[0].finish(0)

    def block(step, carry):
        row = lax.div(step, 8)
        index = lax.rem(step, 8)
        rows_of = pl.ds(pl.multiple_of(row * 128, 128), 128)

        @pl.when(step == 8)
        def _():
            ins[1].finish(1)

        @pl.when(index == 0)
        def _():
            packed = packed_ref[:, rows_of, :].reshape(ROW, WIDE)
            split_packed(packed, keys, queries)
            lane = iota((ROW, LANES), 1)
            values[...] = jnp.where(
                lane == LANES - 1, jnp.ones((ROW, LANES), BF), packed[:, LANES:]
            )

        rows = pl.ds(pl.multiple_of(index * 256, 256), 256)

        def scan(count):
            start = jnp.where(index < 4, 0, ROW - 256 * count)
            query = queries[rows, :]
            mine = column_ids(row_ref[row, :, lanes(index * 256, 256)])
            mine = jnp.concatenate([mine, mine], axis=1)
            top = jnp.full((256, LANES), NEG, F32)
            for part in range(count):
                span = lanes(start + part * 256, 256)
                score = dot_nt(query, keys[span, :])
                score = jnp.where(mine == row_ref[row, :, span], score, NEG)
                scores[:, part * 256 : part * 256 + 256] = score
                top = jnp.maximum(top, jnp.maximum(score[:, :LANES], score[:, LANES:]))
            top = jnp.max(top, axis=1, keepdims=True)
            total = jnp.zeros((256, LANES), F32)
            for part in range(count):
                span = lanes(start + part * 256, 256)
                expo = jnp.exp2(
                    (scores[:, part * 256 : part * 256 + 256] - top) * (SCALE * LOG2E)
                )
                total = total + dot(expo.astype(BF), values[span, :])
            mass = total[:, LANES - 1 :]
            total = total / mass
            o_own[pl.ds(index * 2, 2), rows_of, :] = total.astype(BF).reshape(2, 128, LANES)
            lane = iota((256, LANES), 1)
            logsum = top * (SCALE * LOG2E) + jnp.log2(mass)
            keep_ref[row, rows, :] = jnp.where(lane == 0, logsum, total)

        for count in (5, 6, 7, 8):
            pl.when((index == count - 5) | (index == 12 - count))(functools.partial(scan, count))

        @pl.when(step == 2)
        def _():
            first.fourth(2)

        @pl.when(step == 4)
        def _():
            first.fourth(3)

        @pl.when((step >= 6) & (lax.rem(step, 2) == 0) & (step < 14))
        def _():
            first.fifth(lax.div(step - 6, 2))

        for micro in range(2):
            pl.when(step == 8 * micro + 7)(functools.partial(outs[micro].start, micro))
        return carry

    lax.fori_loop(0, 16, block, 0)
    first.close()
    leave.wait()
    red.drain()
    first.drain()
    for micro in range(2):
        ins[micro].drain(micro)
        outs[micro].finish(micro)
    for micro in range(2):
        outs[micro].drain(micro)


def front(slab, first_slab, tokens, cotangent, lines, picture, tag):
    any_ = pl.BlockSpec(memory_space=pl.ANY)
    vmem = pl.BlockSpec(memory_space=pltpu.VMEM)
    sems = 2 * (3 * Gatherer.SEMS + 3) + 64
    full = (4, 2, 4, 2, 16, ATTN_TOTAL)
    return pl.pallas_call(
        front_kernel,
        out_shape=(
            jax.ShapeDtypeStruct((256, D), BF),
            jax.ShapeDtypeStruct((256, D), BF),
            jax.ShapeDtypeStruct((4, 2, 4, 2, 16, 256), BF),
            jax.ShapeDtypeStruct((TAIL, 256), BF),
            jax.ShapeDtypeStruct((TAIL, QKV), BF),
            jax.ShapeDtypeStruct((TAIL, D), BF),
            jax.ShapeDtypeStruct((8, D), F32),
            jax.ShapeDtypeStruct((16, 256, WIDE), BF),
            jax.ShapeDtypeStruct((2, ROW, LANES), F32),
            jax.ShapeDtypeStruct((16, 256, LANES), BF),
            jax.ShapeDtypeStruct(full, BF),
            jax.ShapeDtypeStruct((4, 2, 4, 2, 16, FIRST_TOTAL), BF),
        ),
        in_specs=[any_] * 3 + [vmem] * 10,
        out_specs=(vmem,) * 9 + (any_,) * 3,
        scratch_shapes=[
            pltpu.VMEM(full, BF),
            pltpu.VMEM((256, D), BF),
            pltpu.VMEM((256, QKV), F32),
            pltpu.VMEM((ATTN_CHUNK // LANES, LEAD, LANES), F32),
            pltpu.VMEM((TAIL, 8 * ATTN_CHUNK), BF),
            pltpu.VMEM((8, D), F32),
            pltpu.VMEM((24, D), BF),
            pltpu.VMEM((16, 256, WIDE), BF),
            pltpu.VMEM((16, 256, LANES), BF),
            pltpu.VMEM((ROW, LANES), BF),
            pltpu.VMEM((ROW, LANES), BF),
            pltpu.VMEM((ROW, LANES), BF),
            pltpu.VMEM((256, ROW), F32),
            pltpu.VMEM((2, ROW), jnp.int32),
            pltpu.VMEM((2, 1, ROW), F32),
            pltpu.SemaphoreType.DMA((sems,)),
            pltpu.SemaphoreType.DMA((sems,)),
            pltpu.SemaphoreType.DMA((2,)),
        ],
        compiler_params=mesh_params(tag),
        name="front",
    )(slab, first_slab, picture, tokens, cotangent, *lines)


def middle_kernel(
    attn,
    first,
    slab,
    o_ref,
    x_ref,
    g_ref,
    out_b_ref,
    vec_ref,
    bias_ref,
    place_ref,
    pick_ref,
    mixed_ref,
    do_ref,
    dmid_ref,
    dy_ref,
    gvec_ref,
    gbias_ref,
    dpre_ref,
    active_ref,
    h_main_ref,
    h_tail_ref,
    g_main_ref,
    g_tail_ref,
    o_main_ref,
    o_tail_ref,
    out_a,
    weights,
    full,
    o_perm,
    mid,
    h2,
    result,
    dh2,
    wide,
    tail,
    bias,
    send,
    recv,
    local,
):
    place, core = here()
    red = Gatherer(SECOND_WIDTHS, place, core, slab, full, send, recv, 0)
    out_in = pltpu.make_async_copy(attn.at[:, pl.ds(QKV, D)], out_a, local.at[0])
    out_in.start()
    first_in = pltpu.make_async_copy(first, weights, local.at[1])
    first_in.start()
    greet(line_peers(place, core) + [device_at(place, 1 - core)])
    red.start()
    bias[...] = jnp.zeros_like(bias)
    bias[:, :FF] = bias_ref[...].reshape(1, FF)
    for group in range(4):
        block = jnp.concatenate([o_ref[4 * group + head] for head in range(4)], axis=1)
        value = dot(block, place_ref[512 * group : 512 * group + 512, :])
        mid[...] = value if group == 0 else mid[...] + value
    o_perm[...] = mid[...].astype(BF)
    red.second()
    out_in.wait()
    for part in range(3):
        columns = slice(384 * part, 384 * part + 384)
        value = dot(o_perm[:, :LEAD], out_a[:, columns])
        value = value + dot(o_perm[:, LEAD:], out_b_ref[:, columns])
        mid[:, columns] = x_ref[:, columns].astype(F32) + value + vec_ref[4:5, columns]
    unit, _ = normal(mid[...])
    h2[...] = (unit * vec_ref[2:3] + vec_ref[3:4]).astype(BF)
    for steps in (1, 2, 3):
        red.third(steps)

    def turn(value, main, rest):
        turned = jnp.transpose(value)
        main[...] = turned[:LEAD].reshape(4, 2, 4, 2, 16, 256)
        rest[...] = turned[LEAD:]

    turn(o_perm[...], o_main_ref, o_tail_ref)
    turn(h2[...], h_main_ref, h_tail_ref)
    turn(g_ref[...], g_main_ref, g_tail_ref)
    result[...] = jnp.zeros_like(result)
    dh2[...] = jnp.zeros_like(dh2)
    first_in.wait()

    def tile_of(ref, main):
        def read(tile):
            start = main + tile * LANES
            return ref[:, :, :, :, :, start : start + LANES].reshape(LEAD, LANES)

        return read

    spread_tail(tile_of(weights, 2 * FIRST), FIRST_CHUNK, wide, tail)
    red.fourth(0)
    red.fourth(1)

    def chunk(ref, span, width, index, size):
        up_place = lanes(index * size, size)
        down_place = lanes(width + index * size, size)
        place_all = lanes(span + index * size, size)
        up = ref[:, :, :, :, :, up_place].reshape(LEAD, size)
        down = ref[:, :, :, :, :, down_place].reshape(LEAD, size)
        up_tail = tail[:, up_place]
        down_tail = tail[:, down_place]
        pre = dot(h2[:, :LEAD], up) + dot(h2[:, LEAD:], up_tail) + bias[:, place_all]
        square = pre * pre
        bend = jnp.tanh(TANH_A * pre * (1.0 + TANH_B * square))
        half = 0.5 * (1.0 + bend)
        active = (pre * half).astype(BF)
        slope = half + 0.5 * pre * (1.0 - bend * bend) * (TANH_A * (1.0 + 3.0 * TANH_B * square))
        back = dot(g_ref[:, :LEAD], down) + dot(g_ref[:, LEAD:], down_tail)
        dpre = (back * slope).astype(BF)
        active_ref[:, place_all] = active
        dpre_ref[:, place_all] = dpre
        active_t = jnp.transpose(active)
        dpre_t = jnp.transpose(dpre)
        result[:LEAD] += dot(down, active_t)
        result[LEAD:] += dot(down_tail, active_t)
        dh2[:LEAD] += dot(up, dpre_t)
        dh2[LEAD:] += dot(up_tail, dpre_t)
        gbias_ref[:, place_all] = column_total(dpre.astype(F32))

    def early(index, carry):
        chunk(weights, 0, FIRST, index, FIRST_STEP)

        @pl.when(index == 0)
        def _():
            red.fourth(2)
            red.fourth(3)

        @pl.when(index == 1)
        def _():
            for steps in range(4):
                red.fifth(steps)

        return carry

    lax.fori_loop(0, FIRST // FIRST_STEP, early, 0)
    red.close()
    spread_tail(tile_of(full, 2 * SECOND), SECOND_CHUNK, wide, tail)

    def late(index, carry):
        chunk(full, FIRST, SECOND, index, SECOND_STEP)
        return carry

    lax.fori_loop(0, SECOND // SECOND_STEP, late, 0)
    red.drain()
    gain = vec_ref[2:3]
    unit, rate = normal(mid[...])
    grad = jnp.transpose(dh2[...])
    gvec_ref[...] = jnp.zeros_like(gvec_ref)
    gvec_ref[0:1] = column_total(grad * unit)
    gvec_ref[1:2] = column_total(grad)
    gvec_ref[3:4] = column_total(g_ref[...].astype(F32))
    dmid = g_ref[...].astype(F32) + normal_back(unit, rate, gain, grad)
    dmid_ref[...] = dmid
    dlow = dmid.astype(BF)
    dy_ref[...] = dlow
    gvec_ref[2:3] = column_total(dlow.astype(F32))
    mixed_ref[...] = (mid[...] + jnp.transpose(result[...]) + vec_ref[5:6]).astype(BF)
    low_t = jnp.transpose(dlow)
    result[:LEAD] = dot(out_a[...], low_t)
    result[LEAD:] = dot(out_b_ref[...], low_t)
    o_perm[...] = jnp.transpose(result[...].astype(BF))

    for group in range(4):
        value = dot(o_perm[...], pick_ref[:, 512 * group : 512 * group + 512]).astype(BF)
        for head in range(4):
            do_ref[4 * group + head] = value[:, LANES * head : LANES * (head + 1)]


def middle(attn, first, slab, o, x, g, out_tail, vec, bias, tag):
    any_ = pl.BlockSpec(memory_space=pl.ANY)
    vmem = pl.BlockSpec(memory_space=pltpu.VMEM)
    sems = 3 * Gatherer.SEMS + 3
    turned = [(4, 2, 4, 2, 16, 256), (TAIL, 256)] * 3
    place = place_matrix().astype(BF)
    found = pl.pallas_call(
        middle_kernel,
        out_shape=tuple(
            [
                jax.ShapeDtypeStruct((256, D), BF),
                jax.ShapeDtypeStruct((HEADS, 256, LANES), BF),
                jax.ShapeDtypeStruct((256, D), F32),
                jax.ShapeDtypeStruct((256, D), BF),
                jax.ShapeDtypeStruct((8, D), F32),
                jax.ShapeDtypeStruct((1, FF_PAD), F32),
                jax.ShapeDtypeStruct((256, FF_PAD), BF),
                jax.ShapeDtypeStruct((256, FF_PAD), BF),
            ]
            + [jax.ShapeDtypeStruct(shape, BF) for shape in turned]
        ),
        in_specs=[any_] * 3 + [vmem] * 8,
        out_specs=(vmem,) * 14,
        scratch_shapes=[
            pltpu.VMEM((LEAD, D), BF),
            pltpu.VMEM((4, 2, 4, 2, 16, FIRST_TOTAL), BF),
            pltpu.VMEM((4, 2, 4, 2, 16, SECOND_TOTAL), BF),
            pltpu.VMEM((256, D), BF),
            pltpu.VMEM((256, D), F32),
            pltpu.VMEM((256, D), BF),
            pltpu.VMEM((D, 256), F32),
            pltpu.VMEM((D, 256), F32),
            pltpu.VMEM((FIRST_CHUNK // LANES, LEAD, LANES), F32),
            pltpu.VMEM((TAIL, 8 * FIRST_CHUNK), BF),
            pltpu.VMEM((1, FF_PAD), F32),
            pltpu.SemaphoreType.DMA((sems,)),
            pltpu.SemaphoreType.DMA((sems,)),
            pltpu.SemaphoreType.DMA((2,)),
        ],
        compiler_params=mesh_params(tag),
        name="middle",
    )(attn, first, slab, o, x, g, out_tail, vec, bias, place, place.T)
    return found[:8], found[12:14], found[8:10], found[10:12]


class Everyone:
    def __init__(self, place, core, slots, send, recv, base):
        self.place, self.core = place, core
        self.slots, self.send, self.recv, self.base = slots, send, recv, base

    def start(self, stage, value):
        if stage == 3:
            spot, targets = self.core, [(1, device_at(self.place, 1 - self.core))]
        else:
            axis = AXES[stage]
            spot = self.place[axis]
            targets = [
                (over, device_at(moved(self.place, axis, over), self.core)) for over in (2, 1, 3)
            ]
        self.slots[stage, spot] = value
        for over, device in targets:
            index = self.base + stage * 3 + over - 1
            slot = self.slots.at[stage, spot]
            remote(slot, slot, self.send.at[index], self.recv.at[index], device).start()

    def finish(self, stage):
        count = 2 if stage == 3 else 4
        for over in range(1, count):
            index = self.base + stage * 3 + over - 1
            spot = 1 - self.core if stage == 3 else cycle(self.place[AXES[stage]], 4 - over)
            slot = self.slots.at[stage, spot]
            remote(
                slot, slot, self.send.at[index], self.recv.at[index], device_at(self.place, self.core)
            ).wait_recv()
        total = self.slots[stage, 0]
        for spot in range(1, count):
            total = total + self.slots[stage, spot]
        return total

    def drain(self):
        for stage in range(4):
            for over in range(1, 2 if stage == 3 else 4):
                index = self.base + stage * 3 + over - 1
                slot = self.slots.at[stage, 0]
                remote(
                    slot,
                    slot,
                    self.send.at[index],
                    self.recv.at[index],
                    device_at(self.place, self.core),
                ).wait_send()


def finish_kernel(
    dheads,
    weight,
    dy,
    dpre,
    active,
    h_main,
    h_tail,
    o_main,
    o_tail,
    h2_main,
    h2_tail,
    g_main,
    g_tail,
    tail_ref,
    x_ref,
    dmid_ref,
    vec_ref,
    gvec_ref,
    gup_ref,
    tokens_ref,
    total_ref,
    share_ref,
    second_ref,
    dheads_all,
    weight_all,
    flat,
    flat_all,
    dy_all,
    dpre_all,
    active_all,
    h_main_all,
    h_tail_all,
    o_main_all,
    o_tail_all,
    h2_main_all,
    h2_tail_all,
    g_main_all,
    g_tail_all,
    extra,
    dh,
    vectors,
    slots,
    *rest,
):
    buffers, (send, recv, local) = rest[:-3], rest[-3:]
    place, core = here()
    red = Reducer(ATTN_WIDTHS, place, core, buffers[:18], share_ref, send, recv)
    base = 3 * Reducer.SEMS
    late = Reducer(SECOND_WIDTHS, place, core, buffers[18:], second_ref, send, recv, base)
    base = 2 * base
    twin = Twin(place, core, send, recv, base)
    late_twin = Twin(place, core, send, recv, base + 12)
    every = Everyone(place, core, slots, send, recv, base + 24)
    heads_in = pltpu.make_async_copy(dheads, dheads_all, local.at[0])
    heads_in.start()
    weight_in = pltpu.make_async_copy(weight.at[:, pl.ds(0, QKV)], weight_all, local.at[1])
    weight_in.start()
    greet(line_peers(place, core) + [device_at(place, 1 - core)])
    for source, target, axis in (
        (h2_main, h2_main_all, 5),
        (h2_tail, h2_tail_all, 1),
        (dpre.at[:, pl.ds(FIRST, SECOND)], dpre_all, 0),
        (g_main, g_main_all, 5),
        (g_tail, g_tail_all, 1),
        (active.at[:, pl.ds(FIRST, SECOND)], active_all, 0),
    ):
        late_twin.give(source, target, axis)
    for source, target, axis in (
        (h_main, h_main_all, 5),
        (h_tail, h_tail_all, 1),
        (o_main, o_main_all, 5),
        (o_tail, o_tail_all, 1),
        (dy, dy_all, 0),
    ):
        twin.give(source, target, axis)
    late_maker = Maker(
        late,
        [((h2_main_all, h2_tail_all), dpre_all), ((g_main_all, g_tail_all), active_all)],
        extra.at[pl.ds(0, SECOND_CHUNK // LANES)],
        SECOND_CHUNK,
    )
    maker = Maker(
        red,
        [((h_main_all, h_tail_all), flat_all), ((o_main_all, o_tail_all), dy_all)],
        extra,
        ATTN_CHUNK,
    )
    late_twin.ready()
    late_maker.run()
    heads_in.wait()
    for head in range(HEADS):
        flat[:, PACK * head : PACK * head + PACK] = dheads_all[head, :, :PACK]
    twin.give(flat, flat_all, 0)
    for spot in range(4):
        late.pass_on(spot)
    twin.ready()
    maker.run()
    for over in (2, 1, 3):
        late.gather_side(over, False)
    for spot in range(4):
        red.pass_on(spot)
    late.gather_side(0, True)
    dh[...] = jnp.zeros_like(dh)
    vectors[...] = jnp.zeros((VEC_ROWS, D), F32)
    vectors[2:6] = gvec_ref[:4]
    for row in range(4):
        span = slice(row * D, min((row + 1) * D, FF_PAD))
        vectors[VEC_UP + row : VEC_UP + row + 1, : span.stop - span.start] = gup_ref[:, span]
    weight_in.wait()

    for row in range(3):

        def columns(index, carry):
            span = lanes(row * D + index * 384, 384)
            value = flat[:, span]
            vectors[VEC_QKV + row : VEC_QKV + row + 1, lanes(index * 384, 384)] = column_total(
                value.astype(F32)
            )
            value_t = jnp.transpose(value)
            dh[:LEAD] += dot(weight_all[:, span], value_t)
            dh[LEAD:] += dot(tail_ref[:, span], value_t)
            return carry

        lax.fori_loop(0, 3, columns, 0)
    late.line_up()
    unit, rate = normal(x_ref[...].astype(F32))
    grad = jnp.transpose(dh[...])
    vectors[0:1] = column_total(grad * unit)
    vectors[1:2] = column_total(grad)
    every.start(0, vectors[...])
    for over in (2, 1, 3):
        red.gather_side(over, False)
    every.start(1, every.finish(0))
    total = dmid_ref[...] + normal_back(unit, rate, vec_ref[0:1], grad)
    tokens_ref[...] = total.astype(BF)
    red.gather_side(0, True)
    late.share()
    every.start(2, every.finish(1))
    red.line_up()
    every.start(3, every.finish(2))
    red.share()
    total_ref[...] = every.finish(3)
    late.close()
    red.close()
    twin.drain()
    late_twin.drain()
    every.drain()


def finish(dheads, weight, dy, dpre, active, turned, tail, x, dmid, vec, gvec, gup, tag):
    any_ = pl.BlockSpec(memory_space=pl.ANY)
    vmem = pl.BlockSpec(memory_space=pltpu.VMEM)
    sems = 6 * Reducer.SEMS + 24 + 12
    rows = [pltpu.VMEM((4, 2, 4, 2, 16, 512), BF), pltpu.VMEM((TAIL, 512), BF)]
    return pl.pallas_call(
        finish_kernel,
        out_shape=(
            jax.ShapeDtypeStruct((256, D), BF),
            jax.ShapeDtypeStruct((VEC_ROWS, D), F32),
            jax.ShapeDtypeStruct((16, ATTN_TOTAL), BF),
            jax.ShapeDtypeStruct((16, SECOND_TOTAL), BF),
        ),
        in_specs=[any_] * 13 + [vmem] * 6,
        out_specs=(vmem,) * 4,
        scratch_shapes=[
            pltpu.VMEM((HEADS, 256, WIDE), BF),
            pltpu.VMEM((LEAD, QKV), BF),
            pltpu.VMEM((256, QKV), BF),
            pltpu.VMEM((512, QKV), BF),
            pltpu.VMEM((512, D), BF),
            pltpu.VMEM((512, SECOND), BF),
            pltpu.VMEM((512, SECOND), BF),
        ]
        + rows * 4
        + [
            pltpu.VMEM((ATTN_CHUNK // LANES, LEAD, LANES), F32),
            pltpu.VMEM((D, 256), F32),
            pltpu.VMEM((VEC_ROWS, D), F32),
            pltpu.VMEM((4, 4, VEC_ROWS, D), F32),
        ]
        + Reducer.scratch(ATTN_WIDTHS)
        + Reducer.scratch(SECOND_WIDTHS)
        + [
            pltpu.SemaphoreType.DMA((sems,)),
            pltpu.SemaphoreType.DMA((sems,)),
            pltpu.SemaphoreType.DMA((2,)),
        ],
        compiler_params=mesh_params(tag),
        name="finish",
    )(dheads, weight, dy, dpre, active, *turned, tail, x, dmid, vec, gvec, gup)


def close_kernel(
    totals_ref,
    attn_ref,
    first_ref,
    second_ref,
    mixed_in,
    tokens_in,
    unmix_ref,
    mixed_ref,
    tokens_ref,
    query_ref,
    key_ref,
    value_ref,
    out_ref,
    up_ref,
    down_ref,
    gain1_ref,
    bias1_ref,
    gain2_ref,
    bias2_ref,
    bias_out_ref,
    bias_down_ref,
    bias_query_ref,
    bias_value_ref,
    bias_up_ref,
    attn,
    first,
    second,
    vec,
    stack,
):
    def unpack(share, full, main, chunk):
        full[0:16, :] = share[:, :main].astype(F32)
        rest = share[:, main : main + chunk].astype(F32)
        for row in range(2):
            for index in range(8):
                size = min(main - index * chunk, chunk)
                if size > 0:
                    start = index * chunk
                    spot = row * 8 + index
                    full[16 + row : 17 + row, start : start + size] = rest[
                        spot : spot + 1, :size
                    ]

    unpack(attn_ref, attn, ATTN_MAIN, ATTN_CHUNK)
    unpack(first_ref, first, 2 * FIRST, FIRST_CHUNK)
    unpack(second_ref, second, 2 * SECOND, SECOND_CHUNK)
    for head in range(HEADS):
        span = slice(head * HEAD_DIM, (head + 1) * HEAD_DIM)
        for index, ref in enumerate((key_ref, query_ref, value_ref)):
            start = head * PACK + index * HEAD_DIM
            ref[:, span] = attn[:18, start : start + HEAD_DIM]
    stack[0:256] = mixed_in[...]
    stack[256:512] = tokens_in[...]
    stack[512:544] = jnp.concatenate(
        [attn[:, QKV:ATTN_MAIN].astype(BF), jnp.zeros((8, D), BF)], axis=0
    )
    stack[544:576] = jnp.concatenate(
        [exact_parts(totals_ref[0:8, :]), jnp.zeros((8, D), BF)], axis=0
    )
    for part in range(3):
        columns = slice(384 * part, 384 * part + 384)
        value = dot(stack[...], unmix_ref[:, columns])
        mixed_ref[:, columns] = value[0:256].astype(BF)
        tokens_ref[:, columns] = value[256:512].astype(BF)
        out_ref[:, columns] = value[512:530]
        vec[0:8, columns] = value[544:552] + value[552:560] + value[560:568]
    lines = (gain1_ref, bias1_ref, gain2_ref, bias2_ref, bias_out_ref, bias_down_ref)
    for index, ref in enumerate(lines):
        ref[...] = vec[index : index + 1, :D].reshape(D)
    for row in range(3):
        vec[8:9, row * D : (row + 1) * D] = totals_ref[VEC_QKV + row : VEC_QKV + row + 1, :]
    for head in range(HEADS):
        span = slice(head * HEAD_DIM, (head + 1) * HEAD_DIM)
        for index, row in ((1, 9), (2, 10)):
            start = head * PACK + index * HEAD_DIM
            vec[row : row + 1, span] = vec[8:9, start : start + HEAD_DIM]
    bias_query_ref[...] = vec[9:10, :D].reshape(D)
    bias_value_ref[...] = vec[10:11, :D].reshape(D)
    for row in range(4):
        size = min(FF - row * D, D)
        vec[11:12, row * D : row * D + size] = totals_ref[
            VEC_UP + row : VEC_UP + row + 1, :size
        ]
    bias_up_ref[...] = vec[11:12, :FF].reshape(FF)
    up_ref[:, :FIRST] = first[:18, :FIRST]
    up_ref[:, FIRST:] = second[:18, : FF - FIRST]
    down_ref[:, :FIRST] = first[:18, FIRST : 2 * FIRST]
    down_ref[:, FIRST:] = second[:18, SECOND : SECOND + FF - FIRST]


def close_layer(totals, attn, first, second, mixed, tokens):
    line = jax.ShapeDtypeStruct((D,), F32)
    square = jax.ShapeDtypeStruct((18, D), F32)
    return pl.pallas_call(
        close_kernel,
        out_shape=(
            jax.ShapeDtypeStruct((256, D), BF),
            jax.ShapeDtypeStruct((256, D), BF),
            square,
            square,
            square,
            square,
            jax.ShapeDtypeStruct((18, FF), F32),
            jax.ShapeDtypeStruct((18, FF), F32),
            *([line] * 8),
            jax.ShapeDtypeStruct((FF,), F32),
        ),
        scratch_shapes=[
            pltpu.VMEM((24, ATTN_MAIN), F32),
            pltpu.VMEM((24, 2 * FIRST), F32),
            pltpu.VMEM((24, 2 * SECOND), F32),
            pltpu.VMEM((16, 4 * D), F32),
            pltpu.VMEM((576, D), BF),
        ],
        compiler_params=params(),
        name="close_layer",
    )(totals, attn, first, second, mixed, tokens, mix_matrix().T.astype(BF))


def pack_slab(weight, chunk, total):
    width = weight.shape[1]
    rest = jnp.pad(weight[16:], ((0, 0), (0, 8 * chunk - width))).reshape(16, chunk)
    return jnp.concatenate(
        [weight[:16], rest, jnp.zeros((16, total - width - chunk), weight.dtype)], axis=1
    )


def by_head(key, query, value):
    rows = key.shape[0]
    parts = [item.reshape(rows, HEADS, 1, HEAD_DIM) for item in (key, query, value)]
    return jnp.concatenate(parts, axis=2).reshape(rows, QKV)


def mixing():
    return onehot(iota((D, D), 0) == origin(iota((D, D), 1)))


def body(
    tokens,
    picture,
    cotangent,
    ln1_gain,
    ln1_bias,
    w_query,
    b_query,
    w_key,
    w_value,
    b_value,
    w_out,
    b_out,
    ln2_gain,
    ln2_bias,
    w_fc1,
    b_fc1,
    w_fc2,
    b_fc2,
):
    mix = mixing()
    out_cols = dot(w_out, mix).astype(BF)
    attn_slab = pack_slab(
        jnp.concatenate([by_head(w_key, w_query, w_value), out_cols], axis=1),
        ATTN_CHUNK,
        ATTN_TOTAL,
    )
    gap = ((0, 0), (0, FF_PAD - FF))
    up, down = jnp.pad(w_fc1, gap), jnp.pad(w_fc2.T, gap)
    first_slab = pack_slab(
        jnp.concatenate([up[:, :FIRST], down[:, :FIRST]], axis=1), FIRST_CHUNK, FIRST_TOTAL
    )
    second_slab = pack_slab(
        jnp.concatenate([up[:, FIRST:], down[:, FIRST:]], axis=1), SECOND_CHUNK, SECOND_TOTAL
    )
    lines = (ln1_gain, ln1_bias, ln2_gain, ln2_bias, b_out, b_fc2, b_query, b_value)
    x, g, h_main, h_tail, attn_tail, out_tail, vec, packed, keep, o, attn, first = front(
        attn_slab,
        first_slab,
        tokens.reshape(256, D),
        cotangent.reshape(256, D),
        lines,
        picture,
        0,
    )
    attn = attn.reshape(LEAD, ATTN_TOTAL)
    (mixed, go, dmid, dy, gvec2, gbias1, dpre, active), o_turned, h_turned, g_turned = middle(
        attn, first, second_slab, o, x, g, out_tail, vec, b_fc1, 2
    )
    first_share, dheads = attend_back_reduce(
        go, dpre, active, (*h_turned, *g_turned), packed, keep, picture, 3
    )
    gtokens, totals, attn_share, second_share = finish(
        dheads,
        attn,
        dy,
        dpre,
        active,
        (h_main, h_tail, *o_turned, *h_turned, *g_turned),
        attn_tail,
        x,
        dmid,
        vec,
        gvec2,
        gbias1,
        4,
    )
    (
        mixed,
        gtokens,
        grad_query,
        grad_key,
        grad_value,
        grad_out,
        grad_up,
        grad_down,
        grad_gain1,
        grad_bias1,
        grad_gain2,
        grad_bias2,
        grad_b_out,
        grad_b_fc2,
        grad_b_query,
        grad_b_value,
        grad_b_fc1,
    ) = close_layer(totals, attn_share, first_share, second_share, mixed, gtokens)
    return (
        mixed.reshape(2, 128, D),
        gtokens.reshape(2, 128, D),
        grad_gain1,
        grad_bias1,
        grad_query,
        grad_b_query,
        grad_key,
        grad_value,
        grad_b_value,
        grad_out,
        grad_b_out,
        grad_gain2,
        grad_bias2,
        grad_up,
        grad_b_fc1,
        grad_down.T,
        grad_b_fc2,
    )


def solution(mesh):
    placed = (
        P(None, ("fsdp", "rep"), None),
        P(),
        P(None, ("fsdp", "rep"), None),
        P(),
        P(),
        P("fsdp", None),
        P(),
        P("fsdp", None),
        P("fsdp", None),
        P(),
        P("fsdp", None),
        P(),
        P(),
        P(),
        P("fsdp", None),
        P(),
        P(None, "fsdp"),
        P(),
    )
    return jax.shard_map(
        body,
        mesh=mesh,
        in_specs=placed,
        out_specs=(
            P(None, ("fsdp", "rep"), None),
            P(None, ("fsdp", "rep"), None),
            P(),
            P(),
            P("fsdp", None),
            P(),
            P("fsdp", None),
            P("fsdp", None),
            P(),
            P("fsdp", None),
            P(),
            P(),
            P(),
            P("fsdp", None),
            P(),
            P(None, "fsdp"),
            P(),
        ),
        check_vma=False,
    )
```

```python
import functools

import jax
import jax.numpy as jnp
import numpy as np
from jax import lax
from jax.experimental import pallas as pl
from jax.experimental.pallas import tpu as pltpu
from jax.sharding import PartitionSpec as P

MESH = pl.DeviceIdType.MESH
BF = jnp.bfloat16
F32 = jnp.float32
LANES = 128
ORDERS = (("x", "y", "z"), ("y", "z", "x"), ("z", "x", "y"))
AXES = ("x", "y", "z")


def here():
    shard = lax.axis_index("fsdp")
    low = lax.axis_index("rep")
    place = {
        "x": lax.div(shard, 16),
        "y": lax.rem(lax.div(shard, 8), 2) * 2 + low,
        "z": lax.rem(lax.div(shard, 2), 4),
    }
    return place, lax.rem(shard, 2)


def moved(place, axis, steps):
    steps = steps % 4
    if steps == 0:
        return place
    other = dict(place)
    other[axis] = lax.rem(place[axis] + steps, 4)
    return other


def device_at(place, core):
    high = lax.div(place["y"], 2)
    return (((place["x"] * 2 + high) * 4 + place["z"]) * 2 + core, lax.rem(place["y"], 2))


def greet(peers):
    barrier = pltpu.get_barrier_semaphore()
    for peer in peers:
        pl.semaphore_signal(barrier, inc=1, device_id=peer, device_id_type=MESH)
    pl.semaphore_wait(barrier, len(peers))


def part_columns(part, half, widths):
    start = 2 * sum(widths[:part]) + half * widths[part]
    return pl.ds(pl.multiple_of(start, LANES), widths[part])


def piece_of(ref, part, widths, place, core):
    return ref.at[
        place["x"],
        lax.div(place["y"], 2),
        place["z"],
        core,
        :,
        part_columns(part, lax.rem(place["y"], 2), widths),
    ]


def block_of(ref, part, widths, place, core, axis, half=None):
    where = {"x": place["x"], "y": lax.div(place["y"], 2), "z": place["z"]}
    if axis == "y":
        where["y"] = pl.ds(0, 2) if half is None else pl.ds(half, 1)
        columns = pl.ds(2 * sum(widths[:part]), 2 * widths[part])
    else:
        where[axis] = pl.ds(0, 4) if half is None else pl.ds(2 * half, 2)
        columns = part_columns(part, lax.rem(place["y"], 2), widths)
    return ref.at[where["x"], where["y"], where["z"], core, :, columns]


def remote(source, target, send, recv, device):
    return pltpu.make_async_remote_copy(
        src_ref=source,
        dst_ref=target,
        send_sem=send,
        recv_sem=recv,
        device_id=device,
        device_id_type=MESH,
    )


def cycle(value, steps):
    return lax.rem(value + steps, 4)


def turned_by(place, axis, steps):
    other = dict(place)
    other[axis] = cycle(place[axis], steps)
    return other


class Gatherer:
    SEMS = 3 + 3 + 8 + 8 + 16
    KINDS = {"one": 0, "two": 3, "three": 6, "four": 14, "twin": 22}

    def __init__(self, widths, place, core, own, full, send, recv, base):
        self.widths, self.place, self.core = widths, place, core
        self.own, self.full, self.send, self.recv, self.base = own, full, send, recv, base
        self.twin = device_at(place, 1 - core)

    def slot(self, part, kind, index):
        return self.base + part * self.SEMS + self.KINDS[kind] + index

    def push(self, source, target, slot, device):
        remote(source, target, self.send.at[slot], self.recv.at[slot], device).start()

    def arrived(self, region, slot):
        remote(region, region, self.send.at[slot], self.recv.at[slot], self.twin).wait_recv()

    def sent(self, region, slot):
        remote(region, region, self.send.at[slot], self.recv.at[slot], self.twin).wait_send()

    def block(self, part, place, half=None, core=None):
        core = self.core if core is None else core
        return block_of(self.full, part, self.widths, place, core, ORDERS[part][0], half)

    def keep(self, part):
        low = lax.rem(self.place["y"], 2)
        source = self.own.at[:, part_columns(part, low, self.widths)]
        target = piece_of(self.full, part, self.widths, self.place, self.core)
        return source, target, pltpu.make_async_copy(
            source, target, self.recv.at[self.base + 3 * self.SEMS + part]
        )

    def start(self):
        for part, (one, two, three) in enumerate(ORDERS):
            source, target, copy = self.keep(part)
            copy.start()
            for steps in (1, 3, 2):
                device = device_at(turned_by(self.place, one, steps), self.core)
                self.push(source, target, self.slot(part, "one", steps - 1), device)

    def second(self):
        for part, (one, two, three) in enumerate(ORDERS):
            self.keep(part)[2].wait()
            for steps in (1, 3, 2):
                origin = turned_by(self.place, one, 4 - steps)
                region = piece_of(self.full, part, self.widths, origin, self.core)
                self.arrived(region, self.slot(part, "one", steps - 1))
            block = self.block(part, self.place)
            for steps in (1, 3, 2):
                device = device_at(turned_by(self.place, two, steps), self.core)
                self.push(block, block, self.slot(part, "two", steps - 1), device)
        self.spread(0)

    def spread(self, steps):
        for part, (one, two, three) in enumerate(ORDERS):
            block = self.block(part, turned_by(self.place, two, 4 - steps))
            for index, way in enumerate((1, 3)):
                device = device_at(turned_by(self.place, three, way), self.core)
                self.push(block, block, self.slot(part, "three", index * 4 + steps), device)
            self.push(block, block, self.slot(part, "twin", steps), self.twin)

    def third(self, steps):
        for part, (one, two, three) in enumerate(ORDERS):
            block = self.block(part, turned_by(self.place, two, 4 - steps))
            self.arrived(block, self.slot(part, "two", steps - 1))
        self.spread(steps)

    def fourth(self, steps):
        for part, (one, two, three) in enumerate(ORDERS):
            side = turned_by(self.place, two, 4 - steps)
            for index, way in enumerate((1, 3)):
                origin = turned_by(side, three, 4 - way)
                block = self.block(part, origin)
                self.arrived(block, self.slot(part, "three", index * 4 + steps))
                half = self.block(part, origin, index)
                device = device_at(turned_by(self.place, three, way), self.core)
                self.push(half, half, self.slot(part, "four", index * 4 + steps), device)
                self.push(block, block, self.slot(part, "twin", way * 4 + steps), self.twin)

    def fifth(self, steps):
        for part, (one, two, three) in enumerate(ORDERS):
            origin = turned_by(turned_by(self.place, two, 4 - steps), three, 2)
            for index in range(2):
                half = self.block(part, origin, index)
                self.arrived(half, self.slot(part, "four", index * 4 + steps))
            block = self.block(part, origin)
            self.push(block, block, self.slot(part, "twin", 8 + steps), self.twin)

    def close(self):
        for part, (one, two, three) in enumerate(ORDERS):
            for way in range(4):
                for steps in range(4):
                    origin = moved(moved(self.place, two, -steps), three, -way)
                    region = self.block(part, origin, core=1 - self.core)
                    self.arrived(region, self.slot(part, "twin", way * 4 + steps))

    def drain(self):
        for part in range(3):
            piece = piece_of(self.full, part, self.widths, self.place, self.core)
            block = self.block(part, self.place)
            half = self.block(part, self.place, 0)
            for kind, region, count in (
                ("one", piece, 3),
                ("two", block, 3),
                ("three", block, 8),
                ("four", half, 8),
                ("twin", block, 16),
            ):
                for index in range(count):
                    self.sent(region, self.slot(part, kind, index))


class Reducer:
    SEMS = 8 + 8 + 3 + 3 + 1
    KINDS = {"mid": 0, "far": 8, "side": 16, "line": 19, "done": 22}

    def __init__(self, widths, place, core, buffers, out, send, recv, base=0):
        self.widths, self.place, self.core, self.base = widths, place, core, base
        self.acc, self.mid, self.far, self.side, self.line, self.done = [
            buffers[3 * i : 3 * i + 3] for i in range(6)
        ]
        self.out, self.send, self.recv = out, send, recv
        self.me = device_at(place, core)

    @staticmethod
    def scratch(widths):
        found = []
        for lead, half in (((4, 4), 1), ((2, 4), 2), ((2, 4), 1), ((3,), 1)):
            for width, (one, two, three) in zip(widths, ORDERS):
                if one == "y":
                    found.append(pltpu.VMEM(lead + (2 // half, 16, 2 * width), BF))
                else:
                    found.append(pltpu.VMEM(lead + (4 // half, 16, width), BF))
        found += [pltpu.VMEM((3, 16, width), BF) for width in widths]
        found += [pltpu.VMEM((16, width), BF) for width in widths]
        return found

    def slot(self, part, kind, index):
        return self.base + part * self.SEMS + self.KINDS[kind] + index

    def push(self, source, target, slot, device):
        remote(source, target, self.send.at[slot], self.recv.at[slot], device).start()

    def arrived(self, region, slot):
        remote(region, region, self.send.at[slot], self.recv.at[slot], self.me).wait_recv()

    def sent(self, region, slot):
        remote(region, region, self.send.at[slot], self.recv.at[slot], self.me).wait_send()

    def add(self, target, *terms):
        for index in range(target.shape[0]):
            total = target[index].astype(F32)
            for term in terms:
                total = total + term[index].astype(F32)
            target[index] = total.astype(BF)

    def half_of(self, ref, half):
        size = ref.shape[0] // 2
        return ref.at[pl.ds(half * size, size)]

    def far_out(self):
        for spot in range(4):
            for part, (one, two, three) in enumerate(ORDERS):
                for half, way in ((0, 3), (1, 1)):
                    self.push(
                        self.half_of(self.acc[part].at[2, spot], half),
                        self.mid[part].at[half, spot],
                        self.slot(part, "mid", half * 4 + spot),
                        device_at(moved(self.place, three, way), self.core),
                    )

    def pass_on(self, spot):
        for part, (one, two, three) in enumerate(ORDERS):
            for half, way in ((0, 3), (1, 1)):
                self.arrived(
                    self.mid[part].at[half, spot], self.slot(part, "mid", half * 4 + spot)
                )
                self.add(
                    self.half_of(self.acc[part].at[way, spot], half), self.mid[part].at[half, spot]
                )
                self.push(
                    self.acc[part].at[way, spot],
                    self.far[part].at[half, spot],
                    self.slot(part, "far", half * 4 + spot),
                    device_at(moved(self.place, three, way), self.core),
                )

    def gather_side(self, over, last):
        for part, (one, two, three) in enumerate(ORDERS):
            spot = cycle(self.place[two], over)
            for half in range(2):
                self.arrived(
                    self.far[part].at[half, spot], self.slot(part, "far", half * 4 + spot)
                )
            self.add(
                self.acc[part].at[0, spot], self.far[part].at[0, spot], self.far[part].at[1, spot]
            )

            def give(part=part, two=two, spot=spot):
                other = dict(self.place)
                other[two] = spot
                self.push(
                    self.acc[part].at[0, spot],
                    self.side[part].at[over - 1],
                    self.slot(part, "side", over - 1),
                    device_at(other, self.core),
                )

            if last is False:
                give()
            elif last is not True:
                pl.when(jnp.logical_not(last))(give)

    def piece(self, part, axis, spot):
        own = self.acc[part].at[0, self.place[ORDERS[part][1]]]
        if axis == "y":
            start = pl.multiple_of(lax.rem(spot["y"], 2) * self.widths[part], LANES)
            return own.at[lax.div(spot["y"], 2), :, pl.ds(start, self.widths[part])]
        return own.at[spot[axis]]

    def line_up(self):
        for part, (one, two, three) in enumerate(ORDERS):
            for over in range(3):
                self.arrived(self.side[part].at[over], self.slot(part, "side", over))
            own = self.acc[part].at[0, self.place[two]]
            self.add(own, self.side[part].at[0], self.side[part].at[1], self.side[part].at[2])
            for over in (2, 1, 3):
                spot = moved(self.place, one, over)
                self.push(
                    self.piece(part, one, spot),
                    self.line[part].at[over - 1],
                    self.slot(part, "line", over - 1),
                    device_at(spot, self.core),
                )

    def share(self):
        low = lax.rem(self.place["y"], 2)
        partner = (lax.axis_index("fsdp"), 1 - low)
        for part, (one, two, three) in enumerate(ORDERS):
            for over in range(3):
                self.arrived(self.line[part].at[over], self.slot(part, "line", over))
            total = self.piece(part, one, self.place)[...].astype(F32)
            for over in range(3):
                total = total + self.line[part][over].astype(F32)
            self.done[part][...] = total.astype(BF)
            columns = part_columns(part, low, self.widths)
            self.push(
                self.done[part], self.out.at[:, columns], self.slot(part, "done", 0), partner
            )
            self.out[:, columns] = self.done[part][...]

    def close(self):
        low = lax.rem(self.place["y"], 2)
        for part, (one, two, three) in enumerate(ORDERS):
            self.arrived(
                self.out.at[:, part_columns(part, 1 - low, self.widths)],
                self.slot(part, "done", 0),
            )
            for half in range(2):
                for spot in range(4):
                    index = half * 4 + spot
                    self.sent(self.mid[part].at[half, spot], self.slot(part, "mid", index))
                    self.sent(self.far[part].at[half, spot], self.slot(part, "far", index))
            for over in range(3):
                self.sent(self.side[part].at[over], self.slot(part, "side", over))
                self.sent(self.line[part].at[over], self.slot(part, "line", over))
            self.sent(self.done[part], self.slot(part, "done", 0))


class Maker:
    def __init__(self, reducer, sources, extra, chunk):
        self.red, self.sources, self.extra, self.chunk = reducer, sources, extra, chunk
        self.main = sum(item[1].shape[1] for item in sources)

    def pack_tail(self):
        start = 0
        pieces = []
        for turned, right in self.sources:
            pieces.append((start, start + right.shape[1], turned, right))
            start += right.shape[1]
        for index in range(8):
            low, high = index * self.chunk, (index + 1) * self.chunk
            for first, last, turned, right in pieces:
                a, b = max(low, first), min(high, last)
                if a < b:
                    value = dot(turned[1][...], right[:, a - first : b - first])
                    self.scatter(index, a - low, value)
            if high > self.main:
                a = max(low, self.main)
                self.scatter(index, a - low, jnp.zeros((TAIL, high - a), F32))

    def scatter(self, index, start, value):
        for tile in range(value.shape[1] // LANES):
            self.extra[start // LANES + tile, pl.ds(index, TAIL, stride=8), :] = value[
                :, tile * LANES : (tile + 1) * LANES
            ]

    def rows(self, ref):
        core = self.red.core
        if len(ref.shape) == 2:
            groups = [
                ref[pl.ds(pl.multiple_of((2 * index + core) * 16, 16), 16)] for index in range(32)
            ]
            return jnp.concatenate(groups, axis=0)
        return ref[:, :, :, core].reshape(512, ref.shape[-1])

    def columns(self, part, half):
        width = self.red.widths[part]
        low = 2 * sum(self.red.widths[:part]) + half * width
        high = low + width
        first = 0
        found = []
        for turned, right in self.sources:
            last = first + right.shape[1]
            a, b = max(low, first), min(high, last)
            if a < b:
                left = self.rows(turned[0])
                found.append(dot(left, right[:, a - first : b - first]).astype(BF))
            first = last
        a, b = max(low, first), min(high, first + self.chunk)
        if a < b:
            for tile in range((a - first) // LANES, (b - first) // LANES):
                found.append(self.rows(self.extra.at[tile]).astype(BF))
        a = max(low, first + self.chunk)
        if a < high:
            found.append(jnp.zeros((512, high - a), BF))
        return found[0] if len(found) == 1 else jnp.concatenate(found, axis=1)

    def make(self, part):
        red, width = self.red, self.red.widths[part]
        acc = red.acc[part]
        three = ORDERS[part][2]
        own = red.place[three]

        def ahead(spot):
            return cycle(spot + 4 - own, 0)

        for half in range(2):
            value = self.columns(part, half).reshape(4, 2, 4, 16, width)
            if three == "z":
                for spot in range(4):
                    for high in range(2):
                        acc[ahead(spot), 2 * high + half] = value[:, high, spot]
            elif three == "x":
                for spot in range(4):
                    for z in range(4):
                        acc[ahead(spot), z, :, :, half * width : (half + 1) * width] = value[
                            spot, :, z
                        ]
            else:
                for high in range(2):
                    for x in range(4):
                        acc[ahead(2 * high + half), x] = value[x, high]

    def run(self):
        self.pack_tail()
        for part in range(3):
            self.make(part)
        self.red.far_out()


SWAP_ORDER = (9, 11, 5, 13, 7, 15, 1, 3, 8, 10, 4, 12, 6, 14, 2)


class Swapper:
    def __init__(self, place, core, own, full, send, recv, base):
        self.place, self.core = place, core
        self.own, self.full, self.send, self.recv, self.base = own, full, send, recv, base
        self.low = lax.rem(place["y"], 2)
        self.mine = (place["z"] * 2 + core) * 2 + self.low
        self.group = lax.div(lax.axis_index("fsdp"), 8) * 8

    def member(self, k, sign=1):
        z = lax.rem(self.place["z"] + (4 + sign * (k // 4)), 4)
        core = lax.rem(self.core + (k // 2) % 2, 2)
        low = lax.rem(self.low + k % 2, 2)
        return (z * 2 + core) * 2 + low

    def device(self, index):
        return (self.group + lax.div(index, 2), lax.rem(index, 2))

    def peers(self):
        return [self.device(self.member(k)) for k in range(1, 16)]

    def view(self, ref, index, micro):
        if len(ref.shape) == 3:
            return ref.at[index, :, pl.ds(micro * 128, 128)]
        return ref.at[:, pl.ds(pl.multiple_of(micro * ROW + index * 128, 128), 128)]

    def start(self, micro):
        for k in SWAP_ORDER:
            target = self.member(k)
            remote(
                self.view(self.own, target, micro),
                self.view(self.full, self.mine, micro),
                self.send.at[self.base + k],
                self.recv.at[self.base + k],
                self.device(target),
            ).start()
        pltpu.make_async_copy(
            self.view(self.own, self.mine, micro),
            self.view(self.full, self.mine, micro),
            self.send.at[self.base],
        ).start()

    def finish(self, micro):
        pltpu.make_async_copy(
            self.view(self.own, self.mine, micro),
            self.view(self.full, self.mine, micro),
            self.send.at[self.base],
        ).wait()
        for k in range(1, 16):
            region = self.view(self.full, self.member(k, -1), micro)
            remote(
                region,
                region,
                self.send.at[self.base + k],
                self.recv.at[self.base + k],
                self.device(self.mine),
            ).wait_recv()

    def drain(self, micro):
        for k in range(1, 16):
            region = self.view(self.own, self.member(k), micro)
            remote(
                region,
                region,
                self.send.at[self.base + k],
                self.recv.at[self.base + k],
                self.device(self.mine),
            ).wait_send()


def line_peers(place, core):
    peers = []
    for axis in AXES:
        for steps in (1, 2, 3):
            peers.append(device_at(moved(place, axis, steps), core))
    return peers


D = 1152
HEADS = 16
HEAD_DIM = 72
FF = 4304
ROW = 2048
EPS = 1e-06
NEG = -1e30
SCALE = HEAD_DIM**-0.5
LEAD = 1024
TAIL = 128
PACK = 3 * HEAD_DIM
WIDE = 256
WIRE = 224
HEAD_WIRE = 80
VALUE_LANE = 16
FF_PAD = 4352
QKV = HEADS * PACK
ATTN_MAIN = QKV + D
ATTN_CHUNK = 640
ATTN_TOTAL = 5376
MLP_MAIN = 2 * FF_PAD
MLP_CHUNK = 1152
MLP_TOTAL = 9984
ATTN_WIDTHS = (896, 896, 896)
MLP_WIDTHS = (1664, 1664, 1664)
FIRST = 3072
FIRST_CHUNK = 768
FIRST_TOTAL = 6912
FIRST_WIDTHS = (1152, 1152, 1152)
FIRST_STEP = 768
SECOND = FF_PAD - FIRST
SECOND_CHUNK = 384
SECOND_TOTAL = 3072
SECOND_WIDTHS = (512, 512, 512)
SECOND_STEP = 640
LOG2E = 1.4426950408889634
QUERIES = 512
KEYS = 512
BLOCKS = ROW // QUERIES
TANH_A = 0.7978845608028654
TANH_B = 0.044715


def dot(left, right):
    return jnp.dot(left, right, preferred_element_type=F32)


def dot_nt(left, right):
    return lax.dot_general(left, right, (((1,), (1,)), ((), ())), preferred_element_type=F32)


def dot_tn(left, right):
    return lax.dot_general(left, right, (((0,), (0,)), ((), ())), preferred_element_type=F32)


def origin(index):
    lead = (index >> 4) * 18 + (index & 15)
    rest = index - LEAD
    tail = (rest >> 1) * 18 + 16 + (rest & 1)
    return jnp.where(index < LEAD, lead, tail)


def iota(shape, axis):
    return lax.broadcasted_iota(jnp.int32, shape, axis)


def onehot(mask):
    return mask.astype(F32).astype(BF)


def normal(values):
    center = values - jnp.mean(values, axis=-1, keepdims=True)
    rate = lax.rsqrt(jnp.mean(center * center, axis=-1, keepdims=True) + EPS)
    return center * rate, rate


def normal_back(unit, rate, gain, grad):
    inner = grad * gain
    first = jnp.mean(inner, axis=-1, keepdims=True)
    second = jnp.mean(inner * unit, axis=-1, keepdims=True)
    return rate * (inner - first - unit * second)


def exact_parts(values):
    high = values.astype(BF)
    rest = values - high.astype(F32)
    middle_part = rest.astype(BF)
    low = (rest - middle_part.astype(F32)).astype(BF)
    return jnp.concatenate([high, middle_part, low], axis=0)


def column_total(values):
    return jnp.sum(values, axis=0, keepdims=True)


def lanes(start, size):
    return pl.ds(pl.multiple_of(start, LANES), size)


def params(limit=60):
    return pltpu.CompilerParams(vmem_limit_bytes=limit << 20)


PERMUTED = np.concatenate(
    [np.arange(64)[:, None] * 18 + np.arange(16), np.arange(64)[:, None] * 18 + [16, 17]], axis=1
)
PERMUTED = np.concatenate([PERMUTED[:, :16].reshape(-1), PERMUTED[:, 16:].reshape(-1)])


def mix_matrix():
    matrix = np.zeros((D, D), np.float32)
    matrix[PERMUTED, np.arange(D)] = 1.0
    return matrix


def place_matrix():
    matrix = np.zeros((HEADS, HEAD_WIRE, D), np.float32)
    matrix[:, :HEAD_DIM] = mix_matrix().reshape(HEADS, HEAD_DIM, D)
    return matrix.reshape(HEADS * HEAD_WIRE, D)


def mesh_params(tag, limit=62):
    return pltpu.CompilerParams(
        collective_id=tag, has_side_effects=True, vmem_limit_bytes=limit << 20
    )


class Twin:
    def __init__(self, place, core, send, recv, base):
        self.core, self.device = core, device_at(place, 1 - core)
        self.send, self.recv, self.base = send, recv, base
        self.items = []

    def half(self, ref, axis, core):
        size = ref.shape[axis] // 2
        if axis == 0:
            return ref.at[pl.ds(pl.multiple_of(core * size, size), size)]
        lead = (slice(None),) * (len(ref.shape) - 1)
        return ref.at[lead + (pl.ds(pl.multiple_of(core * size, LANES), size),)]

    def give(self, source, target, axis):
        index = self.base + 2 * len(self.items)
        place = self.half(target, axis, self.core)
        pltpu.make_async_copy(source, place, self.recv.at[index + 1]).start()
        remote(source, place, self.send.at[index], self.recv.at[index], self.device).start()
        self.items.append((source, target, axis, index))

    def ready(self):
        for source, target, axis, index in self.items:
            place = self.half(target, axis, self.core)
            pltpu.make_async_copy(source, place, self.recv.at[index + 1]).wait()
            other = self.half(target, axis, 1 - self.core)
            remote(
                other, other, self.send.at[index], self.recv.at[index], self.device
            ).wait_recv()

    def pass_part(self, source, target, columns, number):
        index = self.base + 2 * number
        place = target.at[pl.ds(pl.multiple_of(self.core * 256, 256), 256), columns]
        pltpu.make_async_copy(source, place, self.recv.at[index + 1]).start()
        remote(source, place, self.send.at[index], self.recv.at[index], self.device).start()

    def part_done(self, target, columns, number):
        index = self.base + 2 * number
        place = target.at[pl.ds(pl.multiple_of(self.core * 256, 256), 256), columns]
        other = target.at[pl.ds(pl.multiple_of((1 - self.core) * 256, 256), 256), columns]
        pltpu.make_async_copy(place, place, self.recv.at[index + 1]).wait()
        copy = remote(other, other, self.send.at[index], self.recv.at[index], self.device)
        copy.wait_recv()
        copy.wait_send()

    def drain(self):
        for source, target, axis, index in self.items:
            place = self.half(target, axis, self.core)
            remote(
                place, place, self.send.at[index], self.recv.at[index], self.device
            ).wait_send()


def back_kernel(
    go,
    dpre,
    active,
    h_main,
    h_tail,
    g_main,
    g_tail,
    picture,
    packed_ref,
    keep_ref,
    share_ref,
    dheads,
    go_all,
    grads,
    wire,
    backs,
    dpre_all,
    active_all,
    h_main_all,
    h_tail_all,
    g_main_all,
    g_tail_all,
    extra,
    keys,
    queries,
    ids,
    dkeys,
    dvalues,
    found,
    row_ref,
    *rest,
):
    buffers, (send, recv, local) = rest[:-3], rest[-3:]
    place, core = here()
    red = Reducer(FIRST_WIDTHS, place, core, buffers, share_ref, send, recv)
    base = 3 * Reducer.SEMS
    ins = [Swapper(place, core, go, go_all, send, recv, base + 16 * m) for m in range(2)]
    base = base + 32
    outs = [Swapper(place, core, wire, dheads, send, recv, base + 16 * m) for m in range(2)]
    greet(line_peers(place, core) + swap_only(ins[0]))
    for micro in range(2):
        ins[micro].start(micro)
    loads = []
    for source, target in (
        (h_main, h_main_all),
        (h_tail, h_tail_all),
        (g_main, g_main_all),
        (g_tail, g_tail_all),
        (dpre.at[:, pl.ds(0, FIRST)], dpre_all),
        (active.at[:, pl.ds(0, FIRST)], active_all),
    ):
        copy = pltpu.make_async_copy(source, target, local.at[1 + len(loads)])
        copy.start()
        loads.append(copy)
    maker = Maker(
        red,
        [((h_main_all, h_tail_all), dpre_all), ((g_main_all, g_tail_all), active_all)],
        extra,
        FIRST_CHUNK,
    )
    ids_in = fetch_ids(picture, found, local.at[0])
    ids_in.start()
    ids_in.wait()
    for micro in range(2):
        row_ref[micro] = found[micro : micro + 1].astype(F32)
    for copy in loads:
        copy.wait()
    maker.run()
    for spot in range(4):
        red.pass_on(spot)
    ins[0].finish(0)

    def block(step, carry):
        row = lax.div(step, BLOCKS)
        index = lax.rem(step, BLOCKS)
        tokens = pl.ds(pl.multiple_of(row * 128, 128), 128)

        @pl.when(step == BLOCKS)
        def _():
            ins[1].finish(1)

        @pl.when(index == 0)
        def _():
            back_row = jnp.concatenate(
                [
                    jnp.zeros((VALUE_LANE, ROW), BF),
                    go_all[:, lanes(row * ROW, ROW)],
                    jnp.zeros((LANES - VALUE_LANE - HEAD_WIRE, ROW), BF),
                ],
                axis=0,
            )
            backs[...] = jnp.transpose(back_row)
            packed = packed_ref[:, tokens, :].reshape(ROW, WIDE)
            split_packed(packed, keys, queries)
            for part in range(ROW // LANES):
                span = slice(part * LANES, (part + 1) * LANES)
                ids[span, :] = column_ids(row_ref[row, :, span])
            dkeys[...] = jnp.zeros_like(dkeys)
            dvalues[...] = jnp.zeros_like(dvalues)

        rows = pl.ds(pl.multiple_of(index * QUERIES, QUERIES), QUERIES)

        def scan(count):
            start = jnp.where(index < 2, 0, BLOCKS - count)
            query = queries[rows, :]
            back = backs[rows, :]
            mine = row_ref[row, :, lanes(index * QUERIES, QUERIES)]
            kept = keep_ref[row, rows, :]
            inner = jnp.sum(back.astype(F32) * kept, axis=1, keepdims=True)
            lane = iota((QUERIES, LANES), 1)
            stats = jnp.transpose(jnp.where(lane == 0, kept, inner))
            logsum = stats[0:1]
            inner = stats[1:2]
            total = jnp.zeros((QUERIES, LANES), F32)
            for part in range(count):
                span = pl.ds(pl.multiple_of((start + part) * KEYS, KEYS), KEYS)
                blocks = pl.ds((start + part) * (KEYS // 128), KEYS // 128)
                value = packed_ref[blocks, tokens, LANES:].reshape(KEYS, LANES)
                allowed = jnp.concatenate([ids[span, :]] * (QUERIES // LANES), axis=1)
                score = dot_nt(keys[span, :], query) * (SCALE * LOG2E) - logsum
                prob = jnp.exp2(jnp.where(allowed == mine, score, NEG))
                grad = (prob * (dot_nt(value, back) - inner)).astype(BF)
                dvalues[span, :] += dot(prob.astype(BF), back)
                dkeys[span, :] += dot(grad, query)
                total = total + dot_tn(grad, keys[span, :])
            total = total * SCALE
            moved_q = jnp.concatenate(
                [
                    jnp.zeros((QUERIES, HEAD_DIM), F32),
                    total[:, :HEAD_DIM],
                    jnp.zeros((QUERIES, WIDE - 2 * HEAD_DIM), F32),
                ],
                axis=1,
            )
            grads[rows, :] = moved_q.astype(BF)

        edge = (index == 0) | (index == BLOCKS - 1)
        pl.when(edge)(functools.partial(scan, 3))
        pl.when(jnp.logical_not(edge))(functools.partial(scan, 4))

        @pl.when(index == BLOCKS - 1)
        def _():
            wide = jnp.concatenate([dkeys[...] * SCALE, dvalues[...]], axis=1)
            lane = iota((ROW, WIDE), 1)
            old = grads[...]
            inside = (lane >= HEAD_DIM) & (lane < 2 * HEAD_DIM)
            whole = jnp.where(inside, old, wide.astype(BF))
            wire[:, lanes(row * ROW, ROW)] = jnp.transpose(whole)[:WIRE]
            for micro in range(2):
                pl.when(row == micro)(functools.partial(outs[micro].start, micro))

        @pl.when(step >= 4)
        def _():
            red.gather_side(lax.rem(step - 4 + 1, 4), step == 7)

        return carry

    lax.fori_loop(0, 2 * BLOCKS, block, 0)
    red.line_up()
    red.share()
    red.close()
    for micro in range(2):
        outs[micro].finish(micro)
    for micro in range(2):
        ins[micro].drain(micro)
    for micro in range(2):
        outs[micro].drain(micro)


def attend_back_reduce(go, dpre, active, turned, packed, keep, picture, tag):
    any_ = pl.BlockSpec(memory_space=pl.ANY)
    vmem = pl.BlockSpec(memory_space=pltpu.VMEM)
    sems = 3 * Reducer.SEMS + 64
    return pl.pallas_call(
        back_kernel,
        out_shape=(
            jax.ShapeDtypeStruct((16, FIRST_TOTAL), BF),
            jax.ShapeDtypeStruct((16, WIRE, 256), BF),
        ),
        in_specs=[any_] * 8 + [vmem] * 2,
        out_specs=(vmem, any_),
        scratch_shapes=[
            pltpu.VMEM((HEAD_WIRE, 2 * ROW), BF),
            pltpu.VMEM((ROW, WIDE), BF),
            pltpu.VMEM((WIRE, 2 * ROW), BF),
            pltpu.VMEM((ROW, LANES), BF),
            pltpu.VMEM((512, FIRST), BF),
            pltpu.VMEM((512, FIRST), BF),
            pltpu.VMEM((4, 2, 4, 2, 16, 512), BF),
            pltpu.VMEM((TAIL, 512), BF),
            pltpu.VMEM((4, 2, 4, 2, 16, 512), BF),
            pltpu.VMEM((TAIL, 512), BF),
            pltpu.VMEM((FIRST_CHUNK // LANES, LEAD, LANES), F32),
            pltpu.VMEM((ROW, LANES), BF),
            pltpu.VMEM((ROW, LANES), BF),
            pltpu.VMEM((ROW, LANES), F32),
            pltpu.VMEM((ROW, LANES), F32),
            pltpu.VMEM((ROW, LANES), F32),
            pltpu.VMEM((2, ROW), jnp.int32),
            pltpu.VMEM((2, 1, ROW), F32),
        ]
        + Reducer.scratch(FIRST_WIDTHS)
        + [
            pltpu.SemaphoreType.DMA((sems,)),
            pltpu.SemaphoreType.DMA((sems,)),
            pltpu.SemaphoreType.DMA((7,)),
        ],
        compiler_params=mesh_params(tag),
        name="attend_back_reduce",
    )(go, dpre, active, *turned, picture, packed, keep)


VEC_ROWS = 16
VEC_QKV = 6
VEC_UP = 9


def spread_tail(source, chunk, wide, tail):
    for tile in range(chunk // LANES):
        wide[tile] = source(tile).astype(F32)
        for index in range(8):
            start = index * chunk + tile * LANES
            picked = wide[tile, pl.ds(index, TAIL, stride=8), :]
            tail[:, start : start + LANES] = picked.astype(BF)


def column_ids(row_ids):
    size = row_ids.shape[1]
    return jnp.transpose(jnp.broadcast_to(row_ids, (LANES, size)))


def fetch_ids(picture, found, sem):
    start = pl.multiple_of(lax.div(lax.axis_index("fsdp"), 8) * ROW, ROW)
    return pltpu.make_async_copy(picture.at[:, pl.ds(start, ROW)], found, sem)


def split_packed(packed, keys, queries):
    lane = iota((ROW, LANES), 1)
    zero = jnp.zeros((ROW, LANES), BF)
    keys[...] = jnp.where(lane < HEAD_DIM, packed[:, :LANES], zero)
    queries[...] = jnp.concatenate(
        [packed[:, HEAD_DIM : 2 * HEAD_DIM], jnp.zeros((ROW, LANES - HEAD_DIM), BF)], axis=1
    )


def swap_only(swapper):
    return [swapper.device(swapper.member(k)) for k in range(1, 16) if k not in (1, 4, 8, 12)]


def front_kernel(
    slab,
    first_slab,
    picture,
    tokens_ref,
    cotangent_ref,
    *refs,
):
    lines, rest = refs[:8], refs[8:]
    run_front(slab, first_slab, picture, tokens_ref, cotangent_ref, lines, *rest)


def run_front(
    slab,
    first_slab,
    picture,
    tokens_ref,
    cotangent_ref,
    lines,
    x_ref,
    g_ref,
    tail_ref,
    out_tail_ref,
    mixed_vec_ref,
    packed_ref,
    keep_ref,
    o_all,
    weight_out,
    first_out,
    h_main_all,
    h_tail_all,
    h_main,
    h_tail,
    full,
    low,
    flat,
    wide,
    tail,
    vec_ref,
    vec_parts,
    heads,
    wire,
    o_own,
    keys,
    queries,
    values,
    scores,
    found,
    row_ref,
    send,
    recv,
    local,
):
    place, core = here()
    red = Gatherer(ATTN_WIDTHS, place, core, slab, full, send, recv, 0)
    base = 3 * Gatherer.SEMS + 3
    first = Gatherer(FIRST_WIDTHS, place, core, first_slab, first_out, send, recv, base)
    base = 2 * base
    ins = [Swapper(place, core, heads, wire, send, recv, base + 16 * m) for m in range(2)]
    base = base + 32
    outs = [Swapper(place, core, o_own, o_all, send, recv, base + 16 * m) for m in range(2)]
    twin = Twin(place, core, send, recv, base + 32)
    greet(line_peers(place, core) + swap_only(ins[0]))
    red.start()
    first.start()
    ids_in = fetch_ids(picture, found, local.at[0])
    ids_in.start()
    for index, line in enumerate(lines):
        vec_ref[index : index + 1, :] = line[...].reshape(1, D)
    vec_parts[...] = exact_parts(vec_ref[...])

    def mix(index, carry):
        columns = lanes(index * LANES, LANES)
        column = onehot(iota((D, LANES), 0) == origin(index * LANES + iota((D, LANES), 1)))
        x_ref[:, columns] = dot(tokens_ref[...], column).astype(BF)
        g_ref[:, columns] = dot(cotangent_ref[...], column).astype(BF)
        parts = dot(vec_parts[...], column)
        mixed_vec_ref[:, columns] = parts[0:8] + parts[8:16] + parts[16:24]
        return carry

    lax.fori_loop(0, 3, mix, 0)
    red.second()
    lax.fori_loop(3, 9, mix, 0)
    unit, _ = normal(x_ref[...].astype(F32))
    low[...] = (unit * mixed_vec_ref[0:1] + mixed_vec_ref[1:2]).astype(BF)
    for steps in (1, 2, 3):
        red.third(steps)
    turned = jnp.transpose(low[...])
    h_main[...] = turned[:LEAD].reshape(4, 2, 4, 2, 16, 256)
    h_tail[...] = turned[LEAD:]
    twin.give(h_main, h_main_all, 5)
    twin.give(h_tail, h_tail_all, 1)
    ids_in.wait()
    for micro in range(2):
        row_ref[micro] = found[micro : micro + 1].astype(F32)
    for steps in range(4):
        red.fourth(steps)
    first.second()
    for steps in range(4):
        red.fifth(steps)
    red.close()
    leave = pltpu.make_async_copy(full, weight_out, local.at[1])
    leave.start()

    def packed_tile(tile):
        start = ATTN_MAIN + tile * LANES
        return full[:, :, :, :, :, start : start + LANES].reshape(LEAD, LANES)

    for steps in (1, 2, 3):
        first.third(steps)
    spread_tail(packed_tile, ATTN_CHUNK, wide, tail)
    tail_ref[...] = tail[:, :QKV]
    out_tail_ref[...] = tail[:, QKV:ATTN_MAIN]

    def columns(index, carry):
        span = lanes(index * 384, 384)
        weight = full[:, :, :, :, :, span].reshape(LEAD, 384)
        flat[:, span] = dot(low[:, :LEAD], weight) + dot(low[:, LEAD:], tail[:, span])
        return carry

    lax.fori_loop(0, QKV // 384, columns, 0)
    for head in range(HEADS):
        span = slice(head * HEAD_DIM, (head + 1) * HEAD_DIM)
        bias = jnp.concatenate(
            [jnp.zeros((1, HEAD_DIM), F32), vec_ref[6:7, span], vec_ref[7:8, span]], axis=1
        )
        block = flat[:, PACK * head : PACK * head + PACK] + bias
        block = jnp.concatenate([block, jnp.zeros((256, WIDE - PACK), F32)], axis=1)
        heads[head] = jnp.transpose(block.astype(BF))[:WIRE]
    ins[0].start(0)
    first.fourth(0)
    first.fourth(1)
    ins[1].start(1)
    ins[0].finish(0)

    def block(step, carry):
        row = lax.div(step, 8)
        index = lax.rem(step, 8)
        rows_of = pl.ds(pl.multiple_of(row * 128, 128), 128)

        @pl.when(step == 8)
        def _():
            ins[1].finish(1)

        @pl.when(index == 0)
        def _():
            packed = jnp.transpose(wire[:, lanes(row * ROW, ROW)])
            packed = jnp.concatenate([packed, jnp.zeros((ROW, WIDE - WIRE), BF)], axis=1)
            packed_ref[:, rows_of, :] = packed.reshape(16, 128, WIDE)
            split_packed(packed, keys, queries)
            lane = iota((ROW, LANES), 1)
            values[...] = jnp.where(
                lane == LANES - 1, jnp.ones((ROW, LANES), BF), packed[:, LANES:]
            )

        rows = pl.ds(pl.multiple_of(index * 256, 256), 256)

        def scan(count):
            start = jnp.where(index < 4, 0, ROW - 256 * count)
            query = queries[rows, :]
            mine = column_ids(row_ref[row, :, lanes(index * 256, 256)])
            mine = jnp.concatenate([mine, mine], axis=1)
            top = jnp.full((256, LANES), NEG, F32)
            for part in range(count):
                span = lanes(start + part * 256, 256)
                score = dot_nt(query, keys[span, :])
                score = jnp.where(mine == row_ref[row, :, span], score, NEG)
                scores[:, part * 256 : part * 256 + 256] = score
                top = jnp.maximum(top, jnp.maximum(score[:, :LANES], score[:, LANES:]))
            top = jnp.max(top, axis=1, keepdims=True)
            total = jnp.zeros((256, LANES), F32)
            for part in range(count):
                span = lanes(start + part * 256, 256)
                expo = jnp.exp2(
                    (scores[:, part * 256 : part * 256 + 256] - top) * (SCALE * LOG2E)
                )
                total = total + dot(expo.astype(BF), values[span, :])
            mass = total[:, LANES - 1 :]
            total = total / mass
            turned_o = jnp.transpose(total)[VALUE_LANE : VALUE_LANE + HEAD_WIRE]
            o_own[:, lanes(row * ROW + index * 256, 256)] = turned_o.astype(BF)
            lane = iota((256, LANES), 1)
            logsum = top * (SCALE * LOG2E) + jnp.log2(mass)
            keep_ref[row, rows, :] = jnp.where(lane == 0, logsum, total)

        for count in (5, 6, 7, 8):
            pl.when((index == count - 5) | (index == 12 - count))(functools.partial(scan, count))

        @pl.when(step == 2)
        def _():
            first.fourth(2)

        @pl.when(step == 4)
        def _():
            first.fourth(3)

        @pl.when((step >= 6) & (lax.rem(step, 2) == 0) & (step < 14))
        def _():
            first.fifth(lax.div(step - 6, 2))

        for micro in range(2):
            pl.when(step == 8 * micro + 7)(functools.partial(outs[micro].start, micro))
        return carry

    lax.fori_loop(0, 16, block, 0)
    first.close()
    leave.wait()
    red.drain()
    first.drain()
    for micro in range(2):
        ins[micro].drain(micro)
        outs[micro].finish(micro)
    for micro in range(2):
        outs[micro].drain(micro)
    twin.ready()
    twin.drain()


def front(slab, first_slab, tokens, cotangent, lines, picture, tag):
    any_ = pl.BlockSpec(memory_space=pl.ANY)
    vmem = pl.BlockSpec(memory_space=pltpu.VMEM)
    sems = 2 * (3 * Gatherer.SEMS + 3) + 64 + 4
    full = (4, 2, 4, 2, 16, ATTN_TOTAL)
    return pl.pallas_call(
        front_kernel,
        out_shape=(
            jax.ShapeDtypeStruct((256, D), BF),
            jax.ShapeDtypeStruct((256, D), BF),
            jax.ShapeDtypeStruct((TAIL, QKV), BF),
            jax.ShapeDtypeStruct((TAIL, D), BF),
            jax.ShapeDtypeStruct((8, D), F32),
            jax.ShapeDtypeStruct((16, 256, WIDE), BF),
            jax.ShapeDtypeStruct((2, ROW, LANES), F32),
            jax.ShapeDtypeStruct((16, HEAD_WIRE, 256), BF),
            jax.ShapeDtypeStruct(full, BF),
            jax.ShapeDtypeStruct((4, 2, 4, 2, 16, FIRST_TOTAL), BF),
            jax.ShapeDtypeStruct((4, 2, 4, 2, 16, 512), BF),
            jax.ShapeDtypeStruct((TAIL, 512), BF),
        ),
        in_specs=[any_] * 3 + [vmem] * 10,
        out_specs=(vmem,) * 7 + (any_,) * 5,
        scratch_shapes=[
            pltpu.VMEM((4, 2, 4, 2, 16, 256), BF),
            pltpu.VMEM((TAIL, 256), BF),
            pltpu.VMEM(full, BF),
            pltpu.VMEM((256, D), BF),
            pltpu.VMEM((256, QKV), F32),
            pltpu.VMEM((ATTN_CHUNK // LANES, LEAD, LANES), F32),
            pltpu.VMEM((TAIL, 8 * ATTN_CHUNK), BF),
            pltpu.VMEM((8, D), F32),
            pltpu.VMEM((24, D), BF),
            pltpu.VMEM((16, WIRE, 256), BF),
            pltpu.VMEM((WIRE, 2 * ROW), BF),
            pltpu.VMEM((HEAD_WIRE, 2 * ROW), BF),
            pltpu.VMEM((ROW, LANES), BF),
            pltpu.VMEM((ROW, LANES), BF),
            pltpu.VMEM((ROW, LANES), BF),
            pltpu.VMEM((256, ROW), F32),
            pltpu.VMEM((2, ROW), jnp.int32),
            pltpu.VMEM((2, 1, ROW), F32),
            pltpu.SemaphoreType.DMA((sems,)),
            pltpu.SemaphoreType.DMA((sems,)),
            pltpu.SemaphoreType.DMA((2,)),
        ],
        compiler_params=mesh_params(tag),
        name="front",
    )(slab, first_slab, picture, tokens, cotangent, *lines)


def middle_kernel(
    attn,
    first,
    slab,
    o_ref,
    x_ref,
    g_ref,
    out_b_ref,
    vec_ref,
    bias_ref,
    place_ref,
    mixed_ref,
    do_ref,
    dmid_ref,
    gvec_ref,
    gbias_ref,
    dy_all,
    dpre_all,
    active_all,
    h_main_all,
    h_tail_all,
    g_main_all,
    g_tail_all,
    o_main_all,
    o_tail_all,
    dy,
    dpre_ref,
    active_ref,
    h_main_ref,
    h_tail_ref,
    g_main_ref,
    g_tail_ref,
    o_main_ref,
    o_tail_ref,
    out_a,
    weights,
    full,
    o_perm,
    mid,
    h2,
    result,
    dh2,
    wide,
    tail,
    bias,
    send,
    recv,
    local,
):
    place, core = here()
    red = Gatherer(SECOND_WIDTHS, place, core, slab, full, send, recv, 0)
    out_in = pltpu.make_async_copy(attn.at[:, pl.ds(QKV, D)], out_a, local.at[0])
    out_in.start()
    first_in = pltpu.make_async_copy(first, weights, local.at[1])
    first_in.start()
    base = 3 * Gatherer.SEMS + 3
    twin = Twin(place, core, send, recv, base)
    chunks = Twin(place, core, send, recv, base + 14)
    greet(line_peers(place, core) + [device_at(place, 1 - core)])
    red.start()
    bias[...] = jnp.zeros_like(bias)
    bias[:, :FF] = bias_ref[...].reshape(1, FF)
    blocks = jnp.transpose(o_ref[...].reshape(HEADS * HEAD_WIRE, 256))
    o_perm[...] = dot(blocks, place_ref[...]).astype(BF)
    red.second()
    out_in.wait()
    for part in range(3):
        columns = slice(384 * part, 384 * part + 384)
        value = dot(o_perm[:, :LEAD], out_a[:, columns])
        value = value + dot(o_perm[:, LEAD:], out_b_ref[:, columns])
        mid[:, columns] = x_ref[:, columns].astype(F32) + value + vec_ref[4:5, columns]
    unit, _ = normal(mid[...])
    h2[...] = (unit * vec_ref[2:3] + vec_ref[3:4]).astype(BF)
    for steps in (1, 2, 3):
        red.third(steps)

    def turn(value, main, rest, main_all, rest_all):
        turned = jnp.transpose(value)
        main[...] = turned[:LEAD].reshape(4, 2, 4, 2, 16, 256)
        rest[...] = turned[LEAD:]
        twin.give(main, main_all, 5)
        twin.give(rest, rest_all, 1)

    turn(o_perm[...], o_main_ref, o_tail_ref, o_main_all, o_tail_all)
    turn(h2[...], h_main_ref, h_tail_ref, h_main_all, h_tail_all)
    turn(g_ref[...], g_main_ref, g_tail_ref, g_main_all, g_tail_all)
    result[...] = jnp.zeros_like(result)
    dh2[...] = jnp.zeros_like(dh2)
    first_in.wait()

    def tile_of(ref, main):
        def read(tile):
            start = main + tile * LANES
            return ref[:, :, :, :, :, start : start + LANES].reshape(LEAD, LANES)

        return read

    spread_tail(tile_of(weights, 2 * FIRST), FIRST_CHUNK, wide, tail)
    red.fourth(0)
    red.fourth(1)

    def deliver(number, place_all):
        for item, (source, target) in enumerate(((dpre_ref, dpre_all), (active_ref, active_all))):
            chunks.pass_part(source.at[:, place_all], target, place_all, 2 * number + item)

    def chunk(ref, span, width, index, size, number):
        up_place = lanes(index * size, size)
        down_place = lanes(width + index * size, size)
        place_all = lanes(span + index * size, size)
        up = ref[:, :, :, :, :, up_place].reshape(LEAD, size)
        down = ref[:, :, :, :, :, down_place].reshape(LEAD, size)
        up_tail = tail[:, up_place]
        down_tail = tail[:, down_place]
        pre = dot(h2[:, :LEAD], up) + dot(h2[:, LEAD:], up_tail) + bias[:, place_all]
        square = pre * pre
        bend = jnp.tanh(TANH_A * pre * (1.0 + TANH_B * square))
        half = 0.5 * (1.0 + bend)
        active = (pre * half).astype(BF)
        slope = half + 0.5 * pre * (1.0 - bend * bend) * (TANH_A * (1.0 + 3.0 * TANH_B * square))
        back = dot(g_ref[:, :LEAD], down) + dot(g_ref[:, LEAD:], down_tail)
        dpre = (back * slope).astype(BF)
        active_ref[:, place_all] = active
        dpre_ref[:, place_all] = dpre
        active_t = jnp.transpose(active)
        dpre_t = jnp.transpose(dpre)
        result[:LEAD] += dot(down, active_t)
        result[LEAD:] += dot(down_tail, active_t)
        dh2[:LEAD] += dot(up, dpre_t)
        dh2[LEAD:] += dot(up_tail, dpre_t)
        gbias_ref[:, place_all] = column_total(dpre.astype(F32))
        deliver(number, place_all)

    def early(index, carry):
        chunk(weights, 0, FIRST, index, FIRST_STEP, index)

        @pl.when(index == 0)
        def _():
            red.fourth(2)
            red.fourth(3)

        @pl.when(index == 1)
        def _():
            for steps in range(4):
                red.fifth(steps)

        return carry

    lax.fori_loop(0, FIRST // FIRST_STEP, early, 0)
    red.close()
    spread_tail(tile_of(full, 2 * SECOND), SECOND_CHUNK, wide, tail)

    def late(index, carry):
        chunk(full, FIRST, SECOND, index, SECOND_STEP, index + FIRST // FIRST_STEP)
        return carry

    lax.fori_loop(0, SECOND // SECOND_STEP, late, 0)
    red.drain()
    gain = vec_ref[2:3]
    unit, rate = normal(mid[...])
    grad = jnp.transpose(dh2[...])
    gvec_ref[...] = jnp.zeros_like(gvec_ref)
    gvec_ref[0:1] = column_total(grad * unit)
    gvec_ref[1:2] = column_total(grad)
    gvec_ref[3:4] = column_total(g_ref[...].astype(F32))
    dmid = g_ref[...].astype(F32) + normal_back(unit, rate, gain, grad)
    dmid_ref[...] = dmid
    dlow = dmid.astype(BF)
    dy[...] = dlow
    twin.give(dy, dy_all, 0)
    gvec_ref[2:3] = column_total(dlow.astype(F32))
    mixed_ref[...] = (mid[...] + jnp.transpose(result[...]) + vec_ref[5:6]).astype(BF)
    low_t = jnp.transpose(dlow)
    result[:LEAD] = dot(out_a[...], low_t)
    result[LEAD:] = dot(out_b_ref[...], low_t)
    value = dot(place_ref[...], result[...].astype(BF)).astype(BF)
    do_ref[...] = value.reshape(HEADS, HEAD_WIRE, 256)
    twin.ready()
    twin.drain()
    number = 0
    for start, stop, size in ((0, FIRST, FIRST_STEP), (FIRST, FF_PAD, SECOND_STEP)):
        for spot in range(start, stop, size):
            for item, target in enumerate((dpre_all, active_all)):
                chunks.part_done(target, pl.ds(spot, size), 2 * number + item)
            number += 1


def middle(attn, first, slab, o, x, g, out_tail, vec, bias, tag):
    any_ = pl.BlockSpec(memory_space=pl.ANY)
    vmem = pl.BlockSpec(memory_space=pltpu.VMEM)
    sems = 3 * Gatherer.SEMS + 3 + 14 + 24
    turned = [(4, 2, 4, 2, 16, 256), (TAIL, 256)] * 3
    both = [(4, 2, 4, 2, 16, 512), (TAIL, 512)] * 3
    place = place_matrix().astype(BF)
    found = pl.pallas_call(
        middle_kernel,
        out_shape=tuple(
            [
                jax.ShapeDtypeStruct((256, D), BF),
                jax.ShapeDtypeStruct((HEADS, HEAD_WIRE, 256), BF),
                jax.ShapeDtypeStruct((256, D), F32),
                jax.ShapeDtypeStruct((8, D), F32),
                jax.ShapeDtypeStruct((1, FF_PAD), F32),
                jax.ShapeDtypeStruct((512, D), BF),
                jax.ShapeDtypeStruct((512, FF_PAD), BF),
                jax.ShapeDtypeStruct((512, FF_PAD), BF),
            ]
            + [jax.ShapeDtypeStruct(shape, BF) for shape in both]
        ),
        in_specs=[any_] * 3 + [vmem] * 7,
        out_specs=(vmem,) * 5 + (any_,) * 9,
        scratch_shapes=[
            pltpu.VMEM((256, D), BF),
            pltpu.VMEM((256, FF_PAD), BF),
            pltpu.VMEM((256, FF_PAD), BF),
        ]
        + [pltpu.VMEM(shape, BF) for shape in turned]
        + [
            pltpu.VMEM((LEAD, D), BF),
            pltpu.VMEM((4, 2, 4, 2, 16, FIRST_TOTAL), BF),
            pltpu.VMEM((4, 2, 4, 2, 16, SECOND_TOTAL), BF),
            pltpu.VMEM((256, D), BF),
            pltpu.VMEM((256, D), F32),
            pltpu.VMEM((256, D), BF),
            pltpu.VMEM((D, 256), F32),
            pltpu.VMEM((D, 256), F32),
            pltpu.VMEM((FIRST_CHUNK // LANES, LEAD, LANES), F32),
            pltpu.VMEM((TAIL, 8 * FIRST_CHUNK), BF),
            pltpu.VMEM((1, FF_PAD), F32),
            pltpu.SemaphoreType.DMA((sems,)),
            pltpu.SemaphoreType.DMA((sems,)),
            pltpu.SemaphoreType.DMA((2,)),
        ],
        compiler_params=mesh_params(tag),
        name="middle",
    )(attn, first, slab, o, x, g, out_tail, vec, bias, place)
    return found[:8], found[12:14], found[8:10], found[10:12]


class Everyone:
    def __init__(self, place, core, slots, send, recv, base):
        self.place, self.core = place, core
        self.slots, self.send, self.recv, self.base = slots, send, recv, base

    def start(self, stage, value):
        if stage == 3:
            spot, targets = self.core, [(1, device_at(self.place, 1 - self.core))]
        else:
            axis = AXES[stage]
            spot = self.place[axis]
            targets = [
                (over, device_at(moved(self.place, axis, over), self.core)) for over in (2, 1, 3)
            ]
        self.slots[stage, spot] = value
        for over, device in targets:
            index = self.base + stage * 3 + over - 1
            slot = self.slots.at[stage, spot]
            remote(slot, slot, self.send.at[index], self.recv.at[index], device).start()

    def finish(self, stage):
        count = 2 if stage == 3 else 4
        for over in range(1, count):
            index = self.base + stage * 3 + over - 1
            spot = 1 - self.core if stage == 3 else cycle(self.place[AXES[stage]], 4 - over)
            slot = self.slots.at[stage, spot]
            remote(
                slot, slot, self.send.at[index], self.recv.at[index], device_at(self.place, self.core)
            ).wait_recv()
        total = self.slots[stage, 0]
        for spot in range(1, count):
            total = total + self.slots[stage, spot]
        return total

    def drain(self):
        for stage in range(4):
            for over in range(1, 2 if stage == 3 else 4):
                index = self.base + stage * 3 + over - 1
                slot = self.slots.at[stage, 0]
                remote(
                    slot,
                    slot,
                    self.send.at[index],
                    self.recv.at[index],
                    device_at(self.place, self.core),
                ).wait_send()


def finish_kernel(
    dheads,
    weight,
    dy,
    dpre,
    active,
    h_main,
    h_tail,
    o_main,
    o_tail,
    h2_main,
    h2_tail,
    g_main,
    g_tail,
    tail_ref,
    x_ref,
    dmid_ref,
    vec_ref,
    gvec_ref,
    gup_ref,
    tokens_ref,
    total_ref,
    share_ref,
    second_ref,
    dheads_all,
    weight_all,
    flat,
    flat_all,
    dy_all,
    dpre_all,
    active_all,
    h_main_all,
    h_tail_all,
    o_main_all,
    o_tail_all,
    h2_main_all,
    h2_tail_all,
    g_main_all,
    g_tail_all,
    extra,
    dh,
    vectors,
    slots,
    *rest,
):
    buffers, (send, recv, local) = rest[:-3], rest[-3:]
    place, core = here()
    red = Reducer(ATTN_WIDTHS, place, core, buffers[:18], share_ref, send, recv)
    base = 3 * Reducer.SEMS
    late = Reducer(SECOND_WIDTHS, place, core, buffers[18:], second_ref, send, recv, base)
    base = 2 * base
    twin = Twin(place, core, send, recv, base)
    every = Everyone(place, core, slots, send, recv, base + 2)
    heads_in = pltpu.make_async_copy(dheads, dheads_all, local.at[0])
    heads_in.start()
    weight_in = pltpu.make_async_copy(weight.at[:, pl.ds(0, QKV)], weight_all, local.at[1])
    weight_in.start()
    greet(line_peers(place, core) + [device_at(place, 1 - core)])
    loads = []
    for source, target in (
        (h_main, h_main_all),
        (h_tail, h_tail_all),
        (o_main, o_main_all),
        (o_tail, o_tail_all),
        (dy, dy_all),
        (h2_main, h2_main_all),
        (h2_tail, h2_tail_all),
        (g_main, g_main_all),
        (g_tail, g_tail_all),
        (dpre.at[:, pl.ds(FIRST, SECOND)], dpre_all),
        (active.at[:, pl.ds(FIRST, SECOND)], active_all),
    ):
        copy = pltpu.make_async_copy(source, target, local.at[2 + len(loads)])
        copy.start()
        loads.append(copy)
    heads_in.wait()
    for head in range(HEADS):
        flat[:, PACK * head : PACK * head + PACK] = jnp.transpose(dheads_all[head])[:, :PACK]
    twin.give(flat, flat_all, 0)

    late_maker = Maker(
        late,
        [((h2_main_all, h2_tail_all), dpre_all), ((g_main_all, g_tail_all), active_all)],
        extra.at[pl.ds(0, SECOND_CHUNK // LANES)],
        SECOND_CHUNK,
    )
    maker = Maker(
        red,
        [((h_main_all, h_tail_all), flat_all), ((o_main_all, o_tail_all), dy_all)],
        extra,
        ATTN_CHUNK,
    )
    for copy in loads:
        copy.wait()
    late_maker.run()
    twin.ready()
    maker.run()
    dh[...] = jnp.zeros_like(dh)
    vectors[...] = jnp.zeros((VEC_ROWS, D), F32)
    vectors[2:6] = gvec_ref[:4]
    for row in range(4):
        span = slice(row * D, min((row + 1) * D, FF_PAD))
        vectors[VEC_UP + row : VEC_UP + row + 1, : span.stop - span.start] = gup_ref[:, span]
    weight_in.wait()

    for row in range(3):

        def columns(index, carry):
            span = lanes(row * D + index * 384, 384)
            value = flat[:, span]
            vectors[VEC_QKV + row : VEC_QKV + row + 1, lanes(index * 384, 384)] = column_total(
                value.astype(F32)
            )
            value_t = jnp.transpose(value)
            dh[:LEAD] += dot(weight_all[:, span], value_t)
            dh[LEAD:] += dot(tail_ref[:, span], value_t)
            return carry

        lax.fori_loop(0, 3, columns, 0)
    for spot in range(4):
        late.pass_on(spot)
    unit, rate = normal(x_ref[...].astype(F32))
    grad = jnp.transpose(dh[...])
    vectors[0:1] = column_total(grad * unit)
    vectors[1:2] = column_total(grad)
    every.start(0, vectors[...])
    for spot in range(4):
        red.pass_on(spot)
    total = dmid_ref[...] + normal_back(unit, rate, vec_ref[0:1], grad)
    tokens_ref[...] = total.astype(BF)
    every.start(1, every.finish(0))
    for over in (2, 1, 3):
        late.gather_side(over, False)
    late.gather_side(0, True)
    every.start(2, every.finish(1))
    for over in (2, 1, 3):
        red.gather_side(over, False)
    red.gather_side(0, True)
    every.start(3, every.finish(2))
    late.line_up()
    red.line_up()
    late.share()
    total_ref[...] = every.finish(3)
    red.share()
    late.close()
    red.close()
    twin.drain()
    every.drain()


def finish(dheads, weight, dy, dpre, active, turned, tail, x, dmid, vec, gvec, gup, tag):
    any_ = pl.BlockSpec(memory_space=pl.ANY)
    vmem = pl.BlockSpec(memory_space=pltpu.VMEM)
    sems = 6 * Reducer.SEMS + 2 + 12
    rows = [pltpu.VMEM((4, 2, 4, 2, 16, 512), BF), pltpu.VMEM((TAIL, 512), BF)]
    return pl.pallas_call(
        finish_kernel,
        out_shape=(
            jax.ShapeDtypeStruct((256, D), BF),
            jax.ShapeDtypeStruct((VEC_ROWS, D), F32),
            jax.ShapeDtypeStruct((16, ATTN_TOTAL), BF),
            jax.ShapeDtypeStruct((16, SECOND_TOTAL), BF),
        ),
        in_specs=[any_] * 13 + [vmem] * 6,
        out_specs=(vmem,) * 4,
        scratch_shapes=[
            pltpu.VMEM((HEADS, WIRE, 256), BF),
            pltpu.VMEM((LEAD, QKV), BF),
            pltpu.VMEM((256, QKV), BF),
            pltpu.VMEM((512, QKV), BF),
            pltpu.VMEM((512, D), BF),
            pltpu.VMEM((512, SECOND), BF),
            pltpu.VMEM((512, SECOND), BF),
        ]
        + rows * 4
        + [
            pltpu.VMEM((ATTN_CHUNK // LANES, LEAD, LANES), F32),
            pltpu.VMEM((D, 256), F32),
            pltpu.VMEM((VEC_ROWS, D), F32),
            pltpu.VMEM((4, 4, VEC_ROWS, D), F32),
        ]
        + Reducer.scratch(ATTN_WIDTHS)
        + Reducer.scratch(SECOND_WIDTHS)
        + [
            pltpu.SemaphoreType.DMA((sems,)),
            pltpu.SemaphoreType.DMA((sems,)),
            pltpu.SemaphoreType.DMA((13,)),
        ],
        compiler_params=mesh_params(tag),
        name="finish",
    )(dheads, weight, dy, dpre, active, *turned, tail, x, dmid, vec, gvec, gup)


def close_kernel(
    totals_ref,
    attn_ref,
    first_ref,
    second_ref,
    mixed_in,
    tokens_in,
    unmix_ref,
    mixed_ref,
    tokens_ref,
    query_ref,
    key_ref,
    value_ref,
    out_ref,
    up_ref,
    down_ref,
    gain1_ref,
    bias1_ref,
    gain2_ref,
    bias2_ref,
    bias_out_ref,
    bias_down_ref,
    bias_query_ref,
    bias_value_ref,
    bias_up_ref,
    attn,
    first,
    second,
    vec,
    stack,
):
    def unpack(share, full, main, chunk):
        full[0:16, :] = share[:, :main].astype(F32)
        rest = share[:, main : main + chunk].astype(F32)
        for row in range(2):
            for index in range(8):
                size = min(main - index * chunk, chunk)
                if size > 0:
                    start = index * chunk
                    spot = row * 8 + index
                    full[16 + row : 17 + row, start : start + size] = rest[
                        spot : spot + 1, :size
                    ]

    unpack(attn_ref, attn, ATTN_MAIN, ATTN_CHUNK)
    unpack(first_ref, first, 2 * FIRST, FIRST_CHUNK)
    unpack(second_ref, second, 2 * SECOND, SECOND_CHUNK)
    for head in range(HEADS):
        span = slice(head * HEAD_DIM, (head + 1) * HEAD_DIM)
        for index, ref in enumerate((key_ref, query_ref, value_ref)):
            start = head * PACK + index * HEAD_DIM
            ref[:, span] = attn[:18, start : start + HEAD_DIM]
    stack[0:256] = mixed_in[...]
    stack[256:512] = tokens_in[...]
    stack[512:544] = jnp.concatenate(
        [attn[:, QKV:ATTN_MAIN].astype(BF), jnp.zeros((8, D), BF)], axis=0
    )
    stack[544:576] = jnp.concatenate(
        [exact_parts(totals_ref[0:8, :]), jnp.zeros((8, D), BF)], axis=0
    )
    for part in range(3):
        columns = slice(384 * part, 384 * part + 384)
        value = dot(stack[...], unmix_ref[:, columns])
        mixed_ref[:, columns] = value[0:256].astype(BF)
        tokens_ref[:, columns] = value[256:512].astype(BF)
        out_ref[:, columns] = value[512:530]
        vec[0:8, columns] = value[544:552] + value[552:560] + value[560:568]
    lines = (gain1_ref, bias1_ref, gain2_ref, bias2_ref, bias_out_ref, bias_down_ref)
    for index, ref in enumerate(lines):
        ref[...] = vec[index : index + 1, :D].reshape(D)
    for row in range(3):
        vec[8:9, row * D : (row + 1) * D] = totals_ref[VEC_QKV + row : VEC_QKV + row + 1, :]
    for head in range(HEADS):
        span = slice(head * HEAD_DIM, (head + 1) * HEAD_DIM)
        for index, row in ((1, 9), (2, 10)):
            start = head * PACK + index * HEAD_DIM
            vec[row : row + 1, span] = vec[8:9, start : start + HEAD_DIM]
    bias_query_ref[...] = vec[9:10, :D].reshape(D)
    bias_value_ref[...] = vec[10:11, :D].reshape(D)
    for row in range(4):
        size = min(FF - row * D, D)
        vec[11:12, row * D : row * D + size] = totals_ref[
            VEC_UP + row : VEC_UP + row + 1, :size
        ]
    bias_up_ref[...] = vec[11:12, :FF].reshape(FF)
    up_ref[:, :FIRST] = first[:18, :FIRST]
    up_ref[:, FIRST:] = second[:18, : FF - FIRST]
    down_ref[:, :FIRST] = first[:18, FIRST : 2 * FIRST]
    down_ref[:, FIRST:] = second[:18, SECOND : SECOND + FF - FIRST]


def close_layer(totals, attn, first, second, mixed, tokens):
    line = jax.ShapeDtypeStruct((D,), F32)
    square = jax.ShapeDtypeStruct((18, D), F32)
    return pl.pallas_call(
        close_kernel,
        out_shape=(
            jax.ShapeDtypeStruct((256, D), BF),
            jax.ShapeDtypeStruct((256, D), BF),
            square,
            square,
            square,
            square,
            jax.ShapeDtypeStruct((18, FF), F32),
            jax.ShapeDtypeStruct((18, FF), F32),
            *([line] * 8),
            jax.ShapeDtypeStruct((FF,), F32),
        ),
        scratch_shapes=[
            pltpu.VMEM((24, ATTN_MAIN), F32),
            pltpu.VMEM((24, 2 * FIRST), F32),
            pltpu.VMEM((24, 2 * SECOND), F32),
            pltpu.VMEM((16, 4 * D), F32),
            pltpu.VMEM((576, D), BF),
        ],
        compiler_params=params(),
        name="close_layer",
    )(totals, attn, first, second, mixed, tokens, mix_matrix().T.astype(BF))


def pack_slab(weight, chunk, total):
    width = weight.shape[1]
    rest = jnp.pad(weight[16:], ((0, 0), (0, 8 * chunk - width))).reshape(16, chunk)
    return jnp.concatenate(
        [weight[:16], rest, jnp.zeros((16, total - width - chunk), weight.dtype)], axis=1
    )


def by_head(key, query, value):
    rows = key.shape[0]
    parts = [item.reshape(rows, HEADS, 1, HEAD_DIM) for item in (key, query, value)]
    return jnp.concatenate(parts, axis=2).reshape(rows, QKV)


def mixing():
    return onehot(iota((D, D), 0) == origin(iota((D, D), 1)))


def body(
    tokens,
    picture,
    cotangent,
    ln1_gain,
    ln1_bias,
    w_query,
    b_query,
    w_key,
    w_value,
    b_value,
    w_out,
    b_out,
    ln2_gain,
    ln2_bias,
    w_fc1,
    b_fc1,
    w_fc2,
    b_fc2,
):
    mix = mixing()
    out_cols = dot(w_out, mix).astype(BF)
    attn_slab = pack_slab(
        jnp.concatenate([by_head(w_key, w_query, w_value), out_cols], axis=1),
        ATTN_CHUNK,
        ATTN_TOTAL,
    )
    gap = ((0, 0), (0, FF_PAD - FF))
    up, down = jnp.pad(w_fc1, gap), jnp.pad(w_fc2.T, gap)
    first_slab = pack_slab(
        jnp.concatenate([up[:, :FIRST], down[:, :FIRST]], axis=1), FIRST_CHUNK, FIRST_TOTAL
    )
    second_slab = pack_slab(
        jnp.concatenate([up[:, FIRST:], down[:, FIRST:]], axis=1), SECOND_CHUNK, SECOND_TOTAL
    )
    lines = (ln1_gain, ln1_bias, ln2_gain, ln2_bias, b_out, b_fc2, b_query, b_value)
    x, g, attn_tail, out_tail, vec, packed, keep, o, attn, first, h_main, h_tail = front(
        attn_slab,
        first_slab,
        tokens.reshape(256, D),
        cotangent.reshape(256, D),
        lines,
        picture,
        0,
    )
    attn = attn.reshape(LEAD, ATTN_TOTAL)
    (mixed, go, dmid, gvec2, gbias1, dy, dpre, active), o_turned, h_turned, g_turned = middle(
        attn, first, second_slab, o, x, g, out_tail, vec, b_fc1, 2
    )
    first_share, dheads = attend_back_reduce(
        go, dpre, active, (*h_turned, *g_turned), packed, keep, picture, 3
    )
    gtokens, totals, attn_share, second_share = finish(
        dheads,
        attn,
        dy,
        dpre,
        active,
        (h_main, h_tail, *o_turned, *h_turned, *g_turned),
        attn_tail,
        x,
        dmid,
        vec,
        gvec2,
        gbias1,
        4,
    )
    (
        mixed,
        gtokens,
        grad_query,
        grad_key,
        grad_value,
        grad_out,
        grad_up,
        grad_down,
        grad_gain1,
        grad_bias1,
        grad_gain2,
        grad_bias2,
        grad_b_out,
        grad_b_fc2,
        grad_b_query,
        grad_b_value,
        grad_b_fc1,
    ) = close_layer(totals, attn_share, first_share, second_share, mixed, gtokens)
    return (
        mixed.reshape(2, 128, D),
        gtokens.reshape(2, 128, D),
        grad_gain1,
        grad_bias1,
        grad_query,
        grad_b_query,
        grad_key,
        grad_value,
        grad_b_value,
        grad_out,
        grad_b_out,
        grad_gain2,
        grad_bias2,
        grad_up,
        grad_b_fc1,
        grad_down.T,
        grad_b_fc2,
    )


def solution(mesh):
    placed = (
        P(None, ("fsdp", "rep"), None),
        P(),
        P(None, ("fsdp", "rep"), None),
        P(),
        P(),
        P("fsdp", None),
        P(),
        P("fsdp", None),
        P("fsdp", None),
        P(),
        P("fsdp", None),
        P(),
        P(),
        P(),
        P("fsdp", None),
        P(),
        P(None, "fsdp"),
        P(),
    )
    return jax.shard_map(
        body,
        mesh=mesh,
        in_specs=placed,
        out_specs=(
            P(None, ("fsdp", "rep"), None),
            P(None, ("fsdp", "rep"), None),
            P(),
            P(),
            P("fsdp", None),
            P(),
            P("fsdp", None),
            P("fsdp", None),
            P(),
            P("fsdp", None),
            P(),
            P(),
            P(),
            P("fsdp", None),
            P(),
            P(None, "fsdp"),
            P(),
        ),
        check_vma=False,
    )
```

```python
import functools

import jax
import jax.numpy as jnp
import numpy as np
from jax import lax
from jax.experimental import pallas as pl
from jax.experimental.pallas import tpu as pltpu
from jax.sharding import PartitionSpec as P

MESH = pl.DeviceIdType.MESH
BF = jnp.bfloat16
F32 = jnp.float32
LANES = 128
ORDERS = (("x", "y", "z"), ("y", "z", "x"), ("z", "x", "y"))
AXES = ("x", "y", "z")


def here():
    shard = lax.axis_index("fsdp")
    low = lax.axis_index("rep")
    place = {
        "x": lax.div(shard, 16),
        "y": lax.rem(lax.div(shard, 8), 2) * 2 + low,
        "z": lax.rem(lax.div(shard, 2), 4),
    }
    return place, lax.rem(shard, 2)


def moved(place, axis, steps):
    steps = steps % 4
    if steps == 0:
        return place
    other = dict(place)
    other[axis] = lax.rem(place[axis] + steps, 4)
    return other


def device_at(place, core):
    high = lax.div(place["y"], 2)
    return (((place["x"] * 2 + high) * 4 + place["z"]) * 2 + core, lax.rem(place["y"], 2))


def greet(peers):
    barrier = pltpu.get_barrier_semaphore()
    for peer in peers:
        pl.semaphore_signal(barrier, inc=1, device_id=peer, device_id_type=MESH)
    pl.semaphore_wait(barrier, len(peers))


def part_columns(part, half, widths):
    start = 2 * sum(widths[:part]) + half * widths[part]
    return pl.ds(pl.multiple_of(start, LANES), widths[part])


def piece_of(ref, part, widths, place, core):
    return ref.at[
        place["x"],
        lax.div(place["y"], 2),
        place["z"],
        core,
        :,
        part_columns(part, lax.rem(place["y"], 2), widths),
    ]


def block_of(ref, part, widths, place, core, axis, half=None):
    where = {"x": place["x"], "y": lax.div(place["y"], 2), "z": place["z"]}
    if axis == "y":
        where["y"] = pl.ds(0, 2) if half is None else pl.ds(half, 1)
        columns = pl.ds(2 * sum(widths[:part]), 2 * widths[part])
    else:
        where[axis] = pl.ds(0, 4) if half is None else pl.ds(2 * half, 2)
        columns = part_columns(part, lax.rem(place["y"], 2), widths)
    return ref.at[where["x"], where["y"], where["z"], core, :, columns]


def remote(source, target, send, recv, device):
    return pltpu.make_async_remote_copy(
        src_ref=source,
        dst_ref=target,
        send_sem=send,
        recv_sem=recv,
        device_id=device,
        device_id_type=MESH,
    )


def cycle(value, steps):
    return lax.rem(value + steps, 4)


def turned_by(place, axis, steps):
    other = dict(place)
    other[axis] = cycle(place[axis], steps)
    return other


class Gatherer:
    SEMS = 3 + 3 + 8 + 8 + 16
    KINDS = {"one": 0, "two": 3, "three": 6, "four": 14, "twin": 22}

    def __init__(self, widths, place, core, own, full, send, recv, base):
        self.widths, self.place, self.core = widths, place, core
        self.own, self.full, self.send, self.recv, self.base = own, full, send, recv, base
        self.twin = device_at(place, 1 - core)

    def slot(self, part, kind, index):
        return self.base + part * self.SEMS + self.KINDS[kind] + index

    def push(self, source, target, slot, device):
        remote(source, target, self.send.at[slot], self.recv.at[slot], device).start()

    def arrived(self, region, slot):
        remote(region, region, self.send.at[slot], self.recv.at[slot], self.twin).wait_recv()

    def sent(self, region, slot):
        remote(region, region, self.send.at[slot], self.recv.at[slot], self.twin).wait_send()

    def block(self, part, place, half=None, core=None):
        core = self.core if core is None else core
        return block_of(self.full, part, self.widths, place, core, ORDERS[part][0], half)

    def keep(self, part):
        low = lax.rem(self.place["y"], 2)
        source = self.own.at[:, part_columns(part, low, self.widths)]
        target = piece_of(self.full, part, self.widths, self.place, self.core)
        return source, target, pltpu.make_async_copy(
            source, target, self.recv.at[self.base + 3 * self.SEMS + part]
        )

    def start(self):
        for part, (one, two, three) in enumerate(ORDERS):
            source, target, copy = self.keep(part)
            copy.start()
            for steps in (1, 3, 2):
                device = device_at(turned_by(self.place, one, steps), self.core)
                self.push(source, target, self.slot(part, "one", steps - 1), device)

    def second(self):
        for part, (one, two, three) in enumerate(ORDERS):
            self.keep(part)[2].wait()
            for steps in (1, 3, 2):
                origin = turned_by(self.place, one, 4 - steps)
                region = piece_of(self.full, part, self.widths, origin, self.core)
                self.arrived(region, self.slot(part, "one", steps - 1))
            block = self.block(part, self.place)
            for steps in (1, 3, 2):
                device = device_at(turned_by(self.place, two, steps), self.core)
                self.push(block, block, self.slot(part, "two", steps - 1), device)
        self.spread(0)

    def spread(self, steps):
        for part, (one, two, three) in enumerate(ORDERS):
            block = self.block(part, turned_by(self.place, two, 4 - steps))
            for index, way in enumerate((1, 3)):
                device = device_at(turned_by(self.place, three, way), self.core)
                self.push(block, block, self.slot(part, "three", index * 4 + steps), device)
            self.push(block, block, self.slot(part, "twin", steps), self.twin)

    def third(self, steps):
        for part, (one, two, three) in enumerate(ORDERS):
            block = self.block(part, turned_by(self.place, two, 4 - steps))
            self.arrived(block, self.slot(part, "two", steps - 1))
        self.spread(steps)

    def fourth(self, steps):
        for part, (one, two, three) in enumerate(ORDERS):
            side = turned_by(self.place, two, 4 - steps)
            for index, way in enumerate((1, 3)):
                origin = turned_by(side, three, 4 - way)
                block = self.block(part, origin)
                self.arrived(block, self.slot(part, "three", index * 4 + steps))
                half = self.block(part, origin, index)
                device = device_at(turned_by(self.place, three, way), self.core)
                self.push(half, half, self.slot(part, "four", index * 4 + steps), device)
                self.push(block, block, self.slot(part, "twin", way * 4 + steps), self.twin)

    def fifth(self, steps):
        for part, (one, two, three) in enumerate(ORDERS):
            origin = turned_by(turned_by(self.place, two, 4 - steps), three, 2)
            for index in range(2):
                half = self.block(part, origin, index)
                self.arrived(half, self.slot(part, "four", index * 4 + steps))
            block = self.block(part, origin)
            self.push(block, block, self.slot(part, "twin", 8 + steps), self.twin)

    def close(self):
        for part, (one, two, three) in enumerate(ORDERS):
            for way in range(4):
                for steps in range(4):
                    origin = moved(moved(self.place, two, -steps), three, -way)
                    region = self.block(part, origin, core=1 - self.core)
                    self.arrived(region, self.slot(part, "twin", way * 4 + steps))

    def drain(self):
        for part in range(3):
            piece = piece_of(self.full, part, self.widths, self.place, self.core)
            block = self.block(part, self.place)
            half = self.block(part, self.place, 0)
            for kind, region, count in (
                ("one", piece, 3),
                ("two", block, 3),
                ("three", block, 8),
                ("four", half, 8),
                ("twin", block, 16),
            ):
                for index in range(count):
                    self.sent(region, self.slot(part, kind, index))


class Reducer:
    SEMS = 8 + 8 + 3 + 3 + 1
    KINDS = {"mid": 0, "far": 8, "side": 16, "line": 19, "done": 22}

    def __init__(self, widths, place, core, buffers, out, send, recv, base=0):
        self.widths, self.place, self.core, self.base = widths, place, core, base
        self.acc, self.mid, self.far, self.side, self.line, self.done = [
            buffers[3 * i : 3 * i + 3] for i in range(6)
        ]
        self.out, self.send, self.recv = out, send, recv
        self.me = device_at(place, core)

    @staticmethod
    def scratch(widths):
        found = []
        for lead, half in (((4, 4), 1), ((2, 4), 2), ((2, 4), 1), ((3,), 1)):
            for width, (one, two, three) in zip(widths, ORDERS):
                if one == "y":
                    found.append(pltpu.VMEM(lead + (2 // half, 16, 2 * width), BF))
                else:
                    found.append(pltpu.VMEM(lead + (4 // half, 16, width), BF))
        found += [pltpu.VMEM((3, 16, width), BF) for width in widths]
        found += [pltpu.VMEM((16, width), BF) for width in widths]
        return found

    def slot(self, part, kind, index):
        return self.base + part * self.SEMS + self.KINDS[kind] + index

    def push(self, source, target, slot, device):
        remote(source, target, self.send.at[slot], self.recv.at[slot], device).start()

    def arrived(self, region, slot):
        remote(region, region, self.send.at[slot], self.recv.at[slot], self.me).wait_recv()

    def sent(self, region, slot):
        remote(region, region, self.send.at[slot], self.recv.at[slot], self.me).wait_send()

    def add(self, target, *terms):
        for index in range(target.shape[0]):
            total = target[index].astype(F32)
            for term in terms:
                total = total + term[index].astype(F32)
            target[index] = total.astype(BF)

    def half_of(self, ref, half):
        size = ref.shape[0] // 2
        return ref.at[pl.ds(half * size, size)]

    def far_out(self):
        for spot in range(4):
            for part, (one, two, three) in enumerate(ORDERS):
                for half, way in ((0, 3), (1, 1)):
                    self.push(
                        self.half_of(self.acc[part].at[2, spot], half),
                        self.mid[part].at[half, spot],
                        self.slot(part, "mid", half * 4 + spot),
                        device_at(moved(self.place, three, way), self.core),
                    )

    def pass_on(self, spot):
        for part, (one, two, three) in enumerate(ORDERS):
            for half, way in ((0, 3), (1, 1)):
                self.arrived(
                    self.mid[part].at[half, spot], self.slot(part, "mid", half * 4 + spot)
                )
                self.add(
                    self.half_of(self.acc[part].at[way, spot], half), self.mid[part].at[half, spot]
                )
                self.push(
                    self.acc[part].at[way, spot],
                    self.far[part].at[half, spot],
                    self.slot(part, "far", half * 4 + spot),
                    device_at(moved(self.place, three, way), self.core),
                )

    def gather_side(self, over, last):
        for part, (one, two, three) in enumerate(ORDERS):
            spot = cycle(self.place[two], over)
            for half in range(2):
                self.arrived(
                    self.far[part].at[half, spot], self.slot(part, "far", half * 4 + spot)
                )
            self.add(
                self.acc[part].at[0, spot], self.far[part].at[0, spot], self.far[part].at[1, spot]
            )

            def give(part=part, two=two, spot=spot):
                other = dict(self.place)
                other[two] = spot
                self.push(
                    self.acc[part].at[0, spot],
                    self.side[part].at[over - 1],
                    self.slot(part, "side", over - 1),
                    device_at(other, self.core),
                )

            if last is False:
                give()
            elif last is not True:
                pl.when(jnp.logical_not(last))(give)

    def piece(self, part, axis, spot):
        own = self.acc[part].at[0, self.place[ORDERS[part][1]]]
        if axis == "y":
            start = pl.multiple_of(lax.rem(spot["y"], 2) * self.widths[part], LANES)
            return own.at[lax.div(spot["y"], 2), :, pl.ds(start, self.widths[part])]
        return own.at[spot[axis]]

    def line_up(self):
        for part, (one, two, three) in enumerate(ORDERS):
            for over in range(3):
                self.arrived(self.side[part].at[over], self.slot(part, "side", over))
            own = self.acc[part].at[0, self.place[two]]
            self.add(own, self.side[part].at[0], self.side[part].at[1], self.side[part].at[2])
            for over in (2, 1, 3):
                spot = moved(self.place, one, over)
                self.push(
                    self.piece(part, one, spot),
                    self.line[part].at[over - 1],
                    self.slot(part, "line", over - 1),
                    device_at(spot, self.core),
                )

    def share(self):
        low = lax.rem(self.place["y"], 2)
        partner = (lax.axis_index("fsdp"), 1 - low)
        for part, (one, two, three) in enumerate(ORDERS):
            for over in range(3):
                self.arrived(self.line[part].at[over], self.slot(part, "line", over))
            total = self.piece(part, one, self.place)[...].astype(F32)
            for over in range(3):
                total = total + self.line[part][over].astype(F32)
            self.done[part][...] = total.astype(BF)
            columns = part_columns(part, low, self.widths)
            self.push(
                self.done[part], self.out.at[:, columns], self.slot(part, "done", 0), partner
            )
            self.out[:, columns] = self.done[part][...]

    def close(self):
        low = lax.rem(self.place["y"], 2)
        for part, (one, two, three) in enumerate(ORDERS):
            self.arrived(
                self.out.at[:, part_columns(part, 1 - low, self.widths)],
                self.slot(part, "done", 0),
            )
            for half in range(2):
                for spot in range(4):
                    index = half * 4 + spot
                    self.sent(self.mid[part].at[half, spot], self.slot(part, "mid", index))
                    self.sent(self.far[part].at[half, spot], self.slot(part, "far", index))
            for over in range(3):
                self.sent(self.side[part].at[over], self.slot(part, "side", over))
                self.sent(self.line[part].at[over], self.slot(part, "line", over))
            self.sent(self.done[part], self.slot(part, "done", 0))


class Maker:
    def __init__(self, reducer, sources, extra, chunk):
        self.red, self.sources, self.extra, self.chunk = reducer, sources, extra, chunk
        self.main = sum(item[1].shape[1] for item in sources)

    def pack_tail(self):
        start = 0
        pieces = []
        for turned, right in self.sources:
            pieces.append((start, start + right.shape[1], turned, right))
            start += right.shape[1]
        for index in range(8):
            low, high = index * self.chunk, (index + 1) * self.chunk
            for first, last, turned, right in pieces:
                a, b = max(low, first), min(high, last)
                if a < b:
                    value = dot(turned[1][...], right[:, a - first : b - first])
                    self.scatter(index, a - low, value)
            if high > self.main:
                a = max(low, self.main)
                self.scatter(index, a - low, jnp.zeros((TAIL, high - a), F32))

    def scatter(self, index, start, value):
        for tile in range(value.shape[1] // LANES):
            self.extra[start // LANES + tile, pl.ds(index, TAIL, stride=8), :] = value[
                :, tile * LANES : (tile + 1) * LANES
            ]

    def rows(self, ref):
        core = self.red.core
        if len(ref.shape) == 2:
            groups = [
                ref[pl.ds(pl.multiple_of((2 * index + core) * 16, 16), 16)] for index in range(32)
            ]
            return jnp.concatenate(groups, axis=0)
        return ref[:, :, :, core].reshape(512, ref.shape[-1])

    def columns(self, part, half):
        width = self.red.widths[part]
        low = 2 * sum(self.red.widths[:part]) + half * width
        high = low + width
        first = 0
        found = []
        for turned, right in self.sources:
            last = first + right.shape[1]
            a, b = max(low, first), min(high, last)
            if a < b:
                left = self.rows(turned[0])
                found.append(dot(left, right[:, a - first : b - first]).astype(BF))
            first = last
        a, b = max(low, first), min(high, first + self.chunk)
        if a < b:
            for tile in range((a - first) // LANES, (b - first) // LANES):
                found.append(self.rows(self.extra.at[tile]).astype(BF))
        a = max(low, first + self.chunk)
        if a < high:
            found.append(jnp.zeros((512, high - a), BF))
        return found[0] if len(found) == 1 else jnp.concatenate(found, axis=1)

    def make(self, part):
        red, width = self.red, self.red.widths[part]
        acc = red.acc[part]
        three = ORDERS[part][2]
        own = red.place[three]

        def ahead(spot):
            return cycle(spot + 4 - own, 0)

        for half in range(2):
            value = self.columns(part, half).reshape(4, 2, 4, 16, width)
            if three == "z":
                for spot in range(4):
                    for high in range(2):
                        acc[ahead(spot), 2 * high + half] = value[:, high, spot]
            elif three == "x":
                for spot in range(4):
                    for z in range(4):
                        acc[ahead(spot), z, :, :, half * width : (half + 1) * width] = value[
                            spot, :, z
                        ]
            else:
                for high in range(2):
                    for x in range(4):
                        acc[ahead(2 * high + half), x] = value[x, high]

    def run(self):
        self.pack_tail()
        for part in range(3):
            self.make(part)
        self.red.far_out()


SWAP_ORDER = (9, 11, 5, 13, 7, 15, 1, 3, 8, 10, 4, 12, 6, 14, 2)


class Swapper:
    def __init__(self, place, core, own, full, send, recv, base):
        self.place, self.core = place, core
        self.own, self.full, self.send, self.recv, self.base = own, full, send, recv, base
        self.low = lax.rem(place["y"], 2)
        self.mine = (place["z"] * 2 + core) * 2 + self.low
        self.group = lax.div(lax.axis_index("fsdp"), 8) * 8

    def member(self, k, sign=1):
        z = lax.rem(self.place["z"] + (4 + sign * (k // 4)), 4)
        core = lax.rem(self.core + (k // 2) % 2, 2)
        low = lax.rem(self.low + k % 2, 2)
        return (z * 2 + core) * 2 + low

    def device(self, index):
        return (self.group + lax.div(index, 2), lax.rem(index, 2))

    def peers(self):
        return [self.device(self.member(k)) for k in range(1, 16)]

    def view(self, ref, index, micro):
        if len(ref.shape) == 3:
            return ref.at[index, :, pl.ds(micro * 128, 128)]
        return ref.at[:, pl.ds(pl.multiple_of(micro * ROW + index * 128, 128), 128)]

    def start(self, micro):
        for k in SWAP_ORDER:
            target = self.member(k)
            remote(
                self.view(self.own, target, micro),
                self.view(self.full, self.mine, micro),
                self.send.at[self.base + k],
                self.recv.at[self.base + k],
                self.device(target),
            ).start()
        pltpu.make_async_copy(
            self.view(self.own, self.mine, micro),
            self.view(self.full, self.mine, micro),
            self.send.at[self.base],
        ).start()

    def finish(self, micro):
        pltpu.make_async_copy(
            self.view(self.own, self.mine, micro),
            self.view(self.full, self.mine, micro),
            self.send.at[self.base],
        ).wait()
        for k in range(1, 16):
            region = self.view(self.full, self.member(k, -1), micro)
            remote(
                region,
                region,
                self.send.at[self.base + k],
                self.recv.at[self.base + k],
                self.device(self.mine),
            ).wait_recv()

    def drain(self, micro):
        for k in range(1, 16):
            region = self.view(self.own, self.member(k), micro)
            remote(
                region,
                region,
                self.send.at[self.base + k],
                self.recv.at[self.base + k],
                self.device(self.mine),
            ).wait_send()


def line_peers(place, core):
    peers = []
    for axis in AXES:
        for steps in (1, 2, 3):
            peers.append(device_at(moved(place, axis, steps), core))
    return peers


D = 1152
HEADS = 16
HEAD_DIM = 72
FF = 4304
ROW = 2048
EPS = 1e-06
NEG = -1e30
SCALE = HEAD_DIM**-0.5
LEAD = 1024
TAIL = 128
PACK = 3 * HEAD_DIM
WIDE = 256
WIRE = 224
HEAD_WIRE = 80
VALUE_LANE = 16
FF_PAD = 4352
QKV = HEADS * PACK
ATTN_MAIN = QKV + D
ATTN_CHUNK = 640
ATTN_TOTAL = 5376
MLP_MAIN = 2 * FF_PAD
MLP_CHUNK = 1152
MLP_TOTAL = 9984
ATTN_WIDTHS = (896, 896, 896)
MLP_WIDTHS = (1664, 1664, 1664)
FIRST = 3072
FIRST_CHUNK = 768
FIRST_TOTAL = 6912
FIRST_WIDTHS = (896, 1408, 1152)
FIRST_STEP = 768
SECOND = FF_PAD - FIRST
SECOND_CHUNK = 384
SECOND_TOTAL = 3072
SECOND_WIDTHS = (512, 512, 512)
SECOND_STEP = 640
LOG2E = 1.4426950408889634
QUERIES = 512
KEYS = 512
BLOCKS = ROW // QUERIES
TANH_A = 0.7978845608028654
TANH_B = 0.044715


def dot(left, right):
    return jnp.dot(left, right, preferred_element_type=F32)


def dot_nt(left, right):
    return lax.dot_general(left, right, (((1,), (1,)), ((), ())), preferred_element_type=F32)


def dot_tn(left, right):
    return lax.dot_general(left, right, (((0,), (0,)), ((), ())), preferred_element_type=F32)


def origin(index):
    lead = (index >> 4) * 18 + (index & 15)
    rest = index - LEAD
    tail = (rest >> 1) * 18 + 16 + (rest & 1)
    return jnp.where(index < LEAD, lead, tail)


def iota(shape, axis):
    return lax.broadcasted_iota(jnp.int32, shape, axis)


def onehot(mask):
    return mask.astype(F32).astype(BF)


def normal(values):
    center = values - jnp.mean(values, axis=-1, keepdims=True)
    rate = lax.rsqrt(jnp.mean(center * center, axis=-1, keepdims=True) + EPS)
    return center * rate, rate


def normal_back(unit, rate, gain, grad):
    inner = grad * gain
    first = jnp.mean(inner, axis=-1, keepdims=True)
    second = jnp.mean(inner * unit, axis=-1, keepdims=True)
    return rate * (inner - first - unit * second)


def exact_parts(values):
    high = values.astype(BF)
    rest = values - high.astype(F32)
    middle_part = rest.astype(BF)
    low = (rest - middle_part.astype(F32)).astype(BF)
    return jnp.concatenate([high, middle_part, low], axis=0)


def column_total(values):
    return jnp.sum(values, axis=0, keepdims=True)


def lanes(start, size):
    return pl.ds(pl.multiple_of(start, LANES), size)


def params(limit=60):
    return pltpu.CompilerParams(vmem_limit_bytes=limit << 20)


PERMUTED = np.concatenate(
    [np.arange(64)[:, None] * 18 + np.arange(16), np.arange(64)[:, None] * 18 + [16, 17]], axis=1
)
PERMUTED = np.concatenate([PERMUTED[:, :16].reshape(-1), PERMUTED[:, 16:].reshape(-1)])


def mix_matrix():
    matrix = np.zeros((D, D), np.float32)
    matrix[PERMUTED, np.arange(D)] = 1.0
    return matrix


def place_matrix():
    matrix = np.zeros((HEADS, HEAD_WIRE, D), np.float32)
    matrix[:, :HEAD_DIM] = mix_matrix().reshape(HEADS, HEAD_DIM, D)
    return matrix.reshape(HEADS * HEAD_WIRE, D)


def mesh_params(tag, limit=62):
    return pltpu.CompilerParams(
        collective_id=tag, has_side_effects=True, vmem_limit_bytes=limit << 20
    )


class Twin:
    def __init__(self, place, core, send, recv, base):
        self.core, self.device = core, device_at(place, 1 - core)
        self.send, self.recv, self.base = send, recv, base
        self.items = []

    def half(self, ref, axis, core):
        size = ref.shape[axis] // 2
        if axis == 0:
            return ref.at[pl.ds(pl.multiple_of(core * size, size), size)]
        lead = (slice(None),) * (len(ref.shape) - 1)
        return ref.at[lead + (pl.ds(pl.multiple_of(core * size, LANES), size),)]

    def give(self, source, target, axis):
        index = self.base + 2 * len(self.items)
        place = self.half(target, axis, self.core)
        pltpu.make_async_copy(source, place, self.recv.at[index + 1]).start()
        remote(source, place, self.send.at[index], self.recv.at[index], self.device).start()
        self.items.append((source, target, axis, index))

    def ready(self):
        for source, target, axis, index in self.items:
            place = self.half(target, axis, self.core)
            pltpu.make_async_copy(source, place, self.recv.at[index + 1]).wait()
            other = self.half(target, axis, 1 - self.core)
            remote(
                other, other, self.send.at[index], self.recv.at[index], self.device
            ).wait_recv()

    def pass_part(self, source, target, columns, number):
        index = self.base + 2 * number
        place = target.at[pl.ds(pl.multiple_of(self.core * 256, 256), 256), columns]
        pltpu.make_async_copy(source, place, self.recv.at[index + 1]).start()
        remote(source, place, self.send.at[index], self.recv.at[index], self.device).start()

    def part_done(self, target, columns, number):
        index = self.base + 2 * number
        place = target.at[pl.ds(pl.multiple_of(self.core * 256, 256), 256), columns]
        other = target.at[pl.ds(pl.multiple_of((1 - self.core) * 256, 256), 256), columns]
        pltpu.make_async_copy(place, place, self.recv.at[index + 1]).wait()
        copy = remote(other, other, self.send.at[index], self.recv.at[index], self.device)
        copy.wait_recv()
        copy.wait_send()

    def drain(self):
        for source, target, axis, index in self.items:
            place = self.half(target, axis, self.core)
            remote(
                place, place, self.send.at[index], self.recv.at[index], self.device
            ).wait_send()


def back_kernel(
    go,
    dpre,
    active,
    h_main,
    h_tail,
    g_main,
    g_tail,
    picture,
    packed_ref,
    keep_ref,
    share_ref,
    dheads,
    go_all,
    grads,
    wire,
    backs,
    dpre_all,
    active_all,
    h_main_all,
    h_tail_all,
    g_main_all,
    g_tail_all,
    extra,
    keys,
    queries,
    ids,
    dkeys,
    dvalues,
    found,
    row_ref,
    *rest,
):
    buffers, (send, recv, local) = rest[:-3], rest[-3:]
    place, core = here()
    red = Reducer(FIRST_WIDTHS, place, core, buffers, share_ref, send, recv)
    base = 3 * Reducer.SEMS
    ins = [Swapper(place, core, go, go_all, send, recv, base + 16 * m) for m in range(2)]
    base = base + 32
    outs = [Swapper(place, core, wire, dheads, send, recv, base + 16 * m) for m in range(2)]
    greet(line_peers(place, core) + swap_only(ins[0]))
    for micro in range(2):
        ins[micro].start(micro)
    loads = []
    for source, target in (
        (h_main, h_main_all),
        (h_tail, h_tail_all),
        (g_main, g_main_all),
        (g_tail, g_tail_all),
        (dpre.at[:, pl.ds(0, FIRST)], dpre_all),
        (active.at[:, pl.ds(0, FIRST)], active_all),
    ):
        copy = pltpu.make_async_copy(source, target, local.at[1 + len(loads)])
        copy.start()
        loads.append(copy)
    maker = Maker(
        red,
        [((h_main_all, h_tail_all), dpre_all), ((g_main_all, g_tail_all), active_all)],
        extra,
        FIRST_CHUNK,
    )
    ids_in = fetch_ids(picture, found, local.at[0])
    ids_in.start()
    ids_in.wait()
    for micro in range(2):
        row_ref[micro] = found[micro : micro + 1].astype(F32)
    for copy in loads:
        copy.wait()
    maker.run()
    ins[0].finish(0)

    def block(step, carry):
        row = lax.div(step, BLOCKS)
        index = lax.rem(step, BLOCKS)
        tokens = pl.ds(pl.multiple_of(row * 128, 128), 128)

        @pl.when(step == BLOCKS)
        def _():
            ins[1].finish(1)

        @pl.when(index == 0)
        def _():
            back_row = jnp.concatenate(
                [
                    jnp.zeros((VALUE_LANE, ROW), BF),
                    go_all[:, lanes(row * ROW, ROW)],
                    jnp.zeros((LANES - VALUE_LANE - HEAD_WIRE, ROW), BF),
                ],
                axis=0,
            )
            backs[...] = jnp.transpose(back_row)
            packed = packed_ref[:, tokens, :].reshape(ROW, WIDE)
            split_packed(packed, keys, queries)
            for part in range(ROW // LANES):
                span = slice(part * LANES, (part + 1) * LANES)
                ids[span, :] = column_ids(row_ref[row, :, span])
            dkeys[...] = jnp.zeros_like(dkeys)
            dvalues[...] = jnp.zeros_like(dvalues)

        rows = pl.ds(pl.multiple_of(index * QUERIES, QUERIES), QUERIES)

        def scan(count):
            start = jnp.where(index < 2, 0, BLOCKS - count)
            query = queries[rows, :]
            back = backs[rows, :]
            mine = row_ref[row, :, lanes(index * QUERIES, QUERIES)]
            kept = keep_ref[row, rows, :]
            inner = jnp.sum(back.astype(F32) * kept, axis=1, keepdims=True)
            lane = iota((QUERIES, LANES), 1)
            stats = jnp.transpose(jnp.where(lane == 0, kept, inner))
            logsum = stats[0:1]
            inner = stats[1:2]
            total = jnp.zeros((QUERIES, LANES), F32)
            for part in range(count):
                span = pl.ds(pl.multiple_of((start + part) * KEYS, KEYS), KEYS)
                blocks = pl.ds((start + part) * (KEYS // 128), KEYS // 128)
                value = packed_ref[blocks, tokens, LANES:].reshape(KEYS, LANES)
                allowed = jnp.concatenate([ids[span, :]] * (QUERIES // LANES), axis=1)
                score = dot_nt(keys[span, :], query) * (SCALE * LOG2E) - logsum
                prob = jnp.exp2(jnp.where(allowed == mine, score, NEG))
                grad = (prob * (dot_nt(value, back) - inner)).astype(BF)
                dvalues[span, :] += dot(prob.astype(BF), back)
                dkeys[span, :] += dot(grad, query)
                total = total + dot_tn(grad, keys[span, :])
            total = total * SCALE
            moved_q = jnp.concatenate(
                [
                    jnp.zeros((QUERIES, HEAD_DIM), F32),
                    total[:, :HEAD_DIM],
                    jnp.zeros((QUERIES, WIDE - 2 * HEAD_DIM), F32),
                ],
                axis=1,
            )
            grads[rows, :] = moved_q.astype(BF)

        edge = (index == 0) | (index == BLOCKS - 1)
        pl.when(edge)(functools.partial(scan, 3))
        pl.when(jnp.logical_not(edge))(functools.partial(scan, 4))

        @pl.when(index == BLOCKS - 1)
        def _():
            wide = jnp.concatenate([dkeys[...] * SCALE, dvalues[...]], axis=1)
            lane = iota((ROW, WIDE), 1)
            old = grads[...]
            inside = (lane >= HEAD_DIM) & (lane < 2 * HEAD_DIM)
            whole = jnp.where(inside, old, wide.astype(BF))
            wire[:, lanes(row * ROW, ROW)] = jnp.transpose(whole)[:WIRE]
            for micro in range(2):
                pl.when(row == micro)(functools.partial(outs[micro].start, micro))

        @pl.when(step == 1)
        def _():
            for spot in range(4):
                red.pass_on(spot)

        @pl.when(step >= 4)
        def _():
            red.gather_side(lax.rem(step - 4 + 1, 4), step == 7)

        return carry

    lax.fori_loop(0, 2 * BLOCKS, block, 0)
    red.line_up()
    red.share()
    red.close()
    for micro in range(2):
        outs[micro].finish(micro)
    for micro in range(2):
        ins[micro].drain(micro)
    for micro in range(2):
        outs[micro].drain(micro)


def attend_back_reduce(go, dpre, active, turned, packed, keep, picture, tag):
    any_ = pl.BlockSpec(memory_space=pl.ANY)
    vmem = pl.BlockSpec(memory_space=pltpu.VMEM)
    sems = 3 * Reducer.SEMS + 64
    return pl.pallas_call(
        back_kernel,
        out_shape=(
            jax.ShapeDtypeStruct((16, FIRST_TOTAL), BF),
            jax.ShapeDtypeStruct((16, WIRE, 256), BF),
        ),
        in_specs=[any_] * 8 + [vmem] * 2,
        out_specs=(vmem, any_),
        scratch_shapes=[
            pltpu.VMEM((HEAD_WIRE, 2 * ROW), BF),
            pltpu.VMEM((ROW, WIDE), BF),
            pltpu.VMEM((WIRE, 2 * ROW), BF),
            pltpu.VMEM((ROW, LANES), BF),
            pltpu.VMEM((512, FIRST), BF),
            pltpu.VMEM((512, FIRST), BF),
            pltpu.VMEM((4, 2, 4, 2, 16, 512), BF),
            pltpu.VMEM((TAIL, 512), BF),
            pltpu.VMEM((4, 2, 4, 2, 16, 512), BF),
            pltpu.VMEM((TAIL, 512), BF),
            pltpu.VMEM((FIRST_CHUNK // LANES, LEAD, LANES), F32),
            pltpu.VMEM((ROW, LANES), BF),
            pltpu.VMEM((ROW, LANES), BF),
            pltpu.VMEM((ROW, LANES), F32),
            pltpu.VMEM((ROW, LANES), F32),
            pltpu.VMEM((ROW, LANES), F32),
            pltpu.VMEM((2, ROW), jnp.int32),
            pltpu.VMEM((2, 1, ROW), F32),
        ]
        + Reducer.scratch(FIRST_WIDTHS)
        + [
            pltpu.SemaphoreType.DMA((sems,)),
            pltpu.SemaphoreType.DMA((sems,)),
            pltpu.SemaphoreType.DMA((7,)),
        ],
        compiler_params=mesh_params(tag),
        name="attend_back_reduce",
    )(go, dpre, active, *turned, picture, packed, keep)


VEC_ROWS = 16
VEC_QKV = 6
VEC_UP = 9


def spread_tail(source, chunk, wide, tail):
    for tile in range(chunk // LANES):
        wide[tile] = source(tile).astype(F32)
        for index in range(8):
            start = index * chunk + tile * LANES
            picked = wide[tile, pl.ds(index, TAIL, stride=8), :]
            tail[:, start : start + LANES] = picked.astype(BF)


def column_ids(row_ids):
    size = row_ids.shape[1]
    return jnp.transpose(jnp.broadcast_to(row_ids, (LANES, size)))


def fetch_ids(picture, found, sem):
    start = pl.multiple_of(lax.div(lax.axis_index("fsdp"), 8) * ROW, ROW)
    return pltpu.make_async_copy(picture.at[:, pl.ds(start, ROW)], found, sem)


def split_packed(packed, keys, queries):
    lane = iota((ROW, LANES), 1)
    zero = jnp.zeros((ROW, LANES), BF)
    keys[...] = jnp.where(lane < HEAD_DIM, packed[:, :LANES], zero)
    queries[...] = jnp.concatenate(
        [packed[:, HEAD_DIM : 2 * HEAD_DIM], jnp.zeros((ROW, LANES - HEAD_DIM), BF)], axis=1
    )


def swap_only(swapper):
    return [swapper.device(swapper.member(k)) for k in range(1, 16) if k not in (1, 4, 8, 12)]


def pack_rows(sources, width, chunk, slab, rest, block):
    slab[...] = jnp.zeros_like(slab)
    rest[...] = jnp.zeros_like(rest)
    for index, (ref, start, stop) in enumerate(sources):
        place = slice(index * width, index * width + stop - start)
        slab[:, place] = ref[0:16, start:stop]
        rest[:, place] = ref[16:18, start:stop].astype(F32)
    main = len(sources) * width
    for row in range(2):
        for index in range(8):
            spot = row * 8 + index
            block[spot : spot + 1, :chunk] = rest[
                row : row + 1, index * chunk : (index + 1) * chunk
            ]
    slab[:, main : main + chunk] = block[:, :chunk].astype(BF)


def front_kernel(
    slab,
    picture,
    tokens_ref,
    cotangent_ref,
    up_ref,
    down_ref,
    *refs,
):
    lines, rest = refs[:8], refs[8:]
    run_front(slab, picture, tokens_ref, cotangent_ref, up_ref, down_ref, lines, *rest)


def run_front(
    slab,
    picture,
    tokens_ref,
    cotangent_ref,
    up_ref,
    down_ref,
    lines,
    second_slab,
    x_ref,
    g_ref,
    tail_ref,
    out_tail_ref,
    mixed_vec_ref,
    packed_ref,
    keep_ref,
    o_all,
    weight_out,
    first_out,
    h_main_all,
    h_tail_all,
    first_slab,
    rest,
    rest_block,
    h_main,
    h_tail,
    full,
    low,
    flat,
    wide,
    tail,
    vec_ref,
    vec_parts,
    heads,
    wire,
    o_own,
    keys,
    queries,
    values,
    scores,
    found,
    row_ref,
    send,
    recv,
    local,
):
    place, core = here()
    red = Gatherer(ATTN_WIDTHS, place, core, slab, full, send, recv, 0)
    base = 3 * Gatherer.SEMS + 3
    first = Gatherer(FIRST_WIDTHS, place, core, first_slab, first_out, send, recv, base)
    base = 2 * base
    ins = [Swapper(place, core, heads, wire, send, recv, base + 16 * m) for m in range(2)]
    base = base + 32
    outs = [Swapper(place, core, o_own, o_all, send, recv, base + 16 * m) for m in range(2)]
    twin = Twin(place, core, send, recv, base + 32)
    greet(line_peers(place, core) + swap_only(ins[0]))
    red.start()
    pack_rows(
        [(up_ref, 0, FIRST), (down_ref, 0, FIRST)],
        FIRST,
        FIRST_CHUNK,
        first_slab,
        rest,
        rest_block,
    )
    first.start()
    ids_in = fetch_ids(picture, found, local.at[0])
    ids_in.start()
    for index, line in enumerate(lines):
        vec_ref[index : index + 1, :] = line[...].reshape(1, D)
    vec_parts[...] = exact_parts(vec_ref[...])

    def mix(index, carry):
        columns = lanes(index * LANES, LANES)
        column = onehot(iota((D, LANES), 0) == origin(index * LANES + iota((D, LANES), 1)))
        x_ref[:, columns] = dot(tokens_ref[...], column).astype(BF)
        g_ref[:, columns] = dot(cotangent_ref[...], column).astype(BF)
        parts = dot(vec_parts[...], column)
        mixed_vec_ref[:, columns] = parts[0:8] + parts[8:16] + parts[16:24]
        return carry

    lax.fori_loop(0, 3, mix, 0)
    red.second()
    lax.fori_loop(3, 9, mix, 0)
    pack_rows(
        [(up_ref, FIRST, FF), (down_ref, FIRST, FF)],
        SECOND,
        SECOND_CHUNK,
        second_slab,
        rest,
        rest_block,
    )
    unit, _ = normal(x_ref[...].astype(F32))
    low[...] = (unit * mixed_vec_ref[0:1] + mixed_vec_ref[1:2]).astype(BF)
    for steps in (1, 2, 3):
        red.third(steps)
    turned = jnp.transpose(low[...])
    h_main[...] = turned[:LEAD].reshape(4, 2, 4, 2, 16, 256)
    h_tail[...] = turned[LEAD:]
    twin.give(h_main, h_main_all, 5)
    twin.give(h_tail, h_tail_all, 1)
    ids_in.wait()
    for micro in range(2):
        row_ref[micro] = found[micro : micro + 1].astype(F32)
    for steps in range(4):
        red.fourth(steps)
    first.second()
    for steps in range(4):
        red.fifth(steps)
    red.close()
    leave = pltpu.make_async_copy(full, weight_out, local.at[1])
    leave.start()

    def packed_tile(tile):
        start = ATTN_MAIN + tile * LANES
        return full[:, :, :, :, :, start : start + LANES].reshape(LEAD, LANES)

    for steps in (1, 2, 3):
        first.third(steps)
    spread_tail(packed_tile, ATTN_CHUNK, wide, tail)
    tail_ref[...] = tail[:, :QKV]
    out_tail_ref[...] = tail[:, QKV:ATTN_MAIN]

    def columns(index, carry):
        span = lanes(index * 384, 384)
        weight = full[:, :, :, :, :, span].reshape(LEAD, 384)
        flat[:, span] = dot(low[:, :LEAD], weight) + dot(low[:, LEAD:], tail[:, span])
        return carry

    lax.fori_loop(0, QKV // 384, columns, 0)
    for head in range(HEADS):
        span = slice(head * HEAD_DIM, (head + 1) * HEAD_DIM)
        bias = jnp.concatenate(
            [jnp.zeros((1, HEAD_DIM), F32), vec_ref[6:7, span], vec_ref[7:8, span]], axis=1
        )
        block = flat[:, PACK * head : PACK * head + PACK] + bias
        block = jnp.concatenate([block, jnp.zeros((256, WIDE - PACK), F32)], axis=1)
        heads[head] = jnp.transpose(block.astype(BF))[:WIRE]
    ins[0].start(0)
    first.fourth(0)
    first.fourth(1)
    ins[1].start(1)
    ins[0].finish(0)

    def block(step, carry):
        row = lax.div(step, 8)
        index = lax.rem(step, 8)
        rows_of = pl.ds(pl.multiple_of(row * 128, 128), 128)

        @pl.when(step == 8)
        def _():
            ins[1].finish(1)

        @pl.when(index == 0)
        def _():
            packed = jnp.transpose(wire[:, lanes(row * ROW, ROW)])
            packed = jnp.concatenate([packed, jnp.zeros((ROW, WIDE - WIRE), BF)], axis=1)
            packed_ref[:, rows_of, :] = packed.reshape(16, 128, WIDE)
            split_packed(packed, keys, queries)
            lane = iota((ROW, LANES), 1)
            values[...] = jnp.where(
                lane == LANES - 1, jnp.ones((ROW, LANES), BF), packed[:, LANES:]
            )

        rows = pl.ds(pl.multiple_of(index * 256, 256), 256)

        def scan(count):
            start = jnp.where(index < 4, 0, ROW - 256 * count)
            query = queries[rows, :]
            mine = column_ids(row_ref[row, :, lanes(index * 256, 256)])
            mine = jnp.concatenate([mine, mine], axis=1)
            top = jnp.full((256, LANES), NEG, F32)
            for part in range(count):
                span = lanes(start + part * 256, 256)
                score = dot_nt(query, keys[span, :])
                score = jnp.where(mine == row_ref[row, :, span], score, NEG)
                scores[:, part * 256 : part * 256 + 256] = score
                top = jnp.maximum(top, jnp.maximum(score[:, :LANES], score[:, LANES:]))
            top = jnp.max(top, axis=1, keepdims=True)
            total = jnp.zeros((256, LANES), F32)
            for part in range(count):
                span = lanes(start + part * 256, 256)
                expo = jnp.exp2(
                    (scores[:, part * 256 : part * 256 + 256] - top) * (SCALE * LOG2E)
                )
                total = total + dot(expo.astype(BF), values[span, :])
            mass = total[:, LANES - 1 :]
            total = total / mass
            turned_o = jnp.transpose(total)[VALUE_LANE : VALUE_LANE + HEAD_WIRE]
            o_own[:, lanes(row * ROW + index * 256, 256)] = turned_o.astype(BF)
            lane = iota((256, LANES), 1)
            logsum = top * (SCALE * LOG2E) + jnp.log2(mass)
            keep_ref[row, rows, :] = jnp.where(lane == 0, logsum, total)

        for count in (5, 6, 7, 8):
            pl.when((index == count - 5) | (index == 12 - count))(functools.partial(scan, count))

        @pl.when(step == 2)
        def _():
            first.fourth(2)

        @pl.when(step == 4)
        def _():
            first.fourth(3)

        @pl.when((step >= 6) & (lax.rem(step, 2) == 0) & (step < 14))
        def _():
            first.fifth(lax.div(step - 6, 2))

        for micro in range(2):
            pl.when(step == 8 * micro + 7)(functools.partial(outs[micro].start, micro))
        return carry

    lax.fori_loop(0, 16, block, 0)
    first.close()
    leave.wait()
    red.drain()
    first.drain()
    for micro in range(2):
        ins[micro].drain(micro)
        outs[micro].finish(micro)
    for micro in range(2):
        outs[micro].drain(micro)
    twin.ready()
    twin.drain()


def front(slab, up, down, tokens, cotangent, lines, picture, tag):
    any_ = pl.BlockSpec(memory_space=pl.ANY)
    vmem = pl.BlockSpec(memory_space=pltpu.VMEM)
    sems = 2 * (3 * Gatherer.SEMS + 3) + 64 + 4
    full = (4, 2, 4, 2, 16, ATTN_TOTAL)
    return pl.pallas_call(
        front_kernel,
        out_shape=(
            jax.ShapeDtypeStruct((16, SECOND_TOTAL), BF),
            jax.ShapeDtypeStruct((256, D), BF),
            jax.ShapeDtypeStruct((256, D), BF),
            jax.ShapeDtypeStruct((TAIL, QKV), BF),
            jax.ShapeDtypeStruct((TAIL, D), BF),
            jax.ShapeDtypeStruct((8, D), F32),
            jax.ShapeDtypeStruct((16, 256, WIDE), BF),
            jax.ShapeDtypeStruct((2, ROW, LANES), F32),
            jax.ShapeDtypeStruct((16, HEAD_WIRE, 256), BF),
            jax.ShapeDtypeStruct(full, BF),
            jax.ShapeDtypeStruct((4, 2, 4, 2, 16, FIRST_TOTAL), BF),
            jax.ShapeDtypeStruct((4, 2, 4, 2, 16, 512), BF),
            jax.ShapeDtypeStruct((TAIL, 512), BF),
        ),
        in_specs=[any_] * 2 + [vmem] * 12,
        out_specs=(vmem,) * 8 + (any_,) * 5,
        scratch_shapes=[
            pltpu.VMEM((16, FIRST_TOTAL), BF),
            pltpu.VMEM((2, 8 * FIRST_CHUNK), F32),
            pltpu.VMEM((16, FIRST_CHUNK), F32),
            pltpu.VMEM((4, 2, 4, 2, 16, 256), BF),
            pltpu.VMEM((TAIL, 256), BF),
            pltpu.VMEM(full, BF),
            pltpu.VMEM((256, D), BF),
            pltpu.VMEM((256, QKV), F32),
            pltpu.VMEM((ATTN_CHUNK // LANES, LEAD, LANES), F32),
            pltpu.VMEM((TAIL, 8 * ATTN_CHUNK), BF),
            pltpu.VMEM((8, D), F32),
            pltpu.VMEM((24, D), BF),
            pltpu.VMEM((16, WIRE, 256), BF),
            pltpu.VMEM((WIRE, 2 * ROW), BF),
            pltpu.VMEM((HEAD_WIRE, 2 * ROW), BF),
            pltpu.VMEM((ROW, LANES), BF),
            pltpu.VMEM((ROW, LANES), BF),
            pltpu.VMEM((ROW, LANES), BF),
            pltpu.VMEM((256, ROW), F32),
            pltpu.VMEM((2, ROW), jnp.int32),
            pltpu.VMEM((2, 1, ROW), F32),
            pltpu.SemaphoreType.DMA((sems,)),
            pltpu.SemaphoreType.DMA((sems,)),
            pltpu.SemaphoreType.DMA((2,)),
        ],
        compiler_params=mesh_params(tag),
        name="front",
    )(slab, picture, tokens, cotangent, up, down, *lines)


def middle_kernel(
    attn,
    first,
    slab,
    o_ref,
    x_ref,
    g_ref,
    out_b_ref,
    vec_ref,
    bias_ref,
    place_ref,
    mixed_ref,
    do_ref,
    dmid_ref,
    gvec_ref,
    gbias_ref,
    dy_all,
    dpre_all,
    active_all,
    h_main_all,
    h_tail_all,
    g_main_all,
    g_tail_all,
    o_main_all,
    o_tail_all,
    dy,
    dpre_ref,
    active_ref,
    h_main_ref,
    h_tail_ref,
    g_main_ref,
    g_tail_ref,
    o_main_ref,
    o_tail_ref,
    out_a,
    weights,
    full,
    o_perm,
    mid,
    h2,
    result,
    dh2,
    wide,
    tail,
    bias,
    send,
    recv,
    local,
):
    place, core = here()
    red = Gatherer(SECOND_WIDTHS, place, core, slab, full, send, recv, 0)
    out_in = pltpu.make_async_copy(attn.at[:, pl.ds(QKV, D)], out_a, local.at[0])
    out_in.start()
    first_in = pltpu.make_async_copy(first, weights, local.at[1])
    first_in.start()
    base = 3 * Gatherer.SEMS + 3
    twin = Twin(place, core, send, recv, base)
    chunks = Twin(place, core, send, recv, base + 14)
    greet(line_peers(place, core) + [device_at(place, 1 - core)])
    red.start()
    bias[...] = jnp.zeros_like(bias)
    bias[:, :FF] = bias_ref[...].reshape(1, FF)
    blocks = jnp.transpose(o_ref[...].reshape(HEADS * HEAD_WIRE, 256))
    o_perm[...] = dot(blocks, place_ref[...]).astype(BF)
    red.second()
    out_in.wait()
    for part in range(3):
        columns = slice(384 * part, 384 * part + 384)
        value = dot(o_perm[:, :LEAD], out_a[:, columns])
        value = value + dot(o_perm[:, LEAD:], out_b_ref[:, columns])
        mid[:, columns] = x_ref[:, columns].astype(F32) + value + vec_ref[4:5, columns]
    unit, _ = normal(mid[...])
    h2[...] = (unit * vec_ref[2:3] + vec_ref[3:4]).astype(BF)
    for steps in (1, 2, 3):
        red.third(steps)

    def turn(value, main, rest, main_all, rest_all):
        turned = jnp.transpose(value)
        main[...] = turned[:LEAD].reshape(4, 2, 4, 2, 16, 256)
        rest[...] = turned[LEAD:]
        twin.give(main, main_all, 5)
        twin.give(rest, rest_all, 1)

    turn(o_perm[...], o_main_ref, o_tail_ref, o_main_all, o_tail_all)
    turn(h2[...], h_main_ref, h_tail_ref, h_main_all, h_tail_all)
    turn(g_ref[...], g_main_ref, g_tail_ref, g_main_all, g_tail_all)
    result[...] = jnp.zeros_like(result)
    dh2[...] = jnp.zeros_like(dh2)
    first_in.wait()

    def tile_of(ref, main):
        def read(tile):
            start = main + tile * LANES
            return ref[:, :, :, :, :, start : start + LANES].reshape(LEAD, LANES)

        return read

    spread_tail(tile_of(weights, 2 * FIRST), FIRST_CHUNK, wide, tail)
    red.fourth(0)
    red.fourth(1)

    def deliver(number, place_all):
        for item, (source, target) in enumerate(((dpre_ref, dpre_all), (active_ref, active_all))):
            chunks.pass_part(source.at[:, place_all], target, place_all, 2 * number + item)

    def chunk(ref, span, width, index, size, number):
        up_place = lanes(index * size, size)
        down_place = lanes(width + index * size, size)
        place_all = lanes(span + index * size, size)
        up = ref[:, :, :, :, :, up_place].reshape(LEAD, size)
        down = ref[:, :, :, :, :, down_place].reshape(LEAD, size)
        up_tail = tail[:, up_place]
        down_tail = tail[:, down_place]
        pre = dot(h2[:, :LEAD], up) + dot(h2[:, LEAD:], up_tail) + bias[:, place_all]
        square = pre * pre
        bend = jnp.tanh(TANH_A * pre * (1.0 + TANH_B * square))
        half = 0.5 * (1.0 + bend)
        active = (pre * half).astype(BF)
        slope = half + 0.5 * pre * (1.0 - bend * bend) * (TANH_A * (1.0 + 3.0 * TANH_B * square))
        back = dot(g_ref[:, :LEAD], down) + dot(g_ref[:, LEAD:], down_tail)
        dpre = (back * slope).astype(BF)
        active_ref[:, place_all] = active
        dpre_ref[:, place_all] = dpre
        active_t = jnp.transpose(active)
        dpre_t = jnp.transpose(dpre)
        result[:LEAD] += dot(down, active_t)
        result[LEAD:] += dot(down_tail, active_t)
        dh2[:LEAD] += dot(up, dpre_t)
        dh2[LEAD:] += dot(up_tail, dpre_t)
        gbias_ref[:, place_all] = column_total(dpre.astype(F32))
        deliver(number, place_all)

    def early(index, carry):
        chunk(weights, 0, FIRST, index, FIRST_STEP, index)

        @pl.when(index == 0)
        def _():
            red.fourth(2)
            red.fourth(3)

        @pl.when(index == 1)
        def _():
            for steps in range(4):
                red.fifth(steps)

        return carry

    lax.fori_loop(0, FIRST // FIRST_STEP, early, 0)
    red.close()
    spread_tail(tile_of(full, 2 * SECOND), SECOND_CHUNK, wide, tail)

    def late(index, carry):
        chunk(full, FIRST, SECOND, index, SECOND_STEP, index + FIRST // FIRST_STEP)
        return carry

    lax.fori_loop(0, SECOND // SECOND_STEP, late, 0)
    red.drain()
    gain = vec_ref[2:3]
    unit, rate = normal(mid[...])
    grad = jnp.transpose(dh2[...])
    gvec_ref[...] = jnp.zeros_like(gvec_ref)
    gvec_ref[0:1] = column_total(grad * unit)
    gvec_ref[1:2] = column_total(grad)
    gvec_ref[3:4] = column_total(g_ref[...].astype(F32))
    dmid = g_ref[...].astype(F32) + normal_back(unit, rate, gain, grad)
    dmid_ref[...] = dmid
    dlow = dmid.astype(BF)
    dy[...] = dlow
    twin.give(dy, dy_all, 0)
    gvec_ref[2:3] = column_total(dlow.astype(F32))
    mixed_ref[...] = (mid[...] + jnp.transpose(result[...]) + vec_ref[5:6]).astype(BF)
    low_t = jnp.transpose(dlow)
    result[:LEAD] = dot(out_a[...], low_t)
    result[LEAD:] = dot(out_b_ref[...], low_t)
    value = dot(place_ref[...], result[...].astype(BF)).astype(BF)
    do_ref[...] = value.reshape(HEADS, HEAD_WIRE, 256)
    twin.ready()
    twin.drain()
    number = 0
    for start, stop, size in ((0, FIRST, FIRST_STEP), (FIRST, FF_PAD, SECOND_STEP)):
        for spot in range(start, stop, size):
            for item, target in enumerate((dpre_all, active_all)):
                chunks.part_done(target, pl.ds(spot, size), 2 * number + item)
            number += 1


def middle(attn, first, slab, o, x, g, out_tail, vec, bias, tag):
    any_ = pl.BlockSpec(memory_space=pl.ANY)
    vmem = pl.BlockSpec(memory_space=pltpu.VMEM)
    sems = 3 * Gatherer.SEMS + 3 + 14 + 24
    turned = [(4, 2, 4, 2, 16, 256), (TAIL, 256)] * 3
    both = [(4, 2, 4, 2, 16, 512), (TAIL, 512)] * 3
    place = place_matrix().astype(BF)
    found = pl.pallas_call(
        middle_kernel,
        out_shape=tuple(
            [
                jax.ShapeDtypeStruct((256, D), BF),
                jax.ShapeDtypeStruct((HEADS, HEAD_WIRE, 256), BF),
                jax.ShapeDtypeStruct((256, D), F32),
                jax.ShapeDtypeStruct((8, D), F32),
                jax.ShapeDtypeStruct((1, FF_PAD), F32),
                jax.ShapeDtypeStruct((512, D), BF),
                jax.ShapeDtypeStruct((512, FF_PAD), BF),
                jax.ShapeDtypeStruct((512, FF_PAD), BF),
            ]
            + [jax.ShapeDtypeStruct(shape, BF) for shape in both]
        ),
        in_specs=[any_] * 3 + [vmem] * 7,
        out_specs=(vmem,) * 5 + (any_,) * 9,
        scratch_shapes=[
            pltpu.VMEM((256, D), BF),
            pltpu.VMEM((256, FF_PAD), BF),
            pltpu.VMEM((256, FF_PAD), BF),
        ]
        + [pltpu.VMEM(shape, BF) for shape in turned]
        + [
            pltpu.VMEM((LEAD, D), BF),
            pltpu.VMEM((4, 2, 4, 2, 16, FIRST_TOTAL), BF),
            pltpu.VMEM((4, 2, 4, 2, 16, SECOND_TOTAL), BF),
            pltpu.VMEM((256, D), BF),
            pltpu.VMEM((256, D), F32),
            pltpu.VMEM((256, D), BF),
            pltpu.VMEM((D, 256), F32),
            pltpu.VMEM((D, 256), F32),
            pltpu.VMEM((FIRST_CHUNK // LANES, LEAD, LANES), F32),
            pltpu.VMEM((TAIL, 8 * FIRST_CHUNK), BF),
            pltpu.VMEM((1, FF_PAD), F32),
            pltpu.SemaphoreType.DMA((sems,)),
            pltpu.SemaphoreType.DMA((sems,)),
            pltpu.SemaphoreType.DMA((2,)),
        ],
        compiler_params=mesh_params(tag),
        name="middle",
    )(attn, first, slab, o, x, g, out_tail, vec, bias, place)
    return found[:8], found[12:14], found[8:10], found[10:12]


class Everyone:
    def __init__(self, place, core, slots, send, recv, base):
        self.place, self.core = place, core
        self.slots, self.send, self.recv, self.base = slots, send, recv, base

    def start(self, stage, value):
        if stage == 3:
            spot, targets = self.core, [(1, device_at(self.place, 1 - self.core))]
        else:
            axis = AXES[stage]
            spot = self.place[axis]
            targets = [
                (over, device_at(moved(self.place, axis, over), self.core)) for over in (2, 1, 3)
            ]
        self.slots[stage, spot] = value.astype(BF)
        for over, device in targets:
            index = self.base + stage * 3 + over - 1
            slot = self.slots.at[stage, spot]
            remote(slot, slot, self.send.at[index], self.recv.at[index], device).start()

    def finish(self, stage):
        count = 2 if stage == 3 else 4
        for over in range(1, count):
            index = self.base + stage * 3 + over - 1
            spot = 1 - self.core if stage == 3 else cycle(self.place[AXES[stage]], 4 - over)
            slot = self.slots.at[stage, spot]
            remote(
                slot, slot, self.send.at[index], self.recv.at[index], device_at(self.place, self.core)
            ).wait_recv()
        total = self.slots[stage, 0].astype(F32)
        for spot in range(1, count):
            total = total + self.slots[stage, spot].astype(F32)
        return total

    def drain(self):
        for stage in range(4):
            for over in range(1, 2 if stage == 3 else 4):
                index = self.base + stage * 3 + over - 1
                slot = self.slots.at[stage, 0]
                remote(
                    slot,
                    slot,
                    self.send.at[index],
                    self.recv.at[index],
                    device_at(self.place, self.core),
                ).wait_send()


def finish_kernel(
    dheads,
    weight,
    dy,
    dpre,
    active,
    h_main,
    h_tail,
    o_main,
    o_tail,
    h2_main,
    h2_tail,
    g_main,
    g_tail,
    tail_ref,
    x_ref,
    dmid_ref,
    vec_ref,
    gvec_ref,
    gup_ref,
    tokens_ref,
    total_ref,
    share_ref,
    second_ref,
    dheads_all,
    weight_all,
    flat,
    flat_all,
    dy_all,
    dpre_all,
    active_all,
    h_main_all,
    h_tail_all,
    o_main_all,
    o_tail_all,
    h2_main_all,
    h2_tail_all,
    g_main_all,
    g_tail_all,
    extra,
    dh,
    vectors,
    slots,
    *rest,
):
    buffers, (send, recv, local) = rest[:-3], rest[-3:]
    place, core = here()
    red = Reducer(ATTN_WIDTHS, place, core, buffers[:18], share_ref, send, recv)
    base = 3 * Reducer.SEMS
    late = Reducer(SECOND_WIDTHS, place, core, buffers[18:], second_ref, send, recv, base)
    base = 2 * base
    twin = Twin(place, core, send, recv, base)
    every = Everyone(place, core, slots, send, recv, base + 2)
    heads_in = pltpu.make_async_copy(dheads, dheads_all, local.at[0])
    heads_in.start()
    weight_in = pltpu.make_async_copy(weight.at[:, pl.ds(0, QKV)], weight_all, local.at[1])
    weight_in.start()
    greet(line_peers(place, core) + [device_at(place, 1 - core)])
    loads = []
    for source, target in (
        (h_main, h_main_all),
        (h_tail, h_tail_all),
        (o_main, o_main_all),
        (o_tail, o_tail_all),
        (dy, dy_all),
        (h2_main, h2_main_all),
        (h2_tail, h2_tail_all),
        (g_main, g_main_all),
        (g_tail, g_tail_all),
        (dpre.at[:, pl.ds(FIRST, SECOND)], dpre_all),
        (active.at[:, pl.ds(FIRST, SECOND)], active_all),
    ):
        copy = pltpu.make_async_copy(source, target, local.at[2 + len(loads)])
        copy.start()
        loads.append(copy)
    heads_in.wait()
    for head in range(HEADS):
        flat[:, PACK * head : PACK * head + PACK] = jnp.transpose(dheads_all[head])[:, :PACK]
    twin.give(flat, flat_all, 0)

    late_maker = Maker(
        late,
        [((h2_main_all, h2_tail_all), dpre_all), ((g_main_all, g_tail_all), active_all)],
        extra.at[pl.ds(0, SECOND_CHUNK // LANES)],
        SECOND_CHUNK,
    )
    maker = Maker(
        red,
        [((h_main_all, h_tail_all), flat_all), ((o_main_all, o_tail_all), dy_all)],
        extra,
        ATTN_CHUNK,
    )
    for copy in loads:
        copy.wait()
    late_maker.run()
    twin.ready()
    maker.run()
    dh[...] = jnp.zeros_like(dh)
    vectors[...] = jnp.zeros((VEC_ROWS, D), F32)
    vectors[2:6] = gvec_ref[:4]
    for row in range(4):
        span = slice(row * D, min((row + 1) * D, FF_PAD))
        vectors[VEC_UP + row : VEC_UP + row + 1, : span.stop - span.start] = gup_ref[:, span]
    weight_in.wait()

    for row in range(3):

        def columns(index, carry):
            span = lanes(row * D + index * 384, 384)
            value = flat[:, span]
            vectors[VEC_QKV + row : VEC_QKV + row + 1, lanes(index * 384, 384)] = column_total(
                value.astype(F32)
            )
            value_t = jnp.transpose(value)
            dh[:LEAD] += dot(weight_all[:, span], value_t)
            dh[LEAD:] += dot(tail_ref[:, span], value_t)
            return carry

        lax.fori_loop(0, 3, columns, 0)
    for spot in range(4):
        late.pass_on(spot)
    unit, rate = normal(x_ref[...].astype(F32))
    grad = jnp.transpose(dh[...])
    vectors[0:1] = column_total(grad * unit)
    vectors[1:2] = column_total(grad)
    every.start(0, vectors[...])
    for spot in range(4):
        red.pass_on(spot)
    total = dmid_ref[...] + normal_back(unit, rate, vec_ref[0:1], grad)
    tokens_ref[...] = total.astype(BF)
    every.start(1, every.finish(0))
    for over in (2, 1, 3):
        late.gather_side(over, False)
    late.gather_side(0, True)
    every.start(2, every.finish(1))
    for over in (2, 1, 3):
        red.gather_side(over, False)
    red.gather_side(0, True)
    every.start(3, every.finish(2))
    late.line_up()
    red.line_up()
    late.share()
    total_ref[...] = every.finish(3)
    red.share()
    late.close()
    red.close()
    twin.drain()
    every.drain()


def finish(dheads, weight, dy, dpre, active, turned, tail, x, dmid, vec, gvec, gup, tag):
    any_ = pl.BlockSpec(memory_space=pl.ANY)
    vmem = pl.BlockSpec(memory_space=pltpu.VMEM)
    sems = 6 * Reducer.SEMS + 2 + 12
    rows = [pltpu.VMEM((4, 2, 4, 2, 16, 512), BF), pltpu.VMEM((TAIL, 512), BF)]
    return pl.pallas_call(
        finish_kernel,
        out_shape=(
            jax.ShapeDtypeStruct((256, D), BF),
            jax.ShapeDtypeStruct((VEC_ROWS, D), F32),
            jax.ShapeDtypeStruct((16, ATTN_TOTAL), BF),
            jax.ShapeDtypeStruct((16, SECOND_TOTAL), BF),
        ),
        in_specs=[any_] * 13 + [vmem] * 6,
        out_specs=(vmem,) * 4,
        scratch_shapes=[
            pltpu.VMEM((HEADS, WIRE, 256), BF),
            pltpu.VMEM((LEAD, QKV), BF),
            pltpu.VMEM((256, QKV), BF),
            pltpu.VMEM((512, QKV), BF),
            pltpu.VMEM((512, D), BF),
            pltpu.VMEM((512, SECOND), BF),
            pltpu.VMEM((512, SECOND), BF),
        ]
        + rows * 4
        + [
            pltpu.VMEM((ATTN_CHUNK // LANES, LEAD, LANES), F32),
            pltpu.VMEM((D, 256), F32),
            pltpu.VMEM((VEC_ROWS, D), F32),
            pltpu.VMEM((4, 4, VEC_ROWS, D), BF),
        ]
        + Reducer.scratch(ATTN_WIDTHS)
        + Reducer.scratch(SECOND_WIDTHS)
        + [
            pltpu.SemaphoreType.DMA((sems,)),
            pltpu.SemaphoreType.DMA((sems,)),
            pltpu.SemaphoreType.DMA((13,)),
        ],
        compiler_params=mesh_params(tag),
        name="finish",
    )(dheads, weight, dy, dpre, active, *turned, tail, x, dmid, vec, gvec, gup)


def close_kernel(
    totals_ref,
    attn_ref,
    first_ref,
    second_ref,
    mixed_in,
    tokens_in,
    unmix_ref,
    mixed_ref,
    tokens_ref,
    query_ref,
    key_ref,
    value_ref,
    out_ref,
    up_ref,
    down_ref,
    gain1_ref,
    bias1_ref,
    gain2_ref,
    bias2_ref,
    bias_out_ref,
    bias_down_ref,
    bias_query_ref,
    bias_value_ref,
    bias_up_ref,
    attn,
    first,
    second,
    vec,
    stack,
):
    def unpack(share, full, main, chunk):
        full[0:16, :] = share[:, :main].astype(F32)
        rest = share[:, main : main + chunk].astype(F32)
        for row in range(2):
            for index in range(8):
                size = min(main - index * chunk, chunk)
                if size > 0:
                    start = index * chunk
                    spot = row * 8 + index
                    full[16 + row : 17 + row, start : start + size] = rest[
                        spot : spot + 1, :size
                    ]

    unpack(attn_ref, attn, ATTN_MAIN, ATTN_CHUNK)
    unpack(first_ref, first, 2 * FIRST, FIRST_CHUNK)
    unpack(second_ref, second, 2 * SECOND, SECOND_CHUNK)
    for head in range(HEADS):
        span = slice(head * HEAD_DIM, (head + 1) * HEAD_DIM)
        for index, ref in enumerate((key_ref, query_ref, value_ref)):
            start = head * PACK + index * HEAD_DIM
            ref[:, span] = attn[:18, start : start + HEAD_DIM]
    stack[0:256] = mixed_in[...]
    stack[256:512] = tokens_in[...]
    stack[512:544] = jnp.concatenate(
        [attn[:, QKV:ATTN_MAIN].astype(BF), jnp.zeros((8, D), BF)], axis=0
    )
    stack[544:576] = jnp.concatenate(
        [exact_parts(totals_ref[0:8, :]), jnp.zeros((8, D), BF)], axis=0
    )
    for part in range(3):
        columns = slice(384 * part, 384 * part + 384)
        value = dot(stack[...], unmix_ref[:, columns])
        mixed_ref[:, columns] = value[0:256].astype(BF)
        tokens_ref[:, columns] = value[256:512].astype(BF)
        out_ref[:, columns] = value[512:530]
        vec[0:8, columns] = value[544:552] + value[552:560] + value[560:568]
    lines = (gain1_ref, bias1_ref, gain2_ref, bias2_ref, bias_out_ref, bias_down_ref)
    for index, ref in enumerate(lines):
        ref[...] = vec[index : index + 1, :D].reshape(D)
    for row in range(3):
        vec[8:9, row * D : (row + 1) * D] = totals_ref[VEC_QKV + row : VEC_QKV + row + 1, :]
    for head in range(HEADS):
        span = slice(head * HEAD_DIM, (head + 1) * HEAD_DIM)
        for index, row in ((1, 9), (2, 10)):
            start = head * PACK + index * HEAD_DIM
            vec[row : row + 1, span] = vec[8:9, start : start + HEAD_DIM]
    bias_query_ref[...] = vec[9:10, :D].reshape(D)
    bias_value_ref[...] = vec[10:11, :D].reshape(D)
    for row in range(4):
        size = min(FF - row * D, D)
        vec[11:12, row * D : row * D + size] = totals_ref[
            VEC_UP + row : VEC_UP + row + 1, :size
        ]
    bias_up_ref[...] = vec[11:12, :FF].reshape(FF)
    up_ref[:, :FIRST] = first[:18, :FIRST]
    up_ref[:, FIRST:] = second[:18, : FF - FIRST]
    down_ref[:, :FIRST] = first[:18, FIRST : 2 * FIRST]
    down_ref[:, FIRST:] = second[:18, SECOND : SECOND + FF - FIRST]


def close_layer(totals, attn, first, second, mixed, tokens):
    line = jax.ShapeDtypeStruct((D,), F32)
    square = jax.ShapeDtypeStruct((18, D), F32)
    return pl.pallas_call(
        close_kernel,
        out_shape=(
            jax.ShapeDtypeStruct((256, D), BF),
            jax.ShapeDtypeStruct((256, D), BF),
            square,
            square,
            square,
            square,
            jax.ShapeDtypeStruct((18, FF), F32),
            jax.ShapeDtypeStruct((18, FF), F32),
            *([line] * 8),
            jax.ShapeDtypeStruct((FF,), F32),
        ),
        scratch_shapes=[
            pltpu.VMEM((24, ATTN_MAIN), F32),
            pltpu.VMEM((24, 2 * FIRST), F32),
            pltpu.VMEM((24, 2 * SECOND), F32),
            pltpu.VMEM((16, 4 * D), F32),
            pltpu.VMEM((576, D), BF),
        ],
        compiler_params=params(),
        name="close_layer",
    )(totals, attn, first, second, mixed, tokens, mix_matrix().T.astype(BF))


def pack_slab(weight, chunk, total):
    width = weight.shape[1]
    rest = jnp.pad(weight[16:], ((0, 0), (0, 8 * chunk - width))).reshape(16, chunk)
    return jnp.concatenate(
        [weight[:16], rest, jnp.zeros((16, total - width - chunk), weight.dtype)], axis=1
    )


def by_head(key, query, value):
    rows = key.shape[0]
    parts = [item.reshape(rows, HEADS, 1, HEAD_DIM) for item in (key, query, value)]
    return jnp.concatenate(parts, axis=2).reshape(rows, QKV)


def mixing():
    return onehot(iota((D, D), 0) == origin(iota((D, D), 1)))


def body(
    tokens,
    picture,
    cotangent,
    ln1_gain,
    ln1_bias,
    w_query,
    b_query,
    w_key,
    w_value,
    b_value,
    w_out,
    b_out,
    ln2_gain,
    ln2_bias,
    w_fc1,
    b_fc1,
    w_fc2,
    b_fc2,
):
    mix = mixing()
    out_cols = dot(w_out, mix).astype(BF)
    attn_slab = pack_slab(
        jnp.concatenate([by_head(w_key, w_query, w_value), out_cols], axis=1),
        ATTN_CHUNK,
        ATTN_TOTAL,
    )
    lines = (ln1_gain, ln1_bias, ln2_gain, ln2_bias, b_out, b_fc2, b_query, b_value)
    second_slab, x, g, attn_tail, out_tail, vec, packed, keep, o, attn, first, h_main, h_tail = front(
        attn_slab,
        w_fc1,
        w_fc2.T,
        tokens.reshape(256, D),
        cotangent.reshape(256, D),
        lines,
        picture,
        0,
    )
    attn = attn.reshape(LEAD, ATTN_TOTAL)
    (mixed, go, dmid, gvec2, gbias1, dy, dpre, active), o_turned, h_turned, g_turned = middle(
        attn, first, second_slab, o, x, g, out_tail, vec, b_fc1, 2
    )
    first_share, dheads = attend_back_reduce(
        go, dpre, active, (*h_turned, *g_turned), packed, keep, picture, 3
    )
    gtokens, totals, attn_share, second_share = finish(
        dheads,
        attn,
        dy,
        dpre,
        active,
        (h_main, h_tail, *o_turned, *h_turned, *g_turned),
        attn_tail,
        x,
        dmid,
        vec,
        gvec2,
        gbias1,
        4,
    )
    (
        mixed,
        gtokens,
        grad_query,
        grad_key,
        grad_value,
        grad_out,
        grad_up,
        grad_down,
        grad_gain1,
        grad_bias1,
        grad_gain2,
        grad_bias2,
        grad_b_out,
        grad_b_fc2,
        grad_b_query,
        grad_b_value,
        grad_b_fc1,
    ) = close_layer(totals, attn_share, first_share, second_share, mixed, gtokens)
    return (
        mixed.reshape(2, 128, D),
        gtokens.reshape(2, 128, D),
        grad_gain1,
        grad_bias1,
        grad_query,
        grad_b_query,
        grad_key,
        grad_value,
        grad_b_value,
        grad_out,
        grad_b_out,
        grad_gain2,
        grad_bias2,
        grad_up,
        grad_b_fc1,
        grad_down.T,
        grad_b_fc2,
    )


def solution(mesh):
    placed = (
        P(None, ("fsdp", "rep"), None),
        P(),
        P(None, ("fsdp", "rep"), None),
        P(),
        P(),
        P("fsdp", None),
        P(),
        P("fsdp", None),
        P("fsdp", None),
        P(),
        P("fsdp", None),
        P(),
        P(),
        P(),
        P("fsdp", None),
        P(),
        P(None, "fsdp"),
        P(),
    )
    return jax.shard_map(
        body,
        mesh=mesh,
        in_specs=placed,
        out_specs=(
            P(None, ("fsdp", "rep"), None),
            P(None, ("fsdp", "rep"), None),
            P(),
            P(),
            P("fsdp", None),
            P(),
            P("fsdp", None),
            P("fsdp", None),
            P(),
            P("fsdp", None),
            P(),
            P(),
            P(),
            P("fsdp", None),
            P(),
            P(None, "fsdp"),
            P(),
        ),
        check_vma=False,
    )
```

```python
import functools

import jax
import jax.numpy as jnp
import numpy as np
from jax import lax
from jax.experimental import pallas as pl
from jax.experimental.pallas import tpu as pltpu
from jax.sharding import PartitionSpec as P

MESH = pl.DeviceIdType.MESH
BF = jnp.bfloat16
F32 = jnp.float32
LANES = 128
ORDERS = (("x", "y", "z"), ("y", "z", "x"), ("z", "x", "y"))
AXES = ("x", "y", "z")


def here():
    shard = lax.axis_index("fsdp")
    low = lax.axis_index("rep")
    place = {
        "x": lax.div(shard, 16),
        "y": lax.rem(lax.div(shard, 8), 2) * 2 + low,
        "z": lax.rem(lax.div(shard, 2), 4),
    }
    return place, lax.rem(shard, 2)


def moved(place, axis, steps):
    steps = steps % 4
    if steps == 0:
        return place
    other = dict(place)
    other[axis] = lax.rem(place[axis] + steps, 4)
    return other


def device_at(place, core):
    high = lax.div(place["y"], 2)
    return (((place["x"] * 2 + high) * 4 + place["z"]) * 2 + core, lax.rem(place["y"], 2))


def greet(peers):
    barrier = pltpu.get_barrier_semaphore()
    for peer in peers:
        pl.semaphore_signal(barrier, inc=1, device_id=peer, device_id_type=MESH)
    pl.semaphore_wait(barrier, len(peers))


def part_columns(part, half, widths):
    start = 2 * sum(widths[:part]) + half * widths[part]
    return pl.ds(pl.multiple_of(start, LANES), widths[part])


def piece_of(ref, part, widths, place, core):
    return ref.at[
        place["x"],
        lax.div(place["y"], 2),
        place["z"],
        core,
        :,
        part_columns(part, lax.rem(place["y"], 2), widths),
    ]


def block_of(ref, part, widths, place, core, axis, half=None):
    where = {"x": place["x"], "y": lax.div(place["y"], 2), "z": place["z"]}
    if axis == "y":
        where["y"] = pl.ds(0, 2) if half is None else pl.ds(half, 1)
        columns = pl.ds(2 * sum(widths[:part]), 2 * widths[part])
    else:
        where[axis] = pl.ds(0, 4) if half is None else pl.ds(2 * half, 2)
        columns = part_columns(part, lax.rem(place["y"], 2), widths)
    return ref.at[where["x"], where["y"], where["z"], core, :, columns]


def remote(source, target, send, recv, device):
    return pltpu.make_async_remote_copy(
        src_ref=source,
        dst_ref=target,
        send_sem=send,
        recv_sem=recv,
        device_id=device,
        device_id_type=MESH,
    )


def cycle(value, steps):
    return lax.rem(value + steps, 4)


def turned_by(place, axis, steps):
    other = dict(place)
    other[axis] = cycle(place[axis], steps)
    return other


class Gatherer:
    SEMS = 3 + 3 + 8 + 8 + 16
    KINDS = {"one": 0, "two": 3, "three": 6, "four": 14, "twin": 22}

    def __init__(self, widths, place, core, own, full, send, recv, base):
        self.widths, self.place, self.core = widths, place, core
        self.own, self.full, self.send, self.recv, self.base = own, full, send, recv, base
        self.twin = device_at(place, 1 - core)

    def slot(self, part, kind, index):
        return self.base + part * self.SEMS + self.KINDS[kind] + index

    def push(self, source, target, slot, device):
        remote(source, target, self.send.at[slot], self.recv.at[slot], device).start()

    def arrived(self, region, slot):
        remote(region, region, self.send.at[slot], self.recv.at[slot], self.twin).wait_recv()

    def sent(self, region, slot):
        remote(region, region, self.send.at[slot], self.recv.at[slot], self.twin).wait_send()

    def block(self, part, place, half=None, core=None):
        core = self.core if core is None else core
        return block_of(self.full, part, self.widths, place, core, ORDERS[part][0], half)

    def keep(self, part):
        low = lax.rem(self.place["y"], 2)
        source = self.own.at[:, part_columns(part, low, self.widths)]
        target = piece_of(self.full, part, self.widths, self.place, self.core)
        return source, target, pltpu.make_async_copy(
            source, target, self.recv.at[self.base + 3 * self.SEMS + part]
        )

    def start(self):
        for part, (one, two, three) in enumerate(ORDERS):
            source, target, copy = self.keep(part)
            copy.start()
            for steps in (1, 3, 2):
                device = device_at(turned_by(self.place, one, steps), self.core)
                self.push(source, target, self.slot(part, "one", steps - 1), device)

    def second(self):
        for part, (one, two, three) in enumerate(ORDERS):
            self.keep(part)[2].wait()
            for steps in (1, 3, 2):
                origin = turned_by(self.place, one, 4 - steps)
                region = piece_of(self.full, part, self.widths, origin, self.core)
                self.arrived(region, self.slot(part, "one", steps - 1))
            block = self.block(part, self.place)
            for steps in (1, 3, 2):
                device = device_at(turned_by(self.place, two, steps), self.core)
                self.push(block, block, self.slot(part, "two", steps - 1), device)
        self.spread(0)

    def spread(self, steps):
        for part, (one, two, three) in enumerate(ORDERS):
            block = self.block(part, turned_by(self.place, two, 4 - steps))
            for index, way in enumerate((1, 3)):
                device = device_at(turned_by(self.place, three, way), self.core)
                self.push(block, block, self.slot(part, "three", index * 4 + steps), device)
            self.push(block, block, self.slot(part, "twin", steps), self.twin)

    def third(self, steps):
        for part, (one, two, three) in enumerate(ORDERS):
            block = self.block(part, turned_by(self.place, two, 4 - steps))
            self.arrived(block, self.slot(part, "two", steps - 1))
        self.spread(steps)

    def fourth(self, steps):
        for part, (one, two, three) in enumerate(ORDERS):
            side = turned_by(self.place, two, 4 - steps)
            for index, way in enumerate((1, 3)):
                origin = turned_by(side, three, 4 - way)
                block = self.block(part, origin)
                self.arrived(block, self.slot(part, "three", index * 4 + steps))
                half = self.block(part, origin, index)
                device = device_at(turned_by(self.place, three, way), self.core)
                self.push(half, half, self.slot(part, "four", index * 4 + steps), device)
                self.push(block, block, self.slot(part, "twin", way * 4 + steps), self.twin)

    def fifth(self, steps):
        for part, (one, two, three) in enumerate(ORDERS):
            origin = turned_by(turned_by(self.place, two, 4 - steps), three, 2)
            for index in range(2):
                half = self.block(part, origin, index)
                self.arrived(half, self.slot(part, "four", index * 4 + steps))
            block = self.block(part, origin)
            self.push(block, block, self.slot(part, "twin", 8 + steps), self.twin)

    def close(self):
        for part, (one, two, three) in enumerate(ORDERS):
            for way in range(4):
                for steps in range(4):
                    origin = moved(moved(self.place, two, -steps), three, -way)
                    region = self.block(part, origin, core=1 - self.core)
                    self.arrived(region, self.slot(part, "twin", way * 4 + steps))

    def drain(self):
        for part in range(3):
            piece = piece_of(self.full, part, self.widths, self.place, self.core)
            block = self.block(part, self.place)
            half = self.block(part, self.place, 0)
            for kind, region, count in (
                ("one", piece, 3),
                ("two", block, 3),
                ("three", block, 8),
                ("four", half, 8),
                ("twin", block, 16),
            ):
                for index in range(count):
                    self.sent(region, self.slot(part, kind, index))


class Reducer:
    SEMS = 8 + 8 + 3 + 3 + 1
    KINDS = {"mid": 0, "far": 8, "side": 16, "line": 19, "done": 22}

    def __init__(self, widths, place, core, buffers, out, send, recv, base=0):
        self.widths, self.place, self.core, self.base = widths, place, core, base
        self.acc, self.mid, self.far, self.side, self.line, self.done = [
            buffers[3 * i : 3 * i + 3] for i in range(6)
        ]
        self.out, self.send, self.recv = out, send, recv
        self.me = device_at(place, core)

    @staticmethod
    def scratch(widths):
        found = []
        for lead, half in (((4, 4), 1), ((2, 4), 2), ((2, 4), 1), ((3,), 1)):
            for width, (one, two, three) in zip(widths, ORDERS):
                if one == "y":
                    found.append(pltpu.VMEM(lead + (2 // half, 16, 2 * width), BF))
                else:
                    found.append(pltpu.VMEM(lead + (4 // half, 16, width), BF))
        found += [pltpu.VMEM((3, 16, width), BF) for width in widths]
        found += [pltpu.VMEM((16, width), BF) for width in widths]
        return found

    def slot(self, part, kind, index):
        return self.base + part * self.SEMS + self.KINDS[kind] + index

    def push(self, source, target, slot, device):
        remote(source, target, self.send.at[slot], self.recv.at[slot], device).start()

    def arrived(self, region, slot):
        remote(region, region, self.send.at[slot], self.recv.at[slot], self.me).wait_recv()

    def sent(self, region, slot):
        remote(region, region, self.send.at[slot], self.recv.at[slot], self.me).wait_send()

    def add(self, target, *terms):
        for index in range(target.shape[0]):
            total = target[index].astype(F32)
            for term in terms:
                total = total + term[index].astype(F32)
            target[index] = total.astype(BF)

    def half_of(self, ref, half):
        size = ref.shape[0] // 2
        return ref.at[pl.ds(half * size, size)]

    def far_out(self):
        for spot in range(4):
            for part, (one, two, three) in enumerate(ORDERS):
                for half, way in ((0, 3), (1, 1)):
                    self.push(
                        self.half_of(self.acc[part].at[2, spot], half),
                        self.mid[part].at[half, spot],
                        self.slot(part, "mid", half * 4 + spot),
                        device_at(moved(self.place, three, way), self.core),
                    )

    def pass_on(self, spot):
        for part, (one, two, three) in enumerate(ORDERS):
            for half, way in ((0, 3), (1, 1)):
                self.arrived(
                    self.mid[part].at[half, spot], self.slot(part, "mid", half * 4 + spot)
                )
                self.add(
                    self.half_of(self.acc[part].at[way, spot], half), self.mid[part].at[half, spot]
                )
                self.push(
                    self.acc[part].at[way, spot],
                    self.far[part].at[half, spot],
                    self.slot(part, "far", half * 4 + spot),
                    device_at(moved(self.place, three, way), self.core),
                )

    def gather_side(self, over, last):
        for part, (one, two, three) in enumerate(ORDERS):
            spot = cycle(self.place[two], over)
            for half in range(2):
                self.arrived(
                    self.far[part].at[half, spot], self.slot(part, "far", half * 4 + spot)
                )
            self.add(
                self.acc[part].at[0, spot], self.far[part].at[0, spot], self.far[part].at[1, spot]
            )

            def give(part=part, two=two, spot=spot):
                other = dict(self.place)
                other[two] = spot
                self.push(
                    self.acc[part].at[0, spot],
                    self.side[part].at[over - 1],
                    self.slot(part, "side", over - 1),
                    device_at(other, self.core),
                )

            if last is False:
                give()
            elif last is not True:
                pl.when(jnp.logical_not(last))(give)

    def piece(self, part, axis, spot):
        own = self.acc[part].at[0, self.place[ORDERS[part][1]]]
        if axis == "y":
            start = pl.multiple_of(lax.rem(spot["y"], 2) * self.widths[part], LANES)
            return own.at[lax.div(spot["y"], 2), :, pl.ds(start, self.widths[part])]
        return own.at[spot[axis]]

    def line_up(self):
        for part, (one, two, three) in enumerate(ORDERS):
            for over in range(3):
                self.arrived(self.side[part].at[over], self.slot(part, "side", over))
            own = self.acc[part].at[0, self.place[two]]
            self.add(own, self.side[part].at[0], self.side[part].at[1], self.side[part].at[2])
            for over in (2, 1, 3):
                spot = moved(self.place, one, over)
                self.push(
                    self.piece(part, one, spot),
                    self.line[part].at[over - 1],
                    self.slot(part, "line", over - 1),
                    device_at(spot, self.core),
                )

    def share(self):
        low = lax.rem(self.place["y"], 2)
        partner = (lax.axis_index("fsdp"), 1 - low)
        for part, (one, two, three) in enumerate(ORDERS):
            for over in range(3):
                self.arrived(self.line[part].at[over], self.slot(part, "line", over))
            total = self.piece(part, one, self.place)[...].astype(F32)
            for over in range(3):
                total = total + self.line[part][over].astype(F32)
            self.done[part][...] = total.astype(BF)
            columns = part_columns(part, low, self.widths)
            self.push(
                self.done[part], self.out.at[:, columns], self.slot(part, "done", 0), partner
            )
            self.out[:, columns] = self.done[part][...]

    def close(self):
        low = lax.rem(self.place["y"], 2)
        for part, (one, two, three) in enumerate(ORDERS):
            self.arrived(
                self.out.at[:, part_columns(part, 1 - low, self.widths)],
                self.slot(part, "done", 0),
            )
            for half in range(2):
                for spot in range(4):
                    index = half * 4 + spot
                    self.sent(self.mid[part].at[half, spot], self.slot(part, "mid", index))
                    self.sent(self.far[part].at[half, spot], self.slot(part, "far", index))
            for over in range(3):
                self.sent(self.side[part].at[over], self.slot(part, "side", over))
                self.sent(self.line[part].at[over], self.slot(part, "line", over))
            self.sent(self.done[part], self.slot(part, "done", 0))


class Maker:
    def __init__(self, reducer, sources, extra, chunk):
        self.red, self.sources, self.extra, self.chunk = reducer, sources, extra, chunk
        self.main = sum(item[1].shape[1] for item in sources)

    def pack_tail(self):
        start = 0
        pieces = []
        for turned, right in self.sources:
            pieces.append((start, start + right.shape[1], turned, right))
            start += right.shape[1]
        for index in range(8):
            low, high = index * self.chunk, (index + 1) * self.chunk
            for first, last, turned, right in pieces:
                a, b = max(low, first), min(high, last)
                if a < b:
                    value = dot(turned[1][...], right[:, a - first : b - first])
                    self.scatter(index, a - low, value)
            if high > self.main:
                a = max(low, self.main)
                self.scatter(index, a - low, jnp.zeros((TAIL, high - a), F32))

    def scatter(self, index, start, value):
        for tile in range(value.shape[1] // LANES):
            self.extra[start // LANES + tile, pl.ds(index, TAIL, stride=8), :] = value[
                :, tile * LANES : (tile + 1) * LANES
            ]

    def rows(self, ref):
        core = self.red.core
        if len(ref.shape) == 2:
            groups = [
                ref[pl.ds(pl.multiple_of((2 * index + core) * 16, 16), 16)] for index in range(32)
            ]
            return jnp.concatenate(groups, axis=0)
        return ref[:, :, :, core].reshape(512, ref.shape[-1])

    def columns(self, part, half):
        width = self.red.widths[part]
        low = 2 * sum(self.red.widths[:part]) + half * width
        high = low + width
        first = 0
        found = []
        for turned, right in self.sources:
            last = first + right.shape[1]
            a, b = max(low, first), min(high, last)
            if a < b:
                left = self.rows(turned[0])
                found.append(dot(left, right[:, a - first : b - first]).astype(BF))
            first = last
        a, b = max(low, first), min(high, first + self.chunk)
        if a < b:
            for tile in range((a - first) // LANES, (b - first) // LANES):
                found.append(self.rows(self.extra.at[tile]).astype(BF))
        a = max(low, first + self.chunk)
        if a < high:
            found.append(jnp.zeros((512, high - a), BF))
        return found[0] if len(found) == 1 else jnp.concatenate(found, axis=1)

    def make(self, part):
        red, width = self.red, self.red.widths[part]
        acc = red.acc[part]
        three = ORDERS[part][2]
        own = red.place[three]

        def ahead(spot):
            return cycle(spot + 4 - own, 0)

        for half in range(2):
            value = self.columns(part, half).reshape(4, 2, 4, 16, width)
            if three == "z":
                for spot in range(4):
                    for high in range(2):
                        acc[ahead(spot), 2 * high + half] = value[:, high, spot]
            elif three == "x":
                for spot in range(4):
                    for z in range(4):
                        acc[ahead(spot), z, :, :, half * width : (half + 1) * width] = value[
                            spot, :, z
                        ]
            else:
                for high in range(2):
                    for x in range(4):
                        acc[ahead(2 * high + half), x] = value[x, high]

    def run(self):
        self.pack_tail()
        for part in range(3):
            self.make(part)
        self.red.far_out()


SWAP_ORDER = (9, 11, 5, 13, 7, 15, 1, 3, 8, 10, 4, 12, 6, 14, 2)


class Swapper:
    def __init__(self, place, core, own, full, send, recv, base):
        self.place, self.core = place, core
        self.own, self.full, self.send, self.recv, self.base = own, full, send, recv, base
        self.low = lax.rem(place["y"], 2)
        self.mine = (place["z"] * 2 + core) * 2 + self.low
        self.group = lax.div(lax.axis_index("fsdp"), 8) * 8

    def member(self, k, sign=1):
        z = lax.rem(self.place["z"] + (4 + sign * (k // 4)), 4)
        core = lax.rem(self.core + (k // 2) % 2, 2)
        low = lax.rem(self.low + k % 2, 2)
        return (z * 2 + core) * 2 + low

    def device(self, index):
        return (self.group + lax.div(index, 2), lax.rem(index, 2))

    def peers(self):
        return [self.device(self.member(k)) for k in range(1, 16)]

    def view(self, ref, index, micro):
        if len(ref.shape) == 3:
            return ref.at[index, :, pl.ds(micro * 128, 128)]
        return ref.at[:, pl.ds(pl.multiple_of(micro * ROW + index * 128, 128), 128)]

    def start(self, micro):
        for k in SWAP_ORDER:
            target = self.member(k)
            remote(
                self.view(self.own, target, micro),
                self.view(self.full, self.mine, micro),
                self.send.at[self.base + k],
                self.recv.at[self.base + k],
                self.device(target),
            ).start()
        pltpu.make_async_copy(
            self.view(self.own, self.mine, micro),
            self.view(self.full, self.mine, micro),
            self.send.at[self.base],
        ).start()

    def finish(self, micro):
        pltpu.make_async_copy(
            self.view(self.own, self.mine, micro),
            self.view(self.full, self.mine, micro),
            self.send.at[self.base],
        ).wait()
        for k in range(1, 16):
            region = self.view(self.full, self.member(k, -1), micro)
            remote(
                region,
                region,
                self.send.at[self.base + k],
                self.recv.at[self.base + k],
                self.device(self.mine),
            ).wait_recv()

    def drain(self, micro):
        for k in range(1, 16):
            region = self.view(self.own, self.member(k), micro)
            remote(
                region,
                region,
                self.send.at[self.base + k],
                self.recv.at[self.base + k],
                self.device(self.mine),
            ).wait_send()


def line_peers(place, core):
    peers = []
    for axis in AXES:
        for steps in (1, 2, 3):
            peers.append(device_at(moved(place, axis, steps), core))
    return peers


D = 1152
HEADS = 16
HEAD_DIM = 72
FF = 4304
ROW = 2048
EPS = 1e-06
NEG = -1e30
SCALE = HEAD_DIM**-0.5
LEAD = 1024
TAIL = 128
PACK = 3 * HEAD_DIM
WIDE = 256
WIRE = 224
HEAD_WIRE = 80
VALUE_LANE = 16
FF_PAD = 4352
QKV = HEADS * PACK
ATTN_MAIN = QKV + D
ATTN_CHUNK = 640
ATTN_TOTAL = 5376
MLP_MAIN = 2 * FF_PAD
MLP_CHUNK = 1152
MLP_TOTAL = 9984
ATTN_WIDTHS = (896, 896, 896)
MLP_WIDTHS = (1664, 1664, 1664)
FIRST = 3072
FIRST_CHUNK = 768
FIRST_TOTAL = 6912
FIRST_WIDTHS = (896, 1408, 1152)
FIRST_STEP = 768
SECOND = FF_PAD - FIRST
SECOND_CHUNK = 384
SECOND_TOTAL = 3072
SECOND_WIDTHS = (512, 512, 512)
SECOND_STEP = 640
LOG2E = 1.4426950408889634
QUERIES = 512
KEYS = 512
BLOCKS = ROW // QUERIES
TANH_A = 0.7978845608028654
TANH_B = 0.044715


def dot(left, right):
    return jnp.dot(left, right, preferred_element_type=F32)


def dot_nt(left, right):
    return lax.dot_general(left, right, (((1,), (1,)), ((), ())), preferred_element_type=F32)


def dot_tn(left, right):
    return lax.dot_general(left, right, (((0,), (0,)), ((), ())), preferred_element_type=F32)


def origin(index):
    lead = (index >> 4) * 18 + (index & 15)
    rest = index - LEAD
    tail = (rest >> 1) * 18 + 16 + (rest & 1)
    return jnp.where(index < LEAD, lead, tail)


def iota(shape, axis):
    return lax.broadcasted_iota(jnp.int32, shape, axis)


def onehot(mask):
    return mask.astype(F32).astype(BF)


def normal(values):
    center = values - jnp.mean(values, axis=-1, keepdims=True)
    rate = lax.rsqrt(jnp.mean(center * center, axis=-1, keepdims=True) + EPS)
    return center * rate, rate


def normal_back(unit, rate, gain, grad):
    inner = grad * gain
    first = jnp.mean(inner, axis=-1, keepdims=True)
    second = jnp.mean(inner * unit, axis=-1, keepdims=True)
    return rate * (inner - first - unit * second)


def exact_parts(values):
    high = values.astype(BF)
    rest = values - high.astype(F32)
    middle_part = rest.astype(BF)
    low = (rest - middle_part.astype(F32)).astype(BF)
    return jnp.concatenate([high, middle_part, low], axis=0)


def column_total(values):
    return jnp.sum(values, axis=0, keepdims=True)


def lanes(start, size):
    return pl.ds(pl.multiple_of(start, LANES), size)


def params(limit=60):
    return pltpu.CompilerParams(vmem_limit_bytes=limit << 20)


PERMUTED = np.concatenate(
    [np.arange(64)[:, None] * 18 + np.arange(16), np.arange(64)[:, None] * 18 + [16, 17]], axis=1
)
PERMUTED = np.concatenate([PERMUTED[:, :16].reshape(-1), PERMUTED[:, 16:].reshape(-1)])


def mix_matrix():
    matrix = np.zeros((D, D), np.float32)
    matrix[PERMUTED, np.arange(D)] = 1.0
    return matrix


def place_matrix():
    matrix = np.zeros((HEADS, HEAD_WIRE, D), np.float32)
    matrix[:, :HEAD_DIM] = mix_matrix().reshape(HEADS, HEAD_DIM, D)
    return matrix.reshape(HEADS * HEAD_WIRE, D)


def mesh_params(tag, limit=62):
    return pltpu.CompilerParams(
        collective_id=tag, has_side_effects=True, vmem_limit_bytes=limit << 20
    )


class Twin:
    def __init__(self, place, core, send, recv, base):
        self.core, self.device = core, device_at(place, 1 - core)
        self.send, self.recv, self.base = send, recv, base
        self.items = []

    def half(self, ref, axis, core):
        size = ref.shape[axis] // 2
        if axis == 0:
            return ref.at[pl.ds(pl.multiple_of(core * size, size), size)]
        lead = (slice(None),) * (len(ref.shape) - 1)
        return ref.at[lead + (pl.ds(pl.multiple_of(core * size, LANES), size),)]

    def give(self, source, target, axis):
        index = self.base + 2 * len(self.items)
        place = self.half(target, axis, self.core)
        pltpu.make_async_copy(source, place, self.recv.at[index + 1]).start()
        remote(source, place, self.send.at[index], self.recv.at[index], self.device).start()
        self.items.append((source, target, axis, index))

    def ready(self):
        for source, target, axis, index in self.items:
            place = self.half(target, axis, self.core)
            pltpu.make_async_copy(source, place, self.recv.at[index + 1]).wait()
            other = self.half(target, axis, 1 - self.core)
            remote(
                other, other, self.send.at[index], self.recv.at[index], self.device
            ).wait_recv()

    def pass_part(self, source, target, columns, number):
        index = self.base + 2 * number
        place = target.at[pl.ds(pl.multiple_of(self.core * 256, 256), 256), columns]
        pltpu.make_async_copy(source, place, self.recv.at[index + 1]).start()
        remote(source, place, self.send.at[index], self.recv.at[index], self.device).start()

    def part_done(self, target, columns, number):
        index = self.base + 2 * number
        place = target.at[pl.ds(pl.multiple_of(self.core * 256, 256), 256), columns]
        other = target.at[pl.ds(pl.multiple_of((1 - self.core) * 256, 256), 256), columns]
        pltpu.make_async_copy(place, place, self.recv.at[index + 1]).wait()
        copy = remote(other, other, self.send.at[index], self.recv.at[index], self.device)
        copy.wait_recv()
        copy.wait_send()

    def drain(self):
        for source, target, axis, index in self.items:
            place = self.half(target, axis, self.core)
            remote(
                place, place, self.send.at[index], self.recv.at[index], self.device
            ).wait_send()


def back_kernel(
    go,
    dpre,
    active,
    h_main,
    h_tail,
    g_main,
    g_tail,
    picture,
    packed_ref,
    keep_ref,
    share_ref,
    dheads,
    go_all,
    grads,
    wire,
    backs,
    dpre_all,
    active_all,
    h_main_all,
    h_tail_all,
    g_main_all,
    g_tail_all,
    extra,
    keys,
    queries,
    ids,
    dkeys,
    dvalues,
    found,
    row_ref,
    *rest,
):
    buffers, (send, recv, local) = rest[:-3], rest[-3:]
    place, core = here()
    red = Reducer(FIRST_WIDTHS, place, core, buffers, share_ref, send, recv)
    base = 3 * Reducer.SEMS
    ins = [Swapper(place, core, go, go_all, send, recv, base + 16 * m) for m in range(2)]
    base = base + 32
    outs = [Swapper(place, core, wire, dheads, send, recv, base + 16 * m) for m in range(2)]
    greet(line_peers(place, core) + swap_only(ins[0]))
    for micro in range(2):
        ins[micro].start(micro)
    loads = []
    for source, target in (
        (h_main, h_main_all),
        (h_tail, h_tail_all),
        (g_main, g_main_all),
        (g_tail, g_tail_all),
        (dpre.at[:, pl.ds(0, FIRST)], dpre_all),
        (active.at[:, pl.ds(0, FIRST)], active_all),
    ):
        copy = pltpu.make_async_copy(source, target, local.at[1 + len(loads)])
        copy.start()
        loads.append(copy)
    maker = Maker(
        red,
        [((h_main_all, h_tail_all), dpre_all), ((g_main_all, g_tail_all), active_all)],
        extra,
        FIRST_CHUNK,
    )
    ids_in = fetch_ids(picture, found, local.at[0])
    ids_in.start()
    ids_in.wait()
    for micro in range(2):
        row_ref[micro] = found[micro : micro + 1].astype(F32)
    for copy in loads:
        copy.wait()
    maker.run()
    ins[0].finish(0)

    def block(step, carry):
        row = lax.div(step, BLOCKS)
        index = lax.rem(step, BLOCKS)
        tokens = pl.ds(pl.multiple_of(row * 128, 128), 128)

        @pl.when(step == BLOCKS)
        def _():
            ins[1].finish(1)

        @pl.when(index == 0)
        def _():
            back_row = jnp.concatenate(
                [
                    jnp.zeros((VALUE_LANE, ROW), BF),
                    go_all[:, lanes(row * ROW, ROW)],
                    jnp.zeros((LANES - VALUE_LANE - HEAD_WIRE, ROW), BF),
                ],
                axis=0,
            )
            backs[...] = jnp.transpose(back_row)
            packed = packed_ref[:, tokens, :].reshape(ROW, WIDE)
            split_packed(packed, keys, queries)
            for part in range(ROW // LANES):
                span = slice(part * LANES, (part + 1) * LANES)
                ids[span, :] = column_ids(row_ref[row, :, span])
            dkeys[...] = jnp.zeros_like(dkeys)
            dvalues[...] = jnp.zeros_like(dvalues)

        rows = pl.ds(pl.multiple_of(index * QUERIES, QUERIES), QUERIES)

        def scan(count):
            start = jnp.where(index < 2, 0, BLOCKS - count)
            query = queries[rows, :]
            back = backs[rows, :]
            mine = row_ref[row, :, lanes(index * QUERIES, QUERIES)]
            kept = keep_ref[row, rows, :]
            inner = jnp.sum(back.astype(F32) * kept, axis=1, keepdims=True)
            lane = iota((QUERIES, LANES), 1)
            stats = jnp.transpose(jnp.where(lane == 0, kept, inner))
            logsum = stats[0:1]
            inner = stats[1:2]
            total = jnp.zeros((QUERIES, LANES), F32)
            for part in range(count):
                span = pl.ds(pl.multiple_of((start + part) * KEYS, KEYS), KEYS)
                blocks = pl.ds((start + part) * (KEYS // 128), KEYS // 128)
                value = packed_ref[blocks, tokens, LANES:].reshape(KEYS, LANES)
                allowed = jnp.concatenate([ids[span, :]] * (QUERIES // LANES), axis=1)
                score = dot_nt(keys[span, :], query) * (SCALE * LOG2E) - logsum
                prob = jnp.exp2(jnp.where(allowed == mine, score, NEG))
                grad = (prob * (dot_nt(value, back) - inner)).astype(BF)
                dvalues[span, :] += dot(prob.astype(BF), back)
                dkeys[span, :] += dot(grad, query)
                total = total + dot_tn(grad, keys[span, :])
            total = total * SCALE
            moved_q = jnp.concatenate(
                [
                    jnp.zeros((QUERIES, HEAD_DIM), F32),
                    total[:, :HEAD_DIM],
                    jnp.zeros((QUERIES, WIDE - 2 * HEAD_DIM), F32),
                ],
                axis=1,
            )
            grads[rows, :] = moved_q.astype(BF)

        edge = (index == 0) | (index == BLOCKS - 1)
        pl.when(edge)(functools.partial(scan, 3))
        pl.when(jnp.logical_not(edge))(functools.partial(scan, 4))

        @pl.when(index == BLOCKS - 1)
        def _():
            wide = jnp.concatenate([dkeys[...] * SCALE, dvalues[...]], axis=1)
            lane = iota((ROW, WIDE), 1)
            old = grads[...]
            inside = (lane >= HEAD_DIM) & (lane < 2 * HEAD_DIM)
            whole = jnp.where(inside, old, wide.astype(BF))
            wire[:, lanes(row * ROW, ROW)] = jnp.transpose(whole)[:WIRE]
            for micro in range(2):
                pl.when(row == micro)(functools.partial(outs[micro].start, micro))

        @pl.when(step == 1)
        def _():
            for spot in range(4):
                red.pass_on(spot)

        @pl.when(step >= 4)
        def _():
            red.gather_side(lax.rem(step - 4 + 1, 4), step == 7)

        return carry

    lax.fori_loop(0, 2 * BLOCKS, block, 0)
    red.line_up()
    red.share()
    red.close()
    for micro in range(2):
        outs[micro].finish(micro)
    for micro in range(2):
        ins[micro].drain(micro)
    for micro in range(2):
        outs[micro].drain(micro)


def attend_back_reduce(go, dpre, active, turned, packed, keep, picture, tag):
    any_ = pl.BlockSpec(memory_space=pl.ANY)
    vmem = pl.BlockSpec(memory_space=pltpu.VMEM)
    sems = 3 * Reducer.SEMS + 64
    return pl.pallas_call(
        back_kernel,
        out_shape=(
            jax.ShapeDtypeStruct((16, FIRST_TOTAL), BF),
            jax.ShapeDtypeStruct((16, WIRE, 256), BF),
        ),
        in_specs=[any_] * 8 + [vmem] * 2,
        out_specs=(vmem, any_),
        scratch_shapes=[
            pltpu.VMEM((HEAD_WIRE, 2 * ROW), BF),
            pltpu.VMEM((ROW, WIDE), BF),
            pltpu.VMEM((WIRE, 2 * ROW), BF),
            pltpu.VMEM((ROW, LANES), BF),
            pltpu.VMEM((512, FIRST), BF),
            pltpu.VMEM((512, FIRST), BF),
            pltpu.VMEM((4, 2, 4, 2, 16, 512), BF),
            pltpu.VMEM((TAIL, 512), BF),
            pltpu.VMEM((4, 2, 4, 2, 16, 512), BF),
            pltpu.VMEM((TAIL, 512), BF),
            pltpu.VMEM((FIRST_CHUNK // LANES, LEAD, LANES), F32),
            pltpu.VMEM((ROW, LANES), BF),
            pltpu.VMEM((ROW, LANES), BF),
            pltpu.VMEM((ROW, LANES), F32),
            pltpu.VMEM((ROW, LANES), F32),
            pltpu.VMEM((ROW, LANES), F32),
            pltpu.VMEM((2, ROW), jnp.int32),
            pltpu.VMEM((2, 1, ROW), F32),
        ]
        + Reducer.scratch(FIRST_WIDTHS)
        + [
            pltpu.SemaphoreType.DMA((sems,)),
            pltpu.SemaphoreType.DMA((sems,)),
            pltpu.SemaphoreType.DMA((7,)),
        ],
        compiler_params=mesh_params(tag),
        name="attend_back_reduce",
    )(go, dpre, active, *turned, picture, packed, keep)


VEC_ROWS = 16
VEC_QKV = 6
VEC_UP = 9


def spread_tail(source, chunk, wide, tail):
    for tile in range(chunk // LANES):
        wide[tile] = source(tile).astype(F32)
        for index in range(8):
            start = index * chunk + tile * LANES
            picked = wide[tile, pl.ds(index, TAIL, stride=8), :]
            tail[:, start : start + LANES] = picked.astype(BF)


def column_ids(row_ids):
    size = row_ids.shape[1]
    return jnp.transpose(jnp.broadcast_to(row_ids, (LANES, size)))


def fetch_ids(picture, found, sem):
    start = pl.multiple_of(lax.div(lax.axis_index("fsdp"), 8) * ROW, ROW)
    return pltpu.make_async_copy(picture.at[:, pl.ds(start, ROW)], found, sem)


def split_packed(packed, keys, queries):
    lane = iota((ROW, LANES), 1)
    zero = jnp.zeros((ROW, LANES), BF)
    keys[...] = jnp.where(lane < HEAD_DIM, packed[:, :LANES], zero)
    queries[...] = jnp.concatenate(
        [packed[:, HEAD_DIM : 2 * HEAD_DIM], jnp.zeros((ROW, LANES - HEAD_DIM), BF)], axis=1
    )


def swap_only(swapper):
    return [swapper.device(swapper.member(k)) for k in range(1, 16) if k not in (1, 4, 8, 12)]


def pack_rows(sources, width, chunk, slab, rest, block):
    slab[...] = jnp.zeros_like(slab)
    rest[...] = jnp.zeros_like(rest)
    for index, (ref, start, stop) in enumerate(sources):
        place = slice(index * width, index * width + stop - start)
        slab[:, place] = ref[0:16, start:stop]
        rest[:, place] = ref[16:18, start:stop].astype(F32)
    main = len(sources) * width
    for row in range(2):
        for index in range(8):
            spot = row * 8 + index
            block[spot : spot + 1, :chunk] = rest[
                row : row + 1, index * chunk : (index + 1) * chunk
            ]
    slab[:, main : main + chunk] = block[:, :chunk].astype(BF)


def front_kernel(
    slab,
    picture,
    tokens_ref,
    cotangent_ref,
    up_ref,
    down_ref,
    *refs,
):
    lines, rest = refs[:8], refs[8:]
    run_front(slab, picture, tokens_ref, cotangent_ref, up_ref, down_ref, lines, *rest)


def run_front(
    slab,
    picture,
    tokens_ref,
    cotangent_ref,
    up_ref,
    down_ref,
    lines,
    second_slab,
    x_ref,
    g_ref,
    tail_ref,
    out_tail_ref,
    mixed_vec_ref,
    packed_ref,
    keep_ref,
    o_all,
    weight_out,
    first_out,
    h_main_all,
    h_tail_all,
    first_slab,
    rest,
    rest_block,
    h_main,
    h_tail,
    full,
    low,
    flat,
    wide,
    tail,
    vec_ref,
    vec_parts,
    heads,
    wire,
    o_own,
    keys,
    queries,
    values,
    scores,
    found,
    row_ref,
    send,
    recv,
    local,
):
    place, core = here()
    red = Gatherer(ATTN_WIDTHS, place, core, slab, full, send, recv, 0)
    base = 3 * Gatherer.SEMS + 3
    first = Gatherer(FIRST_WIDTHS, place, core, first_slab, first_out, send, recv, base)
    base = 2 * base
    ins = [Swapper(place, core, heads, wire, send, recv, base + 16 * m) for m in range(2)]
    base = base + 32
    outs = [Swapper(place, core, o_own, o_all, send, recv, base + 16 * m) for m in range(2)]
    twin = Twin(place, core, send, recv, base + 32)
    greet(line_peers(place, core) + swap_only(ins[0]))
    red.start()
    pack_rows(
        [(up_ref, 0, FIRST), (down_ref, 0, FIRST)],
        FIRST,
        FIRST_CHUNK,
        first_slab,
        rest,
        rest_block,
    )
    first.start()
    ids_in = fetch_ids(picture, found, local.at[0])
    ids_in.start()
    for index, line in enumerate(lines):
        vec_ref[index : index + 1, :] = line[...].reshape(1, D)
    vec_parts[...] = exact_parts(vec_ref[...])

    def mix(index, carry):
        columns = lanes(index * LANES, LANES)
        column = onehot(iota((D, LANES), 0) == origin(index * LANES + iota((D, LANES), 1)))
        x_ref[:, columns] = dot(tokens_ref[...], column).astype(BF)
        g_ref[:, columns] = dot(cotangent_ref[...], column).astype(BF)
        parts = dot(vec_parts[...], column)
        mixed_vec_ref[:, columns] = parts[0:8] + parts[8:16] + parts[16:24]
        return carry

    lax.fori_loop(0, 3, mix, 0)
    red.second()
    lax.fori_loop(3, 9, mix, 0)
    pack_rows(
        [(up_ref, FIRST, FF), (down_ref, FIRST, FF)],
        SECOND,
        SECOND_CHUNK,
        second_slab,
        rest,
        rest_block,
    )
    unit, _ = normal(x_ref[...].astype(F32))
    low[...] = (unit * mixed_vec_ref[0:1] + mixed_vec_ref[1:2]).astype(BF)
    for steps in (1, 2, 3):
        red.third(steps)
    turned = jnp.transpose(low[...])
    h_main[...] = turned[:LEAD].reshape(4, 2, 4, 2, 16, 256)
    h_tail[...] = turned[LEAD:]
    twin.give(h_main, h_main_all, 5)
    twin.give(h_tail, h_tail_all, 1)
    ids_in.wait()
    for micro in range(2):
        row_ref[micro] = found[micro : micro + 1].astype(F32)
    for steps in range(4):
        red.fourth(steps)
    first.second()
    for steps in range(4):
        red.fifth(steps)
    red.close()
    leave = pltpu.make_async_copy(full, weight_out, local.at[1])
    leave.start()

    def packed_tile(tile):
        start = ATTN_MAIN + tile * LANES
        return full[:, :, :, :, :, start : start + LANES].reshape(LEAD, LANES)

    for steps in (1, 2, 3):
        first.third(steps)
    spread_tail(packed_tile, ATTN_CHUNK, wide, tail)
    tail_ref[...] = tail[:, :QKV]
    out_tail_ref[...] = tail[:, QKV:ATTN_MAIN]

    def columns(index, carry):
        span = lanes(index * 384, 384)
        weight = full[:, :, :, :, :, span].reshape(LEAD, 384)
        flat[:, span] = dot(low[:, :LEAD], weight) + dot(low[:, LEAD:], tail[:, span])
        return carry

    lax.fori_loop(0, QKV // 384, columns, 0)
    for head in range(HEADS):
        span = slice(head * HEAD_DIM, (head + 1) * HEAD_DIM)
        bias = jnp.concatenate(
            [jnp.zeros((1, HEAD_DIM), F32), vec_ref[6:7, span], vec_ref[7:8, span]], axis=1
        )
        block = flat[:, PACK * head : PACK * head + PACK] + bias
        block = jnp.concatenate([block, jnp.zeros((256, WIDE - PACK), F32)], axis=1)
        heads[head] = jnp.transpose(block.astype(BF))[:WIRE]
    ins[0].start(0)
    first.fourth(0)
    first.fourth(1)
    ins[1].start(1)
    ins[0].finish(0)

    def block(step, carry):
        row = lax.div(step, 8)
        index = lax.rem(step, 8)
        rows_of = pl.ds(pl.multiple_of(row * 128, 128), 128)

        @pl.when(step == 8)
        def _():
            ins[1].finish(1)

        @pl.when(index == 0)
        def _():
            packed = jnp.transpose(wire[:, lanes(row * ROW, ROW)])
            packed = jnp.concatenate([packed, jnp.zeros((ROW, WIDE - WIRE), BF)], axis=1)
            packed_ref[:, rows_of, :] = packed.reshape(16, 128, WIDE)
            split_packed(packed, keys, queries)
            lane = iota((ROW, LANES), 1)
            values[...] = jnp.where(
                lane == LANES - 1, jnp.ones((ROW, LANES), BF), packed[:, LANES:]
            )

        rows = pl.ds(pl.multiple_of(index * 256, 256), 256)

        def scan(count):
            start = jnp.where(index < 4, 0, ROW - 256 * count)
            query = queries[rows, :]
            mine = column_ids(row_ref[row, :, lanes(index * 256, 256)])
            mine = jnp.concatenate([mine, mine], axis=1)
            top = jnp.full((256, LANES), NEG, F32)
            for part in range(count):
                span = lanes(start + part * 256, 256)
                score = dot_nt(query, keys[span, :])
                score = jnp.where(mine == row_ref[row, :, span], score, NEG)
                scores[:, part * 256 : part * 256 + 256] = score
                top = jnp.maximum(top, jnp.maximum(score[:, :LANES], score[:, LANES:]))
            top = jnp.max(top, axis=1, keepdims=True)
            total = jnp.zeros((256, LANES), F32)
            for part in range(count):
                span = lanes(start + part * 256, 256)
                expo = jnp.exp2(
                    (scores[:, part * 256 : part * 256 + 256] - top) * (SCALE * LOG2E)
                )
                total = total + dot(expo.astype(BF), values[span, :])
            mass = total[:, LANES - 1 :]
            total = total / mass
            turned_o = jnp.transpose(total)[VALUE_LANE : VALUE_LANE + HEAD_WIRE]
            o_own[:, lanes(row * ROW + index * 256, 256)] = turned_o.astype(BF)
            lane = iota((256, LANES), 1)
            logsum = top * (SCALE * LOG2E) + jnp.log2(mass)
            keep_ref[row, rows, :] = jnp.where(lane == 0, logsum, total)

        for count in (5, 6, 7, 8):
            pl.when((index == count - 5) | (index == 12 - count))(functools.partial(scan, count))

        @pl.when(step == 2)
        def _():
            first.fourth(2)

        @pl.when(step == 4)
        def _():
            first.fourth(3)

        @pl.when((step >= 6) & (lax.rem(step, 2) == 0) & (step < 14))
        def _():
            first.fifth(lax.div(step - 6, 2))

        for micro in range(2):
            pl.when(step == 8 * micro + 7)(functools.partial(outs[micro].start, micro))
        return carry

    lax.fori_loop(0, 16, block, 0)
    first.close()
    leave.wait()
    red.drain()
    first.drain()
    for micro in range(2):
        ins[micro].drain(micro)
        outs[micro].finish(micro)
    for micro in range(2):
        outs[micro].drain(micro)
    twin.ready()
    twin.drain()


def front(slab, up, down, tokens, cotangent, lines, picture, tag):
    any_ = pl.BlockSpec(memory_space=pl.ANY)
    vmem = pl.BlockSpec(memory_space=pltpu.VMEM)
    sems = 2 * (3 * Gatherer.SEMS + 3) + 64 + 4
    full = (4, 2, 4, 2, 16, ATTN_TOTAL)
    return pl.pallas_call(
        front_kernel,
        out_shape=(
            jax.ShapeDtypeStruct((16, SECOND_TOTAL), BF),
            jax.ShapeDtypeStruct((256, D), BF),
            jax.ShapeDtypeStruct((256, D), BF),
            jax.ShapeDtypeStruct((TAIL, QKV), BF),
            jax.ShapeDtypeStruct((TAIL, D), BF),
            jax.ShapeDtypeStruct((8, D), F32),
            jax.ShapeDtypeStruct((16, 256, WIDE), BF),
            jax.ShapeDtypeStruct((2, ROW, LANES), F32),
            jax.ShapeDtypeStruct((16, HEAD_WIRE, 256), BF),
            jax.ShapeDtypeStruct(full, BF),
            jax.ShapeDtypeStruct((4, 2, 4, 2, 16, FIRST_TOTAL), BF),
            jax.ShapeDtypeStruct((4, 2, 4, 2, 16, 512), BF),
            jax.ShapeDtypeStruct((TAIL, 512), BF),
        ),
        in_specs=[any_] * 2 + [vmem] * 12,
        out_specs=(vmem,) * 8 + (any_,) * 5,
        scratch_shapes=[
            pltpu.VMEM((16, FIRST_TOTAL), BF),
            pltpu.VMEM((2, 8 * FIRST_CHUNK), F32),
            pltpu.VMEM((16, FIRST_CHUNK), F32),
            pltpu.VMEM((4, 2, 4, 2, 16, 256), BF),
            pltpu.VMEM((TAIL, 256), BF),
            pltpu.VMEM(full, BF),
            pltpu.VMEM((256, D), BF),
            pltpu.VMEM((256, QKV), F32),
            pltpu.VMEM((ATTN_CHUNK // LANES, LEAD, LANES), F32),
            pltpu.VMEM((TAIL, 8 * ATTN_CHUNK), BF),
            pltpu.VMEM((8, D), F32),
            pltpu.VMEM((24, D), BF),
            pltpu.VMEM((16, WIRE, 256), BF),
            pltpu.VMEM((WIRE, 2 * ROW), BF),
            pltpu.VMEM((HEAD_WIRE, 2 * ROW), BF),
            pltpu.VMEM((ROW, LANES), BF),
            pltpu.VMEM((ROW, LANES), BF),
            pltpu.VMEM((ROW, LANES), BF),
            pltpu.VMEM((256, ROW), F32),
            pltpu.VMEM((2, ROW), jnp.int32),
            pltpu.VMEM((2, 1, ROW), F32),
            pltpu.SemaphoreType.DMA((sems,)),
            pltpu.SemaphoreType.DMA((sems,)),
            pltpu.SemaphoreType.DMA((2,)),
        ],
        compiler_params=mesh_params(tag),
        name="front",
    )(slab, picture, tokens, cotangent, up, down, *lines)


def middle_kernel(
    attn,
    first,
    slab,
    o_ref,
    x_ref,
    g_ref,
    out_b_ref,
    vec_ref,
    bias_ref,
    place_ref,
    mixed_ref,
    do_ref,
    dmid_ref,
    gvec_ref,
    gbias_ref,
    dy_all,
    dpre_all,
    active_all,
    h_main_all,
    h_tail_all,
    g_main_all,
    g_tail_all,
    o_main_all,
    o_tail_all,
    dy,
    dpre_ref,
    active_ref,
    h_main_ref,
    h_tail_ref,
    g_main_ref,
    g_tail_ref,
    o_main_ref,
    o_tail_ref,
    out_a,
    weights,
    full,
    o_perm,
    mid,
    h2,
    result,
    dh2,
    wide,
    tail,
    bias,
    send,
    recv,
    local,
):
    place, core = here()
    red = Gatherer(SECOND_WIDTHS, place, core, slab, full, send, recv, 0)
    out_in = pltpu.make_async_copy(attn.at[:, pl.ds(QKV, D)], out_a, local.at[0])
    out_in.start()
    first_in = pltpu.make_async_copy(first, weights, local.at[1])
    first_in.start()
    base = 3 * Gatherer.SEMS + 3
    twin = Twin(place, core, send, recv, base)
    chunks = Twin(place, core, send, recv, base + 14)
    greet(line_peers(place, core) + [device_at(place, 1 - core)])
    red.start()
    bias[...] = jnp.zeros_like(bias)
    bias[:, :FF] = bias_ref[...].reshape(1, FF)
    blocks = jnp.transpose(o_ref[...].reshape(HEADS * HEAD_WIRE, 256))
    o_perm[...] = dot(blocks, place_ref[...]).astype(BF)
    red.second()
    out_in.wait()
    for part in range(3):
        columns = slice(384 * part, 384 * part + 384)
        value = dot(o_perm[:, :LEAD], out_a[:, columns])
        value = value + dot(o_perm[:, LEAD:], out_b_ref[:, columns])
        mid[:, columns] = x_ref[:, columns].astype(F32) + value + vec_ref[4:5, columns]
    unit, _ = normal(mid[...])
    h2[...] = (unit * vec_ref[2:3] + vec_ref[3:4]).astype(BF)
    for steps in (1, 2, 3):
        red.third(steps)

    def turn(value, main, rest, main_all, rest_all):
        turned = jnp.transpose(value)
        main[...] = turned[:LEAD].reshape(4, 2, 4, 2, 16, 256)
        rest[...] = turned[LEAD:]
        twin.give(main, main_all, 5)
        twin.give(rest, rest_all, 1)

    turn(o_perm[...], o_main_ref, o_tail_ref, o_main_all, o_tail_all)
    turn(h2[...], h_main_ref, h_tail_ref, h_main_all, h_tail_all)
    turn(g_ref[...], g_main_ref, g_tail_ref, g_main_all, g_tail_all)
    result[...] = jnp.zeros_like(result)
    dh2[...] = jnp.zeros_like(dh2)
    first_in.wait()

    def tile_of(ref, main):
        def read(tile):
            start = main + tile * LANES
            return ref[:, :, :, :, :, start : start + LANES].reshape(LEAD, LANES)

        return read

    spread_tail(tile_of(weights, 2 * FIRST), FIRST_CHUNK, wide, tail)

    def deliver(number, place_all):
        for item, (source, target) in enumerate(((dpre_ref, dpre_all), (active_ref, active_all))):
            chunks.pass_part(source.at[:, place_all], target, place_all, 2 * number + item)

    def chunk(ref, span, width, index, size, number):
        up_place = lanes(index * size, size)
        down_place = lanes(width + index * size, size)
        place_all = lanes(span + index * size, size)
        up = ref[:, :, :, :, :, up_place].reshape(LEAD, size)
        down = ref[:, :, :, :, :, down_place].reshape(LEAD, size)
        up_tail = tail[:, up_place]
        down_tail = tail[:, down_place]
        pre = dot(h2[:, :LEAD], up) + dot(h2[:, LEAD:], up_tail) + bias[:, place_all]
        square = pre * pre
        bend = jnp.tanh(TANH_A * pre * (1.0 + TANH_B * square))
        half = 0.5 * (1.0 + bend)
        active = (pre * half).astype(BF)
        slope = half + 0.5 * pre * (1.0 - bend * bend) * (TANH_A * (1.0 + 3.0 * TANH_B * square))
        back = dot(g_ref[:, :LEAD], down) + dot(g_ref[:, LEAD:], down_tail)
        dpre = (back * slope).astype(BF)
        active_ref[:, place_all] = active
        dpre_ref[:, place_all] = dpre
        active_t = jnp.transpose(active)
        dpre_t = jnp.transpose(dpre)
        result[:LEAD] += dot(down, active_t)
        result[LEAD:] += dot(down_tail, active_t)
        dh2[:LEAD] += dot(up, dpre_t)
        dh2[LEAD:] += dot(up_tail, dpre_t)
        gbias_ref[:, place_all] = column_total(dpre.astype(F32))
        deliver(number, place_all)

    def early(index, carry):
        chunk(weights, 0, FIRST, index, FIRST_STEP, index)

        @pl.when(index == 0)
        def _():
            for steps in range(4):
                red.fourth(steps)

        @pl.when(index == 2)
        def _():
            for steps in range(4):
                red.fifth(steps)

        return carry

    lax.fori_loop(0, FIRST // FIRST_STEP, early, 0)
    red.close()
    spread_tail(tile_of(full, 2 * SECOND), SECOND_CHUNK, wide, tail)

    def late(index, carry):
        chunk(full, FIRST, SECOND, index, SECOND_STEP, index + FIRST // FIRST_STEP)
        return carry

    lax.fori_loop(0, SECOND // SECOND_STEP, late, 0)
    red.drain()
    gain = vec_ref[2:3]
    unit, rate = normal(mid[...])
    grad = jnp.transpose(dh2[...])
    gvec_ref[...] = jnp.zeros_like(gvec_ref)
    gvec_ref[0:1] = column_total(grad * unit)
    gvec_ref[1:2] = column_total(grad)
    gvec_ref[3:4] = column_total(g_ref[...].astype(F32))
    dmid = g_ref[...].astype(F32) + normal_back(unit, rate, gain, grad)
    dmid_ref[...] = dmid
    dlow = dmid.astype(BF)
    dy[...] = dlow
    twin.give(dy, dy_all, 0)
    gvec_ref[2:3] = column_total(dlow.astype(F32))
    mixed_ref[...] = (mid[...] + jnp.transpose(result[...]) + vec_ref[5:6]).astype(BF)
    low_t = jnp.transpose(dlow)
    result[:LEAD] = dot(out_a[...], low_t)
    result[LEAD:] = dot(out_b_ref[...], low_t)
    value = dot(place_ref[...], result[...].astype(BF)).astype(BF)
    do_ref[...] = value.reshape(HEADS, HEAD_WIRE, 256)
    twin.ready()
    twin.drain()
    number = 0
    for start, stop, size in ((0, FIRST, FIRST_STEP), (FIRST, FF_PAD, SECOND_STEP)):
        for spot in range(start, stop, size):
            for item, target in enumerate((dpre_all, active_all)):
                chunks.part_done(target, pl.ds(spot, size), 2 * number + item)
            number += 1


def middle(attn, first, slab, o, x, g, out_tail, vec, bias, tag):
    any_ = pl.BlockSpec(memory_space=pl.ANY)
    vmem = pl.BlockSpec(memory_space=pltpu.VMEM)
    sems = 3 * Gatherer.SEMS + 3 + 14 + 24
    turned = [(4, 2, 4, 2, 16, 256), (TAIL, 256)] * 3
    both = [(4, 2, 4, 2, 16, 512), (TAIL, 512)] * 3
    place = place_matrix().astype(BF)
    found = pl.pallas_call(
        middle_kernel,
        out_shape=tuple(
            [
                jax.ShapeDtypeStruct((256, D), BF),
                jax.ShapeDtypeStruct((HEADS, HEAD_WIRE, 256), BF),
                jax.ShapeDtypeStruct((256, D), F32),
                jax.ShapeDtypeStruct((8, D), F32),
                jax.ShapeDtypeStruct((1, FF_PAD), F32),
                jax.ShapeDtypeStruct((512, D), BF),
                jax.ShapeDtypeStruct((512, FF_PAD), BF),
                jax.ShapeDtypeStruct((512, FF_PAD), BF),
            ]
            + [jax.ShapeDtypeStruct(shape, BF) for shape in both]
        ),
        in_specs=[any_] * 3 + [vmem] * 7,
        out_specs=(vmem,) * 5 + (any_,) * 9,
        scratch_shapes=[
            pltpu.VMEM((256, D), BF),
            pltpu.VMEM((256, FF_PAD), BF),
            pltpu.VMEM((256, FF_PAD), BF),
        ]
        + [pltpu.VMEM(shape, BF) for shape in turned]
        + [
            pltpu.VMEM((LEAD, D), BF),
            pltpu.VMEM((4, 2, 4, 2, 16, FIRST_TOTAL), BF),
            pltpu.VMEM((4, 2, 4, 2, 16, SECOND_TOTAL), BF),
            pltpu.VMEM((256, D), BF),
            pltpu.VMEM((256, D), F32),
            pltpu.VMEM((256, D), BF),
            pltpu.VMEM((D, 256), F32),
            pltpu.VMEM((D, 256), F32),
            pltpu.VMEM((FIRST_CHUNK // LANES, LEAD, LANES), F32),
            pltpu.VMEM((TAIL, 8 * FIRST_CHUNK), BF),
            pltpu.VMEM((1, FF_PAD), F32),
            pltpu.SemaphoreType.DMA((sems,)),
            pltpu.SemaphoreType.DMA((sems,)),
            pltpu.SemaphoreType.DMA((2,)),
        ],
        compiler_params=mesh_params(tag),
        name="middle",
    )(attn, first, slab, o, x, g, out_tail, vec, bias, place)
    return found[:8], found[12:14], found[8:10], found[10:12]


class Everyone:
    def __init__(self, place, core, slots, send, recv, base):
        self.place, self.core = place, core
        self.slots, self.send, self.recv, self.base = slots, send, recv, base

    def start(self, stage, value):
        if stage == 3:
            spot, targets = self.core, [(1, device_at(self.place, 1 - self.core))]
        else:
            axis = AXES[stage]
            spot = self.place[axis]
            targets = [
                (over, device_at(moved(self.place, axis, over), self.core)) for over in (2, 1, 3)
            ]
        self.slots[stage, spot] = value.astype(BF)
        for over, device in targets:
            index = self.base + stage * 3 + over - 1
            slot = self.slots.at[stage, spot]
            remote(slot, slot, self.send.at[index], self.recv.at[index], device).start()

    def finish(self, stage):
        count = 2 if stage == 3 else 4
        for over in range(1, count):
            index = self.base + stage * 3 + over - 1
            spot = 1 - self.core if stage == 3 else cycle(self.place[AXES[stage]], 4 - over)
            slot = self.slots.at[stage, spot]
            remote(
                slot, slot, self.send.at[index], self.recv.at[index], device_at(self.place, self.core)
            ).wait_recv()
        total = self.slots[stage, 0].astype(F32)
        for spot in range(1, count):
            total = total + self.slots[stage, spot].astype(F32)
        return total

    def drain(self):
        for stage in range(4):
            for over in range(1, 2 if stage == 3 else 4):
                index = self.base + stage * 3 + over - 1
                slot = self.slots.at[stage, 0]
                remote(
                    slot,
                    slot,
                    self.send.at[index],
                    self.recv.at[index],
                    device_at(self.place, self.core),
                ).wait_send()


def finish_kernel(
    dheads,
    weight,
    dy,
    dpre,
    active,
    h_main,
    h_tail,
    o_main,
    o_tail,
    h2_main,
    h2_tail,
    g_main,
    g_tail,
    tail_ref,
    x_ref,
    dmid_ref,
    vec_ref,
    gvec_ref,
    gup_ref,
    tokens_ref,
    total_ref,
    share_ref,
    second_ref,
    dheads_all,
    weight_all,
    flat,
    flat_all,
    dy_all,
    dpre_all,
    active_all,
    h_main_all,
    h_tail_all,
    o_main_all,
    o_tail_all,
    h2_main_all,
    h2_tail_all,
    g_main_all,
    g_tail_all,
    extra,
    dh,
    vectors,
    slots,
    *rest,
):
    buffers, (send, recv, local) = rest[:-3], rest[-3:]
    place, core = here()
    red = Reducer(ATTN_WIDTHS, place, core, buffers[:18], share_ref, send, recv)
    base = 3 * Reducer.SEMS
    late = Reducer(SECOND_WIDTHS, place, core, buffers[18:], second_ref, send, recv, base)
    base = 2 * base
    twin = Twin(place, core, send, recv, base)
    every = Everyone(place, core, slots, send, recv, base + 2)
    heads_in = pltpu.make_async_copy(dheads, dheads_all, local.at[0])
    heads_in.start()
    weight_in = pltpu.make_async_copy(weight.at[:, pl.ds(0, QKV)], weight_all, local.at[1])
    weight_in.start()
    greet(line_peers(place, core) + [device_at(place, 1 - core)])
    loads = []
    for source, target in (
        (h_main, h_main_all),
        (h_tail, h_tail_all),
        (o_main, o_main_all),
        (o_tail, o_tail_all),
        (dy, dy_all),
        (h2_main, h2_main_all),
        (h2_tail, h2_tail_all),
        (g_main, g_main_all),
        (g_tail, g_tail_all),
        (dpre.at[:, pl.ds(FIRST, SECOND)], dpre_all),
        (active.at[:, pl.ds(FIRST, SECOND)], active_all),
    ):
        copy = pltpu.make_async_copy(source, target, local.at[2 + len(loads)])
        copy.start()
        loads.append(copy)
    heads_in.wait()
    for head in range(HEADS):
        flat[:, PACK * head : PACK * head + PACK] = jnp.transpose(dheads_all[head])[:, :PACK]
    twin.give(flat, flat_all, 0)

    late_maker = Maker(
        late,
        [((h2_main_all, h2_tail_all), dpre_all), ((g_main_all, g_tail_all), active_all)],
        extra.at[pl.ds(0, SECOND_CHUNK // LANES)],
        SECOND_CHUNK,
    )
    maker = Maker(
        red,
        [((h_main_all, h_tail_all), flat_all), ((o_main_all, o_tail_all), dy_all)],
        extra,
        ATTN_CHUNK,
    )
    for copy in loads:
        copy.wait()
    late_maker.run()
    twin.ready()
    maker.run()
    dh[...] = jnp.zeros_like(dh)
    vectors[...] = jnp.zeros((VEC_ROWS, D), F32)
    vectors[2:6] = gvec_ref[:4]
    for row in range(4):
        span = slice(row * D, min((row + 1) * D, FF_PAD))
        vectors[VEC_UP + row : VEC_UP + row + 1, : span.stop - span.start] = gup_ref[:, span]
    weight_in.wait()

    for row in range(3):

        def columns(index, carry):
            span = lanes(row * D + index * 384, 384)
            value = flat[:, span]
            vectors[VEC_QKV + row : VEC_QKV + row + 1, lanes(index * 384, 384)] = column_total(
                value.astype(F32)
            )
            value_t = jnp.transpose(value)
            dh[:LEAD] += dot(weight_all[:, span], value_t)
            dh[LEAD:] += dot(tail_ref[:, span], value_t)
            return carry

        lax.fori_loop(0, 3, columns, 0)
    for spot in range(4):
        late.pass_on(spot)
    unit, rate = normal(x_ref[...].astype(F32))
    grad = jnp.transpose(dh[...])
    vectors[0:1] = column_total(grad * unit)
    vectors[1:2] = column_total(grad)
    every.start(0, vectors[...])
    for spot in range(4):
        red.pass_on(spot)
    total = dmid_ref[...] + normal_back(unit, rate, vec_ref[0:1], grad)
    tokens_ref[...] = total.astype(BF)
    every.start(1, every.finish(0))
    for over in (2, 1, 3):
        late.gather_side(over, False)
    late.gather_side(0, True)
    every.start(2, every.finish(1))
    for over in (2, 1, 3):
        red.gather_side(over, False)
    red.gather_side(0, True)
    every.start(3, every.finish(2))
    late.line_up()
    red.line_up()
    late.share()
    total_ref[...] = every.finish(3)
    red.share()
    late.close()
    red.close()
    twin.drain()
    every.drain()


def finish(dheads, weight, dy, dpre, active, turned, tail, x, dmid, vec, gvec, gup, tag):
    any_ = pl.BlockSpec(memory_space=pl.ANY)
    vmem = pl.BlockSpec(memory_space=pltpu.VMEM)
    sems = 6 * Reducer.SEMS + 2 + 12
    rows = [pltpu.VMEM((4, 2, 4, 2, 16, 512), BF), pltpu.VMEM((TAIL, 512), BF)]
    return pl.pallas_call(
        finish_kernel,
        out_shape=(
            jax.ShapeDtypeStruct((256, D), BF),
            jax.ShapeDtypeStruct((VEC_ROWS, D), F32),
            jax.ShapeDtypeStruct((16, ATTN_TOTAL), BF),
            jax.ShapeDtypeStruct((16, SECOND_TOTAL), BF),
        ),
        in_specs=[any_] * 13 + [vmem] * 6,
        out_specs=(vmem,) * 4,
        scratch_shapes=[
            pltpu.VMEM((HEADS, WIRE, 256), BF),
            pltpu.VMEM((LEAD, QKV), BF),
            pltpu.VMEM((256, QKV), BF),
            pltpu.VMEM((512, QKV), BF),
            pltpu.VMEM((512, D), BF),
            pltpu.VMEM((512, SECOND), BF),
            pltpu.VMEM((512, SECOND), BF),
        ]
        + rows * 4
        + [
            pltpu.VMEM((ATTN_CHUNK // LANES, LEAD, LANES), F32),
            pltpu.VMEM((D, 256), F32),
            pltpu.VMEM((VEC_ROWS, D), F32),
            pltpu.VMEM((4, 4, VEC_ROWS, D), BF),
        ]
        + Reducer.scratch(ATTN_WIDTHS)
        + Reducer.scratch(SECOND_WIDTHS)
        + [
            pltpu.SemaphoreType.DMA((sems,)),
            pltpu.SemaphoreType.DMA((sems,)),
            pltpu.SemaphoreType.DMA((13,)),
        ],
        compiler_params=mesh_params(tag),
        name="finish",
    )(dheads, weight, dy, dpre, active, *turned, tail, x, dmid, vec, gvec, gup)


def close_kernel(
    totals_ref,
    attn_ref,
    first_ref,
    second_ref,
    mixed_in,
    tokens_in,
    unmix_ref,
    mixed_ref,
    tokens_ref,
    query_ref,
    key_ref,
    value_ref,
    out_ref,
    up_ref,
    down_ref,
    gain1_ref,
    bias1_ref,
    gain2_ref,
    bias2_ref,
    bias_out_ref,
    bias_down_ref,
    bias_query_ref,
    bias_value_ref,
    bias_up_ref,
    attn,
    first,
    second,
    vec,
    stack,
):
    def unpack(share, full, main, chunk):
        full[0:16, :] = share[:, :main].astype(F32)
        rest = share[:, main : main + chunk].astype(F32)
        for row in range(2):
            for index in range(8):
                size = min(main - index * chunk, chunk)
                if size > 0:
                    start = index * chunk
                    spot = row * 8 + index
                    full[16 + row : 17 + row, start : start + size] = rest[
                        spot : spot + 1, :size
                    ]

    unpack(attn_ref, attn, ATTN_MAIN, ATTN_CHUNK)
    unpack(first_ref, first, 2 * FIRST, FIRST_CHUNK)
    unpack(second_ref, second, 2 * SECOND, SECOND_CHUNK)
    for head in range(HEADS):
        span = slice(head * HEAD_DIM, (head + 1) * HEAD_DIM)
        for index, ref in enumerate((key_ref, query_ref, value_ref)):
            start = head * PACK + index * HEAD_DIM
            ref[:, span] = attn[:18, start : start + HEAD_DIM]
    stack[0:256] = mixed_in[...]
    stack[256:512] = tokens_in[...]
    stack[512:544] = jnp.concatenate(
        [attn[:, QKV:ATTN_MAIN].astype(BF), jnp.zeros((8, D), BF)], axis=0
    )
    stack[544:576] = jnp.concatenate(
        [exact_parts(totals_ref[0:8, :]), jnp.zeros((8, D), BF)], axis=0
    )
    for part in range(3):
        columns = slice(384 * part, 384 * part + 384)
        value = dot(stack[...], unmix_ref[:, columns])
        mixed_ref[:, columns] = value[0:256].astype(BF)
        tokens_ref[:, columns] = value[256:512].astype(BF)
        out_ref[:, columns] = value[512:530]
        vec[0:8, columns] = value[544:552] + value[552:560] + value[560:568]
    lines = (gain1_ref, bias1_ref, gain2_ref, bias2_ref, bias_out_ref, bias_down_ref)
    for index, ref in enumerate(lines):
        ref[...] = vec[index : index + 1, :D].reshape(D)
    for row in range(3):
        vec[8:9, row * D : (row + 1) * D] = totals_ref[VEC_QKV + row : VEC_QKV + row + 1, :]
    for head in range(HEADS):
        span = slice(head * HEAD_DIM, (head + 1) * HEAD_DIM)
        for index, row in ((1, 9), (2, 10)):
            start = head * PACK + index * HEAD_DIM
            vec[row : row + 1, span] = vec[8:9, start : start + HEAD_DIM]
    bias_query_ref[...] = vec[9:10, :D].reshape(D)
    bias_value_ref[...] = vec[10:11, :D].reshape(D)
    for row in range(4):
        size = min(FF - row * D, D)
        vec[11:12, row * D : row * D + size] = totals_ref[
            VEC_UP + row : VEC_UP + row + 1, :size
        ]
    bias_up_ref[...] = vec[11:12, :FF].reshape(FF)
    up_ref[:, :FIRST] = first[:18, :FIRST]
    up_ref[:, FIRST:] = second[:18, : FF - FIRST]
    down_ref[:, :FIRST] = first[:18, FIRST : 2 * FIRST]
    down_ref[:, FIRST:] = second[:18, SECOND : SECOND + FF - FIRST]


def close_layer(totals, attn, first, second, mixed, tokens):
    line = jax.ShapeDtypeStruct((D,), F32)
    square = jax.ShapeDtypeStruct((18, D), F32)
    return pl.pallas_call(
        close_kernel,
        out_shape=(
            jax.ShapeDtypeStruct((256, D), BF),
            jax.ShapeDtypeStruct((256, D), BF),
            square,
            square,
            square,
            square,
            jax.ShapeDtypeStruct((18, FF), F32),
            jax.ShapeDtypeStruct((18, FF), F32),
            *([line] * 8),
            jax.ShapeDtypeStruct((FF,), F32),
        ),
        scratch_shapes=[
            pltpu.VMEM((24, ATTN_MAIN), F32),
            pltpu.VMEM((24, 2 * FIRST), F32),
            pltpu.VMEM((24, 2 * SECOND), F32),
            pltpu.VMEM((16, 4 * D), F32),
            pltpu.VMEM((576, D), BF),
        ],
        compiler_params=params(),
        name="close_layer",
    )(totals, attn, first, second, mixed, tokens, mix_matrix().T.astype(BF))


def pack_slab(weight, chunk, total):
    width = weight.shape[1]
    rest = jnp.pad(weight[16:], ((0, 0), (0, 8 * chunk - width))).reshape(16, chunk)
    return jnp.concatenate(
        [weight[:16], rest, jnp.zeros((16, total - width - chunk), weight.dtype)], axis=1
    )


def by_head(key, query, value):
    rows = key.shape[0]
    parts = [item.reshape(rows, HEADS, 1, HEAD_DIM) for item in (key, query, value)]
    return jnp.concatenate(parts, axis=2).reshape(rows, QKV)


def mixing():
    return onehot(iota((D, D), 0) == origin(iota((D, D), 1)))


def body(
    tokens,
    picture,
    cotangent,
    ln1_gain,
    ln1_bias,
    w_query,
    b_query,
    w_key,
    w_value,
    b_value,
    w_out,
    b_out,
    ln2_gain,
    ln2_bias,
    w_fc1,
    b_fc1,
    w_fc2,
    b_fc2,
):
    mix = mixing()
    out_cols = dot(w_out, mix).astype(BF)
    attn_slab = pack_slab(
        jnp.concatenate([by_head(w_key, w_query, w_value), out_cols], axis=1),
        ATTN_CHUNK,
        ATTN_TOTAL,
    )
    lines = (ln1_gain, ln1_bias, ln2_gain, ln2_bias, b_out, b_fc2, b_query, b_value)
    second_slab, x, g, attn_tail, out_tail, vec, packed, keep, o, attn, first, h_main, h_tail = front(
        attn_slab,
        w_fc1,
        w_fc2.T,
        tokens.reshape(256, D),
        cotangent.reshape(256, D),
        lines,
        picture,
        0,
    )
    attn = attn.reshape(LEAD, ATTN_TOTAL)
    (mixed, go, dmid, gvec2, gbias1, dy, dpre, active), o_turned, h_turned, g_turned = middle(
        attn, first, second_slab, o, x, g, out_tail, vec, b_fc1, 2
    )
    first_share, dheads = attend_back_reduce(
        go, dpre, active, (*h_turned, *g_turned), packed, keep, picture, 3
    )
    gtokens, totals, attn_share, second_share = finish(
        dheads,
        attn,
        dy,
        dpre,
        active,
        (h_main, h_tail, *o_turned, *h_turned, *g_turned),
        attn_tail,
        x,
        dmid,
        vec,
        gvec2,
        gbias1,
        4,
    )
    (
        mixed,
        gtokens,
        grad_query,
        grad_key,
        grad_value,
        grad_out,
        grad_up,
        grad_down,
        grad_gain1,
        grad_bias1,
        grad_gain2,
        grad_bias2,
        grad_b_out,
        grad_b_fc2,
        grad_b_query,
        grad_b_value,
        grad_b_fc1,
    ) = close_layer(totals, attn_share, first_share, second_share, mixed, gtokens)
    return (
        mixed.reshape(2, 128, D),
        gtokens.reshape(2, 128, D),
        grad_gain1,
        grad_bias1,
        grad_query,
        grad_b_query,
        grad_key,
        grad_value,
        grad_b_value,
        grad_out,
        grad_b_out,
        grad_gain2,
        grad_bias2,
        grad_up,
        grad_b_fc1,
        grad_down.T,
        grad_b_fc2,
    )


def solution(mesh):
    placed = (
        P(None, ("fsdp", "rep"), None),
        P(),
        P(None, ("fsdp", "rep"), None),
        P(),
        P(),
        P("fsdp", None),
        P(),
        P("fsdp", None),
        P("fsdp", None),
        P(),
        P("fsdp", None),
        P(),
        P(),
        P(),
        P("fsdp", None),
        P(),
        P(None, "fsdp"),
        P(),
    )
    return jax.shard_map(
        body,
        mesh=mesh,
        in_specs=placed,
        out_specs=(
            P(None, ("fsdp", "rep"), None),
            P(None, ("fsdp", "rep"), None),
            P(),
            P(),
            P("fsdp", None),
            P(),
            P("fsdp", None),
            P("fsdp", None),
            P(),
            P("fsdp", None),
            P(),
            P(),
            P(),
            P("fsdp", None),
            P(),
            P(None, "fsdp"),
            P(),
        ),
        check_vma=False,
    )
```

```python
import functools

import jax
import jax.numpy as jnp
import numpy as np
from jax import lax
from jax.experimental import pallas as pl
from jax.experimental.pallas import tpu as pltpu
from jax.sharding import PartitionSpec as P

MESH = pl.DeviceIdType.MESH
BF = jnp.bfloat16
F32 = jnp.float32
LANES = 128
ORDERS = (("x", "y", "z"), ("y", "z", "x"), ("z", "x", "y"))
AXES = ("x", "y", "z")


def here():
    shard = lax.axis_index("fsdp")
    low = lax.axis_index("rep")
    place = {
        "x": lax.div(shard, 16),
        "y": lax.rem(lax.div(shard, 8), 2) * 2 + low,
        "z": lax.rem(lax.div(shard, 2), 4),
    }
    return place, lax.rem(shard, 2)


def moved(place, axis, steps):
    steps = steps % 4
    if steps == 0:
        return place
    other = dict(place)
    other[axis] = lax.rem(place[axis] + steps, 4)
    return other


def device_at(place, core):
    high = lax.div(place["y"], 2)
    return (((place["x"] * 2 + high) * 4 + place["z"]) * 2 + core, lax.rem(place["y"], 2))


def greet(peers):
    barrier = pltpu.get_barrier_semaphore()
    for peer in peers:
        pl.semaphore_signal(barrier, inc=1, device_id=peer, device_id_type=MESH)
    pl.semaphore_wait(barrier, len(peers))


def part_columns(part, half, widths):
    start = 2 * sum(widths[:part]) + half * widths[part]
    return pl.ds(pl.multiple_of(start, LANES), widths[part])


def piece_of(ref, part, widths, place, core):
    return ref.at[
        place["x"],
        lax.div(place["y"], 2),
        place["z"],
        core,
        :,
        part_columns(part, lax.rem(place["y"], 2), widths),
    ]


def block_of(ref, part, widths, place, core, axis, half=None):
    where = {"x": place["x"], "y": lax.div(place["y"], 2), "z": place["z"]}
    if axis == "y":
        where["y"] = pl.ds(0, 2) if half is None else pl.ds(half, 1)
        columns = pl.ds(2 * sum(widths[:part]), 2 * widths[part])
    else:
        where[axis] = pl.ds(0, 4) if half is None else pl.ds(2 * half, 2)
        columns = part_columns(part, lax.rem(place["y"], 2), widths)
    return ref.at[where["x"], where["y"], where["z"], core, :, columns]


def remote(source, target, send, recv, device):
    return pltpu.make_async_remote_copy(
        src_ref=source,
        dst_ref=target,
        send_sem=send,
        recv_sem=recv,
        device_id=device,
        device_id_type=MESH,
    )


def cycle(value, steps):
    return lax.rem(value + steps, 4)


def turned_by(place, axis, steps):
    other = dict(place)
    other[axis] = cycle(place[axis], steps)
    return other


class Gatherer:
    SEMS = 3 + 3 + 8 + 8 + 16
    KINDS = {"one": 0, "two": 3, "three": 6, "four": 14, "twin": 22}

    def __init__(self, widths, place, core, own, full, send, recv, base):
        self.widths, self.place, self.core = widths, place, core
        self.own, self.full, self.send, self.recv, self.base = own, full, send, recv, base
        self.twin = device_at(place, 1 - core)

    def slot(self, part, kind, index):
        return self.base + part * self.SEMS + self.KINDS[kind] + index

    def push(self, source, target, slot, device):
        remote(source, target, self.send.at[slot], self.recv.at[slot], device).start()

    def arrived(self, region, slot):
        remote(region, region, self.send.at[slot], self.recv.at[slot], self.twin).wait_recv()

    def sent(self, region, slot):
        remote(region, region, self.send.at[slot], self.recv.at[slot], self.twin).wait_send()

    def block(self, part, place, half=None, core=None):
        core = self.core if core is None else core
        return block_of(self.full, part, self.widths, place, core, ORDERS[part][0], half)

    def keep(self, part):
        low = lax.rem(self.place["y"], 2)
        source = self.own.at[:, part_columns(part, low, self.widths)]
        target = piece_of(self.full, part, self.widths, self.place, self.core)
        return source, target, pltpu.make_async_copy(
            source, target, self.recv.at[self.base + 3 * self.SEMS + part]
        )

    def start(self):
        for part, (one, two, three) in enumerate(ORDERS):
            source, target, copy = self.keep(part)
            copy.start()
            for steps in (1, 3, 2):
                device = device_at(turned_by(self.place, one, steps), self.core)
                self.push(source, target, self.slot(part, "one", steps - 1), device)

    def second(self):
        for part, (one, two, three) in enumerate(ORDERS):
            self.keep(part)[2].wait()
            for steps in (1, 3, 2):
                origin = turned_by(self.place, one, 4 - steps)
                region = piece_of(self.full, part, self.widths, origin, self.core)
                self.arrived(region, self.slot(part, "one", steps - 1))
            block = self.block(part, self.place)
            for steps in (1, 3, 2):
                device = device_at(turned_by(self.place, two, steps), self.core)
                self.push(block, block, self.slot(part, "two", steps - 1), device)
        self.spread(0)

    def spread(self, steps):
        for part, (one, two, three) in enumerate(ORDERS):
            block = self.block(part, turned_by(self.place, two, 4 - steps))
            for index, way in enumerate((1, 3)):
                device = device_at(turned_by(self.place, three, way), self.core)
                self.push(block, block, self.slot(part, "three", index * 4 + steps), device)
            self.push(block, block, self.slot(part, "twin", steps), self.twin)

    def third(self, steps):
        for part, (one, two, three) in enumerate(ORDERS):
            block = self.block(part, turned_by(self.place, two, 4 - steps))
            self.arrived(block, self.slot(part, "two", steps - 1))
        self.spread(steps)

    def fourth(self, steps):
        for part, (one, two, three) in enumerate(ORDERS):
            side = turned_by(self.place, two, 4 - steps)
            for index, way in enumerate((1, 3)):
                origin = turned_by(side, three, 4 - way)
                block = self.block(part, origin)
                self.arrived(block, self.slot(part, "three", index * 4 + steps))
                half = self.block(part, origin, index)
                device = device_at(turned_by(self.place, three, way), self.core)
                self.push(half, half, self.slot(part, "four", index * 4 + steps), device)
                self.push(block, block, self.slot(part, "twin", way * 4 + steps), self.twin)

    def fifth(self, steps):
        for part, (one, two, three) in enumerate(ORDERS):
            origin = turned_by(turned_by(self.place, two, 4 - steps), three, 2)
            for index in range(2):
                half = self.block(part, origin, index)
                self.arrived(half, self.slot(part, "four", index * 4 + steps))
            block = self.block(part, origin)
            self.push(block, block, self.slot(part, "twin", 8 + steps), self.twin)

    def close(self):
        for part, (one, two, three) in enumerate(ORDERS):
            for way in range(4):
                for steps in range(4):
                    origin = moved(moved(self.place, two, -steps), three, -way)
                    region = self.block(part, origin, core=1 - self.core)
                    self.arrived(region, self.slot(part, "twin", way * 4 + steps))

    def drain(self):
        for part in range(3):
            piece = piece_of(self.full, part, self.widths, self.place, self.core)
            block = self.block(part, self.place)
            half = self.block(part, self.place, 0)
            for kind, region, count in (
                ("one", piece, 3),
                ("two", block, 3),
                ("three", block, 8),
                ("four", half, 8),
                ("twin", block, 16),
            ):
                for index in range(count):
                    self.sent(region, self.slot(part, kind, index))


class Reducer:
    SEMS = 8 + 8 + 3 + 3 + 1
    KINDS = {"mid": 0, "far": 8, "side": 16, "line": 19, "done": 22}

    def __init__(self, widths, place, core, buffers, out, send, recv, base=0):
        self.widths, self.place, self.core, self.base = widths, place, core, base
        self.acc, self.mid, self.far, self.side, self.line, self.done = [
            buffers[3 * i : 3 * i + 3] for i in range(6)
        ]
        self.out, self.send, self.recv = out, send, recv
        self.me = device_at(place, core)

    @staticmethod
    def scratch(widths):
        found = []
        for lead, half in (((4, 4), 1), ((2, 4), 2), ((2, 4), 1), ((3,), 1)):
            for width, (one, two, three) in zip(widths, ORDERS):
                if one == "y":
                    found.append(pltpu.VMEM(lead + (2 // half, 16, 2 * width), BF))
                else:
                    found.append(pltpu.VMEM(lead + (4 // half, 16, width), BF))
        found += [pltpu.VMEM((3, 16, width), BF) for width in widths]
        found += [pltpu.VMEM((16, width), BF) for width in widths]
        return found

    def slot(self, part, kind, index):
        return self.base + part * self.SEMS + self.KINDS[kind] + index

    def push(self, source, target, slot, device):
        remote(source, target, self.send.at[slot], self.recv.at[slot], device).start()

    def arrived(self, region, slot):
        remote(region, region, self.send.at[slot], self.recv.at[slot], self.me).wait_recv()

    def sent(self, region, slot):
        remote(region, region, self.send.at[slot], self.recv.at[slot], self.me).wait_send()

    def add(self, target, *terms):
        for index in range(target.shape[0]):
            total = target[index].astype(F32)
            for term in terms:
                total = total + term[index].astype(F32)
            target[index] = total.astype(BF)

    def half_of(self, ref, half):
        size = ref.shape[0] // 2
        return ref.at[pl.ds(half * size, size)]

    def far_out(self, part):
        three = ORDERS[part][2]
        for spot in range(4):
            for half, way in ((0, 3), (1, 1)):
                self.push(
                    self.half_of(self.acc[part].at[2, spot], half),
                    self.mid[part].at[half, spot],
                    self.slot(part, "mid", half * 4 + spot),
                    device_at(moved(self.place, three, way), self.core),
                )

    def pass_on(self, spot):
        for part, (one, two, three) in enumerate(ORDERS):
            for half, way in ((0, 3), (1, 1)):
                self.arrived(
                    self.mid[part].at[half, spot], self.slot(part, "mid", half * 4 + spot)
                )
                self.add(
                    self.half_of(self.acc[part].at[way, spot], half), self.mid[part].at[half, spot]
                )
                self.push(
                    self.acc[part].at[way, spot],
                    self.far[part].at[half, spot],
                    self.slot(part, "far", half * 4 + spot),
                    device_at(moved(self.place, three, way), self.core),
                )

    def gather_side(self, over, last):
        for part, (one, two, three) in enumerate(ORDERS):
            spot = cycle(self.place[two], over)
            for half in range(2):
                self.arrived(
                    self.far[part].at[half, spot], self.slot(part, "far", half * 4 + spot)
                )
            self.add(
                self.acc[part].at[0, spot], self.far[part].at[0, spot], self.far[part].at[1, spot]
            )

            def give(part=part, two=two, spot=spot):
                other = dict(self.place)
                other[two] = spot
                self.push(
                    self.acc[part].at[0, spot],
                    self.side[part].at[over - 1],
                    self.slot(part, "side", over - 1),
                    device_at(other, self.core),
                )

            if last is False:
                give()
            elif last is not True:
                pl.when(jnp.logical_not(last))(give)

    def piece(self, part, axis, spot):
        own = self.acc[part].at[0, self.place[ORDERS[part][1]]]
        if axis == "y":
            start = pl.multiple_of(lax.rem(spot["y"], 2) * self.widths[part], LANES)
            return own.at[lax.div(spot["y"], 2), :, pl.ds(start, self.widths[part])]
        return own.at[spot[axis]]

    def line_up(self):
        for part, (one, two, three) in enumerate(ORDERS):
            for over in range(3):
                self.arrived(self.side[part].at[over], self.slot(part, "side", over))
            own = self.acc[part].at[0, self.place[two]]
            self.add(own, self.side[part].at[0], self.side[part].at[1], self.side[part].at[2])
            for over in (2, 1, 3):
                spot = moved(self.place, one, over)
                self.push(
                    self.piece(part, one, spot),
                    self.line[part].at[over - 1],
                    self.slot(part, "line", over - 1),
                    device_at(spot, self.core),
                )

    def share(self):
        low = lax.rem(self.place["y"], 2)
        partner = (lax.axis_index("fsdp"), 1 - low)
        for part, (one, two, three) in enumerate(ORDERS):
            for over in range(3):
                self.arrived(self.line[part].at[over], self.slot(part, "line", over))
            total = self.piece(part, one, self.place)[...].astype(F32)
            for over in range(3):
                total = total + self.line[part][over].astype(F32)
            self.done[part][...] = total.astype(BF)
            columns = part_columns(part, low, self.widths)
            self.push(
                self.done[part], self.out.at[:, columns], self.slot(part, "done", 0), partner
            )
            self.out[:, columns] = self.done[part][...]

    def close(self):
        low = lax.rem(self.place["y"], 2)
        for part, (one, two, three) in enumerate(ORDERS):
            self.arrived(
                self.out.at[:, part_columns(part, 1 - low, self.widths)],
                self.slot(part, "done", 0),
            )
            for half in range(2):
                for spot in range(4):
                    index = half * 4 + spot
                    self.sent(self.mid[part].at[half, spot], self.slot(part, "mid", index))
                    self.sent(self.far[part].at[half, spot], self.slot(part, "far", index))
            for over in range(3):
                self.sent(self.side[part].at[over], self.slot(part, "side", over))
                self.sent(self.line[part].at[over], self.slot(part, "line", over))
            self.sent(self.done[part], self.slot(part, "done", 0))


class Maker:
    def __init__(self, reducer, sources, extra, chunk):
        self.red, self.sources, self.extra, self.chunk = reducer, sources, extra, chunk
        self.main = sum(item[1].shape[1] for item in sources)

    def pack_tail(self):
        start = 0
        pieces = []
        for turned, right in self.sources:
            pieces.append((start, start + right.shape[1], turned, right))
            start += right.shape[1]
        for index in range(8):
            low, high = index * self.chunk, (index + 1) * self.chunk
            for first, last, turned, right in pieces:
                a, b = max(low, first), min(high, last)
                if a < b:
                    value = dot(turned[1][...], right[:, a - first : b - first])
                    self.scatter(index, a - low, value)
            if high > self.main:
                a = max(low, self.main)
                self.scatter(index, a - low, jnp.zeros((TAIL, high - a), F32))

    def scatter(self, index, start, value):
        for tile in range(value.shape[1] // LANES):
            self.extra[start // LANES + tile, pl.ds(index, TAIL, stride=8), :] = value[
                :, tile * LANES : (tile + 1) * LANES
            ]

    def rows(self, ref):
        core = self.red.core
        if len(ref.shape) == 2:
            groups = [
                ref[pl.ds(pl.multiple_of((2 * index + core) * 16, 16), 16)] for index in range(32)
            ]
            return jnp.concatenate(groups, axis=0)
        return ref[:, :, :, core].reshape(512, ref.shape[-1])

    def columns(self, part, half):
        width = self.red.widths[part]
        low = 2 * sum(self.red.widths[:part]) + half * width
        high = low + width
        first = 0
        found = []
        for turned, right in self.sources:
            last = first + right.shape[1]
            a, b = max(low, first), min(high, last)
            if a < b:
                left = self.rows(turned[0])
                found.append(dot(left, right[:, a - first : b - first]).astype(BF))
            first = last
        a, b = max(low, first), min(high, first + self.chunk)
        if a < b:
            for tile in range((a - first) // LANES, (b - first) // LANES):
                found.append(self.rows(self.extra.at[tile]).astype(BF))
        a = max(low, first + self.chunk)
        if a < high:
            found.append(jnp.zeros((512, high - a), BF))
        return found[0] if len(found) == 1 else jnp.concatenate(found, axis=1)

    def make(self, part):
        red, width = self.red, self.red.widths[part]
        acc = red.acc[part]
        three = ORDERS[part][2]
        own = red.place[three]

        def ahead(spot):
            return cycle(spot + 4 - own, 0)

        for half in range(2):
            value = self.columns(part, half).reshape(4, 2, 4, 16, width)
            if three == "z":
                for spot in range(4):
                    for high in range(2):
                        acc[ahead(spot), 2 * high + half] = value[:, high, spot]
            elif three == "x":
                for spot in range(4):
                    for z in range(4):
                        acc[ahead(spot), z, :, :, half * width : (half + 1) * width] = value[
                            spot, :, z
                        ]
            else:
                for high in range(2):
                    for x in range(4):
                        acc[ahead(2 * high + half), x] = value[x, high]

    def run(self):
        self.pack_tail()
        for part in range(3):
            self.make(part)
            self.red.far_out(part)


SWAP_ORDER = (9, 11, 5, 13, 7, 15, 1, 3, 8, 10, 4, 12, 6, 14, 2)


class Swapper:
    def __init__(self, place, core, own, full, send, recv, base):
        self.place, self.core = place, core
        self.own, self.full, self.send, self.recv, self.base = own, full, send, recv, base
        self.low = lax.rem(place["y"], 2)
        self.mine = (place["z"] * 2 + core) * 2 + self.low
        self.group = lax.div(lax.axis_index("fsdp"), 8) * 8

    def member(self, k, sign=1):
        z = lax.rem(self.place["z"] + (4 + sign * (k // 4)), 4)
        core = lax.rem(self.core + (k // 2) % 2, 2)
        low = lax.rem(self.low + k % 2, 2)
        return (z * 2 + core) * 2 + low

    def device(self, index):
        return (self.group + lax.div(index, 2), lax.rem(index, 2))

    def peers(self):
        return [self.device(self.member(k)) for k in range(1, 16)]

    def view(self, ref, index, micro):
        if len(ref.shape) == 3:
            return ref.at[index, :, pl.ds(micro * 128, 128)]
        return ref.at[:, pl.ds(pl.multiple_of(micro * ROW + index * 128, 128), 128)]

    def start(self, micro):
        for k in SWAP_ORDER:
            target = self.member(k)
            remote(
                self.view(self.own, target, micro),
                self.view(self.full, self.mine, micro),
                self.send.at[self.base + k],
                self.recv.at[self.base + k],
                self.device(target),
            ).start()
        pltpu.make_async_copy(
            self.view(self.own, self.mine, micro),
            self.view(self.full, self.mine, micro),
            self.send.at[self.base],
        ).start()

    def finish(self, micro):
        pltpu.make_async_copy(
            self.view(self.own, self.mine, micro),
            self.view(self.full, self.mine, micro),
            self.send.at[self.base],
        ).wait()
        for k in range(1, 16):
            region = self.view(self.full, self.member(k, -1), micro)
            remote(
                region,
                region,
                self.send.at[self.base + k],
                self.recv.at[self.base + k],
                self.device(self.mine),
            ).wait_recv()

    def drain(self, micro):
        for k in range(1, 16):
            region = self.view(self.own, self.member(k), micro)
            remote(
                region,
                region,
                self.send.at[self.base + k],
                self.recv.at[self.base + k],
                self.device(self.mine),
            ).wait_send()


def line_peers(place, core):
    peers = []
    for axis in AXES:
        for steps in (1, 2, 3):
            peers.append(device_at(moved(place, axis, steps), core))
    return peers


D = 1152
HEADS = 16
HEAD_DIM = 72
FF = 4304
ROW = 2048
EPS = 1e-06
NEG = -1e30
SCALE = HEAD_DIM**-0.5
LEAD = 1024
TAIL = 128
PACK = 3 * HEAD_DIM
WIDE = 256
WIRE = 224
HEAD_WIRE = 80
VALUE_LANE = 16
FF_PAD = 4352
QKV = HEADS * PACK
ATTN_MAIN = QKV + D
ATTN_CHUNK = 640
ATTN_TOTAL = 5376
MLP_MAIN = 2 * FF_PAD
MLP_CHUNK = 1152
MLP_TOTAL = 9984
ATTN_WIDTHS = (896, 896, 896)
MLP_WIDTHS = (1664, 1664, 1664)
FIRST = 3072
FIRST_CHUNK = 768
FIRST_TOTAL = 6912
FIRST_WIDTHS = (896, 1408, 1152)
FIRST_STEP = 768
SECOND = FF_PAD - FIRST
SECOND_CHUNK = 384
SECOND_TOTAL = 3072
SECOND_WIDTHS = (512, 512, 512)
SECOND_STEP = 640
LOG2E = 1.4426950408889634
QUERIES = 512
KEYS = 512
BLOCKS = ROW // QUERIES
TANH_A = 0.7978845608028654
TANH_B = 0.044715


def dot(left, right):
    return jnp.dot(left, right, preferred_element_type=F32)


def dot_nt(left, right):
    return lax.dot_general(left, right, (((1,), (1,)), ((), ())), preferred_element_type=F32)


def dot_tn(left, right):
    return lax.dot_general(left, right, (((0,), (0,)), ((), ())), preferred_element_type=F32)


def origin(index):
    lead = (index >> 4) * 18 + (index & 15)
    rest = index - LEAD
    tail = (rest >> 1) * 18 + 16 + (rest & 1)
    return jnp.where(index < LEAD, lead, tail)


def iota(shape, axis):
    return lax.broadcasted_iota(jnp.int32, shape, axis)


def onehot(mask):
    return mask.astype(F32).astype(BF)


def normal(values):
    center = values - jnp.mean(values, axis=-1, keepdims=True)
    rate = lax.rsqrt(jnp.mean(center * center, axis=-1, keepdims=True) + EPS)
    return center * rate, rate


def normal_back(unit, rate, gain, grad):
    inner = grad * gain
    first = jnp.mean(inner, axis=-1, keepdims=True)
    second = jnp.mean(inner * unit, axis=-1, keepdims=True)
    return rate * (inner - first - unit * second)


def exact_parts(values):
    high = values.astype(BF)
    rest = values - high.astype(F32)
    middle_part = rest.astype(BF)
    low = (rest - middle_part.astype(F32)).astype(BF)
    return jnp.concatenate([high, middle_part, low], axis=0)


def column_total(values):
    return jnp.sum(values, axis=0, keepdims=True)


def lanes(start, size):
    return pl.ds(pl.multiple_of(start, LANES), size)


def params(limit=60):
    return pltpu.CompilerParams(vmem_limit_bytes=limit << 20)


PERMUTED = np.concatenate(
    [np.arange(64)[:, None] * 18 + np.arange(16), np.arange(64)[:, None] * 18 + [16, 17]], axis=1
)
PERMUTED = np.concatenate([PERMUTED[:, :16].reshape(-1), PERMUTED[:, 16:].reshape(-1)])


def mix_matrix():
    matrix = np.zeros((D, D), np.float32)
    matrix[PERMUTED, np.arange(D)] = 1.0
    return matrix


def place_matrix():
    matrix = np.zeros((HEADS, HEAD_WIRE, D), np.float32)
    matrix[:, :HEAD_DIM] = mix_matrix().reshape(HEADS, HEAD_DIM, D)
    return matrix.reshape(HEADS * HEAD_WIRE, D)


def mesh_params(tag, limit=62):
    return pltpu.CompilerParams(
        collective_id=tag, has_side_effects=True, vmem_limit_bytes=limit << 20
    )


class Twin:
    def __init__(self, place, core, send, recv, base):
        self.core, self.device = core, device_at(place, 1 - core)
        self.send, self.recv, self.base = send, recv, base
        self.items = []

    def half(self, ref, axis, core):
        size = ref.shape[axis] // 2
        if axis == 0:
            return ref.at[pl.ds(pl.multiple_of(core * size, size), size)]
        lead = (slice(None),) * (len(ref.shape) - 1)
        return ref.at[lead + (pl.ds(pl.multiple_of(core * size, LANES), size),)]

    def give(self, source, target, axis):
        index = self.base + 2 * len(self.items)
        place = self.half(target, axis, self.core)
        pltpu.make_async_copy(source, place, self.recv.at[index + 1]).start()
        remote(source, place, self.send.at[index], self.recv.at[index], self.device).start()
        self.items.append((source, target, axis, index))

    def ready(self):
        for source, target, axis, index in self.items:
            place = self.half(target, axis, self.core)
            pltpu.make_async_copy(source, place, self.recv.at[index + 1]).wait()
            other = self.half(target, axis, 1 - self.core)
            remote(
                other, other, self.send.at[index], self.recv.at[index], self.device
            ).wait_recv()

    def pass_part(self, source, target, columns, number):
        index = self.base + 2 * number
        place = target.at[pl.ds(pl.multiple_of(self.core * 256, 256), 256), columns]
        pltpu.make_async_copy(source, place, self.recv.at[index + 1]).start()
        remote(source, place, self.send.at[index], self.recv.at[index], self.device).start()

    def part_done(self, target, columns, number):
        index = self.base + 2 * number
        place = target.at[pl.ds(pl.multiple_of(self.core * 256, 256), 256), columns]
        other = target.at[pl.ds(pl.multiple_of((1 - self.core) * 256, 256), 256), columns]
        pltpu.make_async_copy(place, place, self.recv.at[index + 1]).wait()
        copy = remote(other, other, self.send.at[index], self.recv.at[index], self.device)
        copy.wait_recv()
        copy.wait_send()

    def drain(self):
        for source, target, axis, index in self.items:
            place = self.half(target, axis, self.core)
            remote(
                place, place, self.send.at[index], self.recv.at[index], self.device
            ).wait_send()


def back_kernel(
    go,
    dpre,
    active,
    h_main,
    h_tail,
    g_main,
    g_tail,
    picture,
    packed_ref,
    keep_ref,
    share_ref,
    dheads,
    go_all,
    grads,
    wire,
    backs,
    dpre_all,
    active_all,
    h_main_all,
    h_tail_all,
    g_main_all,
    g_tail_all,
    extra,
    keys,
    queries,
    ids,
    dkeys,
    dvalues,
    found,
    row_ref,
    *rest,
):
    buffers, (send, recv, local) = rest[:-3], rest[-3:]
    place, core = here()
    red = Reducer(FIRST_WIDTHS, place, core, buffers, share_ref, send, recv)
    base = 3 * Reducer.SEMS
    ins = [Swapper(place, core, go, go_all, send, recv, base + 16 * m) for m in range(2)]
    base = base + 32
    outs = [Swapper(place, core, wire, dheads, send, recv, base + 16 * m) for m in range(2)]
    greet(line_peers(place, core) + swap_only(ins[0]))
    for micro in range(2):
        ins[micro].start(micro)
    loads = []
    for source, target in (
        (h_main, h_main_all),
        (h_tail, h_tail_all),
        (g_main, g_main_all),
        (g_tail, g_tail_all),
        (dpre.at[:, pl.ds(0, FIRST)], dpre_all),
        (active.at[:, pl.ds(0, FIRST)], active_all),
    ):
        copy = pltpu.make_async_copy(source, target, local.at[1 + len(loads)])
        copy.start()
        loads.append(copy)
    maker = Maker(
        red,
        [((h_main_all, h_tail_all), dpre_all), ((g_main_all, g_tail_all), active_all)],
        extra,
        FIRST_CHUNK,
    )
    ids_in = fetch_ids(picture, found, local.at[0])
    ids_in.start()
    ids_in.wait()
    for micro in range(2):
        row_ref[micro] = found[micro : micro + 1].astype(F32)
    for copy in loads:
        copy.wait()
    maker.run()
    ins[0].finish(0)

    def block(step, carry):
        row = lax.div(step, BLOCKS)
        index = lax.rem(step, BLOCKS)
        tokens = pl.ds(pl.multiple_of(row * 128, 128), 128)

        @pl.when(step == BLOCKS)
        def _():
            ins[1].finish(1)

        @pl.when(index == 0)
        def _():
            back_row = jnp.concatenate(
                [
                    jnp.zeros((VALUE_LANE, ROW), BF),
                    go_all[:, lanes(row * ROW, ROW)],
                    jnp.zeros((LANES - VALUE_LANE - HEAD_WIRE, ROW), BF),
                ],
                axis=0,
            )
            backs[...] = jnp.transpose(back_row)
            packed = packed_ref[:, tokens, :].reshape(ROW, WIDE)
            split_packed(packed, keys, queries)
            for part in range(ROW // LANES):
                span = slice(part * LANES, (part + 1) * LANES)
                ids[span, :] = column_ids(row_ref[row, :, span])
            dkeys[...] = jnp.zeros_like(dkeys)
            dvalues[...] = jnp.zeros_like(dvalues)

        rows = pl.ds(pl.multiple_of(index * QUERIES, QUERIES), QUERIES)

        def scan(count):
            start = jnp.where(index < 2, 0, BLOCKS - count)
            query = queries[rows, :]
            back = backs[rows, :]
            mine = row_ref[row, :, lanes(index * QUERIES, QUERIES)]
            kept = keep_ref[row, rows, :]
            inner = jnp.sum(back.astype(F32) * kept, axis=1, keepdims=True)
            lane = iota((QUERIES, LANES), 1)
            stats = jnp.transpose(jnp.where(lane == 0, kept, inner))
            logsum = stats[0:1]
            inner = stats[1:2]
            total = jnp.zeros((QUERIES, LANES), F32)
            for part in range(count):
                span = pl.ds(pl.multiple_of((start + part) * KEYS, KEYS), KEYS)
                blocks = pl.ds((start + part) * (KEYS // 128), KEYS // 128)
                value = packed_ref[blocks, tokens, LANES:].reshape(KEYS, LANES)
                allowed = jnp.concatenate([ids[span, :]] * (QUERIES // LANES), axis=1)
                score = dot_nt(keys[span, :], query) * (SCALE * LOG2E) - logsum
                prob = jnp.exp2(jnp.where(allowed == mine, score, NEG))
                grad = (prob * (dot_nt(value, back) - inner)).astype(BF)
                dvalues[span, :] += dot(prob.astype(BF), back)
                dkeys[span, :] += dot(grad, query)
                total = total + dot_tn(grad, keys[span, :])
            total = total * SCALE
            moved_q = jnp.concatenate(
                [
                    jnp.zeros((QUERIES, HEAD_DIM), F32),
                    total[:, :HEAD_DIM],
                    jnp.zeros((QUERIES, WIDE - 2 * HEAD_DIM), F32),
                ],
                axis=1,
            )
            grads[rows, :] = moved_q.astype(BF)

        edge = (index == 0) | (index == BLOCKS - 1)
        pl.when(edge)(functools.partial(scan, 3))
        pl.when(jnp.logical_not(edge))(functools.partial(scan, 4))

        @pl.when(index == BLOCKS - 1)
        def _():
            wide = jnp.concatenate([dkeys[...] * SCALE, dvalues[...]], axis=1)
            lane = iota((ROW, WIDE), 1)
            old = grads[...]
            inside = (lane >= HEAD_DIM) & (lane < 2 * HEAD_DIM)
            whole = jnp.where(inside, old, wide.astype(BF))
            wire[:, lanes(row * ROW, ROW)] = jnp.transpose(whole)[:WIRE]
            for micro in range(2):
                pl.when(row == micro)(functools.partial(outs[micro].start, micro))

        @pl.when(step == 1)
        def _():
            for spot in range(4):
                red.pass_on(spot)

        @pl.when(step >= 4)
        def _():
            red.gather_side(lax.rem(step - 4 + 1, 4), step == 7)

        return carry

    lax.fori_loop(0, 2 * BLOCKS, block, 0)
    red.line_up()
    red.share()
    red.close()
    for micro in range(2):
        outs[micro].finish(micro)
    for micro in range(2):
        ins[micro].drain(micro)
    for micro in range(2):
        outs[micro].drain(micro)


def attend_back_reduce(go, dpre, active, turned, packed, keep, picture, tag):
    any_ = pl.BlockSpec(memory_space=pl.ANY)
    vmem = pl.BlockSpec(memory_space=pltpu.VMEM)
    sems = 3 * Reducer.SEMS + 64
    return pl.pallas_call(
        back_kernel,
        out_shape=(
            jax.ShapeDtypeStruct((16, FIRST_TOTAL), BF),
            jax.ShapeDtypeStruct((16, WIRE, 256), BF),
        ),
        in_specs=[any_] * 8 + [vmem] * 2,
        out_specs=(vmem, any_),
        scratch_shapes=[
            pltpu.VMEM((HEAD_WIRE, 2 * ROW), BF),
            pltpu.VMEM((ROW, WIDE), BF),
            pltpu.VMEM((WIRE, 2 * ROW), BF),
            pltpu.VMEM((ROW, LANES), BF),
            pltpu.VMEM((512, FIRST), BF),
            pltpu.VMEM((512, FIRST), BF),
            pltpu.VMEM((4, 2, 4, 2, 16, 512), BF),
            pltpu.VMEM((TAIL, 512), BF),
            pltpu.VMEM((4, 2, 4, 2, 16, 512), BF),
            pltpu.VMEM((TAIL, 512), BF),
            pltpu.VMEM((FIRST_CHUNK // LANES, LEAD, LANES), F32),
            pltpu.VMEM((ROW, LANES), BF),
            pltpu.VMEM((ROW, LANES), BF),
            pltpu.VMEM((ROW, LANES), F32),
            pltpu.VMEM((ROW, LANES), F32),
            pltpu.VMEM((ROW, LANES), F32),
            pltpu.VMEM((2, ROW), jnp.int32),
            pltpu.VMEM((2, 1, ROW), F32),
        ]
        + Reducer.scratch(FIRST_WIDTHS)
        + [
            pltpu.SemaphoreType.DMA((sems,)),
            pltpu.SemaphoreType.DMA((sems,)),
            pltpu.SemaphoreType.DMA((7,)),
        ],
        compiler_params=mesh_params(tag),
        name="attend_back_reduce",
    )(go, dpre, active, *turned, picture, packed, keep)


VEC_ROWS = 16
VEC_QKV = 6
VEC_UP = 9


def spread_tail(source, chunk, wide, tail):
    for tile in range(chunk // LANES):
        wide[tile] = source(tile).astype(F32)
        for index in range(8):
            start = index * chunk + tile * LANES
            picked = wide[tile, pl.ds(index, TAIL, stride=8), :]
            tail[:, start : start + LANES] = picked.astype(BF)


def column_ids(row_ids):
    size = row_ids.shape[1]
    return jnp.transpose(jnp.broadcast_to(row_ids, (LANES, size)))


def fetch_ids(picture, found, sem):
    start = pl.multiple_of(lax.div(lax.axis_index("fsdp"), 8) * ROW, ROW)
    return pltpu.make_async_copy(picture.at[:, pl.ds(start, ROW)], found, sem)


def split_packed(packed, keys, queries):
    lane = iota((ROW, LANES), 1)
    zero = jnp.zeros((ROW, LANES), BF)
    keys[...] = jnp.where(lane < HEAD_DIM, packed[:, :LANES], zero)
    queries[...] = jnp.concatenate(
        [packed[:, HEAD_DIM : 2 * HEAD_DIM], jnp.zeros((ROW, LANES - HEAD_DIM), BF)], axis=1
    )


def swap_only(swapper):
    return [swapper.device(swapper.member(k)) for k in range(1, 16) if k not in (1, 4, 8, 12)]


def pack_rows(sources, width, chunk, slab, rest, block):
    slab[...] = jnp.zeros_like(slab)
    rest[...] = jnp.zeros_like(rest)
    for index, (ref, start, stop) in enumerate(sources):
        place = slice(index * width, index * width + stop - start)
        slab[:, place] = ref[0:16, start:stop]
        rest[:, place] = ref[16:18, start:stop].astype(F32)
    main = len(sources) * width
    for row in range(2):
        for index in range(8):
            spot = row * 8 + index
            block[spot : spot + 1, :chunk] = rest[
                row : row + 1, index * chunk : (index + 1) * chunk
            ]
    slab[:, main : main + chunk] = block[:, :chunk].astype(BF)


def front_kernel(
    slab,
    picture,
    tokens_ref,
    cotangent_ref,
    up_ref,
    down_ref,
    *refs,
):
    lines, rest = refs[:8], refs[8:]
    run_front(slab, picture, tokens_ref, cotangent_ref, up_ref, down_ref, lines, *rest)


def run_front(
    slab,
    picture,
    tokens_ref,
    cotangent_ref,
    up_ref,
    down_ref,
    lines,
    second_slab,
    x_ref,
    g_ref,
    tail_ref,
    out_tail_ref,
    mixed_vec_ref,
    packed_ref,
    keep_ref,
    o_all,
    weight_out,
    first_out,
    h_main_all,
    h_tail_all,
    first_slab,
    rest,
    rest_block,
    h_main,
    h_tail,
    full,
    low,
    flat,
    wide,
    tail,
    vec_ref,
    vec_parts,
    heads,
    wire,
    o_own,
    keys,
    queries,
    values,
    scores,
    found,
    row_ref,
    send,
    recv,
    local,
):
    place, core = here()
    red = Gatherer(ATTN_WIDTHS, place, core, slab, full, send, recv, 0)
    base = 3 * Gatherer.SEMS + 3
    first = Gatherer(FIRST_WIDTHS, place, core, first_slab, first_out, send, recv, base)
    base = 2 * base
    ins = [Swapper(place, core, heads, wire, send, recv, base + 16 * m) for m in range(2)]
    base = base + 32
    outs = [Swapper(place, core, o_own, o_all, send, recv, base + 16 * m) for m in range(2)]
    twin = Twin(place, core, send, recv, base + 32)
    greet(line_peers(place, core) + swap_only(ins[0]))
    red.start()
    pack_rows(
        [(up_ref, 0, FIRST), (down_ref, 0, FIRST)],
        FIRST,
        FIRST_CHUNK,
        first_slab,
        rest,
        rest_block,
    )
    first.start()
    ids_in = fetch_ids(picture, found, local.at[0])
    ids_in.start()
    for index, line in enumerate(lines):
        vec_ref[index : index + 1, :] = line[...].reshape(1, D)
    vec_parts[...] = exact_parts(vec_ref[...])

    def mix(index, carry):
        columns = lanes(index * LANES, LANES)
        column = onehot(iota((D, LANES), 0) == origin(index * LANES + iota((D, LANES), 1)))
        x_ref[:, columns] = dot(tokens_ref[...], column).astype(BF)
        g_ref[:, columns] = dot(cotangent_ref[...], column).astype(BF)
        parts = dot(vec_parts[...], column)
        mixed_vec_ref[:, columns] = parts[0:8] + parts[8:16] + parts[16:24]
        return carry

    lax.fori_loop(0, 3, mix, 0)
    red.second()
    lax.fori_loop(3, 9, mix, 0)
    pack_rows(
        [(up_ref, FIRST, FF), (down_ref, FIRST, FF)],
        SECOND,
        SECOND_CHUNK,
        second_slab,
        rest,
        rest_block,
    )
    unit, _ = normal(x_ref[...].astype(F32))
    low[...] = (unit * mixed_vec_ref[0:1] + mixed_vec_ref[1:2]).astype(BF)
    for steps in (1, 2, 3):
        red.third(steps)
    turned = jnp.transpose(low[...])
    h_main[...] = turned[:LEAD].reshape(4, 2, 4, 2, 16, 256)
    h_tail[...] = turned[LEAD:]
    twin.give(h_main, h_main_all, 5)
    twin.give(h_tail, h_tail_all, 1)
    ids_in.wait()
    for micro in range(2):
        row_ref[micro] = found[micro : micro + 1].astype(F32)
    for steps in range(4):
        red.fourth(steps)
    first.second()
    for steps in range(4):
        red.fifth(steps)
    red.close()
    leave = pltpu.make_async_copy(full, weight_out, local.at[1])
    leave.start()

    def packed_tile(tile):
        start = ATTN_MAIN + tile * LANES
        return full[:, :, :, :, :, start : start + LANES].reshape(LEAD, LANES)

    for steps in (1, 2, 3):
        first.third(steps)
    spread_tail(packed_tile, ATTN_CHUNK, wide, tail)
    tail_ref[...] = tail[:, :QKV]
    out_tail_ref[...] = tail[:, QKV:ATTN_MAIN]

    def columns(index, carry):
        span = lanes(index * 384, 384)
        weight = full[:, :, :, :, :, span].reshape(LEAD, 384)
        flat[:, span] = dot(low[:, :LEAD], weight) + dot(low[:, LEAD:], tail[:, span])
        return carry

    lax.fori_loop(0, QKV // 384, columns, 0)
    for head in range(HEADS):
        span = slice(head * HEAD_DIM, (head + 1) * HEAD_DIM)
        bias = jnp.concatenate(
            [jnp.zeros((1, HEAD_DIM), F32), vec_ref[6:7, span], vec_ref[7:8, span]], axis=1
        )
        block = flat[:, PACK * head : PACK * head + PACK] + bias
        block = jnp.concatenate([block, jnp.zeros((256, WIDE - PACK), F32)], axis=1)
        heads[head] = jnp.transpose(block.astype(BF))[:WIRE]
    ins[0].start(0)
    first.fourth(0)
    first.fourth(1)
    ins[1].start(1)
    ins[0].finish(0)

    def block(step, carry):
        row = lax.div(step, 8)
        index = lax.rem(step, 8)
        rows_of = pl.ds(pl.multiple_of(row * 128, 128), 128)

        @pl.when(step == 8)
        def _():
            ins[1].finish(1)

        @pl.when(index == 0)
        def _():
            packed = jnp.transpose(wire[:, lanes(row * ROW, ROW)])
            packed = jnp.concatenate([packed, jnp.zeros((ROW, WIDE - WIRE), BF)], axis=1)
            packed_ref[:, rows_of, :] = packed.reshape(16, 128, WIDE)
            split_packed(packed, keys, queries)
            lane = iota((ROW, LANES), 1)
            values[...] = jnp.where(
                lane == LANES - 1, jnp.ones((ROW, LANES), BF), packed[:, LANES:]
            )

        rows = pl.ds(pl.multiple_of(index * 256, 256), 256)

        def scan(count):
            start = jnp.where(index < 4, 0, ROW - 256 * count)
            query = queries[rows, :]
            mine = column_ids(row_ref[row, :, lanes(index * 256, 256)])
            mine = jnp.concatenate([mine, mine], axis=1)
            top = jnp.full((256, LANES), NEG, F32)
            for part in range(count):
                span = lanes(start + part * 256, 256)
                score = dot_nt(query, keys[span, :])
                score = jnp.where(mine == row_ref[row, :, span], score, NEG)
                scores[:, part * 256 : part * 256 + 256] = score
                top = jnp.maximum(top, jnp.maximum(score[:, :LANES], score[:, LANES:]))
            top = jnp.max(top, axis=1, keepdims=True)
            total = jnp.zeros((256, LANES), F32)
            for part in range(count):
                span = lanes(start + part * 256, 256)
                expo = jnp.exp2(
                    (scores[:, part * 256 : part * 256 + 256] - top) * (SCALE * LOG2E)
                )
                total = total + dot(expo.astype(BF), values[span, :])
            mass = total[:, LANES - 1 :]
            total = total / mass
            turned_o = jnp.transpose(total)[VALUE_LANE : VALUE_LANE + HEAD_WIRE]
            o_own[:, lanes(row * ROW + index * 256, 256)] = turned_o.astype(BF)
            lane = iota((256, LANES), 1)
            logsum = top * (SCALE * LOG2E) + jnp.log2(mass)
            keep_ref[row, rows, :] = jnp.where(lane == 0, logsum, total)

        for count in (5, 6, 7, 8):
            pl.when((index == count - 5) | (index == 12 - count))(functools.partial(scan, count))

        @pl.when(step == 2)
        def _():
            first.fourth(2)

        @pl.when(step == 4)
        def _():
            first.fourth(3)

        @pl.when((step >= 6) & (lax.rem(step, 2) == 0) & (step < 14))
        def _():
            first.fifth(lax.div(step - 6, 2))

        for micro in range(2):
            pl.when(step == 8 * micro + 7)(functools.partial(outs[micro].start, micro))
        return carry

    lax.fori_loop(0, 16, block, 0)
    first.close()
    leave.wait()
    red.drain()
    first.drain()
    for micro in range(2):
        ins[micro].drain(micro)
        outs[micro].finish(micro)
    for micro in range(2):
        outs[micro].drain(micro)
    twin.ready()
    twin.drain()


def front(slab, up, down, tokens, cotangent, lines, picture, tag):
    any_ = pl.BlockSpec(memory_space=pl.ANY)
    vmem = pl.BlockSpec(memory_space=pltpu.VMEM)
    sems = 2 * (3 * Gatherer.SEMS + 3) + 64 + 4
    full = (4, 2, 4, 2, 16, ATTN_TOTAL)
    return pl.pallas_call(
        front_kernel,
        out_shape=(
            jax.ShapeDtypeStruct((16, SECOND_TOTAL), BF),
            jax.ShapeDtypeStruct((256, D), BF),
            jax.ShapeDtypeStruct((256, D), BF),
            jax.ShapeDtypeStruct((TAIL, QKV), BF),
            jax.ShapeDtypeStruct((TAIL, D), BF),
            jax.ShapeDtypeStruct((8, D), F32),
            jax.ShapeDtypeStruct((16, 256, WIDE), BF),
            jax.ShapeDtypeStruct((2, ROW, LANES), F32),
            jax.ShapeDtypeStruct((16, HEAD_WIRE, 256), BF),
            jax.ShapeDtypeStruct(full, BF),
            jax.ShapeDtypeStruct((4, 2, 4, 2, 16, FIRST_TOTAL), BF),
            jax.ShapeDtypeStruct((4, 2, 4, 2, 16, 512), BF),
            jax.ShapeDtypeStruct((TAIL, 512), BF),
        ),
        in_specs=[any_] * 2 + [vmem] * 12,
        out_specs=(vmem,) * 8 + (any_,) * 5,
        scratch_shapes=[
            pltpu.VMEM((16, FIRST_TOTAL), BF),
            pltpu.VMEM((2, 8 * FIRST_CHUNK), F32),
            pltpu.VMEM((16, FIRST_CHUNK), F32),
            pltpu.VMEM((4, 2, 4, 2, 16, 256), BF),
            pltpu.VMEM((TAIL, 256), BF),
            pltpu.VMEM(full, BF),
            pltpu.VMEM((256, D), BF),
            pltpu.VMEM((256, QKV), F32),
            pltpu.VMEM((ATTN_CHUNK // LANES, LEAD, LANES), F32),
            pltpu.VMEM((TAIL, 8 * ATTN_CHUNK), BF),
            pltpu.VMEM((8, D), F32),
            pltpu.VMEM((24, D), BF),
            pltpu.VMEM((16, WIRE, 256), BF),
            pltpu.VMEM((WIRE, 2 * ROW), BF),
            pltpu.VMEM((HEAD_WIRE, 2 * ROW), BF),
            pltpu.VMEM((ROW, LANES), BF),
            pltpu.VMEM((ROW, LANES), BF),
            pltpu.VMEM((ROW, LANES), BF),
            pltpu.VMEM((256, ROW), F32),
            pltpu.VMEM((2, ROW), jnp.int32),
            pltpu.VMEM((2, 1, ROW), F32),
            pltpu.SemaphoreType.DMA((sems,)),
            pltpu.SemaphoreType.DMA((sems,)),
            pltpu.SemaphoreType.DMA((2,)),
        ],
        compiler_params=mesh_params(tag),
        name="front",
    )(slab, picture, tokens, cotangent, up, down, *lines)


def middle_kernel(
    attn,
    first,
    slab,
    o_ref,
    x_ref,
    g_ref,
    out_b_ref,
    vec_ref,
    bias_ref,
    place_ref,
    mixed_ref,
    do_ref,
    dmid_ref,
    gvec_ref,
    gbias_ref,
    dy_all,
    dpre_all,
    active_all,
    h_main_all,
    h_tail_all,
    g_main_all,
    g_tail_all,
    o_main_all,
    o_tail_all,
    dy,
    dpre_ref,
    active_ref,
    h_main_ref,
    h_tail_ref,
    g_main_ref,
    g_tail_ref,
    o_main_ref,
    o_tail_ref,
    out_a,
    weights,
    full,
    o_perm,
    mid,
    h2,
    result,
    dh2,
    wide,
    tail,
    bias,
    send,
    recv,
    local,
):
    place, core = here()
    red = Gatherer(SECOND_WIDTHS, place, core, slab, full, send, recv, 0)
    out_in = pltpu.make_async_copy(attn.at[:, pl.ds(QKV, D)], out_a, local.at[0])
    out_in.start()
    first_in = pltpu.make_async_copy(first, weights, local.at[1])
    first_in.start()
    base = 3 * Gatherer.SEMS + 3
    twin = Twin(place, core, send, recv, base)
    chunks = Twin(place, core, send, recv, base + 14)
    greet(line_peers(place, core) + [device_at(place, 1 - core)])
    red.start()
    bias[...] = jnp.zeros_like(bias)
    bias[:, :FF] = bias_ref[...].reshape(1, FF)
    blocks = jnp.transpose(o_ref[...].reshape(HEADS * HEAD_WIRE, 256))
    o_perm[...] = dot(blocks, place_ref[...]).astype(BF)
    red.second()
    out_in.wait()
    for part in range(3):
        columns = slice(384 * part, 384 * part + 384)
        value = dot(o_perm[:, :LEAD], out_a[:, columns])
        value = value + dot(o_perm[:, LEAD:], out_b_ref[:, columns])
        mid[:, columns] = x_ref[:, columns].astype(F32) + value + vec_ref[4:5, columns]
    unit, _ = normal(mid[...])
    h2[...] = (unit * vec_ref[2:3] + vec_ref[3:4]).astype(BF)
    for steps in (1, 2, 3):
        red.third(steps)

    def turn(value, main, rest, main_all, rest_all):
        turned = jnp.transpose(value)
        main[...] = turned[:LEAD].reshape(4, 2, 4, 2, 16, 256)
        rest[...] = turned[LEAD:]
        twin.give(main, main_all, 5)
        twin.give(rest, rest_all, 1)

    turn(o_perm[...], o_main_ref, o_tail_ref, o_main_all, o_tail_all)
    turn(h2[...], h_main_ref, h_tail_ref, h_main_all, h_tail_all)
    turn(g_ref[...], g_main_ref, g_tail_ref, g_main_all, g_tail_all)
    result[...] = jnp.zeros_like(result)
    dh2[...] = jnp.zeros_like(dh2)
    first_in.wait()

    def tile_of(ref, main):
        def read(tile):
            start = main + tile * LANES
            return ref[:, :, :, :, :, start : start + LANES].reshape(LEAD, LANES)

        return read

    spread_tail(tile_of(weights, 2 * FIRST), FIRST_CHUNK, wide, tail)

    def deliver(number, place_all):
        for item, (source, target) in enumerate(((dpre_ref, dpre_all), (active_ref, active_all))):
            chunks.pass_part(source.at[:, place_all], target, place_all, 2 * number + item)

    def chunk(ref, span, width, index, size, number):
        up_place = lanes(index * size, size)
        down_place = lanes(width + index * size, size)
        place_all = lanes(span + index * size, size)
        up = ref[:, :, :, :, :, up_place].reshape(LEAD, size)
        down = ref[:, :, :, :, :, down_place].reshape(LEAD, size)
        up_tail = tail[:, up_place]
        down_tail = tail[:, down_place]
        pre = dot(h2[:, :LEAD], up) + dot(h2[:, LEAD:], up_tail) + bias[:, place_all]
        square = pre * pre
        bend = jnp.tanh(TANH_A * pre * (1.0 + TANH_B * square))
        half = 0.5 * (1.0 + bend)
        active = (pre * half).astype(BF)
        slope = half + 0.5 * pre * (1.0 - bend * bend) * (TANH_A * (1.0 + 3.0 * TANH_B * square))
        back = dot(g_ref[:, :LEAD], down) + dot(g_ref[:, LEAD:], down_tail)
        dpre = (back * slope).astype(BF)
        active_ref[:, place_all] = active
        dpre_ref[:, place_all] = dpre
        active_t = jnp.transpose(active)
        dpre_t = jnp.transpose(dpre)
        result[:LEAD] += dot(down, active_t)
        result[LEAD:] += dot(down_tail, active_t)
        dh2[:LEAD] += dot(up, dpre_t)
        dh2[LEAD:] += dot(up_tail, dpre_t)
        gbias_ref[:, place_all] = column_total(dpre.astype(F32))
        deliver(number, place_all)

    def early(index, carry):
        chunk(weights, 0, FIRST, index, FIRST_STEP, index)

        @pl.when(index == 0)
        def _():
            for steps in range(4):
                red.fourth(steps)

        @pl.when(index == 2)
        def _():
            for steps in range(4):
                red.fifth(steps)

        return carry

    lax.fori_loop(0, FIRST // FIRST_STEP, early, 0)
    red.close()
    spread_tail(tile_of(full, 2 * SECOND), SECOND_CHUNK, wide, tail)

    def late(index, carry):
        chunk(full, FIRST, SECOND, index, SECOND_STEP, index + FIRST // FIRST_STEP)
        return carry

    lax.fori_loop(0, SECOND // SECOND_STEP, late, 0)
    red.drain()
    gain = vec_ref[2:3]
    unit, rate = normal(mid[...])
    grad = jnp.transpose(dh2[...])
    gvec_ref[...] = jnp.zeros_like(gvec_ref)
    gvec_ref[0:1] = column_total(grad * unit)
    gvec_ref[1:2] = column_total(grad)
    gvec_ref[3:4] = column_total(g_ref[...].astype(F32))
    dmid = g_ref[...].astype(F32) + normal_back(unit, rate, gain, grad)
    dmid_ref[...] = dmid
    dlow = dmid.astype(BF)
    dy[...] = dlow
    twin.give(dy, dy_all, 0)
    gvec_ref[2:3] = column_total(dlow.astype(F32))
    mixed_ref[...] = (mid[...] + jnp.transpose(result[...]) + vec_ref[5:6]).astype(BF)
    low_t = jnp.transpose(dlow)
    result[:LEAD] = dot(out_a[...], low_t)
    result[LEAD:] = dot(out_b_ref[...], low_t)
    value = dot(place_ref[...], result[...].astype(BF)).astype(BF)
    do_ref[...] = value.reshape(HEADS, HEAD_WIRE, 256)
    twin.ready()
    twin.drain()
    number = 0
    for start, stop, size in ((0, FIRST, FIRST_STEP), (FIRST, FF_PAD, SECOND_STEP)):
        for spot in range(start, stop, size):
            for item, target in enumerate((dpre_all, active_all)):
                chunks.part_done(target, pl.ds(spot, size), 2 * number + item)
            number += 1


def middle(attn, first, slab, o, x, g, out_tail, vec, bias, tag):
    any_ = pl.BlockSpec(memory_space=pl.ANY)
    vmem = pl.BlockSpec(memory_space=pltpu.VMEM)
    sems = 3 * Gatherer.SEMS + 3 + 14 + 24
    turned = [(4, 2, 4, 2, 16, 256), (TAIL, 256)] * 3
    both = [(4, 2, 4, 2, 16, 512), (TAIL, 512)] * 3
    place = place_matrix().astype(BF)
    found = pl.pallas_call(
        middle_kernel,
        out_shape=tuple(
            [
                jax.ShapeDtypeStruct((256, D), BF),
                jax.ShapeDtypeStruct((HEADS, HEAD_WIRE, 256), BF),
                jax.ShapeDtypeStruct((256, D), F32),
                jax.ShapeDtypeStruct((8, D), F32),
                jax.ShapeDtypeStruct((1, FF_PAD), F32),
                jax.ShapeDtypeStruct((512, D), BF),
                jax.ShapeDtypeStruct((512, FF_PAD), BF),
                jax.ShapeDtypeStruct((512, FF_PAD), BF),
            ]
            + [jax.ShapeDtypeStruct(shape, BF) for shape in both]
        ),
        in_specs=[any_] * 3 + [vmem] * 7,
        out_specs=(vmem,) * 5 + (any_,) * 9,
        scratch_shapes=[
            pltpu.VMEM((256, D), BF),
            pltpu.VMEM((256, FF_PAD), BF),
            pltpu.VMEM((256, FF_PAD), BF),
        ]
        + [pltpu.VMEM(shape, BF) for shape in turned]
        + [
            pltpu.VMEM((LEAD, D), BF),
            pltpu.VMEM((4, 2, 4, 2, 16, FIRST_TOTAL), BF),
            pltpu.VMEM((4, 2, 4, 2, 16, SECOND_TOTAL), BF),
            pltpu.VMEM((256, D), BF),
            pltpu.VMEM((256, D), F32),
            pltpu.VMEM((256, D), BF),
            pltpu.VMEM((D, 256), F32),
            pltpu.VMEM((D, 256), F32),
            pltpu.VMEM((FIRST_CHUNK // LANES, LEAD, LANES), F32),
            pltpu.VMEM((TAIL, 8 * FIRST_CHUNK), BF),
            pltpu.VMEM((1, FF_PAD), F32),
            pltpu.SemaphoreType.DMA((sems,)),
            pltpu.SemaphoreType.DMA((sems,)),
            pltpu.SemaphoreType.DMA((2,)),
        ],
        compiler_params=mesh_params(tag),
        name="middle",
    )(attn, first, slab, o, x, g, out_tail, vec, bias, place)
    return found[:8], found[12:14], found[8:10], found[10:12]


class Everyone:
    def __init__(self, place, core, slots, send, recv, base):
        self.place, self.core = place, core
        self.slots, self.send, self.recv, self.base = slots, send, recv, base

    def start(self, stage, value):
        if stage == 3:
            spot, targets = self.core, [(1, device_at(self.place, 1 - self.core))]
        else:
            axis = AXES[stage]
            spot = self.place[axis]
            targets = [
                (over, device_at(moved(self.place, axis, over), self.core)) for over in (2, 1, 3)
            ]
        self.slots[stage, spot] = value.astype(BF)
        for over, device in targets:
            index = self.base + stage * 3 + over - 1
            slot = self.slots.at[stage, spot]
            remote(slot, slot, self.send.at[index], self.recv.at[index], device).start()

    def finish(self, stage):
        count = 2 if stage == 3 else 4
        for over in range(1, count):
            index = self.base + stage * 3 + over - 1
            spot = 1 - self.core if stage == 3 else cycle(self.place[AXES[stage]], 4 - over)
            slot = self.slots.at[stage, spot]
            remote(
                slot, slot, self.send.at[index], self.recv.at[index], device_at(self.place, self.core)
            ).wait_recv()
        total = self.slots[stage, 0].astype(F32)
        for spot in range(1, count):
            total = total + self.slots[stage, spot].astype(F32)
        return total

    def drain(self):
        for stage in range(4):
            for over in range(1, 2 if stage == 3 else 4):
                index = self.base + stage * 3 + over - 1
                slot = self.slots.at[stage, 0]
                remote(
                    slot,
                    slot,
                    self.send.at[index],
                    self.recv.at[index],
                    device_at(self.place, self.core),
                ).wait_send()


def finish_kernel(
    dheads,
    weight,
    dy,
    dpre,
    active,
    h_main,
    h_tail,
    o_main,
    o_tail,
    h2_main,
    h2_tail,
    g_main,
    g_tail,
    tail_ref,
    x_ref,
    dmid_ref,
    vec_ref,
    gvec_ref,
    gup_ref,
    tokens_ref,
    total_ref,
    share_ref,
    second_ref,
    dheads_all,
    weight_all,
    flat,
    flat_all,
    dy_all,
    dpre_all,
    active_all,
    h_main_all,
    h_tail_all,
    o_main_all,
    o_tail_all,
    h2_main_all,
    h2_tail_all,
    g_main_all,
    g_tail_all,
    extra,
    dh,
    vectors,
    slots,
    *rest,
):
    buffers, (send, recv, local) = rest[:-3], rest[-3:]
    place, core = here()
    red = Reducer(ATTN_WIDTHS, place, core, buffers[:18], share_ref, send, recv)
    base = 3 * Reducer.SEMS
    late = Reducer(SECOND_WIDTHS, place, core, buffers[18:], second_ref, send, recv, base)
    base = 2 * base
    twin = Twin(place, core, send, recv, base)
    every = Everyone(place, core, slots, send, recv, base + 2)
    heads_in = pltpu.make_async_copy(dheads, dheads_all, local.at[0])
    heads_in.start()
    weight_in = pltpu.make_async_copy(weight.at[:, pl.ds(0, QKV)], weight_all, local.at[1])
    weight_in.start()
    greet(line_peers(place, core) + [device_at(place, 1 - core)])
    loads = []
    for source, target in (
        (h_main, h_main_all),
        (h_tail, h_tail_all),
        (o_main, o_main_all),
        (o_tail, o_tail_all),
        (dy, dy_all),
        (h2_main, h2_main_all),
        (h2_tail, h2_tail_all),
        (g_main, g_main_all),
        (g_tail, g_tail_all),
        (dpre.at[:, pl.ds(FIRST, SECOND)], dpre_all),
        (active.at[:, pl.ds(FIRST, SECOND)], active_all),
    ):
        copy = pltpu.make_async_copy(source, target, local.at[2 + len(loads)])
        copy.start()
        loads.append(copy)
    heads_in.wait()
    for head in range(HEADS):
        flat[:, PACK * head : PACK * head + PACK] = jnp.transpose(dheads_all[head])[:, :PACK]
    twin.give(flat, flat_all, 0)

    late_maker = Maker(
        late,
        [((h2_main_all, h2_tail_all), dpre_all), ((g_main_all, g_tail_all), active_all)],
        extra.at[pl.ds(0, SECOND_CHUNK // LANES)],
        SECOND_CHUNK,
    )
    maker = Maker(
        red,
        [((h_main_all, h_tail_all), flat_all), ((o_main_all, o_tail_all), dy_all)],
        extra,
        ATTN_CHUNK,
    )
    for copy in loads:
        copy.wait()
    late_maker.run()
    twin.ready()
    maker.run()
    dh[...] = jnp.zeros_like(dh)
    vectors[...] = jnp.zeros((VEC_ROWS, D), F32)
    vectors[2:6] = gvec_ref[:4]
    for row in range(4):
        span = slice(row * D, min((row + 1) * D, FF_PAD))
        vectors[VEC_UP + row : VEC_UP + row + 1, : span.stop - span.start] = gup_ref[:, span]
    weight_in.wait()

    for row in range(3):

        def columns(index, carry):
            span = lanes(row * D + index * 384, 384)
            value = flat[:, span]
            vectors[VEC_QKV + row : VEC_QKV + row + 1, lanes(index * 384, 384)] = column_total(
                value.astype(F32)
            )
            value_t = jnp.transpose(value)
            dh[:LEAD] += dot(weight_all[:, span], value_t)
            dh[LEAD:] += dot(tail_ref[:, span], value_t)
            return carry

        lax.fori_loop(0, 3, columns, 0)
    for spot in range(4):
        late.pass_on(spot)
    unit, rate = normal(x_ref[...].astype(F32))
    grad = jnp.transpose(dh[...])
    vectors[0:1] = column_total(grad * unit)
    vectors[1:2] = column_total(grad)
    every.start(0, vectors[...])
    for spot in range(4):
        red.pass_on(spot)
    total = dmid_ref[...] + normal_back(unit, rate, vec_ref[0:1], grad)
    tokens_ref[...] = total.astype(BF)
    every.start(1, every.finish(0))
    for over in (2, 1, 3):
        late.gather_side(over, False)
    late.gather_side(0, True)
    every.start(2, every.finish(1))
    for over in (2, 1, 3):
        red.gather_side(over, False)
    red.gather_side(0, True)
    every.start(3, every.finish(2))
    late.line_up()
    red.line_up()
    late.share()
    total_ref[...] = every.finish(3)
    red.share()
    late.close()
    red.close()
    twin.drain()
    every.drain()


def finish(dheads, weight, dy, dpre, active, turned, tail, x, dmid, vec, gvec, gup, tag):
    any_ = pl.BlockSpec(memory_space=pl.ANY)
    vmem = pl.BlockSpec(memory_space=pltpu.VMEM)
    sems = 6 * Reducer.SEMS + 2 + 12
    rows = [pltpu.VMEM((4, 2, 4, 2, 16, 512), BF), pltpu.VMEM((TAIL, 512), BF)]
    return pl.pallas_call(
        finish_kernel,
        out_shape=(
            jax.ShapeDtypeStruct((256, D), BF),
            jax.ShapeDtypeStruct((VEC_ROWS, D), F32),
            jax.ShapeDtypeStruct((16, ATTN_TOTAL), BF),
            jax.ShapeDtypeStruct((16, SECOND_TOTAL), BF),
        ),
        in_specs=[any_] * 13 + [vmem] * 6,
        out_specs=(vmem,) * 4,
        scratch_shapes=[
            pltpu.VMEM((HEADS, WIRE, 256), BF),
            pltpu.VMEM((LEAD, QKV), BF),
            pltpu.VMEM((256, QKV), BF),
            pltpu.VMEM((512, QKV), BF),
            pltpu.VMEM((512, D), BF),
            pltpu.VMEM((512, SECOND), BF),
            pltpu.VMEM((512, SECOND), BF),
        ]
        + rows * 4
        + [
            pltpu.VMEM((ATTN_CHUNK // LANES, LEAD, LANES), F32),
            pltpu.VMEM((D, 256), F32),
            pltpu.VMEM((VEC_ROWS, D), F32),
            pltpu.VMEM((4, 4, VEC_ROWS, D), BF),
        ]
        + Reducer.scratch(ATTN_WIDTHS)
        + Reducer.scratch(SECOND_WIDTHS)
        + [
            pltpu.SemaphoreType.DMA((sems,)),
            pltpu.SemaphoreType.DMA((sems,)),
            pltpu.SemaphoreType.DMA((13,)),
        ],
        compiler_params=mesh_params(tag),
        name="finish",
    )(dheads, weight, dy, dpre, active, *turned, tail, x, dmid, vec, gvec, gup)


def close_kernel(
    totals_ref,
    attn_ref,
    first_ref,
    second_ref,
    mixed_in,
    tokens_in,
    unmix_ref,
    mixed_ref,
    tokens_ref,
    query_ref,
    key_ref,
    value_ref,
    out_ref,
    up_ref,
    down_ref,
    gain1_ref,
    bias1_ref,
    gain2_ref,
    bias2_ref,
    bias_out_ref,
    bias_down_ref,
    bias_query_ref,
    bias_value_ref,
    bias_up_ref,
    attn,
    first,
    second,
    vec,
    stack,
):
    def unpack(share, full, main, chunk):
        full[0:16, :] = share[:, :main].astype(F32)
        rest = share[:, main : main + chunk].astype(F32)
        for row in range(2):
            for index in range(8):
                size = min(main - index * chunk, chunk)
                if size > 0:
                    start = index * chunk
                    spot = row * 8 + index
                    full[16 + row : 17 + row, start : start + size] = rest[
                        spot : spot + 1, :size
                    ]

    unpack(attn_ref, attn, ATTN_MAIN, ATTN_CHUNK)
    unpack(first_ref, first, 2 * FIRST, FIRST_CHUNK)
    unpack(second_ref, second, 2 * SECOND, SECOND_CHUNK)
    for head in range(HEADS):
        span = slice(head * HEAD_DIM, (head + 1) * HEAD_DIM)
        for index, ref in enumerate((key_ref, query_ref, value_ref)):
            start = head * PACK + index * HEAD_DIM
            ref[:, span] = attn[:18, start : start + HEAD_DIM]
    stack[0:256] = mixed_in[...]
    stack[256:512] = tokens_in[...]
    stack[512:544] = jnp.concatenate(
        [attn[:, QKV:ATTN_MAIN].astype(BF), jnp.zeros((8, D), BF)], axis=0
    )
    stack[544:576] = jnp.concatenate(
        [exact_parts(totals_ref[0:8, :]), jnp.zeros((8, D), BF)], axis=0
    )
    for part in range(3):
        columns = slice(384 * part, 384 * part + 384)
        value = dot(stack[...], unmix_ref[:, columns])
        mixed_ref[:, columns] = value[0:256].astype(BF)
        tokens_ref[:, columns] = value[256:512].astype(BF)
        out_ref[:, columns] = value[512:530]
        vec[0:8, columns] = value[544:552] + value[552:560] + value[560:568]
    lines = (gain1_ref, bias1_ref, gain2_ref, bias2_ref, bias_out_ref, bias_down_ref)
    for index, ref in enumerate(lines):
        ref[...] = vec[index : index + 1, :D].reshape(D)
    for row in range(3):
        vec[8:9, row * D : (row + 1) * D] = totals_ref[VEC_QKV + row : VEC_QKV + row + 1, :]
    for head in range(HEADS):
        span = slice(head * HEAD_DIM, (head + 1) * HEAD_DIM)
        for index, row in ((1, 9), (2, 10)):
            start = head * PACK + index * HEAD_DIM
            vec[row : row + 1, span] = vec[8:9, start : start + HEAD_DIM]
    bias_query_ref[...] = vec[9:10, :D].reshape(D)
    bias_value_ref[...] = vec[10:11, :D].reshape(D)
    for row in range(4):
        size = min(FF - row * D, D)
        vec[11:12, row * D : row * D + size] = totals_ref[
            VEC_UP + row : VEC_UP + row + 1, :size
        ]
    bias_up_ref[...] = vec[11:12, :FF].reshape(FF)
    up_ref[:, :FIRST] = first[:18, :FIRST]
    up_ref[:, FIRST:] = second[:18, : FF - FIRST]
    down_ref[:, :FIRST] = first[:18, FIRST : 2 * FIRST]
    down_ref[:, FIRST:] = second[:18, SECOND : SECOND + FF - FIRST]


def close_layer(totals, attn, first, second, mixed, tokens):
    line = jax.ShapeDtypeStruct((D,), F32)
    square = jax.ShapeDtypeStruct((18, D), F32)
    return pl.pallas_call(
        close_kernel,
        out_shape=(
            jax.ShapeDtypeStruct((256, D), BF),
            jax.ShapeDtypeStruct((256, D), BF),
            square,
            square,
            square,
            square,
            jax.ShapeDtypeStruct((18, FF), F32),
            jax.ShapeDtypeStruct((18, FF), F32),
            *([line] * 8),
            jax.ShapeDtypeStruct((FF,), F32),
        ),
        scratch_shapes=[
            pltpu.VMEM((24, ATTN_MAIN), F32),
            pltpu.VMEM((24, 2 * FIRST), F32),
            pltpu.VMEM((24, 2 * SECOND), F32),
            pltpu.VMEM((16, 4 * D), F32),
            pltpu.VMEM((576, D), BF),
        ],
        compiler_params=params(),
        name="close_layer",
    )(totals, attn, first, second, mixed, tokens, mix_matrix().T.astype(BF))


def pack_slab(weight, chunk, total):
    width = weight.shape[1]
    rest = jnp.pad(weight[16:], ((0, 0), (0, 8 * chunk - width))).reshape(16, chunk)
    return jnp.concatenate(
        [weight[:16], rest, jnp.zeros((16, total - width - chunk), weight.dtype)], axis=1
    )


def by_head(key, query, value):
    rows = key.shape[0]
    parts = [item.reshape(rows, HEADS, 1, HEAD_DIM) for item in (key, query, value)]
    return jnp.concatenate(parts, axis=2).reshape(rows, QKV)


def mixing():
    return onehot(iota((D, D), 0) == origin(iota((D, D), 1)))


def body(
    tokens,
    picture,
    cotangent,
    ln1_gain,
    ln1_bias,
    w_query,
    b_query,
    w_key,
    w_value,
    b_value,
    w_out,
    b_out,
    ln2_gain,
    ln2_bias,
    w_fc1,
    b_fc1,
    w_fc2,
    b_fc2,
):
    mix = mixing()
    out_cols = dot(w_out, mix).astype(BF)
    attn_slab = pack_slab(
        jnp.concatenate([by_head(w_key, w_query, w_value), out_cols], axis=1),
        ATTN_CHUNK,
        ATTN_TOTAL,
    )
    lines = (ln1_gain, ln1_bias, ln2_gain, ln2_bias, b_out, b_fc2, b_query, b_value)
    second_slab, x, g, attn_tail, out_tail, vec, packed, keep, o, attn, first, h_main, h_tail = front(
        attn_slab,
        w_fc1,
        w_fc2.T,
        tokens.reshape(256, D),
        cotangent.reshape(256, D),
        lines,
        picture,
        0,
    )
    attn = attn.reshape(LEAD, ATTN_TOTAL)
    (mixed, go, dmid, gvec2, gbias1, dy, dpre, active), o_turned, h_turned, g_turned = middle(
        attn, first, second_slab, o, x, g, out_tail, vec, b_fc1, 2
    )
    first_share, dheads = attend_back_reduce(
        go, dpre, active, (*h_turned, *g_turned), packed, keep, picture, 3
    )
    gtokens, totals, attn_share, second_share = finish(
        dheads,
        attn,
        dy,
        dpre,
        active,
        (h_main, h_tail, *o_turned, *h_turned, *g_turned),
        attn_tail,
        x,
        dmid,
        vec,
        gvec2,
        gbias1,
        4,
    )
    (
        mixed,
        gtokens,
        grad_query,
        grad_key,
        grad_value,
        grad_out,
        grad_up,
        grad_down,
        grad_gain1,
        grad_bias1,
        grad_gain2,
        grad_bias2,
        grad_b_out,
        grad_b_fc2,
        grad_b_query,
        grad_b_value,
        grad_b_fc1,
    ) = close_layer(totals, attn_share, first_share, second_share, mixed, gtokens)
    return (
        mixed.reshape(2, 128, D),
        gtokens.reshape(2, 128, D),
        grad_gain1,
        grad_bias1,
        grad_query,
        grad_b_query,
        grad_key,
        grad_value,
        grad_b_value,
        grad_out,
        grad_b_out,
        grad_gain2,
        grad_bias2,
        grad_up,
        grad_b_fc1,
        grad_down.T,
        grad_b_fc2,
    )


def solution(mesh):
    placed = (
        P(None, ("fsdp", "rep"), None),
        P(),
        P(None, ("fsdp", "rep"), None),
        P(),
        P(),
        P("fsdp", None),
        P(),
        P("fsdp", None),
        P("fsdp", None),
        P(),
        P("fsdp", None),
        P(),
        P(),
        P(),
        P("fsdp", None),
        P(),
        P(None, "fsdp"),
        P(),
    )
    return jax.shard_map(
        body,
        mesh=mesh,
        in_specs=placed,
        out_specs=(
            P(None, ("fsdp", "rep"), None),
            P(None, ("fsdp", "rep"), None),
            P(),
            P(),
            P("fsdp", None),
            P(),
            P("fsdp", None),
            P("fsdp", None),
            P(),
            P("fsdp", None),
            P(),
            P(),
            P(),
            P("fsdp", None),
            P(),
            P(None, "fsdp"),
            P(),
        ),
        check_vma=False,
    )
```
